32 devices in a mesh: dp: 4 (over y, x), cp: 8 (over z, core).
Axes of the slice: x: 2, y: 2, z: 4, core: 2. Of those that a mesh axis runs over, the one named last changes fastest.
Arguments:
- tokens: bfloat16 [4096, 1536], P(('dp', 'cp')), may hold values from -6 to 6
- output_cotangent: bfloat16 [4096, 1536], P(('dp', 'cp')), may hold values from -6 to 6
- sequence_lengths: int32 [4, 4], P('dp'), may hold values from 1 to 512, as said below
- block_order: int32 [4, 8], P('dp'), may hold values from 0 to 7, as said below
- attn_input: float32 [1536, 2560], P(('dp', 'cp')), may hold values from -0.15625 to 0.15625
- input_moment: float32 [1536, 2560], P(('dp', 'cp')), may hold values from -40 to 40
- input_square: float32 [1536, 2560], P(('dp', 'cp')), may hold values from 217.088 to 860.16
- attn_output: float32 [1536, 1536], P(('dp', 'cp')), may hold values from -1.25 to 1.25
- output_moment: float32 [1536, 1536], P(('dp', 'cp')), may hold values from -5 to 5
- output_square: float32 [1536, 1536], P(('dp', 'cp')), may hold values from 3.36 to 13.6
- gate_up: float32 [1536, 13824], P(('dp', 'cp')), may hold values from -0.15625 to 0.15625
- gateup_moment: float32 [1536, 13824], P(('dp', 'cp')), may hold values from -8 to 8
- gateup_square: float32 [1536, 13824], P(('dp', 'cp')), may hold values from 8.6016 to 34.4064
- down_weight: float32 [6912, 1536], P(('dp', 'cp')), may hold values from -0.078125 to 0.078125
- down_moment: float32 [6912, 1536], P(('dp', 'cp')), may hold values from -20 to 20
- down_square: float32 [6912, 1536], P(('dp', 'cp')), may hold values from 53.248 to 217.088
- norm_gains: float32 [3200], replicated, may hold values from 0.5 to 1.5
- gains_moment: float32 [3200], replicated, may hold values from -40 to 40
- gains_square: float32 [3200], replicated, may hold values from 217.088 to 860.16
Outputs:
- mixed: bfloat16 [4096, 1536], P(('dp', 'cp'))
- token_gradient: float32 [4096, 1536], P(('dp', 'cp'))
- input_next: float32 [1536, 2560], P(('dp', 'cp'))
- input_moment_next: float32 [1536, 2560], P(('dp', 'cp'))
- input_square_next: float32 [1536, 2560], P(('dp', 'cp'))
- output_next: float32 [1536, 1536], P(('dp', 'cp'))
- output_moment_next: float32 [1536, 1536], P(('dp', 'cp'))
- output_square_next: float32 [1536, 1536], P(('dp', 'cp'))
- gateup_next: float32 [1536, 13824], P(('dp', 'cp'))
- gateup_moment_next: float32 [1536, 13824], P(('dp', 'cp'))
- gateup_square_next: float32 [1536, 13824], P(('dp', 'cp'))
- down_next: float32 [6912, 1536], P(('dp', 'cp'))
- down_moment_next: float32 [6912, 1536], P(('dp', 'cp'))
- down_square_next: float32 [6912, 1536], P(('dp', 'cp'))
- gains_next: float32 [3200], replicated
- gains_moment_next: float32 [3200], replicated
- gains_square_next: float32 [3200], replicated
The draws below stay inside these ranges and needn't reach their ends.
Inputs may be any that keep to these rules, and one draw needn't show every extreme that they name: `sequence_lengths`: each row holds 4 lengths, packed in order into its group's 1024 positions and summing to 1024; the largest in each row is exactly 512. `block_order`: each row is a permutation of the 8 blocks of its group's packed tokens.
All inputs are finite; a program needn't handle non-finite values.
Results may differ from the reference program's by a relative error of at most 0.025.
Values may be sent and summed in bfloat16 or wider, within the bound.
A program may use at most 384 MiB of HBM per device.

```python
import math
import jax
import jax.numpy as jnp
from jax import lax

D = 1536
HEADS = 24
KV_HEADS = 8
HEAD_DIM = 64
FF = 6912
TOK_DEV = 128
SEQS = 4
STEP = 10
TOKENS = 4096
GROUP_TOK = 1024
MAXLEN = 512
QW = 1536
KVW = 512
KBLOCK = 512
N_DP = 4
N_CP = 8


def sequence_layout(key):
    remain = GROUP_TOK - MAXLEN
    group_keys = jax.random.split(key, N_DP)

    def one_group(group_key):
        long_key = jax.random.fold_in(group_key, 1)
        cut_key = jax.random.fold_in(group_key, 2)
        order_key = jax.random.fold_in(group_key, 3)
        long_index = jax.random.randint(long_key, (), 0, SEQS)
        cut_points = jnp.sort(jax.random.permutation(cut_key, remain - 1)[:SEQS - 2] + 1).astype(jnp.int32)
        bounds = jnp.concatenate([jnp.zeros((1,), jnp.int32), cut_points, jnp.full((1,), remain, jnp.int32)])
        others = bounds[1:] - bounds[:-1]
        slots = jnp.arange(SEQS, dtype=jnp.int32)
        below = jnp.clip(slots, 0, SEQS - 2)
        above = jnp.clip(slots - 1, 0, SEQS - 2)
        lengths = jnp.where(slots < long_index, others[below], jnp.where(slots == long_index, MAXLEN, others[above])).astype(jnp.int32)
        before = jnp.sum(jnp.where(slots < long_index, lengths, 0))
        first_block = before // TOK_DEV
        last_block = (before + MAXLEN - 1) // TOK_DEV
        priority = jax.random.permutation(order_key, N_CP).astype(jnp.int32)
        blocks = jnp.arange(N_CP, dtype=jnp.int32)
        priority = jnp.where(blocks == first_block, -1, jnp.where(blocks == last_block, N_CP, priority))
        order = jnp.argsort(priority, stable=True).astype(jnp.int32)
        return (lengths, order)
    return jax.vmap(one_group)(group_keys)


def draw_sequence_lengths(key, part):
    return sequence_layout(key)[0]


def draw_block_order(key, part):
    return sequence_layout(key)[1]


def strengthened(values, key, source, target, blocks, factor):
    def block_of(position):
        return (jnp.arange(values.shape[position]) // (values.shape[position] // blocks)).reshape((-1,) + (1,) * (values.ndim - 1 - position))

    first = jax.random.permutation(key, blocks)[block_of(target)]
    far = (block_of(target) + blocks // 2) % blocks
    return jnp.where((block_of(source) == first) | (block_of(source) == far), factor * values, values)


def shard_levels(key, dims, cuts, low, top_value):
    def one(dim, shards_of):
        draws = jax.random.uniform(jax.random.fold_in(jax.random.fold_in(key, 6), dim), (shards_of,), jnp.float32, low / len(cuts), top_value / len(cuts))
        return jnp.repeat(jnp.exp(draws), dims[dim] // shards_of).reshape((-1,) + (1,) * (len(dims) - dim - 1))

    level = one(*cuts[0])
    for cut in cuts[1:]:
        level = level * one(*cut)
    return level


def scatter_about(key, dims, scale, most, cuts=(), held_as=jnp.bfloat16):
    array = jax.random.normal(key, dims, jnp.float32) * scale
    if len(cuts) > 0:
        array = shard_levels(key, dims, cuts, -0.22, 0.18) * array
    return jnp.clip(array, min=-most, max=most).astype(held_as)


def heavy_noise(own_key, dims, scale, most, cuts, heavy, kind=jnp.bfloat16):
    array = scale * jax.random.normal(own_key, dims, jnp.float32)
    if cuts:
        array = array * shard_levels(own_key, dims, cuts, -0.22, 0.18)
    return jnp.clip(strengthened(array, jax.random.fold_in(own_key, 3), *heavy), -most, most).astype(kind)


def setup_inputs(seed: int = 0) -> dict:
    streams_of = jax.random.split(jax.random.key(seed), 20)
    return {
        "tokens": heavy_noise(streams_of[0], (TOKENS, D), 1.0, 6.0, ((0, 32),), (0, 1, 32, 2.75)),
        "output_cotangent": scatter_about(streams_of[1], (TOKENS, D), 1.0, 6.0, ((0, 32),)),
        "sequence_lengths": draw_sequence_lengths(jax.random.fold_in(streams_of[19], 71), 0),
        "block_order": draw_block_order(jax.random.fold_in(streams_of[19], 71), 0),
        "attn_input": scatter_about(streams_of[4], (D, QW + 2 * KVW), D ** -0.5, 0.15625, ((0, 32),), jnp.float32),
        "input_moment": scatter_about(streams_of[5], (D, QW + 2 * KVW), (0.11 * TOKENS ** 0.5), 40.0, ((0, 32),), jnp.float32),
        "input_square": jnp.clip(jnp.exp(math.log(860.16) - 1.3768156 * jax.random.uniform(streams_of[6], (D, QW + 2 * KVW), jnp.float32) ** shard_levels(streams_of[6], (D, QW + 2 * KVW), ((0, 32),), -0.2, 0.2)), 217.088, 860.16),
        "attn_output": scatter_about(streams_of[7], (QW, D), (max(QW * 16 // GROUP_TOK, 1)) ** -0.5, 1.25, ((0, 32),), jnp.float32),
        "output_moment": scatter_about(streams_of[8], (QW, D), (0.44 * N_DP ** 0.5), 5.0, ((0, 32),), jnp.float32),
        "output_square": jnp.clip(jnp.exp(math.log(13.6) - 1.3981289 * jax.random.uniform(streams_of[9], (QW, D), jnp.float32) ** shard_levels(streams_of[9], (QW, D), ((0, 32),), -0.2, 0.2)), 3.36, 13.6),
        "gate_up": scatter_about(streams_of[10], (D, 2 * FF), D ** -0.5, 0.15625, ((0, 32),), jnp.float32),
        "gateup_moment": scatter_about(streams_of[11], (D, 2 * FF), (0.022 * TOKENS ** 0.5), 8.0, ((0, 32),), jnp.float32),
        "gateup_square": jnp.clip(jnp.exp(math.log(34.4064) - 1.3862944 * jax.random.uniform(streams_of[12], (D, 2 * FF), jnp.float32) ** shard_levels(streams_of[12], (D, 2 * FF), ((0, 32),), -0.2, 0.2)), 8.6016, 34.4064),
        "down_weight": scatter_about(streams_of[13], (FF, D), FF ** -0.5, 0.078125, ((0, 32),), jnp.float32),
        "down_moment": scatter_about(streams_of[14], (FF, D), (0.055 * TOKENS ** 0.5), 20.0, ((0, 32),), jnp.float32),
        "down_square": jnp.clip(jnp.exp(math.log(217.088) - 1.40534252 * jax.random.uniform(streams_of[15], (FF, D), jnp.float32) ** shard_levels(streams_of[15], (FF, D), ((0, 32),), -0.2, 0.2)), 53.248, 217.088),
        "norm_gains": jnp.clip(1.0 + 0.1 * jax.random.normal(streams_of[16], (2 * D + 2 * HEAD_DIM,), jnp.float32), 0.5, 1.5),
        "gains_moment": scatter_about(streams_of[17], (2 * D + 2 * HEAD_DIM,), (0.11 * TOKENS ** 0.5), 40.0, (), jnp.float32),
        "gains_square": jnp.clip(jnp.exp(jax.random.uniform(streams_of[18], (2 * D + 2 * HEAD_DIM,), jnp.float32, math.log(217.088), math.log(860.16))), 217.088, 860.16),
    }


norm_eps = 1e-05
rope_base = 1000000.0
beta_one = 0.9
beta_two = 0.95
adam_eps = 1e-08
rate_input = 0.06
rate_output = 0.9
rate_gateup = 0.06
rate_down = 0.03
rate_gains = 0.5
weight_decay = 0.1
masked_score = -1e+30
highest = lax.Precision.HIGHEST

@jax.custom_vjp
def low(v):
    return lax.optimization_barrier(v.astype(jnp.bfloat16)).astype(jnp.float32)

@jax.custom_vjp
def low_back(v):
    return v

def low_keep(v):
    return (low(v), None)

def low_pass(kept, grad):
    return (grad,)

def back_keep(v):
    return (v, None)

def back_low(kept, grad):
    return (low(grad),)
low.defvjp(low_keep, low_pass)
low_back.defvjp(back_keep, back_low)

def rms_norm(values, gain):
    return values * lax.rsqrt(lax.optimization_barrier(jnp.mean(values * values, axis=-1, keepdims=True)) + norm_eps) * gain

def rope_tables(offsets):
    half_dim = HEAD_DIM // 2
    freqs = jnp.exp(jnp.arange(half_dim, dtype=jnp.float32) * (-2.0 * math.log(rope_base) / HEAD_DIM))
    angles = offsets.astype(jnp.float32)[:, None] * freqs[None, :]
    return (jnp.cos(angles), jnp.sin(angles))

def rotate(values, cosine, sine):
    half_dim = HEAD_DIM // 2
    first_half = values[..., :half_dim]
    second_half = values[..., half_dim:]
    cos_wide = cosine[:, None, :]
    sin_wide = sine[:, None, :]
    return jnp.concatenate([first_half * cos_wide - second_half * sin_wide, second_half * cos_wide + first_half * sin_wide], axis=-1)

def locate(positions, lengths):
    seq_ends = jnp.cumsum(lengths).astype(jnp.int32)
    starts = seq_ends - lengths
    doc_index = lax.optimization_barrier(jnp.sum((positions[:, None] >= seq_ends[None, :]).astype(jnp.int32), axis=1))
    picked = (doc_index[:, None] == jnp.arange(lengths.shape[0], dtype=jnp.int32)[None, :]).astype(jnp.int32)
    return (doc_index, positions - lax.optimization_barrier(jnp.sum(picked * starts[None, :], axis=1)))

def group_forward(x_group, pos_group, len_group, w_input, w_output, w_gateup, w_down, gains):
    model_width = x_group.shape[1]
    row_count = x_group.shape[0]
    q_width = HEADS * HEAD_DIM
    kv_width = KV_HEADS * HEAD_DIM
    head_groups = HEADS // KV_HEADS
    gain_one = gains[:model_width]
    gain_two = gains[model_width:2 * model_width]
    gain_query = gains[2 * model_width:2 * model_width + HEAD_DIM]
    gain_key = gains[2 * model_width + HEAD_DIM:]
    normed_one = low(rms_norm(x_group, gain_one))
    projected = low_back(jnp.dot(normed_one, w_input, precision=highest))
    queries = projected[:, :q_width].reshape(row_count, HEADS, HEAD_DIM)
    key_heads = projected[:, q_width:q_width + kv_width].reshape(row_count, KV_HEADS, HEAD_DIM)
    value_heads = low(projected[:, q_width + kv_width:].reshape(row_count, KV_HEADS, HEAD_DIM))
    doc_index, seq_offset = locate(pos_group, len_group)
    cosine, sine = rope_tables(seq_offset)
    queries = low(rotate(rms_norm(queries, gain_query), cosine, sine))
    key_heads = low(rotate(rms_norm(key_heads, gain_key), cosine, sine))
    block_count = row_count // KBLOCK
    score_scale = HEAD_DIM ** (-0.5)
    query_blocks = queries.reshape(block_count, KBLOCK, KV_HEADS, head_groups, HEAD_DIM)

    def attend(items):
        query_block, query_pos, query_doc = items
        scores = jnp.einsum('qhgd,khd->hgqk', query_block, key_heads, precision=highest) * score_scale
        scores = low_back(scores)
        allowed = (query_doc[:, None] == doc_index[None, :]) & (pos_group[None, :] <= query_pos[:, None])
        scores = jnp.where(allowed, scores, masked_score)
        weights = jnp.exp(scores - lax.optimization_barrier(jnp.max(scores, axis=-1, keepdims=True)))
        probs = weights / lax.optimization_barrier(jnp.sum(weights, axis=-1, keepdims=True))
        return jnp.einsum('hgqk,khd->qhgd', low(probs), value_heads, precision=highest)
    attended = lax.map(jax.checkpoint(attend), (query_blocks, pos_group.reshape(block_count, KBLOCK), doc_index.reshape(block_count, KBLOCK)))
    attn_flat = low(low_back(attended.reshape(row_count, q_width)))
    residual = x_group + low_back(jnp.dot(attn_flat, w_output, precision=highest))
    normed_two = low(rms_norm(residual, gain_two))
    gate_both = low_back(jnp.dot(normed_two, w_gateup, precision=highest))
    hidden = low(jax.nn.silu(gate_both[:, :FF]) * gate_both[:, FF:])
    return residual + jnp.dot(hidden, w_down, precision=highest)

def forward(tokens_f, w_input, w_output, w_gateup, w_down, gains, positions, lengths):
    w_input = low(w_input)
    w_output = low(w_output)
    w_gateup = low(w_gateup)
    w_down = low(w_down)
    grouped = tokens_f.reshape(N_DP, GROUP_TOK, tokens_f.shape[1])

    def group_step(carry, items):
        x_group, pos_group, len_group = items
        return (carry, group_forward(x_group, pos_group, len_group, w_input, w_output, w_gateup, w_down, gains))
    unused, outputs = lax.scan(jax.checkpoint(group_step), jnp.zeros((), jnp.float32), (grouped, positions, lengths))
    return outputs.reshape(tokens_f.shape)

def adam_update(weight, first_moment, second_moment, gradient, rate, decay):
    first_moment = beta_one * first_moment + (1.0 - beta_one) * gradient
    second_moment = beta_two * second_moment + (1.0 - beta_two) * gradient * gradient
    first_fix = 1.0 - beta_one ** STEP
    second_fix = 1.0 - beta_two ** STEP
    direction = first_moment / first_fix / (jnp.sqrt(second_moment / second_fix) + adam_eps)
    return (weight - rate * (direction + decay * weight), first_moment, second_moment)

def reference(tokens, output_cotangent, sequence_lengths, block_order, attn_input, input_moment, input_square, attn_output, output_moment, output_square, gate_up, gateup_moment, gateup_square, down_weight, down_moment, down_square, norm_gains, gains_moment, gains_square):
    offsets = jnp.arange(TOK_DEV, dtype=jnp.int32)
    positions = (block_order[:, :, None] * TOK_DEV + offsets[None, None, :]).reshape(N_DP, GROUP_TOK).astype(jnp.int32)

    def run(tokens_f, w_input, w_output, w_gateup, w_down, gains):
        return forward(tokens_f, w_input, w_output, w_gateup, w_down, gains, positions, sequence_lengths)
    mixed, pull = jax.vjp(run, tokens.astype(jnp.float32), attn_input, attn_output, gate_up, down_weight, norm_gains)
    token_gradient, grad_input, grad_output, grad_gateup, grad_down, grad_gains = pull(output_cotangent.astype(jnp.float32))
    input_next, input_moment_next, input_square_next = adam_update(attn_input, input_moment, input_square, grad_input, rate_input, weight_decay)
    output_next, output_moment_next, output_square_next = adam_update(attn_output, output_moment, output_square, grad_output, rate_output, weight_decay)
    gateup_next, gateup_moment_next, gateup_square_next = adam_update(gate_up, gateup_moment, gateup_square, grad_gateup, rate_gateup, weight_decay)
    down_next, down_moment_next, down_square_next = adam_update(down_weight, down_moment, down_square, grad_down, rate_down, weight_decay)
    gains_next, gains_moment_next, gains_square_next = adam_update(norm_gains, gains_moment, gains_square, grad_gains, rate_gains, 0.0)
    return (mixed.astype(jnp.bfloat16), token_gradient, input_next, input_moment_next, input_square_next, output_next, output_moment_next, output_square_next, gateup_next, gateup_moment_next, gateup_square_next, down_next, down_moment_next, down_square_next, gains_next, gains_moment_next, gains_square_next)
```

```python
import functools
import math

import jax
import jax.numpy as jnp
from jax import lax
from jax.experimental import pallas as pl
from jax.experimental.pallas import tpu as pltpu
from jax.sharding import PartitionSpec as P

HEADS = 24
KV_HEADS = 8
HEAD_DIM = 64
FF = 6912
STEP = 10


norm_eps = 1e-05
rope_base = 1000000.0
beta_one = 0.9
beta_two = 0.95
adam_eps = 1e-08
rate_input = 0.06
rate_output = 0.9
rate_gateup = 0.06
rate_down = 0.03
rate_gains = 0.5
weight_decay = 0.1
masked_score = -1e30


def rope_tables(offsets):
    half_dim = HEAD_DIM // 2
    freqs = jnp.exp(
        jnp.arange(half_dim, dtype=jnp.float32) * (-2.0 * math.log(rope_base) / HEAD_DIM)
    )
    angles = offsets.astype(jnp.float32)[:, None] * freqs[None, :]
    return (jnp.cos(angles), jnp.sin(angles))


def rotate(values, cosine, sine):
    half_dim = HEAD_DIM // 2
    first_half = values[..., :half_dim]
    second_half = values[..., half_dim:]
    cos_wide = cosine[:, None, :]
    sin_wide = sine[:, None, :]
    return jnp.concatenate(
        [
            first_half * cos_wide - second_half * sin_wide,
            second_half * cos_wide + first_half * sin_wide,
        ],
        axis=-1,
    )


def locate(positions, lengths):
    seq_ends = jnp.cumsum(lengths)
    starts = seq_ends - lengths
    doc_index = jnp.sum((positions[:, None] >= seq_ends[None, :]).astype(jnp.int32), axis=1)
    picked = (doc_index[:, None] == jnp.arange(lengths.shape[0], dtype=jnp.int32)[None, :]).astype(
        jnp.int32
    )
    return (doc_index, positions - jnp.sum(picked * starts[None, :], axis=1))


def rms_parts(values):
    inverse = lax.rsqrt(jnp.mean(values * values, axis=-1, keepdims=True) + norm_eps)
    return (values * inverse, inverse)


def norm_back(d_normed, normal_hat, inverse):
    return inverse * (
        d_normed - normal_hat * jnp.mean(d_normed * normal_hat, axis=-1, keepdims=True)
    )


def contract_rows(left, right):
    return lax.dot_general(
        left, right, (((0,), (0,)), ((), ())), preferred_element_type=jnp.float32
    )


def contract_cols(left, right):
    return lax.dot_general(
        left, right, (((1,), (1,)), ((), ())), preferred_element_type=jnp.float32
    )


def owner_order(values, data_count, context_count):
    lead = values.shape[0]
    each = values.shape[1] // (data_count * context_count)
    return (
        values.reshape(lead, data_count, context_count, each)
        .transpose(0, 2, 1, 3)
        .reshape(lead, values.shape[1])
    )


def adam_update(weight, first_moment, second_moment, gradient, rate, decay):
    first_moment = beta_one * first_moment + (1.0 - beta_one) * gradient
    second_moment = beta_two * second_moment + (1.0 - beta_two) * gradient * gradient
    first_fix = 1.0 - beta_one**STEP
    second_fix = 1.0 - beta_two**STEP
    direction = first_moment / first_fix / (jnp.sqrt(second_moment / second_fix) + adam_eps)
    return (weight - rate * (direction + decay * weight), first_moment, second_moment)


def on_device(
    tokens,
    output_cotangent,
    sequence_lengths,
    block_order,
    attn_input,
    input_moment,
    input_square,
    attn_output,
    output_moment,
    output_square,
    gate_up,
    gateup_moment,
    gateup_square,
    down_weight,
    down_moment,
    down_square,
    norm_gains,
    gains_moment,
    gains_square,
):
    row_count = tokens.shape[0]
    model_width = tokens.shape[1]
    q_width = HEADS * HEAD_DIM
    kv_width = KV_HEADS * HEAD_DIM
    proj_width = q_width + 2 * kv_width
    head_groups = HEADS // KV_HEADS
    score_scale = HEAD_DIM ** (-0.5)
    gain_one = norm_gains[:model_width]
    gain_two = norm_gains[model_width : 2 * model_width]
    gain_query = norm_gains[2 * model_width : 2 * model_width + HEAD_DIM]
    gain_key = norm_gains[2 * model_width + HEAD_DIM :]
    seq_lens = sequence_lengths[0]
    order_row = block_order[0]
    context_count = lax.axis_size("cp")
    data_count = lax.axis_size("dp")
    own_slot = lax.axis_index("cp")
    offsets = jnp.arange(row_count, dtype=jnp.int32)
    own_block = jnp.sum(
        jnp.where(jnp.arange(context_count, dtype=jnp.int32) == own_slot, order_row, 0)
    )
    positions = own_block * row_count + offsets
    key_positions = (order_row[:, None] * row_count + offsets[None, :]).reshape(
        context_count * row_count
    )
    doc_index, seq_offset = locate(positions, seq_lens)
    key_doc = locate(key_positions, seq_lens)[0]
    cosine, sine = rope_tables(seq_offset)
    input_bf = attn_input.astype(jnp.bfloat16)
    output_bf = attn_output.astype(jnp.bfloat16)
    gateup_bf = gate_up.astype(jnp.bfloat16)
    down_bf = down_weight.astype(jnp.bfloat16)
    input_all, output_all = (
        lax.all_gather(input_bf, ("dp", "cp"), axis=0, tiled=True),
        lax.all_gather(output_bf, ("dp", "cp"), axis=0, tiled=True),
    )
    x_float = tokens.astype(jnp.float32)
    hat_one, inv_one = rms_parts(x_float)
    normed_one = (hat_one * gain_one).astype(jnp.bfloat16)
    projected = jnp.dot(normed_one, input_all, preferred_element_type=jnp.float32)
    query_raw = projected[:, :q_width].reshape(row_count, HEADS, HEAD_DIM)
    key_raw = projected[:, q_width : q_width + kv_width].reshape(row_count, KV_HEADS, HEAD_DIM)
    value_raw = projected[:, q_width + kv_width :]
    hat_query, inv_query = rms_parts(query_raw)
    hat_key, inv_key = rms_parts(key_raw)
    queries = rotate(hat_query * gain_query, cosine, sine).astype(jnp.bfloat16)
    key_rot = rotate(hat_key * gain_key, cosine, sine)
    key_value = jnp.concatenate([key_rot.reshape(row_count, kv_width), value_raw], axis=1).astype(
        jnp.bfloat16
    )
    kv_all = lax.all_gather(key_value, "cp", axis=0, tiled=True)
    total_keys = kv_all.shape[0]
    key_span = min(512, total_keys)
    block_count = total_keys // key_span
    kv_blocks = kv_all.reshape(block_count, key_span, 2 * kv_width)
    pos_blocks = key_positions.reshape(block_count, key_span)
    doc_blocks = key_doc.reshape(block_count, key_span)
    query_group = queries.reshape(row_count, KV_HEADS, head_groups, HEAD_DIM)

    def block_scores(kv_block, key_pos, key_docs):
        key_block = kv_block[:, :kv_width].reshape(key_span, KV_HEADS, HEAD_DIM)
        value_block = kv_block[:, kv_width:].reshape(key_span, KV_HEADS, HEAD_DIM)
        scores = (
            jnp.einsum("qhgd,khd->hgqk", query_group, key_block, preferred_element_type=jnp.float32)
            * score_scale
        )
        allowed = (doc_index[:, None] == key_docs[None, :]) & (
            key_pos[None, :] <= positions[:, None]
        )
        return (key_block, value_block, jnp.where(allowed, scores, masked_score), allowed)

    def forward_block(carry, items):
        run_max, run_total, run_sum = carry
        key_block, value_block, scores, allowed = block_scores(*items)
        new_max = jnp.maximum(run_max, jnp.max(scores, axis=-1))
        weights = jnp.where(allowed, jnp.exp(scores - new_max[..., None]), 0.0)
        factor = jnp.exp(run_max - new_max)
        run_total = run_total * factor + jnp.sum(weights, axis=-1)
        run_sum = run_sum * factor[..., None] + jnp.einsum(
            "hgqk,khd->hgqd",
            weights.astype(jnp.bfloat16),
            value_block,
            preferred_element_type=jnp.float32,
        )
        return ((new_max, run_total, run_sum), None)

    start_state = (
        jnp.full((KV_HEADS, head_groups, row_count), masked_score, jnp.float32),
        jnp.zeros((KV_HEADS, head_groups, row_count), jnp.float32),
        jnp.zeros((KV_HEADS, head_groups, row_count, HEAD_DIM), jnp.float32),
    )
    (run_max, run_total, run_sum), unused = lax.scan(
        forward_block, start_state, (kv_blocks, pos_blocks, doc_blocks)
    )
    attended = run_sum / run_total[..., None]
    log_total = run_max + jnp.log(run_total)
    attn_flat = attended.transpose(2, 0, 1, 3).reshape(row_count, q_width).astype(jnp.bfloat16)
    residual = x_float + jnp.dot(attn_flat, output_all, preferred_element_type=jnp.float32)
    hat_two, inv_two = rms_parts(residual)
    normed_two = (hat_two * gain_two).astype(jnp.bfloat16)
    columns = normed_two
    gate_both = jnp.dot(
        columns,
        lax.all_gather(gateup_bf, ("dp", "cp"), axis=0, tiled=True),
        preferred_element_type=jnp.float32,
    )
    gate_part = gate_both[:, :FF]
    up_part = gate_both[:, FF:]
    gate_sig = jax.nn.sigmoid(gate_part)
    gate_act = gate_part * gate_sig
    hidden = (gate_act * up_part).astype(jnp.bfloat16)
    columns = hidden
    ff_result = jnp.dot(
        columns,
        lax.all_gather(down_bf, ("dp", "cp"), axis=0, tiled=True),
        preferred_element_type=jnp.float32,
    )
    mixed = (residual + ff_result).astype(jnp.bfloat16)
    d_hidden = contract_cols(
        output_cotangent, lax.all_gather(down_bf, ("dp", "cp"), axis=0, tiled=True)
    )
    d_gate = d_hidden * up_part * (gate_sig * (1.0 + gate_part * (1.0 - gate_sig)))
    d_up = d_hidden * gate_act
    d_gate_both = jnp.concatenate([d_gate, d_up], axis=1).astype(jnp.bfloat16)
    d_normed_two = contract_cols(
        d_gate_both, lax.all_gather(gateup_bf, ("dp", "cp"), axis=0, tiled=True)
    )
    grad_gain_two = jnp.sum(d_normed_two * hat_two, axis=0)
    d_residual = output_cotangent.astype(jnp.float32) + norm_back(
        d_normed_two * gain_two, hat_two, inv_two
    )
    d_branch = d_residual.astype(jnp.bfloat16)
    input_back, output_back = (input_all, output_all)
    d_flat = contract_cols(d_branch, output_back).astype(jnp.bfloat16)
    d_attended = d_flat.reshape(row_count, KV_HEADS, head_groups, HEAD_DIM).transpose(1, 2, 0, 3)
    delta = jnp.sum(d_attended.astype(jnp.float32) * attended, axis=-1)

    def backward_block(d_query_sum, items):
        key_block, value_block, scores, allowed = block_scores(*items)
        probs = jnp.where(allowed, jnp.exp(scores - log_total[..., None]), 0.0)
        d_probs = jnp.einsum(
            "hgqd,khd->hgqk", d_attended, value_block, preferred_element_type=jnp.float32
        )
        d_scores = (probs * (d_probs - delta[..., None])).astype(jnp.bfloat16)
        d_query_sum = (
            d_query_sum
            + jnp.einsum("hgqk,khd->hgqd", d_scores, key_block, preferred_element_type=jnp.float32)
            * score_scale
        )
        d_keys = (
            jnp.einsum("hgqk,qhgd->khd", d_scores, query_group, preferred_element_type=jnp.float32)
            * score_scale
        )
        d_values = jnp.einsum(
            "hgqk,hgqd->khd",
            probs.astype(jnp.bfloat16),
            d_attended,
            preferred_element_type=jnp.float32,
        )
        return (
            d_query_sum,
            jnp.concatenate(
                [d_keys.reshape(key_span, kv_width), d_values.reshape(key_span, kv_width)], axis=1
            ),
        )

    d_query_sum, d_kv_blocks = lax.scan(
        backward_block,
        jnp.zeros((KV_HEADS, head_groups, row_count, HEAD_DIM), jnp.float32),
        (kv_blocks, pos_blocks, doc_blocks),
    )
    d_kv = lax.psum_scatter(
        d_kv_blocks.reshape(total_keys, 2 * kv_width).astype(jnp.bfloat16),
        "cp",
        scatter_dimension=0,
        tiled=True,
    ).astype(jnp.float32)
    d_query_rot = rotate(
        d_query_sum.transpose(2, 0, 1, 3).reshape(row_count, HEADS, HEAD_DIM), cosine, -sine
    )
    grad_gain_query = jnp.sum(d_query_rot * hat_query, axis=(0, 1))
    d_query_raw = norm_back(d_query_rot * gain_query, hat_query, inv_query)
    d_key_rot = rotate(d_kv[:, :kv_width].reshape(row_count, KV_HEADS, HEAD_DIM), cosine, -sine)
    grad_gain_key = jnp.sum(d_key_rot * hat_key, axis=(0, 1))
    d_key_raw = norm_back(d_key_rot * gain_key, hat_key, inv_key)
    d_projected = jnp.concatenate(
        [
            d_query_raw.reshape(row_count, q_width),
            d_key_raw.reshape(row_count, kv_width),
            d_kv[:, kv_width:],
        ],
        axis=1,
    ).astype(jnp.bfloat16)
    d_normed_one = contract_cols(d_projected, input_back)
    grad_gain_one = jnp.sum(d_normed_one * hat_one, axis=0)
    token_gradient = d_residual + norm_back(d_normed_one * gain_one, hat_one, inv_one)

    def make_wide(first_src, attn_src, second_src):

        def wide_terms(row_start, row_total):
            return jnp.concatenate(
                [
                    contract_rows(first_src, d_projected),
                    contract_rows(attn_src, d_branch),
                    contract_rows(second_src, d_gate_both),
                ],
                axis=1,
            )

        return wide_terms

    def make_down(hidden_src):

        def down_terms(row_start, row_total):
            return contract_rows(hidden_src, output_cotangent)

        return down_terms

    shard_rows = attn_input.shape[0]
    down_rows = down_weight.shape[0]
    wide_fn = make_wide(
        owner_order(normed_one, data_count, context_count),
        owner_order(attn_flat, data_count, context_count),
        owner_order(normed_two, data_count, context_count),
    )
    down_fn = make_down(owner_order(hidden, data_count, context_count))
    group_wide = lax.psum_scatter(
        wide_fn(jnp.int32(0), lax.axis_size("cp") * (shard_rows * data_count)).astype(jnp.bfloat16),
        "cp",
        scatter_dimension=0,
        tiled=True,
    )
    group_down = lax.psum_scatter(
        down_fn(jnp.int32(0), lax.axis_size("cp") * (down_rows * data_count)).astype(jnp.bfloat16),
        "cp",
        scatter_dimension=0,
        tiled=True,
    )
    wide_grads, down_grads = (
        lax.psum_scatter(group_wide, "dp", scatter_dimension=0, tiled=True).astype(jnp.float32),
        lax.psum_scatter(group_down, "dp", scatter_dimension=0, tiled=True).astype(jnp.float32),
    )
    gain_grads = lax.psum(
        jnp.concatenate([grad_gain_one, grad_gain_two, grad_gain_query, grad_gain_key]),
        ("dp", "cp"),
    )
    grad_input = wide_grads[:, :proj_width]
    grad_output = wide_grads[:, proj_width : proj_width + model_width]
    grad_gateup = wide_grads[:, proj_width + model_width :]
    input_next, input_moment_next, input_square_next = adam_update(
        attn_input, input_moment, input_square, grad_input, rate_input, weight_decay
    )
    output_next, output_moment_next, output_square_next = adam_update(
        attn_output, output_moment, output_square, grad_output, rate_output, weight_decay
    )
    gateup_next, gateup_moment_next, gateup_square_next = adam_update(
        gate_up, gateup_moment, gateup_square, grad_gateup, rate_gateup, weight_decay
    )
    down_next, down_moment_next, down_square_next = adam_update(
        down_weight, down_moment, down_square, down_grads, rate_down, weight_decay
    )
    gains_next, gains_moment_next, gains_square_next = adam_update(
        norm_gains, gains_moment, gains_square, gain_grads, rate_gains, 0.0
    )
    return (
        mixed,
        token_gradient,
        input_next,
        input_moment_next,
        input_square_next,
        output_next,
        output_moment_next,
        output_square_next,
        gateup_next,
        gateup_moment_next,
        gateup_square_next,
        down_next,
        down_moment_next,
        down_square_next,
        gains_next,
        gains_moment_next,
        gains_square_next,
    )


MESH = pl.DeviceIdType.MESH


def place():
    dp = lax.axis_index("dp")
    cp = lax.axis_index("cp")
    return dp, cp, cp // 2, cp % 2


def greet(targets):
    barrier = pltpu.get_barrier_semaphore()
    for target in targets:
        pl.semaphore_signal(barrier, inc=1, device_id=target, device_id_type=MESH)
    pl.semaphore_wait(barrier, len(targets))


def send(source, target, send_sem, recv_sem, device):
    return pltpu.make_async_remote_copy(
        src_ref=source,
        dst_ref=target,
        send_sem=send_sem,
        recv_sem=recv_sem,
        device_id=device,
        device_id_type=MESH,
    )


class LineGather:
    def __init__(self, own_ref, all_ref, sems, where, depth, both=True):
        self.own, self.where, self.depth, self.both = own_ref, where, depth, both
        self.slot = all_ref if callable(all_ref) else lambda slot: all_ref.at[slot]
        self.right, self.left, self.sib, self.recv, self.local = sems

    @staticmethod
    def scratch(depth):
        return [pltpu.SemaphoreType.DMA((2 * depth,))] * 4 + [pltpu.SemaphoreType.DMA]

    def copy(self, kind, slot, source):
        dp, cp, z, core = self.where
        device = {"right": (dp, cp + 2), "left": (dp, cp - 2), "sib": (dp, cp ^ 1)}[kind]
        sem = {"right": self.right, "left": self.left, "sib": self.sib}[kind]
        return send(source, self.slot(slot), sem.at[slot], self.recv.at[slot], device)

    def keep(self):
        return pltpu.make_async_copy(self.own, self.slot(self.where[1]), self.local)

    def start(self):
        dp, cp, z, core = self.where

        @pl.when(z < self.depth - 1)
        def _():
            self.copy("right", cp, self.own).start()

        @pl.when(z > 0)
        def _():
            self.copy("left", cp, self.own).start()

        if self.both:
            self.copy("sib", cp, self.own).start()
        self.keep().start()

    def step(self, far):
        dp, cp, z, core = self.where

        @pl.when(z >= far)
        def _():
            slot = cp - 2 * far
            self.copy("right", slot, self.own).wait_recv()

            @pl.when(z < self.depth - 1)
            def _():
                self.copy("right", slot, self.slot(slot)).start()

            if self.both:
                self.copy("sib", slot, self.slot(slot)).start()

        @pl.when(z + far < self.depth)
        def _():
            slot = cp + 2 * far
            self.copy("left", slot, self.own).wait_recv()

            @pl.when(z > 0)
            def _():
                self.copy("left", slot, self.slot(slot)).start()

            if self.both:
                self.copy("sib", slot, self.slot(slot)).start()

    def finish(self):
        dp, cp, z, core = self.where
        if self.both:
            for spot in range(self.depth):
                self.copy("sib", 1 - core + 2 * spot, self.own).wait_recv()
        self.keep().wait()
        for spot in range(self.depth):
            slot = 2 * spot + core
            if self.both:
                self.copy("sib", slot, self.own).wait_send()

            @pl.when((spot <= z) & (z < self.depth - 1))
            def _():
                self.copy("right", slot, self.own).wait_send()

            @pl.when((spot >= z) & (z > 0))
            def _():
                self.copy("left", slot, self.own).wait_send()


class Swap:
    def __init__(self, source_ref, target_ref, sems, where, count):
        self.source, self.where, self.count = source_ref, where, count
        self.slot = target_ref if callable(target_ref) else lambda slot: target_ref.at[slot]
        self.sent, self.recv, self.local = sems

    @staticmethod
    def scratch(count):
        return [pltpu.SemaphoreType.DMA((count,))] * 2 + [pltpu.SemaphoreType.DMA]

    def copy(self, peer):
        dp, cp, z, core = self.where
        return send(
            self.source.at[peer],
            self.slot(cp),
            self.sent.at[peer],
            self.recv.at[cp],
            (dp, peer),
        )

    def keep(self):
        cp = self.where[1]
        return pltpu.make_async_copy(self.source.at[cp], self.slot(cp), self.local)

    def start(self):
        cp = self.where[1]
        for turn in range(self.count - 1, 0, -1):
            self.copy(cp ^ turn).start()
        self.keep().start()

    def arrive(self, peer):
        dp, cp, z, core = self.where
        send(
            self.source.at[peer],
            self.slot(peer),
            self.sent.at[peer],
            self.recv.at[peer],
            (dp, peer),
        ).wait_recv()

    def finish_recv(self):
        cp = self.where[1]
        for turn in range(1, self.count):
            self.arrive(cp ^ turn)
        self.keep().wait()

    def finish_send(self):
        cp = self.where[1]
        for turn in range(1, self.count):
            self.copy(cp ^ turn).wait_send()


class RingSpread:
    def __init__(self, block, half, sems, where):
        self.block, self.half, self.where = block, half, where
        self.sent, self.recv = sems

    @staticmethod
    def scratch():
        return [pltpu.SemaphoreType.DMA((4,))] * 2

    def copy(self, kind, mine):
        dp, cp, z, core = self.where
        turn = (1, 2, 2, 1)[kind]
        if kind < 2:
            part = self.block(dp if mine else dp ^ turn)
        else:
            part = self.half(dp ^ (3 - turn) if mine else dp ^ 3, kind - 2)
        return send(part, part, self.sent.at[kind], self.recv.at[kind], (dp ^ turn, cp))

    def start(self):
        self.copy(0, True).start()
        self.copy(1, True).start()

    def forward(self):
        self.copy(0, False).wait_recv()
        self.copy(2, True).start()
        self.copy(1, False).wait_recv()
        self.copy(3, True).start()

    def finish(self):
        self.copy(2, False).wait_recv()
        self.copy(3, False).wait_recv()
        for kind in range(4):
            self.copy(kind, True).wait_send()


def turn_heads(values, cosine, sine):
    half = values.shape[0] // 2
    first, second = values[:half], values[half:]
    return jnp.concatenate([first * cosine - second * sine, second * cosine + first * sine], axis=0)


def head_hat(values):
    inverse = lax.rsqrt(jnp.mean(values * values, axis=0, keepdims=True) + norm_eps)
    return values * inverse, inverse


def score_block(keys, queries, key_place, query_place, query_start):
    scores = jnp.dot(keys, queries, preferred_element_type=jnp.float32) * HEAD_DIM ** (-0.5)
    allowed = (key_place <= query_place) & (key_place >= query_start)
    return jnp.where(allowed, scores, masked_score), allowed


def front_kernel(
    tile,
    tokens_ref,
    gain_one_ref,
    gain_two_ref,
    gain_query_ref,
    gain_key_ref,
    cosine_ref,
    sine_ref,
    key_place_ref,
    query_place_ref,
    query_start_ref,
    input_send,
    output_own,
    gate_send,
    up_send,
    cotangent_own,
    normed_one_out,
    normed_two_out,
    cotangent_all,
    input_out,
    output_out,
    gateup_out,
    raw_out,
    flat_out,
    total_out,
    residual_out,
    normed_one,
    normed_two,
    own_one,
    own_two,
    inputs,
    outputs,
    raw,
    queries,
    keys_up,
    values,
    flat_send,
    flat_recv,
    out_sems,
    *sems,
):
    where = place()
    dp, cp, z, core = where
    context_count = normed_one.shape[0]
    depth = context_count // 2
    rows = tokens_ref.shape[0]
    width = tokens_ref.shape[1]
    q_each = HEADS // KV_HEADS * HEAD_DIM
    take = iter(range(len(sems)))

    def some(count):
        return [sems[next(take)] for _ in range(count)]

    greet([(dp, cp ^ turn) for turn in range(1, context_count)] + [(dp ^ 1, cp), (dp ^ 2, cp)])
    token_line = LineGather(own_one, normed_one, some(5), where, depth)
    second_line = LineGather(own_two, normed_two, some(5), where, depth)
    cotangent_line = LineGather(cotangent_own, cotangent_all, some(5), where, depth)
    output_line = LineGather(
        output_own, lambda slot: outputs.at[dp, slot // 2, core], some(5), where, depth, False
    )
    input_swap = Swap(input_send, inputs.at[dp], some(3), where, context_count)
    shard = input_send.shape[1]

    def gateup_slot(index):
        return lambda slot: gateup_out.at[index, dp, pl.ds(pl.multiple_of(slot * shard, 16), shard)]

    gate_swap = Swap(gate_send, gateup_slot(0), some(3), where, context_count)
    up_swap = Swap(up_send, gateup_slot(1), some(3), where, context_count)
    flat_swap = Swap(flat_send, flat_recv, some(3), where, context_count)
    input_ring = RingSpread(
        lambda d: inputs.at[d],
        lambda d, h: inputs.at[d, pl.ds(h * (context_count // 2), context_count // 2)],
        some(2),
        where,
    )
    output_ring = RingSpread(
        lambda d: outputs.at[d, :, core],
        lambda d, h: outputs.at[d, pl.ds(h * (depth // 2), depth // 2), core],
        some(2),
        where,
    )
    half_rows = gateup_out.shape[2] // 2

    def gateup_ring(index):
        return RingSpread(
            lambda d: gateup_out.at[index, d],
            lambda d, h: gateup_out.at[index, d, pl.ds(h * half_rows, half_rows)],
            some(2),
            where,
        )

    gate_ring, up_ring = gateup_ring(0), gateup_ring(1)
    share_sent, share_recv = some(2)

    def share(mine):
        part = outputs.at[:, :, core if mine else 1 - core]
        return send(part, part, share_sent, share_recv, (dp, cp ^ 1))

    x_float = tokens_ref[...].astype(jnp.float32)
    hat_one, _ = rms_parts(x_float)
    own_one[...] = (hat_one * gain_one_ref[...]).astype(jnp.bfloat16)
    input_swap.start()
    token_line.start()
    output_line.start()
    token_line.step(1)
    output_line.step(1)
    input_swap.finish_recv()
    input_ring.start()
    token_line.step(2)
    output_line.step(2)
    gate_swap.start()
    input_ring.forward()
    token_line.step(3)
    output_line.step(3)
    up_swap.start()
    output_line.finish()
    output_ring.start()
    token_line.finish()
    input_ring.finish()
    one_copy = pltpu.make_async_copy(normed_one, normed_one_out, out_sems.at[0])
    one_copy.start()
    input_copy = pltpu.make_async_copy(inputs, input_out, out_sems.at[1])
    input_copy.start()

    weights = inputs[...].reshape(width, inputs.shape[-1])

    def project(turn, carry):
        lanes = pl.ds(pl.multiple_of(turn * tile, tile), tile)
        block = normed_one[pl.ds(turn * (tile // rows), tile // rows)].reshape(tile, width)
        part = jnp.dot(block, weights, preferred_element_type=jnp.float32).T
        raw[:, lanes] = part
        cosine, sine = cosine_ref[:, lanes], sine_ref[:, lanes]
        for head in range(HEADS // KV_HEADS):
            hat, _ = head_hat(part[head * HEAD_DIM : (head + 1) * HEAD_DIM])
            queries[head * HEAD_DIM : (head + 1) * HEAD_DIM, lanes] = turn_heads(
                hat * gain_query_ref[...], cosine, sine
            ).astype(jnp.bfloat16)
        hat, _ = head_hat(part[q_each : q_each + HEAD_DIM])
        key = turn_heads(hat * gain_key_ref[...], cosine, sine)
        keys_up[pl.ds(pl.multiple_of(turn * tile, tile), tile)] = key.T.astype(jnp.bfloat16)
        values[:, lanes] = part[q_each + HEAD_DIM :].astype(jnp.bfloat16)
        return carry

    lax.fori_loop(0, normed_one.shape[0] * rows // tile, project, 0)
    raw_copy = pltpu.make_async_copy(raw, raw_out, out_sems.at[2])
    raw_copy.start()

    def attend(turn, carry):
        lanes = pl.ds(pl.multiple_of(turn * tile, tile), tile)
        query_place, query_start = query_place_ref[:, lanes], query_start_ref[:, lanes]
        for head in range(HEADS // KV_HEADS):
            spot = pl.ds(head * HEAD_DIM, HEAD_DIM)
            scores, allowed = score_block(
                keys_up[...], queries[spot, lanes], key_place_ref[...], query_place, query_start
            )
            top = jnp.max(scores, axis=0, keepdims=True)
            exps = jnp.exp(scores - top)
            total = jnp.sum(exps, axis=0, keepdims=True)
            total_out[pl.ds(head, 1), lanes] = top + jnp.log(total)
            probs = (exps * (1.0 / total)).astype(jnp.bfloat16)
            attended = jnp.dot(values[...], probs, preferred_element_type=jnp.float32)
            for part in range(tile // rows):
                flat_send[turn * (tile // rows) + part, spot] = attended[
                    :, part * rows : (part + 1) * rows
                ].astype(jnp.bfloat16)
        return carry

    turns = normed_one.shape[0] * rows // tile
    attend(0, 0)
    gate_swap.finish_recv()
    gate_ring.start()
    output_ring.forward()
    lax.fori_loop(1, turns, attend, 0)
    flat_swap.start()
    up_swap.finish_recv()
    up_ring.start()
    output_ring.finish()
    share(True).start()
    gate_ring.forward()
    cotangent_line.start()
    share(False).wait_recv()
    output_copy = pltpu.make_async_copy(outputs, output_out, out_sems.at[3])
    output_copy.start()
    flat_swap.finish_recv()
    flat_copy = pltpu.make_async_copy(flat_recv, flat_out, out_sems.at[4])
    flat_copy.start()
    flat = flat_recv[...].reshape(HEADS * HEAD_DIM, rows).astype(jnp.float32).T.astype(jnp.bfloat16)
    residual = x_float + jnp.dot(
        flat, outputs[...].reshape(HEADS * HEAD_DIM, width), preferred_element_type=jnp.float32
    )
    residual_out[...] = residual
    hat_two, _ = rms_parts(residual)
    own_two[...] = (hat_two * gain_two_ref[...]).astype(jnp.bfloat16)
    second_line.start()
    for far in range(1, depth):
        second_line.step(far)
        cotangent_line.step(far)
        if far == 1:
            up_ring.forward()
    second_line.finish()
    two_copy = pltpu.make_async_copy(normed_two, normed_two_out, out_sems.at[5])
    two_copy.start()
    cotangent_line.finish()
    gate_ring.finish()
    up_ring.finish()
    share(True).wait_send()
    for swap in (input_swap, gate_swap, up_swap, flat_swap):
        swap.finish_send()
    for copy in (one_copy, input_copy, raw_copy, output_copy, flat_copy, two_copy):
        copy.wait()


def front(
    tokens,
    gain_one,
    gain_two,
    gain_query,
    gain_key,
    cosine,
    sine,
    places,
    starts,
    input_send,
    output_own,
    gate_send,
    up_send,
    cotangent,
    data_count,
    context_count,
):
    rows, width = tokens.shape
    depth = context_count // 2
    group_rows = rows * context_count
    shard = input_send.shape[1]
    each = input_send.shape[2]
    hidden = gate_send.shape[2]
    q_each = HEADS // KV_HEADS * HEAD_DIM
    flat_width = HEADS * HEAD_DIM
    bf = jnp.bfloat16
    any_space = pl.BlockSpec(memory_space=pl.ANY)
    in_vmem = pl.BlockSpec(memory_space=pltpu.VMEM)
    shapes = [
        ((context_count, rows, width), bf, any_space),
        ((context_count, rows, width), bf, any_space),
        ((context_count, rows, width), bf, any_space),
        ((data_count, context_count, shard, each), bf, any_space),
        ((data_count, depth, 2, shard, width), bf, any_space),
        ((2, data_count, context_count * shard, hidden), bf, any_space),
        ((each, group_rows), jnp.float32, any_space),
        ((context_count, q_each, rows), bf, any_space),
        ((HEADS // KV_HEADS, group_rows), jnp.float32, in_vmem),
        ((rows, width), jnp.float32, in_vmem),
    ]
    return pl.pallas_call(
        functools.partial(front_kernel, 2 * rows),
        out_shape=[jax.ShapeDtypeStruct(shape, kind) for shape, kind, _ in shapes],
        in_specs=[in_vmem] * 10 + [any_space] * 5,
        out_specs=[space for _, _, space in shapes],
        scratch_shapes=[
            pltpu.VMEM((context_count, rows, width), bf),
            pltpu.VMEM((context_count, rows, width), bf),
            pltpu.VMEM((rows, width), bf),
            pltpu.VMEM((rows, width), bf),
            pltpu.VMEM((data_count, context_count, shard, each), bf),
            pltpu.VMEM((data_count, depth, 2, shard, width), bf),
            pltpu.VMEM((each, group_rows), jnp.float32),
            pltpu.VMEM((q_each, group_rows), bf),
            pltpu.VMEM((group_rows, HEAD_DIM), bf),
            pltpu.VMEM((HEAD_DIM, group_rows), bf),
            pltpu.VMEM((context_count, q_each, rows), bf),
            pltpu.VMEM((context_count, q_each, rows), bf),
            pltpu.SemaphoreType.DMA((6,)),
        ]
        + LineGather.scratch(depth) * 4
        + Swap.scratch(context_count) * 4
        + RingSpread.scratch() * 4
        + [pltpu.SemaphoreType.DMA] * 2,
        compiler_params=pltpu.CompilerParams(
            collective_id=0, has_side_effects=True, vmem_limit_bytes=56 * 2**20
        ),
        name="front",
    )(
        tokens,
        gain_one.reshape(1, width),
        gain_two.reshape(1, width),
        gain_query.reshape(HEAD_DIM, 1),
        gain_key.reshape(HEAD_DIM, 1),
        cosine,
        sine,
        places.reshape(group_rows, 1),
        places.reshape(1, group_rows),
        starts.reshape(1, group_rows),
        input_send,
        output_own,
        gate_send,
        up_send,
        cotangent,
    )


def swap_kernel(context_count, source_ref, target_ref, *sems):
    where = place()
    dp, cp, z, core = where
    greet([(dp, cp ^ turn) for turn in range(1, context_count)])
    swap = Swap(source_ref, target_ref, sems, where, context_count)
    swap.start()
    swap.finish_recv()
    swap.finish_send()


def swap_blocks(source, collective_id, name):
    any_space = pl.BlockSpec(memory_space=pl.ANY)
    return pl.pallas_call(
        functools.partial(swap_kernel, source.shape[0]),
        out_shape=jax.ShapeDtypeStruct(source.shape, source.dtype),
        in_specs=[any_space],
        out_specs=any_space,
        scratch_shapes=Swap.scratch(source.shape[0]),
        compiler_params=pltpu.CompilerParams(collective_id=collective_id, has_side_effects=True),
        name=name,
    )(source)


def gather_kernel(depth, own_ref, all_ref, *sems):
    where = place()
    dp, cp, z, core = where
    greet([(dp, cp ^ turn) for turn in range(1, 2 * depth)])
    line = LineGather(own_ref, all_ref, sems, where, depth)
    line.start()
    for far in range(1, depth):
        line.step(far)
    line.finish()


def gather_line(own, context_count, collective_id, name):
    any_space = pl.BlockSpec(memory_space=pl.ANY)
    depth = context_count // 2
    return pl.pallas_call(
        functools.partial(gather_kernel, depth),
        out_shape=jax.ShapeDtypeStruct((context_count,) + own.shape, own.dtype),
        in_specs=[any_space],
        out_specs=any_space,
        scratch_shapes=LineGather.scratch(depth),
        compiler_params=pltpu.CompilerParams(collective_id=collective_id, has_side_effects=True),
        name=name,
    )(own)


class LineScatter:
    def __init__(self, part_ref, out_ref, scratch, where, depth):
        self.part, self.out, self.where, self.depth = part_ref, out_ref, where, depth
        self.sib, self.msg, self.right, self.left = scratch[:4]
        (
            self.sib_sent,
            self.sib_recv,
            self.right_sent,
            self.right_recv,
            self.left_sent,
            self.left_recv,
        ) = scratch[4:]

    @staticmethod
    def scratch(depth, rows, width):
        return [pltpu.VMEM((depth, rows, width), jnp.bfloat16)] * 4 + [
            pltpu.SemaphoreType.DMA((depth,))
        ] * 6

    def pair(self, spot):
        dp, cp, z, core = self.where
        return send(
            self.part.at[2 * spot + 1 - core],
            self.sib.at[spot],
            self.sib_sent.at[spot],
            self.sib_recv.at[spot],
            (dp, cp ^ 1),
        )

    def hop_right(self, spot):
        dp, cp, z, core = self.where
        return send(
            self.msg.at[spot],
            self.right.at[spot],
            self.right_sent.at[spot],
            self.right_recv.at[spot],
            (dp, cp + 2),
        )

    def hop_left(self, spot):
        dp, cp, z, core = self.where
        return send(
            self.msg.at[spot],
            self.left.at[spot],
            self.left_sent.at[spot],
            self.left_recv.at[spot],
            (dp, cp - 2),
        )

    def order(self):
        spots = []
        for turn in range(self.depth):
            spots += [self.depth - 1 - turn, turn]
        return list(dict.fromkeys(spots))

    def chip_sum(self, spot):
        core = self.where[3]
        self.pair(spot).wait_recv()
        return self.part[2 * spot + core].astype(jnp.float32) + self.sib[spot].astype(jnp.float32)

    def forward(self, spot):
        z = self.where[2]

        @pl.when((z < spot) & (z > 0))
        def _():
            total = self.chip_sum(spot)
            self.hop_right(spot).wait_recv()
            self.msg[spot] = (total + self.right[spot].astype(jnp.float32)).astype(jnp.bfloat16)
            self.hop_right(spot).start()

        @pl.when((z < spot) & (z == 0))
        def _():
            self.msg[spot] = self.chip_sum(spot).astype(jnp.bfloat16)
            self.hop_right(spot).start()

        @pl.when((z > spot) & (z < self.depth - 1))
        def _():
            total = self.chip_sum(spot)
            self.hop_left(spot).wait_recv()
            self.msg[spot] = (total + self.left[spot].astype(jnp.float32)).astype(jnp.bfloat16)
            self.hop_left(spot).start()

        @pl.when((z > spot) & (z == self.depth - 1))
        def _():
            self.msg[spot] = self.chip_sum(spot).astype(jnp.bfloat16)
            self.hop_left(spot).start()

    def finish(self):
        z = self.where[2]
        self.out[...] = self.chip_sum(z)

        @pl.when(z > 0)
        def _():
            self.hop_right(z).wait_recv()
            self.out[...] += self.right[z].astype(jnp.float32)

        @pl.when(z < self.depth - 1)
        def _():
            self.hop_left(z).wait_recv()
            self.out[...] += self.left[z].astype(jnp.float32)

        for spot in range(self.depth):
            self.pair(spot).wait_send()

            @pl.when(z < spot)
            def _():
                self.hop_right(spot).wait_send()

            @pl.when(z > spot)
            def _():
                self.hop_left(spot).wait_send()


def scatter_kernel(depth, part_ref, out_ref, *scratch):
    where = place()
    dp, cp, z, core = where
    greet([(dp, cp ^ turn) for turn in range(1, 2 * depth)])
    line = LineScatter(part_ref, out_ref, scratch, where, depth)
    for spot in line.order():
        line.pair(spot).start()
    for spot in line.order():
        line.forward(spot)
    line.finish()


def scatter_line(parts, collective_id, name):
    context_count, rows, width = parts.shape
    depth = context_count // 2
    in_vmem = pl.BlockSpec(memory_space=pltpu.VMEM)
    return pl.pallas_call(
        functools.partial(scatter_kernel, depth),
        out_shape=jax.ShapeDtypeStruct((rows, width), jnp.float32),
        in_specs=[in_vmem],
        out_specs=in_vmem,
        scratch_shapes=LineScatter.scratch(depth, rows, width),
        compiler_params=pltpu.CompilerParams(
            collective_id=collective_id, has_side_effects=True, vmem_limit_bytes=40 * 2**20
        ),
        name=name,
    )(parts)


def total_kernel(data_count, context_count, own_ref, out_ref, line_buf, all_buf, *sems):
    where = place()
    dp, cp, z, core = where
    line_sent, line_recv, all_sent, all_recv = sems
    greet(
        [(dp, cp ^ turn) for turn in range(1, context_count)]
        + [(dp ^ turn, cp) for turn in range(1, data_count)]
    )
    line_buf[cp] = own_ref[...]
    for turn in range(1, context_count):
        send(
            own_ref, line_buf.at[cp], line_sent.at[turn], line_recv.at[turn], (dp, cp ^ turn)
        ).start()
    for turn in range(1, context_count):
        copy = send(
            own_ref, line_buf.at[cp ^ turn], line_sent.at[turn], line_recv.at[turn], (dp, cp ^ turn)
        )
        copy.wait_recv()
        copy.wait_send()
    all_buf[dp] = jnp.sum(line_buf[...], axis=0)
    for turn in range(1, data_count):
        send(
            all_buf.at[dp], all_buf.at[dp], all_sent.at[turn], all_recv.at[turn], (dp ^ turn, cp)
        ).start()
    for turn in range(1, data_count):
        copy = send(
            all_buf.at[dp], all_buf.at[dp ^ turn], all_sent.at[turn], all_recv.at[turn], (dp ^ turn, cp)
        )
        copy.wait_recv()
        copy.wait_send()
    out_ref[...] = jnp.sum(all_buf[...], axis=0)


def total_everywhere(own, data_count, context_count, collective_id):
    in_vmem = pl.BlockSpec(memory_space=pltpu.VMEM)
    return pl.pallas_call(
        functools.partial(total_kernel, data_count, context_count),
        out_shape=jax.ShapeDtypeStruct(own.shape, jnp.float32),
        in_specs=[in_vmem],
        out_specs=in_vmem,
        scratch_shapes=[
            pltpu.VMEM((context_count,) + own.shape, jnp.float32),
            pltpu.VMEM((data_count,) + own.shape, jnp.float32),
            pltpu.SemaphoreType.DMA((context_count,)),
            pltpu.SemaphoreType.DMA((context_count,)),
            pltpu.SemaphoreType.DMA((data_count,)),
            pltpu.SemaphoreType.DMA((data_count,)),
        ],
        compiler_params=pltpu.CompilerParams(collective_id=collective_id, has_side_effects=True),
        name="total_gains",
    )(own)


def split_heads_columns(rows_by_columns):
    rows = rows_by_columns.shape[0]
    q_width = HEADS * HEAD_DIM
    kv_width = KV_HEADS * HEAD_DIM
    query = rows_by_columns[:, :q_width].reshape(rows, KV_HEADS, q_width // KV_HEADS)
    key = rows_by_columns[:, q_width : q_width + kv_width].reshape(rows, KV_HEADS, HEAD_DIM)
    value = rows_by_columns[:, q_width + kv_width :].reshape(rows, KV_HEADS, HEAD_DIM)
    return jnp.concatenate([query, key, value], axis=2).transpose(1, 0, 2)


def join_heads_columns(by_head):
    rows = by_head.shape[1]
    q_each = HEADS // KV_HEADS * HEAD_DIM
    ordered = by_head.transpose(1, 0, 2)
    return jnp.concatenate(
        [
            ordered[:, :, :q_each].reshape(rows, -1),
            ordered[:, :, q_each : q_each + HEAD_DIM].reshape(rows, -1),
            ordered[:, :, q_each + HEAD_DIM :].reshape(rows, -1),
        ],
        axis=1,
    )


def on_device_split(
    tokens,
    output_cotangent,
    sequence_lengths,
    block_order,
    attn_input,
    input_moment,
    input_square,
    attn_output,
    output_moment,
    output_square,
    gate_up,
    gateup_moment,
    gateup_square,
    down_weight,
    down_moment,
    down_square,
    norm_gains,
    gains_moment,
    gains_square,
):
    row_count, model_width = tokens.shape
    head_groups = HEADS // KV_HEADS
    q_each = head_groups * HEAD_DIM
    score_scale = HEAD_DIM ** (-0.5)
    gain_one = norm_gains[:model_width]
    gain_two = norm_gains[model_width : 2 * model_width]
    gain_query = norm_gains[2 * model_width : 2 * model_width + HEAD_DIM]
    gain_key = norm_gains[2 * model_width + HEAD_DIM :]
    seq_lens = sequence_lengths[0]
    order_row = block_order[0]
    context_count = lax.axis_size("cp")
    data_count = lax.axis_size("dp")
    group_rows = context_count * row_count
    shard_rows = attn_input.shape[0]
    down_rows = down_weight.shape[0]
    offsets = jnp.arange(row_count, dtype=jnp.int32)
    positions = (order_row[:, None] * row_count + offsets[None, :]).reshape(group_rows)
    doc_index, seq_offset = locate(positions, seq_lens)
    cosine, sine = rope_tables(seq_offset)
    x_float = tokens.astype(jnp.float32)
    hat_one, inv_one = rms_parts(x_float)
    gateup_send = (
        gate_up.astype(jnp.bfloat16)
        .reshape(shard_rows, 2, data_count, context_count, down_rows)
        .transpose(1, 3, 0, 2, 4)
        .reshape(2, context_count, shard_rows, data_count * down_rows)
    )
    down_part = lax.all_gather(down_weight.astype(jnp.bfloat16), "dp", axis=0, tiled=True)
    (
        normed_one,
        normed_two,
        cotangent_all,
        input_part,
        output_all,
        gateup_part,
        raw,
        flat_parts,
        log_total,
        residual,
    ) = front(
        tokens,
        gain_one,
        gain_two,
        gain_query,
        gain_key,
        cosine.T,
        sine.T,
        positions,
        positions - seq_offset,
        split_heads_columns(attn_input.astype(jnp.bfloat16)),
        attn_output.astype(jnp.bfloat16),
        gateup_send[0],
        gateup_send[1],
        output_cotangent,
        data_count,
        context_count,
    )
    normed_one = normed_one.reshape(group_rows, model_width)
    normed_two = normed_two.reshape(group_rows, model_width)
    cotangent_all = cotangent_all.reshape(group_rows, model_width)
    input_part = input_part.reshape(model_width, -1)
    output_all = output_all.reshape(HEADS * HEAD_DIM, model_width)
    gateup_part = gateup_part.reshape(2, model_width, -1)
    flat_parts = flat_parts.reshape(HEADS * HEAD_DIM, row_count)
    projected = raw.T
    query_raw = projected[:, :q_each].reshape(group_rows, head_groups, HEAD_DIM)
    key_raw = projected[:, q_each : q_each + HEAD_DIM].reshape(group_rows, 1, HEAD_DIM)
    values = projected[:, q_each + HEAD_DIM :].astype(jnp.bfloat16)
    hat_query, inv_query = rms_parts(query_raw)
    hat_key, inv_key = rms_parts(key_raw)
    queries = rotate(hat_query * gain_query, cosine, sine).astype(jnp.bfloat16)
    keys = rotate(hat_key * gain_key, cosine, sine).astype(jnp.bfloat16)[:, 0]
    hat_two, inv_two = rms_parts(residual)
    gate_part = jnp.dot(normed_two, gateup_part[0], preferred_element_type=jnp.float32)
    up_part = jnp.dot(normed_two, gateup_part[1], preferred_element_type=jnp.float32)
    gate_sig = jax.nn.sigmoid(gate_part)
    gate_act = gate_part * gate_sig
    hidden = (gate_act * up_part).astype(jnp.bfloat16)
    d_hidden = contract_cols(cotangent_all, down_part)
    d_gate = d_hidden * up_part * (gate_sig * (1.0 + gate_part * (1.0 - gate_sig)))
    d_up = d_hidden * gate_act
    d_gate = d_gate.astype(jnp.bfloat16)
    d_up = d_up.astype(jnp.bfloat16)
    d_normed_two = scatter_line(
        (contract_cols(d_gate, gateup_part[0]) + contract_cols(d_up, gateup_part[1]))
        .astype(jnp.bfloat16)
        .reshape(context_count, row_count, model_width),
        3,
        "scatter_second",
    )
    grad_gain_two = jnp.sum(d_normed_two * hat_two, axis=0)
    d_residual = output_cotangent.astype(jnp.float32) + norm_back(
        d_normed_two * gain_two, hat_two, inv_two
    )
    d_branch = d_residual.astype(jnp.bfloat16)
    d_flat = contract_cols(d_branch, output_all).astype(jnp.bfloat16)
    d_attended = swap_blocks(
        d_flat.reshape(row_count, context_count, q_each).transpose(1, 0, 2), 4, "swap_back"
    ).reshape(group_rows, head_groups, HEAD_DIM)
    allowed = (doc_index[:, None] == doc_index[None, :]) & (
        positions[None, :] <= positions[:, None]
    )
    scores = (
        jnp.einsum("qgd,kd->gqk", queries, keys, preferred_element_type=jnp.float32) * score_scale
    )
    probs = jnp.exp(jnp.where(allowed, scores, masked_score) - log_total[:, :, None])
    probs_bf = probs.astype(jnp.bfloat16)
    d_probs = jnp.einsum("qgd,kd->gqk", d_attended, values, preferred_element_type=jnp.float32)
    delta = jnp.sum(probs * d_probs, axis=-1, keepdims=True)
    d_scores = (probs * (d_probs - delta)).astype(jnp.bfloat16)
    d_query_sum = (
        jnp.einsum("gqk,kd->qgd", d_scores, keys, preferred_element_type=jnp.float32) * score_scale
    )
    d_key_sum = (
        jnp.einsum("gqk,qgd->kd", d_scores, queries, preferred_element_type=jnp.float32)
        * score_scale
    )
    d_value = jnp.einsum("gqk,qgd->kd", probs_bf, d_attended, preferred_element_type=jnp.float32)
    d_query_rot = rotate(d_query_sum, cosine, -sine)
    grad_gain_query = jnp.sum(d_query_rot * hat_query, axis=(0, 1))
    d_query_raw = norm_back(d_query_rot * gain_query, hat_query, inv_query)
    d_key_rot = rotate(d_key_sum[:, None, :], cosine, -sine)
    grad_gain_key = jnp.sum(d_key_rot * hat_key, axis=(0, 1))
    d_key_raw = norm_back(d_key_rot * gain_key, hat_key, inv_key)
    d_projected = jnp.concatenate(
        [
            d_query_raw.reshape(group_rows, q_each),
            d_key_raw.reshape(group_rows, HEAD_DIM),
            d_value,
        ],
        axis=1,
    ).astype(jnp.bfloat16)
    d_normed_one = scatter_line(
        contract_cols(d_projected, input_part)
        .astype(jnp.bfloat16)
        .reshape(context_count, row_count, model_width),
        5,
        "scatter_first",
    )
    grad_gain_one = jnp.sum(d_normed_one * hat_one, axis=0)
    token_gradient = d_residual + norm_back(d_normed_one * gain_one, hat_one, inv_one)
    mixed = (
        residual
        + scatter_line(
            jnp.dot(hidden, down_part, preferred_element_type=jnp.float32)
            .astype(jnp.bfloat16)
            .reshape(context_count, row_count, model_width),
            6,
            "scatter_down",
        )
    ).astype(jnp.bfloat16)

    def owned_rows(grad, collective_id, name):
        share = lax.psum_scatter(
            grad.astype(jnp.bfloat16), "dp", scatter_dimension=0, tiled=True
        )
        return swap_blocks(share.reshape(context_count, shard_rows, -1), collective_id, name)

    grad_down = lax.psum_scatter(
        contract_rows(hidden, cotangent_all).astype(jnp.bfloat16),
        "dp",
        scatter_dimension=0,
        tiled=True,
    ).astype(jnp.float32)
    grad_gateup = [
        owned_rows(contract_rows(normed_two, part), 7 + index, "swap_gateup")
        .reshape(context_count, shard_rows, data_count, down_rows)
        .transpose(1, 2, 0, 3)
        .reshape(shard_rows, -1)
        for index, part in enumerate((d_gate, d_up))
    ]
    grad_gateup = jnp.concatenate(grad_gateup, axis=1).astype(jnp.float32)
    grad_output = lax.psum_scatter(
        lax.psum_scatter(
            jnp.dot(flat_parts, d_branch, preferred_element_type=jnp.float32).astype(jnp.bfloat16),
            "dp",
            scatter_dimension=0,
            tiled=True,
        ),
        "cp",
        scatter_dimension=0,
        tiled=True,
    ).astype(jnp.float32)
    grad_input = join_heads_columns(
        owned_rows(contract_rows(normed_one, d_projected), 9, "swap_input")
    ).astype(jnp.float32)
    gain_grads = jnp.concatenate([grad_gain_one, grad_gain_two, grad_gain_query, grad_gain_key])
    gain_grads = total_everywhere(
        gain_grads.reshape(-1, 128), data_count, context_count, 10
    ).reshape(-1)
    input_next, input_moment_next, input_square_next = adam_update(
        attn_input, input_moment, input_square, grad_input, rate_input, weight_decay
    )
    output_next, output_moment_next, output_square_next = adam_update(
        attn_output, output_moment, output_square, grad_output, rate_output, weight_decay
    )
    gateup_next, gateup_moment_next, gateup_square_next = adam_update(
        gate_up, gateup_moment, gateup_square, grad_gateup, rate_gateup, weight_decay
    )
    down_next, down_moment_next, down_square_next = adam_update(
        down_weight, down_moment, down_square, grad_down, rate_down, weight_decay
    )
    gains_next, gains_moment_next, gains_square_next = adam_update(
        norm_gains, gains_moment, gains_square, gain_grads, rate_gains, 0.0
    )
    return (
        mixed,
        token_gradient,
        input_next,
        input_moment_next,
        input_square_next,
        output_next,
        output_moment_next,
        output_square_next,
        gateup_next,
        gateup_moment_next,
        gateup_square_next,
        down_next,
        down_moment_next,
        down_square_next,
        gains_next,
        gains_moment_next,
        gains_square_next,
    )


def solution(mesh):
    in_specs = (
        P(("dp", "cp"), None),
        P(("dp", "cp"), None),
        P("dp", None),
        P("dp", None),
        P(("dp", "cp"), None),
        P(("dp", "cp"), None),
        P(("dp", "cp"), None),
        P(("dp", "cp"), None),
        P(("dp", "cp"), None),
        P(("dp", "cp"), None),
        P(("dp", "cp"), None),
        P(("dp", "cp"), None),
        P(("dp", "cp"), None),
        P(("dp", "cp"), None),
        P(("dp", "cp"), None),
        P(("dp", "cp"), None),
        P(),
        P(),
        P(),
    )
    out_specs = (
        P(("dp", "cp"), None),
        P(("dp", "cp"), None),
        P(("dp", "cp"), None),
        P(("dp", "cp"), None),
        P(("dp", "cp"), None),
        P(("dp", "cp"), None),
        P(("dp", "cp"), None),
        P(("dp", "cp"), None),
        P(("dp", "cp"), None),
        P(("dp", "cp"), None),
        P(("dp", "cp"), None),
        P(("dp", "cp"), None),
        P(("dp", "cp"), None),
        P(("dp", "cp"), None),
        P(),
        P(),
        P(),
    )
    sizes = (mesh.shape["dp"], mesh.shape["cp"])
    body = on_device_split if sizes == (4, KV_HEADS) else on_device
    return jax.shard_map(
        body, mesh=mesh, in_specs=in_specs, out_specs=out_specs, check_vma=False
    )
```

```python
import functools
import math

import jax
import jax.numpy as jnp
from jax import lax
from jax.experimental import pallas as pl
from jax.experimental.pallas import tpu as pltpu
from jax.sharding import PartitionSpec as P

HEADS = 24
KV_HEADS = 8
HEAD_DIM = 64
FF = 6912
STEP = 10


norm_eps = 1e-05
rope_base = 1000000.0
beta_one = 0.9
beta_two = 0.95
adam_eps = 1e-08
rate_input = 0.06
rate_output = 0.9
rate_gateup = 0.06
rate_down = 0.03
rate_gains = 0.5
weight_decay = 0.1
masked_score = -1e30


def rope_tables(offsets):
    half_dim = HEAD_DIM // 2
    freqs = jnp.exp(
        jnp.arange(half_dim, dtype=jnp.float32) * (-2.0 * math.log(rope_base) / HEAD_DIM)
    )
    angles = offsets.astype(jnp.float32)[:, None] * freqs[None, :]
    return (jnp.cos(angles), jnp.sin(angles))


def rotate(values, cosine, sine):
    half_dim = HEAD_DIM // 2
    first_half = values[..., :half_dim]
    second_half = values[..., half_dim:]
    cos_wide = cosine[:, None, :]
    sin_wide = sine[:, None, :]
    return jnp.concatenate(
        [
            first_half * cos_wide - second_half * sin_wide,
            second_half * cos_wide + first_half * sin_wide,
        ],
        axis=-1,
    )


def locate(positions, lengths):
    seq_ends = jnp.cumsum(lengths)
    starts = seq_ends - lengths
    doc_index = jnp.sum((positions[:, None] >= seq_ends[None, :]).astype(jnp.int32), axis=1)
    picked = (doc_index[:, None] == jnp.arange(lengths.shape[0], dtype=jnp.int32)[None, :]).astype(
        jnp.int32
    )
    return (doc_index, positions - jnp.sum(picked * starts[None, :], axis=1))


def rms_parts(values):
    inverse = lax.rsqrt(jnp.mean(values * values, axis=-1, keepdims=True) + norm_eps)
    return (values * inverse, inverse)


def norm_back(d_normed, normal_hat, inverse):
    return inverse * (
        d_normed - normal_hat * jnp.mean(d_normed * normal_hat, axis=-1, keepdims=True)
    )


def contract_rows(left, right):
    return lax.dot_general(
        left, right, (((0,), (0,)), ((), ())), preferred_element_type=jnp.float32
    )


def contract_cols(left, right):
    return lax.dot_general(
        left, right, (((1,), (1,)), ((), ())), preferred_element_type=jnp.float32
    )


def owner_order(values, data_count, context_count):
    lead = values.shape[0]
    each = values.shape[1] // (data_count * context_count)
    return (
        values.reshape(lead, data_count, context_count, each)
        .transpose(0, 2, 1, 3)
        .reshape(lead, values.shape[1])
    )


def adam_update(weight, first_moment, second_moment, gradient, rate, decay):
    first_moment = beta_one * first_moment + (1.0 - beta_one) * gradient
    second_moment = beta_two * second_moment + (1.0 - beta_two) * gradient * gradient
    first_fix = 1.0 - beta_one**STEP
    second_fix = 1.0 - beta_two**STEP
    direction = first_moment / first_fix / (jnp.sqrt(second_moment / second_fix) + adam_eps)
    return (weight - rate * (direction + decay * weight), first_moment, second_moment)


def on_device(
    tokens,
    output_cotangent,
    sequence_lengths,
    block_order,
    attn_input,
    input_moment,
    input_square,
    attn_output,
    output_moment,
    output_square,
    gate_up,
    gateup_moment,
    gateup_square,
    down_weight,
    down_moment,
    down_square,
    norm_gains,
    gains_moment,
    gains_square,
):
    row_count = tokens.shape[0]
    model_width = tokens.shape[1]
    q_width = HEADS * HEAD_DIM
    kv_width = KV_HEADS * HEAD_DIM
    proj_width = q_width + 2 * kv_width
    head_groups = HEADS // KV_HEADS
    score_scale = HEAD_DIM ** (-0.5)
    gain_one = norm_gains[:model_width]
    gain_two = norm_gains[model_width : 2 * model_width]
    gain_query = norm_gains[2 * model_width : 2 * model_width + HEAD_DIM]
    gain_key = norm_gains[2 * model_width + HEAD_DIM :]
    seq_lens = sequence_lengths[0]
    order_row = block_order[0]
    context_count = lax.axis_size("cp")
    data_count = lax.axis_size("dp")
    own_slot = lax.axis_index("cp")
    offsets = jnp.arange(row_count, dtype=jnp.int32)
    own_block = jnp.sum(
        jnp.where(jnp.arange(context_count, dtype=jnp.int32) == own_slot, order_row, 0)
    )
    positions = own_block * row_count + offsets
    key_positions = (order_row[:, None] * row_count + offsets[None, :]).reshape(
        context_count * row_count
    )
    doc_index, seq_offset = locate(positions, seq_lens)
    key_doc = locate(key_positions, seq_lens)[0]
    cosine, sine = rope_tables(seq_offset)
    input_bf = attn_input.astype(jnp.bfloat16)
    output_bf = attn_output.astype(jnp.bfloat16)
    gateup_bf = gate_up.astype(jnp.bfloat16)
    down_bf = down_weight.astype(jnp.bfloat16)
    input_all, output_all = (
        lax.all_gather(input_bf, ("dp", "cp"), axis=0, tiled=True),
        lax.all_gather(output_bf, ("dp", "cp"), axis=0, tiled=True),
    )
    x_float = tokens.astype(jnp.float32)
    hat_one, inv_one = rms_parts(x_float)
    normed_one = (hat_one * gain_one).astype(jnp.bfloat16)
    projected = jnp.dot(normed_one, input_all, preferred_element_type=jnp.float32)
    query_raw = projected[:, :q_width].reshape(row_count, HEADS, HEAD_DIM)
    key_raw = projected[:, q_width : q_width + kv_width].reshape(row_count, KV_HEADS, HEAD_DIM)
    value_raw = projected[:, q_width + kv_width :]
    hat_query, inv_query = rms_parts(query_raw)
    hat_key, inv_key = rms_parts(key_raw)
    queries = rotate(hat_query * gain_query, cosine, sine).astype(jnp.bfloat16)
    key_rot = rotate(hat_key * gain_key, cosine, sine)
    key_value = jnp.concatenate([key_rot.reshape(row_count, kv_width), value_raw], axis=1).astype(
        jnp.bfloat16
    )
    kv_all = lax.all_gather(key_value, "cp", axis=0, tiled=True)
    total_keys = kv_all.shape[0]
    key_span = min(512, total_keys)
    block_count = total_keys // key_span
    kv_blocks = kv_all.reshape(block_count, key_span, 2 * kv_width)
    pos_blocks = key_positions.reshape(block_count, key_span)
    doc_blocks = key_doc.reshape(block_count, key_span)
    query_group = queries.reshape(row_count, KV_HEADS, head_groups, HEAD_DIM)

    def block_scores(kv_block, key_pos, key_docs):
        key_block = kv_block[:, :kv_width].reshape(key_span, KV_HEADS, HEAD_DIM)
        value_block = kv_block[:, kv_width:].reshape(key_span, KV_HEADS, HEAD_DIM)
        scores = (
            jnp.einsum("qhgd,khd->hgqk", query_group, key_block, preferred_element_type=jnp.float32)
            * score_scale
        )
        allowed = (doc_index[:, None] == key_docs[None, :]) & (
            key_pos[None, :] <= positions[:, None]
        )
        return (key_block, value_block, jnp.where(allowed, scores, masked_score), allowed)

    def forward_block(carry, items):
        run_max, run_total, run_sum = carry
        key_block, value_block, scores, allowed = block_scores(*items)
        new_max = jnp.maximum(run_max, jnp.max(scores, axis=-1))
        weights = jnp.where(allowed, jnp.exp(scores - new_max[..., None]), 0.0)
        factor = jnp.exp(run_max - new_max)
        run_total = run_total * factor + jnp.sum(weights, axis=-1)
        run_sum = run_sum * factor[..., None] + jnp.einsum(
            "hgqk,khd->hgqd",
            weights.astype(jnp.bfloat16),
            value_block,
            preferred_element_type=jnp.float32,
        )
        return ((new_max, run_total, run_sum), None)

    start_state = (
        jnp.full((KV_HEADS, head_groups, row_count), masked_score, jnp.float32),
        jnp.zeros((KV_HEADS, head_groups, row_count), jnp.float32),
        jnp.zeros((KV_HEADS, head_groups, row_count, HEAD_DIM), jnp.float32),
    )
    (run_max, run_total, run_sum), unused = lax.scan(
        forward_block, start_state, (kv_blocks, pos_blocks, doc_blocks)
    )
    attended = run_sum / run_total[..., None]
    log_total = run_max + jnp.log(run_total)
    attn_flat = attended.transpose(2, 0, 1, 3).reshape(row_count, q_width).astype(jnp.bfloat16)
    residual = x_float + jnp.dot(attn_flat, output_all, preferred_element_type=jnp.float32)
    hat_two, inv_two = rms_parts(residual)
    normed_two = (hat_two * gain_two).astype(jnp.bfloat16)
    columns = normed_two
    gate_both = jnp.dot(
        columns,
        lax.all_gather(gateup_bf, ("dp", "cp"), axis=0, tiled=True),
        preferred_element_type=jnp.float32,
    )
    gate_part = gate_both[:, :FF]
    up_part = gate_both[:, FF:]
    gate_sig = jax.nn.sigmoid(gate_part)
    gate_act = gate_part * gate_sig
    hidden = (gate_act * up_part).astype(jnp.bfloat16)
    columns = hidden
    ff_result = jnp.dot(
        columns,
        lax.all_gather(down_bf, ("dp", "cp"), axis=0, tiled=True),
        preferred_element_type=jnp.float32,
    )
    mixed = (residual + ff_result).astype(jnp.bfloat16)
    d_hidden = contract_cols(
        output_cotangent, lax.all_gather(down_bf, ("dp", "cp"), axis=0, tiled=True)
    )
    d_gate = d_hidden * up_part * (gate_sig * (1.0 + gate_part * (1.0 - gate_sig)))
    d_up = d_hidden * gate_act
    d_gate_both = jnp.concatenate([d_gate, d_up], axis=1).astype(jnp.bfloat16)
    d_normed_two = contract_cols(
        d_gate_both, lax.all_gather(gateup_bf, ("dp", "cp"), axis=0, tiled=True)
    )
    grad_gain_two = jnp.sum(d_normed_two * hat_two, axis=0)
    d_residual = output_cotangent.astype(jnp.float32) + norm_back(
        d_normed_two * gain_two, hat_two, inv_two
    )
    d_branch = d_residual.astype(jnp.bfloat16)
    input_back, output_back = (input_all, output_all)
    d_flat = contract_cols(d_branch, output_back).astype(jnp.bfloat16)
    d_attended = d_flat.reshape(row_count, KV_HEADS, head_groups, HEAD_DIM).transpose(1, 2, 0, 3)
    delta = jnp.sum(d_attended.astype(jnp.float32) * attended, axis=-1)

    def backward_block(d_query_sum, items):
        key_block, value_block, scores, allowed = block_scores(*items)
        probs = jnp.where(allowed, jnp.exp(scores - log_total[..., None]), 0.0)
        d_probs = jnp.einsum(
            "hgqd,khd->hgqk", d_attended, value_block, preferred_element_type=jnp.float32
        )
        d_scores = (probs * (d_probs - delta[..., None])).astype(jnp.bfloat16)
        d_query_sum = (
            d_query_sum
            + jnp.einsum("hgqk,khd->hgqd", d_scores, key_block, preferred_element_type=jnp.float32)
            * score_scale
        )
        d_keys = (
            jnp.einsum("hgqk,qhgd->khd", d_scores, query_group, preferred_element_type=jnp.float32)
            * score_scale
        )
        d_values = jnp.einsum(
            "hgqk,hgqd->khd",
            probs.astype(jnp.bfloat16),
            d_attended,
            preferred_element_type=jnp.float32,
        )
        return (
            d_query_sum,
            jnp.concatenate(
                [d_keys.reshape(key_span, kv_width), d_values.reshape(key_span, kv_width)], axis=1
            ),
        )

    d_query_sum, d_kv_blocks = lax.scan(
        backward_block,
        jnp.zeros((KV_HEADS, head_groups, row_count, HEAD_DIM), jnp.float32),
        (kv_blocks, pos_blocks, doc_blocks),
    )
    d_kv = lax.psum_scatter(
        d_kv_blocks.reshape(total_keys, 2 * kv_width).astype(jnp.bfloat16),
        "cp",
        scatter_dimension=0,
        tiled=True,
    ).astype(jnp.float32)
    d_query_rot = rotate(
        d_query_sum.transpose(2, 0, 1, 3).reshape(row_count, HEADS, HEAD_DIM), cosine, -sine
    )
    grad_gain_query = jnp.sum(d_query_rot * hat_query, axis=(0, 1))
    d_query_raw = norm_back(d_query_rot * gain_query, hat_query, inv_query)
    d_key_rot = rotate(d_kv[:, :kv_width].reshape(row_count, KV_HEADS, HEAD_DIM), cosine, -sine)
    grad_gain_key = jnp.sum(d_key_rot * hat_key, axis=(0, 1))
    d_key_raw = norm_back(d_key_rot * gain_key, hat_key, inv_key)
    d_projected = jnp.concatenate(
        [
            d_query_raw.reshape(row_count, q_width),
            d_key_raw.reshape(row_count, kv_width),
            d_kv[:, kv_width:],
        ],
        axis=1,
    ).astype(jnp.bfloat16)
    d_normed_one = contract_cols(d_projected, input_back)
    grad_gain_one = jnp.sum(d_normed_one * hat_one, axis=0)
    token_gradient = d_residual + norm_back(d_normed_one * gain_one, hat_one, inv_one)

    def make_wide(first_src, attn_src, second_src):

        def wide_terms(row_start, row_total):
            return jnp.concatenate(
                [
                    contract_rows(first_src, d_projected),
                    contract_rows(attn_src, d_branch),
                    contract_rows(second_src, d_gate_both),
                ],
                axis=1,
            )

        return wide_terms

    def make_down(hidden_src):

        def down_terms(row_start, row_total):
            return contract_rows(hidden_src, output_cotangent)

        return down_terms

    shard_rows = attn_input.shape[0]
    down_rows = down_weight.shape[0]
    wide_fn = make_wide(
        owner_order(normed_one, data_count, context_count),
        owner_order(attn_flat, data_count, context_count),
        owner_order(normed_two, data_count, context_count),
    )
    down_fn = make_down(owner_order(hidden, data_count, context_count))
    group_wide = lax.psum_scatter(
        wide_fn(jnp.int32(0), lax.axis_size("cp") * (shard_rows * data_count)).astype(jnp.bfloat16),
        "cp",
        scatter_dimension=0,
        tiled=True,
    )
    group_down = lax.psum_scatter(
        down_fn(jnp.int32(0), lax.axis_size("cp") * (down_rows * data_count)).astype(jnp.bfloat16),
        "cp",
        scatter_dimension=0,
        tiled=True,
    )
    wide_grads, down_grads = (
        lax.psum_scatter(group_wide, "dp", scatter_dimension=0, tiled=True).astype(jnp.float32),
        lax.psum_scatter(group_down, "dp", scatter_dimension=0, tiled=True).astype(jnp.float32),
    )
    gain_grads = lax.psum(
        jnp.concatenate([grad_gain_one, grad_gain_two, grad_gain_query, grad_gain_key]),
        ("dp", "cp"),
    )
    grad_input = wide_grads[:, :proj_width]
    grad_output = wide_grads[:, proj_width : proj_width + model_width]
    grad_gateup = wide_grads[:, proj_width + model_width :]
    input_next, input_moment_next, input_square_next = adam_update(
        attn_input, input_moment, input_square, grad_input, rate_input, weight_decay
    )
    output_next, output_moment_next, output_square_next = adam_update(
        attn_output, output_moment, output_square, grad_output, rate_output, weight_decay
    )
    gateup_next, gateup_moment_next, gateup_square_next = adam_update(
        gate_up, gateup_moment, gateup_square, grad_gateup, rate_gateup, weight_decay
    )
    down_next, down_moment_next, down_square_next = adam_update(
        down_weight, down_moment, down_square, down_grads, rate_down, weight_decay
    )
    gains_next, gains_moment_next, gains_square_next = adam_update(
        norm_gains, gains_moment, gains_square, gain_grads, rate_gains, 0.0
    )
    return (
        mixed,
        token_gradient,
        input_next,
        input_moment_next,
        input_square_next,
        output_next,
        output_moment_next,
        output_square_next,
        gateup_next,
        gateup_moment_next,
        gateup_square_next,
        down_next,
        down_moment_next,
        down_square_next,
        gains_next,
        gains_moment_next,
        gains_square_next,
    )


MESH = pl.DeviceIdType.MESH


def place():
    dp = lax.axis_index("dp")
    cp = lax.axis_index("cp")
    return dp, cp, cp // 2, cp % 2


def greet(targets):
    barrier = pltpu.get_barrier_semaphore()
    for target in targets:
        pl.semaphore_signal(barrier, inc=1, device_id=target, device_id_type=MESH)
    pl.semaphore_wait(barrier, len(targets))


def send(source, target, send_sem, recv_sem, device):
    return pltpu.make_async_remote_copy(
        src_ref=source,
        dst_ref=target,
        send_sem=send_sem,
        recv_sem=recv_sem,
        device_id=device,
        device_id_type=MESH,
    )


class LineGather:
    def __init__(self, own_ref, all_ref, sems, where, depth, both=True):
        self.own, self.where, self.depth, self.both = own_ref, where, depth, both
        self.slot = all_ref if callable(all_ref) else lambda slot: all_ref.at[slot]
        self.right, self.left, self.sib, self.recv, self.local = sems

    @staticmethod
    def scratch(depth):
        return [pltpu.SemaphoreType.DMA((2 * depth,))] * 4 + [pltpu.SemaphoreType.DMA]

    def copy(self, kind, slot, source):
        dp, cp, z, core = self.where
        device = {"right": (dp, cp + 2), "left": (dp, cp - 2), "sib": (dp, cp ^ 1)}[kind]
        sem = {"right": self.right, "left": self.left, "sib": self.sib}[kind]
        return send(source, self.slot(slot), sem.at[slot], self.recv.at[slot], device)

    def keep(self):
        return pltpu.make_async_copy(self.own, self.slot(self.where[1]), self.local)

    def start(self):
        dp, cp, z, core = self.where

        @pl.when(z < self.depth - 1)
        def _():
            self.copy("right", cp, self.own).start()

        @pl.when(z > 0)
        def _():
            self.copy("left", cp, self.own).start()

        if self.both:
            self.copy("sib", cp, self.own).start()
        self.keep().start()

    def step(self, far):
        dp, cp, z, core = self.where

        @pl.when(z >= far)
        def _():
            slot = cp - 2 * far
            self.copy("right", slot, self.own).wait_recv()

            @pl.when(z < self.depth - 1)
            def _():
                self.copy("right", slot, self.slot(slot)).start()

            if self.both:
                self.copy("sib", slot, self.slot(slot)).start()

        @pl.when(z + far < self.depth)
        def _():
            slot = cp + 2 * far
            self.copy("left", slot, self.own).wait_recv()

            @pl.when(z > 0)
            def _():
                self.copy("left", slot, self.slot(slot)).start()

            if self.both:
                self.copy("sib", slot, self.slot(slot)).start()

    def finish(self):
        dp, cp, z, core = self.where
        if self.both:
            for spot in range(self.depth):
                self.copy("sib", 1 - core + 2 * spot, self.own).wait_recv()
        self.keep().wait()
        for spot in range(self.depth):
            slot = 2 * spot + core
            if self.both:
                self.copy("sib", slot, self.own).wait_send()

            @pl.when((spot <= z) & (z < self.depth - 1))
            def _():
                self.copy("right", slot, self.own).wait_send()

            @pl.when((spot >= z) & (z > 0))
            def _():
                self.copy("left", slot, self.own).wait_send()


class Swap:
    def __init__(self, source_ref, target_ref, sems, where, count):
        self.source, self.where, self.count = source_ref, where, count
        self.slot = target_ref if callable(target_ref) else lambda slot: target_ref.at[slot]
        self.origin = source_ref if callable(source_ref) else lambda slot: source_ref.at[slot]
        self.sent, self.recv, self.local = sems

    @staticmethod
    def scratch(count):
        return [pltpu.SemaphoreType.DMA((count,))] * 2 + [pltpu.SemaphoreType.DMA]

    def copy(self, peer):
        dp, cp, z, core = self.where
        return send(
            self.origin(peer),
            self.slot(cp),
            self.sent.at[peer],
            self.recv.at[cp],
            (dp, peer),
        )

    def keep(self):
        cp = self.where[1]
        return pltpu.make_async_copy(self.origin(cp), self.slot(cp), self.local)

    def start(self):
        cp = self.where[1]
        for turn in range(self.count - 1, 0, -1):
            self.copy(cp ^ turn).start()
        self.keep().start()

    def arrive(self, peer):
        dp, cp, z, core = self.where
        send(
            self.origin(peer),
            self.slot(peer),
            self.sent.at[peer],
            self.recv.at[peer],
            (dp, peer),
        ).wait_recv()

    def finish_recv(self):
        cp = self.where[1]
        for turn in range(1, self.count):
            self.arrive(cp ^ turn)
        self.keep().wait()

    def finish_send(self):
        cp = self.where[1]
        for turn in range(1, self.count):
            self.copy(cp ^ turn).wait_send()


class RingSpread:
    def __init__(self, block, half, sems, where):
        self.block, self.half, self.where = block, half, where
        self.sent, self.recv = sems

    @staticmethod
    def scratch():
        return [pltpu.SemaphoreType.DMA((4,))] * 2

    def copy(self, kind, mine):
        dp, cp, z, core = self.where
        turn = (1, 2, 2, 1)[kind]
        if kind < 2:
            part = self.block(dp if mine else dp ^ turn)
        else:
            part = self.half(dp ^ (3 - turn) if mine else dp ^ 3, kind - 2)
        return send(part, part, self.sent.at[kind], self.recv.at[kind], (dp ^ turn, cp))

    def start(self):
        self.copy(0, True).start()
        self.copy(1, True).start()

    def forward(self):
        self.copy(0, False).wait_recv()
        self.copy(2, True).start()
        self.copy(1, False).wait_recv()
        self.copy(3, True).start()

    def finish(self):
        self.copy(2, False).wait_recv()
        self.copy(3, False).wait_recv()
        for kind in range(4):
            self.copy(kind, True).wait_send()


def turn_heads(values, cosine, sine):
    half = values.shape[0] // 2
    first, second = values[:half], values[half:]
    return jnp.concatenate([first * cosine - second * sine, second * cosine + first * sine], axis=0)


def head_hat(values):
    inverse = lax.rsqrt(jnp.mean(values * values, axis=0, keepdims=True) + norm_eps)
    return values * inverse, inverse


def score_block(keys, queries, key_place, query_place, query_start):
    scores = jnp.dot(keys, queries, preferred_element_type=jnp.float32) * HEAD_DIM ** (-0.5)
    allowed = (key_place <= query_place) & (key_place >= query_start)
    return jnp.where(allowed, scores, masked_score), allowed


def front_kernel(
    tile,
    tokens_ref,
    gain_one_ref,
    gain_two_ref,
    gain_query_ref,
    gain_key_ref,
    cosine_ref,
    sine_ref,
    key_place_ref,
    query_place_ref,
    query_start_ref,
    input_send,
    output_own,
    gate_send,
    up_send,
    cotangent_own,
    normed_one_out,
    normed_two_out,
    cotangent_all,
    input_out,
    output_out,
    gateup_out,
    raw_out,
    flat_out,
    total_out,
    residual_out,
    normed_one,
    normed_two,
    own_one,
    own_two,
    inputs,
    outputs,
    raw,
    queries,
    keys_up,
    values,
    flat_send,
    flat_recv,
    out_sems,
    *sems,
):
    where = place()
    dp, cp, z, core = where
    context_count = normed_one.shape[0]
    depth = context_count // 2
    rows = tokens_ref.shape[0]
    width = tokens_ref.shape[1]
    q_each = HEADS // KV_HEADS * HEAD_DIM
    take = iter(range(len(sems)))

    def some(count):
        return [sems[next(take)] for _ in range(count)]

    greet([(dp, cp ^ turn) for turn in range(1, context_count)] + [(dp ^ 1, cp), (dp ^ 2, cp)])
    token_line = LineGather(own_one, normed_one, some(5), where, depth)
    second_line = LineGather(own_two, normed_two, some(5), where, depth)
    cotangent_line = LineGather(cotangent_own, cotangent_all, some(5), where, depth)
    output_line = LineGather(
        output_own, lambda slot: outputs.at[dp, slot // 2, core], some(5), where, depth, False
    )
    input_swap = Swap(input_send, inputs.at[dp], some(3), where, context_count)
    shard = input_send.shape[1]

    def gateup_slot(index):
        return lambda slot: gateup_out.at[index, dp, pl.ds(pl.multiple_of(slot * shard, 16), shard)]

    gate_swap = Swap(gate_send, gateup_slot(0), some(3), where, context_count)
    up_swap = Swap(up_send, gateup_slot(1), some(3), where, context_count)
    flat_swap = Swap(flat_send, flat_recv, some(3), where, context_count)
    input_ring = RingSpread(
        lambda d: inputs.at[d],
        lambda d, h: inputs.at[d, pl.ds(h * (context_count // 2), context_count // 2)],
        some(2),
        where,
    )
    output_ring = RingSpread(
        lambda d: outputs.at[d, :, core],
        lambda d, h: outputs.at[d, pl.ds(h * (depth // 2), depth // 2), core],
        some(2),
        where,
    )
    half_rows = gateup_out.shape[2] // 2

    def gateup_ring(index):
        return RingSpread(
            lambda d: gateup_out.at[index, d],
            lambda d, h: gateup_out.at[index, d, pl.ds(h * half_rows, half_rows)],
            some(2),
            where,
        )

    gate_ring, up_ring = gateup_ring(0), gateup_ring(1)
    share_sent, share_recv = some(2)

    def share(mine):
        part = outputs.at[:, :, core if mine else 1 - core]
        return send(part, part, share_sent, share_recv, (dp, cp ^ 1))

    x_float = tokens_ref[...].astype(jnp.float32)
    hat_one, _ = rms_parts(x_float)
    own_one[...] = (hat_one * gain_one_ref[...]).astype(jnp.bfloat16)
    input_swap.start()
    token_line.start()
    output_line.start()
    token_line.step(1)
    output_line.step(1)
    input_swap.finish_recv()
    input_ring.start()
    token_line.step(2)
    output_line.step(2)
    gate_swap.start()
    input_ring.forward()
    token_line.step(3)
    output_line.step(3)
    up_swap.start()
    output_line.finish()
    output_ring.start()
    token_line.finish()
    input_ring.finish()
    one_copy = pltpu.make_async_copy(normed_one, normed_one_out, out_sems.at[0])
    one_copy.start()
    input_copy = pltpu.make_async_copy(inputs, input_out, out_sems.at[1])
    input_copy.start()

    weights = inputs[...].reshape(width, inputs.shape[-1])

    def project(turn, carry):
        lanes = pl.ds(pl.multiple_of(turn * tile, tile), tile)
        block = normed_one[pl.ds(turn * (tile // rows), tile // rows)].reshape(tile, width)
        part = jnp.dot(block, weights, preferred_element_type=jnp.float32).T
        raw[:, lanes] = part
        cosine, sine = cosine_ref[:, lanes], sine_ref[:, lanes]
        for head in range(HEADS // KV_HEADS):
            hat, _ = head_hat(part[head * HEAD_DIM : (head + 1) * HEAD_DIM])
            queries[head * HEAD_DIM : (head + 1) * HEAD_DIM, lanes] = turn_heads(
                hat * gain_query_ref[...], cosine, sine
            ).astype(jnp.bfloat16)
        hat, _ = head_hat(part[q_each : q_each + HEAD_DIM])
        key = turn_heads(hat * gain_key_ref[...], cosine, sine)
        keys_up[pl.ds(pl.multiple_of(turn * tile, tile), tile)] = key.T.astype(jnp.bfloat16)
        values[:, lanes] = part[q_each + HEAD_DIM :].astype(jnp.bfloat16)
        return carry

    lax.fori_loop(0, normed_one.shape[0] * rows // tile, project, 0)
    raw_copy = pltpu.make_async_copy(raw, raw_out, out_sems.at[2])
    raw_copy.start()

    def attend(turn, carry):
        lanes = pl.ds(pl.multiple_of(turn * tile, tile), tile)
        query_place, query_start = query_place_ref[:, lanes], query_start_ref[:, lanes]
        for head in range(HEADS // KV_HEADS):
            spot = pl.ds(head * HEAD_DIM, HEAD_DIM)
            scores, allowed = score_block(
                keys_up[...], queries[spot, lanes], key_place_ref[...], query_place, query_start
            )
            top = jnp.max(scores, axis=0, keepdims=True)
            exps = jnp.exp(scores - top)
            total = jnp.sum(exps, axis=0, keepdims=True)
            total_out[pl.ds(head, 1), lanes] = top + jnp.log(total)
            probs = (exps * (1.0 / total)).astype(jnp.bfloat16)
            attended = jnp.dot(values[...], probs, preferred_element_type=jnp.float32)
            for part in range(tile // rows):
                flat_send[turn * (tile // rows) + part, spot] = attended[
                    :, part * rows : (part + 1) * rows
                ].astype(jnp.bfloat16)
        return carry

    turns = normed_one.shape[0] * rows // tile
    attend(0, 0)
    gate_swap.finish_recv()
    gate_ring.start()
    output_ring.forward()
    lax.fori_loop(1, turns, attend, 0)
    flat_swap.start()
    up_swap.finish_recv()
    up_ring.start()
    output_ring.finish()
    share(True).start()
    gate_ring.forward()
    cotangent_line.start()
    share(False).wait_recv()
    output_copy = pltpu.make_async_copy(outputs, output_out, out_sems.at[3])
    output_copy.start()
    flat_swap.finish_recv()
    flat_copy = pltpu.make_async_copy(flat_recv, flat_out, out_sems.at[4])
    flat_copy.start()
    flat = flat_recv[...].reshape(HEADS * HEAD_DIM, rows).astype(jnp.float32).T.astype(jnp.bfloat16)
    residual = x_float + jnp.dot(
        flat, outputs[...].reshape(HEADS * HEAD_DIM, width), preferred_element_type=jnp.float32
    )
    residual_out[...] = residual
    hat_two, _ = rms_parts(residual)
    own_two[...] = (hat_two * gain_two_ref[...]).astype(jnp.bfloat16)
    second_line.start()
    for far in range(1, depth):
        second_line.step(far)
        cotangent_line.step(far)
        if far == 1:
            up_ring.forward()
    second_line.finish()
    two_copy = pltpu.make_async_copy(normed_two, normed_two_out, out_sems.at[5])
    two_copy.start()
    cotangent_line.finish()
    gate_ring.finish()
    up_ring.finish()
    share(True).wait_send()
    for swap in (input_swap, gate_swap, up_swap, flat_swap):
        swap.finish_send()
    for copy in (one_copy, input_copy, raw_copy, output_copy, flat_copy, two_copy):
        copy.wait()


def front(
    tokens,
    gain_one,
    gain_two,
    gain_query,
    gain_key,
    cosine,
    sine,
    places,
    starts,
    input_send,
    output_own,
    gate_send,
    up_send,
    cotangent,
    data_count,
    context_count,
):
    rows, width = tokens.shape
    depth = context_count // 2
    group_rows = rows * context_count
    shard = input_send.shape[1]
    each = input_send.shape[2]
    hidden = gate_send.shape[2]
    q_each = HEADS // KV_HEADS * HEAD_DIM
    flat_width = HEADS * HEAD_DIM
    bf = jnp.bfloat16
    any_space = pl.BlockSpec(memory_space=pl.ANY)
    in_vmem = pl.BlockSpec(memory_space=pltpu.VMEM)
    shapes = [
        ((context_count, rows, width), bf, any_space),
        ((context_count, rows, width), bf, any_space),
        ((context_count, rows, width), bf, any_space),
        ((data_count, context_count, shard, each), bf, any_space),
        ((data_count, depth, 2, shard, width), bf, any_space),
        ((2, data_count, context_count * shard, hidden), bf, any_space),
        ((each, group_rows), jnp.float32, any_space),
        ((context_count, q_each, rows), bf, any_space),
        ((HEADS // KV_HEADS, group_rows), jnp.float32, in_vmem),
        ((rows, width), jnp.float32, in_vmem),
    ]
    return pl.pallas_call(
        functools.partial(front_kernel, 2 * rows),
        out_shape=[jax.ShapeDtypeStruct(shape, kind) for shape, kind, _ in shapes],
        in_specs=[in_vmem] * 10 + [any_space] * 5,
        out_specs=[space for _, _, space in shapes],
        scratch_shapes=[
            pltpu.VMEM((context_count, rows, width), bf),
            pltpu.VMEM((context_count, rows, width), bf),
            pltpu.VMEM((rows, width), bf),
            pltpu.VMEM((rows, width), bf),
            pltpu.VMEM((data_count, context_count, shard, each), bf),
            pltpu.VMEM((data_count, depth, 2, shard, width), bf),
            pltpu.VMEM((each, group_rows), jnp.float32),
            pltpu.VMEM((q_each, group_rows), bf),
            pltpu.VMEM((group_rows, HEAD_DIM), bf),
            pltpu.VMEM((HEAD_DIM, group_rows), bf),
            pltpu.VMEM((context_count, q_each, rows), bf),
            pltpu.VMEM((context_count, q_each, rows), bf),
            pltpu.SemaphoreType.DMA((6,)),
        ]
        + LineGather.scratch(depth) * 4
        + Swap.scratch(context_count) * 4
        + RingSpread.scratch() * 4
        + [pltpu.SemaphoreType.DMA] * 2,
        compiler_params=pltpu.CompilerParams(
            collective_id=0, has_side_effects=True, vmem_limit_bytes=56 * 2**20
        ),
        name="front",
    )(
        tokens,
        gain_one.reshape(1, width),
        gain_two.reshape(1, width),
        gain_query.reshape(HEAD_DIM, 1),
        gain_key.reshape(HEAD_DIM, 1),
        cosine,
        sine,
        places.reshape(group_rows, 1),
        places.reshape(1, group_rows),
        starts.reshape(1, group_rows),
        input_send,
        output_own,
        gate_send,
        up_send,
        cotangent,
    )


class LineScatter:
    def __init__(self, part_ref, out_ref, scratch, where, depth):
        self.part, self.out, self.where, self.depth = part_ref, out_ref, where, depth
        self.sib, self.right, self.left = scratch[:3]
        (
            self.sib_sent,
            self.sib_recv,
            self.right_sent,
            self.right_recv,
            self.left_sent,
            self.left_recv,
        ) = scratch[3:]

    @staticmethod
    def scratch(depth, rows, width):
        return [pltpu.VMEM((depth, rows, width), jnp.bfloat16)] * 3 + [
            pltpu.SemaphoreType.DMA((depth,))
        ] * 6

    def pair(self, spot):
        dp, cp, z, core = self.where
        return send(
            self.part.at[2 * spot + 1 - core],
            self.sib.at[spot],
            self.sib_sent.at[spot],
            self.sib_recv.at[spot],
            (dp, cp ^ 1),
        )

    def hop_right(self, spot):
        dp, cp, z, core = self.where
        return send(
            self.part.at[2 * spot + core],
            self.right.at[spot],
            self.right_sent.at[spot],
            self.right_recv.at[spot],
            (dp, cp + 2),
        )

    def hop_left(self, spot):
        dp, cp, z, core = self.where
        return send(
            self.part.at[2 * spot + core],
            self.left.at[spot],
            self.left_sent.at[spot],
            self.left_recv.at[spot],
            (dp, cp - 2),
        )

    def order(self):
        spots = []
        for turn in range(self.depth):
            spots += [self.depth - 1 - turn, turn]
        return list(dict.fromkeys(spots))

    def chip_sum(self, spot):
        core = self.where[3]
        self.pair(spot).wait_recv()
        return self.part[2 * spot + core].astype(jnp.float32) + self.sib[spot].astype(jnp.float32)

    def forward(self, spot):
        z, core = self.where[2], self.where[3]

        @pl.when((z < spot) & (z > 0))
        def _():
            total = self.chip_sum(spot)
            self.hop_right(spot).wait_recv()
            self.part[2 * spot + core] = (total + self.right[spot].astype(jnp.float32)).astype(
                jnp.bfloat16
            )
            self.hop_right(spot).start()

        @pl.when((z < spot) & (z == 0))
        def _():
            self.part[2 * spot + core] = self.chip_sum(spot).astype(jnp.bfloat16)
            self.hop_right(spot).start()

        @pl.when((z > spot) & (z < self.depth - 1))
        def _():
            total = self.chip_sum(spot)
            self.hop_left(spot).wait_recv()
            self.part[2 * spot + core] = (total + self.left[spot].astype(jnp.float32)).astype(
                jnp.bfloat16
            )
            self.hop_left(spot).start()

        @pl.when((z > spot) & (z == self.depth - 1))
        def _():
            self.part[2 * spot + core] = self.chip_sum(spot).astype(jnp.bfloat16)
            self.hop_left(spot).start()

    def finish(self):
        z = self.where[2]
        self.out[...] = self.chip_sum(z)

        @pl.when(z > 0)
        def _():
            self.hop_right(z).wait_recv()
            self.out[...] += self.right[z].astype(jnp.float32)

        @pl.when(z < self.depth - 1)
        def _():
            self.hop_left(z).wait_recv()
            self.out[...] += self.left[z].astype(jnp.float32)

        for spot in range(self.depth):
            self.pair(spot).wait_send()

            @pl.when(z < spot)
            def _():
                self.hop_right(spot).wait_send()

            @pl.when(z > spot)
            def _():
                self.hop_left(spot).wait_send()


class RingReduce:
    def __init__(self, part, work, scratch, where):
        self.part, self.work, self.where = part, work, where
        self.from_x, self.from_y, self.x_sent, self.x_recv, self.y_sent, self.y_recv = scratch

    @staticmethod
    def scratch(*half):
        return [pltpu.VMEM((3,) + half, jnp.bfloat16)] * 2 + [pltpu.SemaphoreType.DMA((3,))] * 4

    def to_x(self, kind):
        dp, cp, z, core = self.where
        source = (
            self.part(dp ^ 3, 0) if kind == 0 else self.part(dp ^ 1, 0) if kind == 1 else self.work(1)
        )
        return send(
            source, self.from_x.at[kind], self.x_sent.at[kind], self.x_recv.at[kind], (dp ^ 1, cp)
        )

    def to_y(self, kind):
        dp, cp, z, core = self.where
        source = (
            self.part(dp ^ 3, 1) if kind == 0 else self.part(dp ^ 2, 1) if kind == 1 else self.work(0)
        )
        return send(
            source, self.from_y.at[kind], self.y_sent.at[kind], self.y_recv.at[kind], (dp ^ 2, cp)
        )

    def start(self):
        for kind in range(2):
            self.to_x(kind).start()
            self.to_y(kind).start()

    def add(self, index, *arrived):
        target = self.work(index)
        total = target[...].astype(jnp.float32)
        for block in arrived:
            total = total + block[...].astype(jnp.float32)
        target[...] = total.astype(jnp.bfloat16)

    def middle(self):
        self.to_x(0).wait_recv()
        self.add(0, self.from_x.at[0])
        self.to_y(2).start()
        self.to_y(0).wait_recv()
        self.add(1, self.from_y.at[0])
        self.to_x(2).start()

    def finish(self):
        for kind in (1, 2):
            self.to_x(kind).wait_recv()
            self.to_y(kind).wait_recv()
        self.add(2, self.from_x.at[1], self.from_y.at[2])
        self.add(3, self.from_y.at[1], self.from_x.at[2])

    def finish_send(self):
        for kind in range(3):
            self.to_x(kind).wait_send()
            self.to_y(kind).wait_send()

    def places(self):
        dp = self.where[0]
        return [(dp ^ 2, 0), (dp ^ 1, 1), (dp, 0), (dp, 1)]


def far_first(turn, z, depth):
    order = []
    for spot in range(depth):
        rest = sorted((other for other in range(depth) if other != spot), key=lambda other: (-abs(other - spot), other))
        ends = [other for other in rest if other in (0, depth - 1)]
        order.append(ends + [other for other in rest if other not in ends] + [spot])
    picked = 0
    for step in range(depth):
        for spot in range(depth):
            picked = picked + order[spot][step] * ((turn == step) & (z == spot)).astype(jnp.int32)
    return picked


def middle_kernel(
    normed_in,
    cotangent_in,
    gateup_in,
    down_in,
    d_normed_out,
    forward_out,
    down_out,
    gateup_out,
    normed,
    cotangent,
    gate_weight,
    up_weight,
    down_weight,
    hidden_up,
    d_gates,
    d_ups,
    parts,
    forwards,
    down_grad,
    gateup_grad,
    load_sems,
    save_sems,
    *scratch,
):
    where = place()
    dp, cp, z, core = where
    count, rows, width = normed.shape
    depth = count // 2
    tile = 2 * rows
    group_rows = count * rows
    loads = [
        pltpu.make_async_copy(source, target, load_sems.at[index])
        for index, (source, target) in enumerate(
            [
                (normed_in, normed),
                (gateup_in.at[0], gate_weight),
                (gateup_in.at[1], up_weight),
                (cotangent_in, cotangent),
                (down_in, down_weight),
            ]
        )
    ]
    for load in loads:
        load.start()
    greet([(dp, cp ^ turn) for turn in range(1, count)])
    line = LineScatter(parts, d_normed_out, scratch, where, depth)
    at_end = (z == 0) | (z == depth - 1)
    for load in loads:
        load.wait()

    def feed(turn, carry):
        spot = far_first(turn, z, depth)
        pair = pl.ds(2 * spot, 2)
        lanes = pl.ds(pl.multiple_of(spot * tile, tile), tile)
        block = normed[pair].reshape(tile, width)
        gate = jnp.dot(block, gate_weight[...], preferred_element_type=jnp.float32)
        up = jnp.dot(block, up_weight[...], preferred_element_type=jnp.float32)
        sig = 1.0 / (1.0 + jnp.exp(-gate))
        act = gate * sig
        hidden_up[:, lanes] = (act * up).T.astype(jnp.bfloat16)
        d_hidden = contract_cols(cotangent[pair].reshape(tile, width), down_weight[...])
        d_gate = (d_hidden * up * (sig * (1.0 + gate * (1.0 - sig)))).astype(jnp.bfloat16)
        d_up = (d_hidden * act).astype(jnp.bfloat16)
        d_gates[lanes] = d_gate
        d_ups[lanes] = d_up
        part = contract_cols(d_gate, gate_weight[...]) + contract_cols(d_up, up_weight[...])
        parts[pair] = part.astype(jnp.bfloat16).reshape(2, rows, width)
        line.pair(spot).start()

        @pl.when(at_end)
        def _():
            line.forward(spot)

        @pl.when(jnp.logical_not(at_end) & (turn >= 2))
        def _():
            line.forward(far_first(turn - 2, z, depth))

        return carry

    lax.fori_loop(0, depth, feed, 0)
    chunk = 256

    def down_step(step, carry):
        lanes = pl.ds(pl.multiple_of(step * chunk, chunk), chunk)
        right = cotangent[:, :, lanes].reshape(group_rows, chunk)
        down_grad[:, :, lanes] = (
            jnp.dot(hidden_up[...], right, preferred_element_type=jnp.float32)
            .reshape(down_grad.shape[:2] + (chunk,))
            .astype(jnp.bfloat16)
        )
        return carry

    lax.fori_loop(0, width // chunk, down_step, 0)
    saves = [pltpu.make_async_copy(down_grad, down_out, save_sems.at[0])]
    saves[0].start()

    @pl.when(jnp.logical_not(at_end))
    def _():
        line.forward(far_first(depth - 2, z, depth))

    def gateup_step(step, carry):
        lanes = pl.ds(pl.multiple_of(step * chunk, chunk), chunk)
        left = normed[:, :, lanes].reshape(group_rows, chunk)
        gateup_grad[0, lanes] = contract_rows(left, d_gates[...]).astype(jnp.bfloat16)
        gateup_grad[1, lanes] = contract_rows(left, d_ups[...]).astype(jnp.bfloat16)
        return carry

    lax.fori_loop(0, width // chunk, gateup_step, 0)
    saves.append(pltpu.make_async_copy(gateup_grad, gateup_out, save_sems.at[1]))
    saves[1].start()

    def forward_step(step, carry):
        lanes = pl.ds(pl.multiple_of(step * tile, tile), tile)
        forwards[pl.ds(2 * step, 2)] = (
            contract_rows(hidden_up[:, lanes], down_weight[...])
            .astype(jnp.bfloat16)
            .reshape(2, rows, width)
        )
        return carry

    lax.fori_loop(0, depth, forward_step, 0)
    saves.append(pltpu.make_async_copy(forwards, forward_out, save_sems.at[2]))
    saves[2].start()
    line.finish()
    for save in saves:
        save.wait()


def middle(normed, cotangent, gateup, down, data_count, collective_id):
    count, rows, width = normed.shape
    depth = count // 2
    hidden = down.shape[0]
    group_rows = count * rows
    bf = jnp.bfloat16
    any_space = pl.BlockSpec(memory_space=pl.ANY)
    in_vmem = pl.BlockSpec(memory_space=pltpu.VMEM)
    return pl.pallas_call(
        middle_kernel,
        out_shape=[
            jax.ShapeDtypeStruct((rows, width), jnp.float32),
            jax.ShapeDtypeStruct((count, rows, width), bf),
            jax.ShapeDtypeStruct((data_count, hidden // data_count, width), bf),
            jax.ShapeDtypeStruct((2, width, hidden), bf),
        ],
        in_specs=[any_space] * 4,
        out_specs=[in_vmem] + [any_space] * 3,
        scratch_shapes=[
            pltpu.VMEM((count, rows, width), bf),
            pltpu.VMEM((count, rows, width), bf),
            pltpu.VMEM((width, hidden), bf),
            pltpu.VMEM((width, hidden), bf),
            pltpu.VMEM((hidden, width), bf),
            pltpu.VMEM((hidden, group_rows), bf),
            pltpu.VMEM((group_rows, hidden), bf),
            pltpu.VMEM((group_rows, hidden), bf),
            pltpu.VMEM((count, rows, width), bf),
            pltpu.VMEM((count, rows, width), bf),
            pltpu.VMEM((data_count, hidden // data_count, width), bf),
            pltpu.VMEM((2, width, hidden), bf),
            pltpu.SemaphoreType.DMA((5,)),
            pltpu.SemaphoreType.DMA((3,)),
        ]
        + LineScatter.scratch(depth, rows, width),
        compiler_params=pltpu.CompilerParams(
            collective_id=collective_id, has_side_effects=True, vmem_limit_bytes=60 * 2**20
        ),
        name="middle",
    )(normed, cotangent, gateup, down)


def back_kernel(
    tokens_ref,
    cotangent_ref,
    residual_ref,
    d_normed_ref,
    gain_one_ref,
    gain_two_ref,
    gain_query_ref,
    gain_key_ref,
    cosine_ref,
    sine_ref,
    key_place_ref,
    query_place_ref,
    query_start_ref,
    total_ref,
    normed_in,
    input_in,
    output_in,
    raw_in,
    flat_in,
    forward_in,
    down_in,
    gateup_in,
    mixed_out,
    token_out,
    gains_out,
    down_grad_out,
    output_grad_out,
    input_grad_out,
    gateup_grad_out,
    inputs,
    outputs,
    raw,
    flat,
    forwards,
    forward_sum,
    d_first,
    d_residual,
    branch,
    swap_send,
    swap_recv,
    queries,
    keys,
    keys_up,
    values_up,
    d_query,
    d_key,
    d_value,
    d_projected,
    parts,
    input_grad,
    output_sib,
    output_line,
    down_work,
    gateup_work,
    gain_sums,
    own_gains,
    line_gains,
    all_gains,
    load_sems,
    work_sems,
    share_sems,
    output_sent,
    output_recv,
    line_sent,
    line_recv,
    all_sent,
    all_recv,
    *scratch,
):
    where = place()
    dp, cp, z, core = where
    count, rows, width = forwards.shape
    depth = count // 2
    data_count = all_gains.shape[0]
    shard = inputs.shape[2]
    tile = 2 * rows
    group_rows = count * rows
    heads = HEADS // KV_HEADS
    q_each = heads * HEAD_DIM
    flat_width = HEADS * HEAD_DIM
    score_scale = HEAD_DIM ** (-0.5)
    load_pairs = [
        (output_in, outputs),
        (raw_in, raw),
        (forward_in, forwards),
        (flat_in, flat),
        (normed_in, forwards),
        (input_in, inputs),
    ]
    loads = [
        pltpu.make_async_copy(source, target, load_sems.at[index])
        for index, (source, target) in enumerate(load_pairs)
    ]
    for index in (0, 1, 2, 3, 5):
        loads[index].start()
    greet(
        [(dp, cp ^ turn) for turn in range(1, count)]
        + [(dp ^ turn, cp) for turn in range(1, data_count)]
    )
    swap = Swap(swap_send, swap_recv, scratch[:3], where, count)
    take = iter(scratch[3:])

    def some(amount):
        return [next(take) for _ in range(amount)]

    forward_line = LineScatter(forwards, forward_sum, some(9), where, depth)
    first_line = LineScatter(parts, d_first, some(9), where, depth)
    gateup_rows = data_count * count * shard // data_count
    lane_half = width // 2

    def in_place(part):
        spots = [(dp ^ 2, 0), (dp ^ 1, 1), (dp, 0), (dp, 1)]
        return lambda index: part(*spots[index])

    def down_part(d, h):
        return down_in.at[d, :, pl.ds(h * lane_half, lane_half)]

    def gateup_part(d, h):
        return gateup_in.at[h, pl.ds(pl.multiple_of(d * gateup_rows, 16), gateup_rows)]

    def output_part(d, h):
        return outputs.at[d, pl.ds(h * (depth // 2), depth // 2), core]

    def input_part(d, h):
        half = gateup_rows // 2
        return input_grad.at[pl.ds(pl.multiple_of(d * gateup_rows + h * half, 16), half)]

    down_ring = RingReduce(down_part, lambda index: down_work.at[index], some(6), where)
    gateup_ring = RingReduce(gateup_part, lambda index: gateup_work.at[index], some(6), where)
    output_ring = RingReduce(output_part, in_place(output_part), some(6), where)
    input_ring = RingReduce(input_part, in_place(input_part), some(6), where)

    def own_shard(source):
        return lambda slot: source.at[pl.ds(pl.multiple_of(slot * shard, 16), shard)]

    gate_swap = Swap(own_shard(gateup_work.at[2]), gateup_grad_out.at[0], some(3), where, count)
    up_swap = Swap(own_shard(gateup_work.at[3]), gateup_grad_out.at[1], some(3), where, count)
    own_rows = input_grad.at[pl.ds(pl.multiple_of(dp * gateup_rows, 16), gateup_rows)]
    input_swap = Swap(own_shard(own_rows), input_grad_out, some(3), where, count)
    works = [
        pltpu.make_async_copy(ring.part(*spot), ring.work(index), work_sems.at[4 * turn + index])
        for turn, ring in enumerate((down_ring, gateup_ring))
        for index, spot in enumerate(ring.places())
    ]
    down_ring.start()
    gateup_ring.start()
    for work in works:
        work.start()

    def share(mine):
        return send(
            outputs.at[:, :, 1 - core], output_sib, share_sems.at[0], share_sems.at[1], (dp, cp ^ 1)
        )

    def output_hop(far, mine):
        return send(
            outputs.at[dp, z ^ far, core],
            output_line.at[z if mine else z ^ far],
            output_sent.at[far],
            output_recv.at[far],
            (dp, cp ^ (2 * far)),
        )

    at_end = (z == 0) | (z == depth - 1)
    chunk = 256

    hat_two, inv_two = rms_parts(residual_ref[...])
    d_normed = d_normed_ref[...]
    own_gains[:, pl.ds(width, width)] = jnp.sum(d_normed * hat_two, axis=0, keepdims=True)
    d_res = cotangent_ref[...].astype(jnp.float32) + norm_back(
        d_normed * gain_two_ref[...], hat_two, inv_two
    )
    d_residual[...] = d_res
    branch[...] = d_res.astype(jnp.bfloat16)
    loads[0].wait()
    swap_send[...] = (
        contract_cols(outputs[...].reshape(flat_width, width), branch[...])
        .astype(jnp.bfloat16)
        .reshape(count, q_each, rows)
    )
    swap.start()
    loads[2].wait()
    for spot in forward_line.order():
        forward_line.pair(spot).start()
    loads[1].wait()

    def prepare(turn, carry):
        lanes = pl.ds(pl.multiple_of(turn * tile, tile), tile)
        cosine, sine = cosine_ref[:, lanes], sine_ref[:, lanes]
        for head in range(heads):
            spot = pl.ds(head * HEAD_DIM, HEAD_DIM)
            hat, _ = head_hat(raw[spot, lanes])
            queries[spot, lanes] = turn_heads(hat * gain_query_ref[...], cosine, sine).astype(
                jnp.bfloat16
            )
        hat, _ = head_hat(raw[pl.ds(q_each, HEAD_DIM), lanes])
        key = turn_heads(hat * gain_key_ref[...], cosine, sine)
        keys[:, lanes] = key.astype(jnp.bfloat16)
        keys_up[lanes] = key.T.astype(jnp.bfloat16)
        values_up[lanes] = raw[pl.ds(q_each + HEAD_DIM, HEAD_DIM), lanes].T.astype(jnp.bfloat16)
        return carry

    lax.fori_loop(0, depth, prepare, 0)
    d_key[...] = jnp.zeros_like(d_key)
    d_value[...] = jnp.zeros_like(d_value)
    gain_sums[...] = jnp.zeros_like(gain_sums)

    @pl.when(at_end)
    def _():
        for turn in range(depth - 1):
            forward_line.forward(far_first(turn, z, depth))

    loads[3].wait()

    def output_step(step, carry):
        lanes = pl.ds(pl.multiple_of(step * chunk, chunk), chunk)
        outputs[:, :, :, :, lanes] = (
            jnp.dot(
                flat[...].reshape(flat_width, rows),
                branch[:, lanes],
                preferred_element_type=jnp.float32,
            )
            .astype(jnp.bfloat16)
            .reshape(outputs.shape[:4] + (chunk,))
        )
        return carry

    lax.fori_loop(0, width // chunk, output_step, 0)
    share(True).start()
    for work in works[:4]:
        work.wait()
    down_ring.middle()
    swap.finish_recv()

    def attend(turn, carry):
        lanes = pl.ds(pl.multiple_of(turn * tile, tile), tile)
        query_place, query_start = query_place_ref[:, lanes], query_start_ref[:, lanes]

        @pl.when(jnp.logical_not(at_end) & (turn >= 1))
        def _():
            forward_line.forward(far_first(turn - 1, z, depth))

        @pl.when(turn == 2)
        def _():
            for work in works[4:]:
                work.wait()
            gateup_ring.middle()

        for head in range(heads):
            spot = pl.ds(head * HEAD_DIM, HEAD_DIM)
            scores, allowed = score_block(
                keys_up[...], queries[spot, lanes], key_place_ref[...], query_place, query_start
            )
            probs = jnp.where(allowed, jnp.exp(scores - total_ref[pl.ds(head, 1), lanes]), 0.0)
            d_out = jnp.concatenate(
                [swap_recv[2 * turn, spot], swap_recv[2 * turn + 1, spot]], axis=1
            )
            d_probs = jnp.dot(values_up[...], d_out, preferred_element_type=jnp.float32)
            delta = jnp.sum(probs * d_probs, axis=0, keepdims=True)
            d_scores = (probs * (d_probs - delta)).astype(jnp.bfloat16)
            d_query[spot, lanes] = (
                jnp.dot(keys[...], d_scores, preferred_element_type=jnp.float32) * score_scale
            )
            d_key[...] += contract_cols(queries[spot, lanes], d_scores) * score_scale
            d_value[...] += contract_cols(d_out, probs.astype(jnp.bfloat16))
        return carry

    lax.fori_loop(0, depth, attend, 0)
    loads[5].wait()
    share(False).wait_recv()

    def share_step(step, carry):
        total = outputs[step, :, core].astype(jnp.float32) + output_sib[step].astype(jnp.float32)
        outputs[step, :, core] = total.astype(jnp.bfloat16)
        return carry

    lax.fori_loop(0, data_count, share_step, 0)
    output_ring.start()

    def feed(turn, carry):
        spot = far_first(turn, z, depth)
        lanes = pl.ds(pl.multiple_of(spot * tile, tile), tile)
        cosine, sine = cosine_ref[:, lanes], sine_ref[:, lanes]
        pieces = []
        for head in range(heads + 1):
            place_in = pl.ds(head * HEAD_DIM, HEAD_DIM)
            hat, inverse = head_hat(raw[place_in, lanes])
            if head < heads:
                turned = turn_heads(d_query[place_in, lanes], cosine, -sine)
                gain, kind = gain_query_ref[...], 0
            else:
                turned = turn_heads(d_key[:, lanes], cosine, -sine)
                gain, kind = gain_key_ref[...], 1
            gain_sums[kind] += turned * hat
            scaled = turned * gain
            pieces.append(
                inverse * (scaled - hat * jnp.mean(scaled * hat, axis=0, keepdims=True))
            )
        pieces.append(d_value[:, lanes])
        block = jnp.concatenate(pieces, axis=0).T.astype(jnp.bfloat16)
        d_projected[lanes] = block
        part = contract_cols(block, inputs[...].reshape(width, block.shape[1]))
        parts[pl.ds(2 * spot, 2)] = part.astype(jnp.bfloat16).reshape(2, rows, width)
        first_line.pair(spot).start()

        @pl.when(at_end & (turn < depth - 1))
        def _():
            first_line.forward(spot)

        return carry

    lax.fori_loop(0, depth, feed, 0)
    forward_line.finish()
    loads[4].start()
    mixed_out[...] = (residual_ref[...] + forward_sum[...]).astype(jnp.bfloat16)
    for kind in range(2):
        own_gains[:, pl.ds(2 * width + kind * HEAD_DIM, HEAD_DIM)] = jnp.sum(
            gain_sums[kind].T, axis=0, keepdims=True
        )
    down_ring.finish()
    for half in range(2):
        down_grad_out[:, pl.ds(half * lane_half, lane_half)] = down_work[2 + half]

    @pl.when(jnp.logical_not(at_end))
    def _():
        first_line.forward(far_first(0, z, depth))

    loads[4].wait()

    def input_step(step, carry):
        lanes = pl.ds(pl.multiple_of(step * chunk, chunk), chunk)
        left = forwards[:, :, lanes].reshape(group_rows, chunk)
        input_grad[lanes] = contract_rows(left, d_projected[...]).astype(jnp.bfloat16)
        return carry

    lax.fori_loop(0, width // chunk, input_step, 0)
    input_ring.start()

    @pl.when(jnp.logical_not(at_end))
    def _():
        first_line.forward(far_first(1, z, depth))
        first_line.forward(far_first(2, z, depth))

    gateup_ring.finish()
    gate_swap.start()
    up_swap.start()
    output_ring.middle()
    input_ring.middle()
    first_line.finish()
    hat_one, inv_one = rms_parts(tokens_ref[...].astype(jnp.float32))
    d_one = d_first[...]
    own_gains[:, pl.ds(0, width)] = jnp.sum(d_one * hat_one, axis=0, keepdims=True)
    line_gains[cp] = own_gains[...]
    for turn in range(1, count):
        send(
            own_gains, line_gains.at[cp], line_sent.at[turn], line_recv.at[turn], (dp, cp ^ turn)
        ).start()
    token_out[...] = d_residual[...] + norm_back(d_one * gain_one_ref[...], hat_one, inv_one)
    output_ring.finish()
    for far in range(depth - 1, 0, -1):
        output_hop(far, True).start()
    input_ring.finish()
    input_swap.start()
    for turn in range(1, count):
        copy = send(
            own_gains,
            line_gains.at[cp ^ turn],
            line_sent.at[turn],
            line_recv.at[turn],
            (dp, cp ^ turn),
        )
        copy.wait_recv()
        copy.wait_send()
    all_gains[dp] = jnp.sum(line_gains[...], axis=0)
    for turn in range(1, data_count):
        send(
            all_gains.at[dp],
            all_gains.at[dp],
            all_sent.at[turn],
            all_recv.at[turn],
            (dp ^ turn, cp),
        ).start()
    for turn in range(1, data_count):
        copy = send(
            all_gains.at[dp],
            all_gains.at[dp ^ turn],
            all_sent.at[turn],
            all_recv.at[turn],
            (dp ^ turn, cp),
        )
        copy.wait_recv()
        copy.wait_send()
    gains_out[...] = jnp.sum(all_gains[...], axis=0)
    total = outputs[dp, z, core].astype(jnp.float32)
    for far in range(1, depth):
        output_hop(far, False).wait_recv()
        total = total + output_line[z ^ far].astype(jnp.float32)
    output_grad_out[...] = total
    for done in (input_swap, gate_swap, up_swap):
        done.finish_recv()
    for done in (swap, input_swap, gate_swap, up_swap, down_ring, gateup_ring, output_ring, input_ring):
        done.finish_send()
    for far in range(1, depth):
        output_hop(far, True).wait_send()
    share(True).wait_send()


def back(
    tokens,
    cotangent,
    residual,
    d_normed,
    gain_one,
    gain_two,
    gain_query,
    gain_key,
    cosine,
    sine,
    places,
    starts,
    log_total,
    normed,
    inputs,
    outputs,
    raw,
    flat,
    forwards,
    down_grad,
    gateup_grad,
    collective_id,
):
    count, rows, width = normed.shape
    depth = count // 2
    data_count = inputs.shape[0]
    shard, each = inputs.shape[2:]
    down_rows = down_grad.shape[1]
    hidden = gateup_grad.shape[2]
    group_rows = count * rows
    heads = HEADS // KV_HEADS
    q_each = heads * HEAD_DIM
    flat_width = HEADS * HEAD_DIM
    gain_width = 2 * width + 2 * HEAD_DIM
    bf = jnp.bfloat16
    f32 = jnp.float32
    any_space = pl.BlockSpec(memory_space=pl.ANY)
    in_vmem = pl.BlockSpec(memory_space=pltpu.VMEM)
    return pl.pallas_call(
        back_kernel,
        out_shape=[
            jax.ShapeDtypeStruct((rows, width), bf),
            jax.ShapeDtypeStruct((rows, width), f32),
            jax.ShapeDtypeStruct((1, gain_width), f32),
            jax.ShapeDtypeStruct((down_rows, width), bf),
            jax.ShapeDtypeStruct((shard, width), f32),
            jax.ShapeDtypeStruct((count, shard, each), bf),
            jax.ShapeDtypeStruct((2, count, shard, hidden), bf),
        ],
        in_specs=[in_vmem] * 14 + [any_space] * 8,
        out_specs=[in_vmem] * 5 + [any_space] * 2,
        scratch_shapes=[
            pltpu.VMEM(inputs.shape, bf),
            pltpu.VMEM(outputs.shape, bf),
            pltpu.VMEM(raw.shape, f32),
            pltpu.VMEM(flat.shape, bf),
            pltpu.VMEM(forwards.shape, bf),
            pltpu.VMEM((rows, width), f32),
            pltpu.VMEM((rows, width), f32),
            pltpu.VMEM((rows, width), f32),
            pltpu.VMEM((rows, width), bf),
            pltpu.VMEM((count, q_each, rows), bf),
            pltpu.VMEM((count, q_each, rows), bf),
            pltpu.VMEM((q_each, group_rows), bf),
            pltpu.VMEM((HEAD_DIM, group_rows), bf),
            pltpu.VMEM((group_rows, HEAD_DIM), bf),
            pltpu.VMEM((group_rows, HEAD_DIM), bf),
            pltpu.VMEM((q_each, group_rows), f32),
            pltpu.VMEM((HEAD_DIM, group_rows), f32),
            pltpu.VMEM((HEAD_DIM, group_rows), f32),
            pltpu.VMEM((group_rows, each), bf),
            pltpu.VMEM(forwards.shape, bf),
            pltpu.VMEM((width, each), bf),
            pltpu.VMEM((data_count, depth, shard, width), bf),
            pltpu.VMEM((depth, shard, width), bf),
            pltpu.VMEM((4, down_rows, width // 2), bf),
            pltpu.VMEM((4, count * shard, hidden), bf),
            pltpu.VMEM((2, HEAD_DIM, 2 * rows), f32),
            pltpu.VMEM((1, gain_width), f32),
            pltpu.VMEM((count, 1, gain_width), f32),
            pltpu.VMEM((data_count, 1, gain_width), f32),
            pltpu.SemaphoreType.DMA((6,)),
            pltpu.SemaphoreType.DMA((8,)),
            pltpu.SemaphoreType.DMA((2,)),
            pltpu.SemaphoreType.DMA((depth,)),
            pltpu.SemaphoreType.DMA((depth,)),
            pltpu.SemaphoreType.DMA((count,)),
            pltpu.SemaphoreType.DMA((count,)),
            pltpu.SemaphoreType.DMA((data_count,)),
            pltpu.SemaphoreType.DMA((data_count,)),
        ]
        + Swap.scratch(count)
        + LineScatter.scratch(depth, rows, width) * 2
        + RingReduce.scratch(down_rows, width // 2)
        + RingReduce.scratch(count * shard, hidden)
        + RingReduce.scratch(depth // 2, shard, width)
        + RingReduce.scratch(count * shard // 2, each)
        + Swap.scratch(count) * 3,
        compiler_params=pltpu.CompilerParams(
            collective_id=collective_id, has_side_effects=True, vmem_limit_bytes=63 * 2**20
        ),
        name="back",
    )(
        tokens,
        cotangent,
        residual,
        d_normed,
        gain_one.reshape(1, width),
        gain_two.reshape(1, width),
        gain_query.reshape(HEAD_DIM, 1),
        gain_key.reshape(HEAD_DIM, 1),
        cosine,
        sine,
        places.reshape(group_rows, 1),
        places.reshape(1, group_rows),
        starts.reshape(1, group_rows),
        log_total,
        normed,
        inputs,
        outputs,
        raw,
        flat,
        forwards,
        down_grad,
        gateup_grad,
    )


def split_heads_columns(rows_by_columns):
    rows = rows_by_columns.shape[0]
    q_width = HEADS * HEAD_DIM
    kv_width = KV_HEADS * HEAD_DIM
    query = rows_by_columns[:, :q_width].reshape(rows, KV_HEADS, q_width // KV_HEADS)
    key = rows_by_columns[:, q_width : q_width + kv_width].reshape(rows, KV_HEADS, HEAD_DIM)
    value = rows_by_columns[:, q_width + kv_width :].reshape(rows, KV_HEADS, HEAD_DIM)
    return jnp.concatenate([query, key, value], axis=2).transpose(1, 0, 2)


def join_heads_columns(by_head):
    rows = by_head.shape[1]
    q_each = HEADS // KV_HEADS * HEAD_DIM
    ordered = by_head.transpose(1, 0, 2)
    return jnp.concatenate(
        [
            ordered[:, :, :q_each].reshape(rows, -1),
            ordered[:, :, q_each : q_each + HEAD_DIM].reshape(rows, -1),
            ordered[:, :, q_each + HEAD_DIM :].reshape(rows, -1),
        ],
        axis=1,
    )


def on_device_split(
    tokens,
    output_cotangent,
    sequence_lengths,
    block_order,
    attn_input,
    input_moment,
    input_square,
    attn_output,
    output_moment,
    output_square,
    gate_up,
    gateup_moment,
    gateup_square,
    down_weight,
    down_moment,
    down_square,
    norm_gains,
    gains_moment,
    gains_square,
):
    row_count, model_width = tokens.shape
    gain_one = norm_gains[:model_width]
    gain_two = norm_gains[model_width : 2 * model_width]
    gain_query = norm_gains[2 * model_width : 2 * model_width + HEAD_DIM]
    gain_key = norm_gains[2 * model_width + HEAD_DIM :]
    seq_lens = sequence_lengths[0]
    order_row = block_order[0]
    context_count = lax.axis_size("cp")
    data_count = lax.axis_size("dp")
    group_rows = context_count * row_count
    shard_rows = attn_input.shape[0]
    down_rows = down_weight.shape[0]
    offsets = jnp.arange(row_count, dtype=jnp.int32)
    positions = (order_row[:, None] * row_count + offsets[None, :]).reshape(group_rows)
    doc_index, seq_offset = locate(positions, seq_lens)
    cosine, sine = rope_tables(seq_offset)
    gateup_send = (
        gate_up.astype(jnp.bfloat16)
        .reshape(shard_rows, 2, data_count, context_count, down_rows)
        .transpose(1, 3, 0, 2, 4)
        .reshape(2, context_count, shard_rows, data_count * down_rows)
    )
    down_part = lax.all_gather(down_weight.astype(jnp.bfloat16), "dp", axis=0, tiled=True)
    (
        normed_one,
        normed_two,
        cotangent_all,
        input_part,
        output_all,
        gateup_part,
        raw,
        flat_parts,
        log_total,
        residual,
    ) = front(
        tokens,
        gain_one,
        gain_two,
        gain_query,
        gain_key,
        cosine.T,
        sine.T,
        positions,
        positions - seq_offset,
        split_heads_columns(attn_input.astype(jnp.bfloat16)),
        attn_output.astype(jnp.bfloat16),
        gateup_send[0],
        gateup_send[1],
        output_cotangent,
        data_count,
        context_count,
    )
    gateup_part = gateup_part.reshape(2, model_width, -1)
    d_normed_two, forward_parts, down_grad, gateup_grad = middle(
        normed_two, cotangent_all, gateup_part, down_part, data_count, 3
    )
    (
        mixed,
        token_gradient,
        gain_grads,
        grad_down,
        grad_output,
        grad_input,
        grad_gateup,
    ) = back(
        tokens,
        output_cotangent,
        residual,
        d_normed_two,
        gain_one,
        gain_two,
        gain_query,
        gain_key,
        cosine.T,
        sine.T,
        positions,
        positions - seq_offset,
        log_total,
        normed_one,
        input_part,
        output_all,
        raw,
        flat_parts,
        forward_parts,
        down_grad,
        gateup_grad,
        4,
    )
    gain_grads = gain_grads.reshape(-1)

    grad_down = grad_down.astype(jnp.float32)
    grad_input = join_heads_columns(grad_input).astype(jnp.float32)
    grad_gateup = (
        grad_gateup.reshape(2, context_count, shard_rows, data_count, down_rows)
        .transpose(2, 0, 3, 1, 4)
        .reshape(shard_rows, -1)
        .astype(jnp.float32)
    )
    input_next, input_moment_next, input_square_next = adam_update(
        attn_input, input_moment, input_square, grad_input, rate_input, weight_decay
    )
    output_next, output_moment_next, output_square_next = adam_update(
        attn_output, output_moment, output_square, grad_output, rate_output, weight_decay
    )
    gateup_next, gateup_moment_next, gateup_square_next = adam_update(
        gate_up, gateup_moment, gateup_square, grad_gateup, rate_gateup, weight_decay
    )
    down_next, down_moment_next, down_square_next = adam_update(
        down_weight, down_moment, down_square, grad_down, rate_down, weight_decay
    )
    gains_next, gains_moment_next, gains_square_next = adam_update(
        norm_gains, gains_moment, gains_square, gain_grads, rate_gains, 0.0
    )
    return (
        mixed,
        token_gradient,
        input_next,
        input_moment_next,
        input_square_next,
        output_next,
        output_moment_next,
        output_square_next,
        gateup_next,
        gateup_moment_next,
        gateup_square_next,
        down_next,
        down_moment_next,
        down_square_next,
        gains_next,
        gains_moment_next,
        gains_square_next,
    )


def solution(mesh):
    in_specs = (
        P(("dp", "cp"), None),
        P(("dp", "cp"), None),
        P("dp", None),
        P("dp", None),
        P(("dp", "cp"), None),
        P(("dp", "cp"), None),
        P(("dp", "cp"), None),
        P(("dp", "cp"), None),
        P(("dp", "cp"), None),
        P(("dp", "cp"), None),
        P(("dp", "cp"), None),
        P(("dp", "cp"), None),
        P(("dp", "cp"), None),
        P(("dp", "cp"), None),
        P(("dp", "cp"), None),
        P(("dp", "cp"), None),
        P(),
        P(),
        P(),
    )
    out_specs = (
        P(("dp", "cp"), None),
        P(("dp", "cp"), None),
        P(("dp", "cp"), None),
        P(("dp", "cp"), None),
        P(("dp", "cp"), None),
        P(("dp", "cp"), None),
        P(("dp", "cp"), None),
        P(("dp", "cp"), None),
        P(("dp", "cp"), None),
        P(("dp", "cp"), None),
        P(("dp", "cp"), None),
        P(("dp", "cp"), None),
        P(("dp", "cp"), None),
        P(("dp", "cp"), None),
        P(),
        P(),
        P(),
    )
    sizes = (mesh.shape["dp"], mesh.shape["cp"])
    body = on_device_split if sizes == (4, KV_HEADS) else on_device
    return jax.shard_map(
        body, mesh=mesh, in_specs=in_specs, out_specs=out_specs, check_vma=False
    )
```

```python
import functools
import math

import jax
import jax.numpy as jnp
from jax import lax
from jax.experimental import pallas as pl
from jax.experimental.pallas import tpu as pltpu
from jax.sharding import PartitionSpec as P

HEADS = 24
KV_HEADS = 8
HEAD_DIM = 64
FF = 6912
STEP = 10


norm_eps = 1e-05
rope_base = 1000000.0
beta_one = 0.9
beta_two = 0.95
adam_eps = 1e-08
rate_input = 0.06
rate_output = 0.9
rate_gateup = 0.06
rate_down = 0.03
rate_gains = 0.5
weight_decay = 0.1
masked_score = -1e30


def rope_tables(offsets):
    half_dim = HEAD_DIM // 2
    freqs = jnp.exp(
        jnp.arange(half_dim, dtype=jnp.float32) * (-2.0 * math.log(rope_base) / HEAD_DIM)
    )
    angles = offsets.astype(jnp.float32)[:, None] * freqs[None, :]
    return (jnp.cos(angles), jnp.sin(angles))


def rotate(values, cosine, sine):
    half_dim = HEAD_DIM // 2
    first_half = values[..., :half_dim]
    second_half = values[..., half_dim:]
    cos_wide = cosine[:, None, :]
    sin_wide = sine[:, None, :]
    return jnp.concatenate(
        [
            first_half * cos_wide - second_half * sin_wide,
            second_half * cos_wide + first_half * sin_wide,
        ],
        axis=-1,
    )


def locate(positions, lengths):
    seq_ends = jnp.cumsum(lengths)
    starts = seq_ends - lengths
    doc_index = jnp.sum((positions[:, None] >= seq_ends[None, :]).astype(jnp.int32), axis=1)
    picked = (doc_index[:, None] == jnp.arange(lengths.shape[0], dtype=jnp.int32)[None, :]).astype(
        jnp.int32
    )
    return (doc_index, positions - jnp.sum(picked * starts[None, :], axis=1))


def rms_parts(values):
    inverse = lax.rsqrt(jnp.mean(values * values, axis=-1, keepdims=True) + norm_eps)
    return (values * inverse, inverse)


def norm_back(d_normed, normal_hat, inverse):
    return inverse * (
        d_normed - normal_hat * jnp.mean(d_normed * normal_hat, axis=-1, keepdims=True)
    )


def contract_rows(left, right):
    return lax.dot_general(
        left, right, (((0,), (0,)), ((), ())), preferred_element_type=jnp.float32
    )


def contract_cols(left, right):
    return lax.dot_general(
        left, right, (((1,), (1,)), ((), ())), preferred_element_type=jnp.float32
    )


def owner_order(values, data_count, context_count):
    lead = values.shape[0]
    each = values.shape[1] // (data_count * context_count)
    return (
        values.reshape(lead, data_count, context_count, each)
        .transpose(0, 2, 1, 3)
        .reshape(lead, values.shape[1])
    )


def adam_update(weight, first_moment, second_moment, gradient, rate, decay):
    first_moment = beta_one * first_moment + (1.0 - beta_one) * gradient
    second_moment = beta_two * second_moment + (1.0 - beta_two) * gradient * gradient
    first_fix = 1.0 - beta_one**STEP
    second_fix = 1.0 - beta_two**STEP
    direction = first_moment / first_fix / (jnp.sqrt(second_moment / second_fix) + adam_eps)
    return (weight - rate * (direction + decay * weight), first_moment, second_moment)


def on_device(
    tokens,
    output_cotangent,
    sequence_lengths,
    block_order,
    attn_input,
    input_moment,
    input_square,
    attn_output,
    output_moment,
    output_square,
    gate_up,
    gateup_moment,
    gateup_square,
    down_weight,
    down_moment,
    down_square,
    norm_gains,
    gains_moment,
    gains_square,
):
    row_count = tokens.shape[0]
    model_width = tokens.shape[1]
    q_width = HEADS * HEAD_DIM
    kv_width = KV_HEADS * HEAD_DIM
    proj_width = q_width + 2 * kv_width
    head_groups = HEADS // KV_HEADS
    score_scale = HEAD_DIM ** (-0.5)
    gain_one = norm_gains[:model_width]
    gain_two = norm_gains[model_width : 2 * model_width]
    gain_query = norm_gains[2 * model_width : 2 * model_width + HEAD_DIM]
    gain_key = norm_gains[2 * model_width + HEAD_DIM :]
    seq_lens = sequence_lengths[0]
    order_row = block_order[0]
    context_count = lax.axis_size("cp")
    data_count = lax.axis_size("dp")
    own_slot = lax.axis_index("cp")
    offsets = jnp.arange(row_count, dtype=jnp.int32)
    own_block = jnp.sum(
        jnp.where(jnp.arange(context_count, dtype=jnp.int32) == own_slot, order_row, 0)
    )
    positions = own_block * row_count + offsets
    key_positions = (order_row[:, None] * row_count + offsets[None, :]).reshape(
        context_count * row_count
    )
    doc_index, seq_offset = locate(positions, seq_lens)
    key_doc = locate(key_positions, seq_lens)[0]
    cosine, sine = rope_tables(seq_offset)
    input_bf = attn_input.astype(jnp.bfloat16)
    output_bf = attn_output.astype(jnp.bfloat16)
    gateup_bf = gate_up.astype(jnp.bfloat16)
    down_bf = down_weight.astype(jnp.bfloat16)
    input_all, output_all = (
        lax.all_gather(input_bf, ("dp", "cp"), axis=0, tiled=True),
        lax.all_gather(output_bf, ("dp", "cp"), axis=0, tiled=True),
    )
    x_float = tokens.astype(jnp.float32)
    hat_one, inv_one = rms_parts(x_float)
    normed_one = (hat_one * gain_one).astype(jnp.bfloat16)
    projected = jnp.dot(normed_one, input_all, preferred_element_type=jnp.float32)
    query_raw = projected[:, :q_width].reshape(row_count, HEADS, HEAD_DIM)
    key_raw = projected[:, q_width : q_width + kv_width].reshape(row_count, KV_HEADS, HEAD_DIM)
    value_raw = projected[:, q_width + kv_width :]
    hat_query, inv_query = rms_parts(query_raw)
    hat_key, inv_key = rms_parts(key_raw)
    queries = rotate(hat_query * gain_query, cosine, sine).astype(jnp.bfloat16)
    key_rot = rotate(hat_key * gain_key, cosine, sine)
    key_value = jnp.concatenate([key_rot.reshape(row_count, kv_width), value_raw], axis=1).astype(
        jnp.bfloat16
    )
    kv_all = lax.all_gather(key_value, "cp", axis=0, tiled=True)
    total_keys = kv_all.shape[0]
    key_span = min(512, total_keys)
    block_count = total_keys // key_span
    kv_blocks = kv_all.reshape(block_count, key_span, 2 * kv_width)
    pos_blocks = key_positions.reshape(block_count, key_span)
    doc_blocks = key_doc.reshape(block_count, key_span)
    query_group = queries.reshape(row_count, KV_HEADS, head_groups, HEAD_DIM)

    def block_scores(kv_block, key_pos, key_docs):
        key_block = kv_block[:, :kv_width].reshape(key_span, KV_HEADS, HEAD_DIM)
        value_block = kv_block[:, kv_width:].reshape(key_span, KV_HEADS, HEAD_DIM)
        scores = (
            jnp.einsum("qhgd,khd->hgqk", query_group, key_block, preferred_element_type=jnp.float32)
            * score_scale
        )
        allowed = (doc_index[:, None] == key_docs[None, :]) & (
            key_pos[None, :] <= positions[:, None]
        )
        return (key_block, value_block, jnp.where(allowed, scores, masked_score), allowed)

    def forward_block(carry, items):
        run_max, run_total, run_sum = carry
        key_block, value_block, scores, allowed = block_scores(*items)
        new_max = jnp.maximum(run_max, jnp.max(scores, axis=-1))
        weights = jnp.where(allowed, jnp.exp(scores - new_max[..., None]), 0.0)
        factor = jnp.exp(run_max - new_max)
        run_total = run_total * factor + jnp.sum(weights, axis=-1)
        run_sum = run_sum * factor[..., None] + jnp.einsum(
            "hgqk,khd->hgqd",
            weights.astype(jnp.bfloat16),
            value_block,
            preferred_element_type=jnp.float32,
        )
        return ((new_max, run_total, run_sum), None)

    start_state = (
        jnp.full((KV_HEADS, head_groups, row_count), masked_score, jnp.float32),
        jnp.zeros((KV_HEADS, head_groups, row_count), jnp.float32),
        jnp.zeros((KV_HEADS, head_groups, row_count, HEAD_DIM), jnp.float32),
    )
    (run_max, run_total, run_sum), unused = lax.scan(
        forward_block, start_state, (kv_blocks, pos_blocks, doc_blocks)
    )
    attended = run_sum / run_total[..., None]
    log_total = run_max + jnp.log(run_total)
    attn_flat = attended.transpose(2, 0, 1, 3).reshape(row_count, q_width).astype(jnp.bfloat16)
    residual = x_float + jnp.dot(attn_flat, output_all, preferred_element_type=jnp.float32)
    hat_two, inv_two = rms_parts(residual)
    normed_two = (hat_two * gain_two).astype(jnp.bfloat16)
    columns = normed_two
    gate_both = jnp.dot(
        columns,
        lax.all_gather(gateup_bf, ("dp", "cp"), axis=0, tiled=True),
        preferred_element_type=jnp.float32,
    )
    gate_part = gate_both[:, :FF]
    up_part = gate_both[:, FF:]
    gate_sig = jax.nn.sigmoid(gate_part)
    gate_act = gate_part * gate_sig
    hidden = (gate_act * up_part).astype(jnp.bfloat16)
    columns = hidden
    ff_result = jnp.dot(
        columns,
        lax.all_gather(down_bf, ("dp", "cp"), axis=0, tiled=True),
        preferred_element_type=jnp.float32,
    )
    mixed = (residual + ff_result).astype(jnp.bfloat16)
    d_hidden = contract_cols(
        output_cotangent, lax.all_gather(down_bf, ("dp", "cp"), axis=0, tiled=True)
    )
    d_gate = d_hidden * up_part * (gate_sig * (1.0 + gate_part * (1.0 - gate_sig)))
    d_up = d_hidden * gate_act
    d_gate_both = jnp.concatenate([d_gate, d_up], axis=1).astype(jnp.bfloat16)
    d_normed_two = contract_cols(
        d_gate_both, lax.all_gather(gateup_bf, ("dp", "cp"), axis=0, tiled=True)
    )
    grad_gain_two = jnp.sum(d_normed_two * hat_two, axis=0)
    d_residual = output_cotangent.astype(jnp.float32) + norm_back(
        d_normed_two * gain_two, hat_two, inv_two
    )
    d_branch = d_residual.astype(jnp.bfloat16)
    input_back, output_back = (input_all, output_all)
    d_flat = contract_cols(d_branch, output_back).astype(jnp.bfloat16)
    d_attended = d_flat.reshape(row_count, KV_HEADS, head_groups, HEAD_DIM).transpose(1, 2, 0, 3)
    delta = jnp.sum(d_attended.astype(jnp.float32) * attended, axis=-1)

    def backward_block(d_query_sum, items):
        key_block, value_block, scores, allowed = block_scores(*items)
        probs = jnp.where(allowed, jnp.exp(scores - log_total[..., None]), 0.0)
        d_probs = jnp.einsum(
            "hgqd,khd->hgqk", d_attended, value_block, preferred_element_type=jnp.float32
        )
        d_scores = (probs * (d_probs - delta[..., None])).astype(jnp.bfloat16)
        d_query_sum = (
            d_query_sum
            + jnp.einsum("hgqk,khd->hgqd", d_scores, key_block, preferred_element_type=jnp.float32)
            * score_scale
        )
        d_keys = (
            jnp.einsum("hgqk,qhgd->khd", d_scores, query_group, preferred_element_type=jnp.float32)
            * score_scale
        )
        d_values = jnp.einsum(
            "hgqk,hgqd->khd",
            probs.astype(jnp.bfloat16),
            d_attended,
            preferred_element_type=jnp.float32,
        )
        return (
            d_query_sum,
            jnp.concatenate(
                [d_keys.reshape(key_span, kv_width), d_values.reshape(key_span, kv_width)], axis=1
            ),
        )

    d_query_sum, d_kv_blocks = lax.scan(
        backward_block,
        jnp.zeros((KV_HEADS, head_groups, row_count, HEAD_DIM), jnp.float32),
        (kv_blocks, pos_blocks, doc_blocks),
    )
    d_kv = lax.psum_scatter(
        d_kv_blocks.reshape(total_keys, 2 * kv_width).astype(jnp.bfloat16),
        "cp",
        scatter_dimension=0,
        tiled=True,
    ).astype(jnp.float32)
    d_query_rot = rotate(
        d_query_sum.transpose(2, 0, 1, 3).reshape(row_count, HEADS, HEAD_DIM), cosine, -sine
    )
    grad_gain_query = jnp.sum(d_query_rot * hat_query, axis=(0, 1))
    d_query_raw = norm_back(d_query_rot * gain_query, hat_query, inv_query)
    d_key_rot = rotate(d_kv[:, :kv_width].reshape(row_count, KV_HEADS, HEAD_DIM), cosine, -sine)
    grad_gain_key = jnp.sum(d_key_rot * hat_key, axis=(0, 1))
    d_key_raw = norm_back(d_key_rot * gain_key, hat_key, inv_key)
    d_projected = jnp.concatenate(
        [
            d_query_raw.reshape(row_count, q_width),
            d_key_raw.reshape(row_count, kv_width),
            d_kv[:, kv_width:],
        ],
        axis=1,
    ).astype(jnp.bfloat16)
    d_normed_one = contract_cols(d_projected, input_back)
    grad_gain_one = jnp.sum(d_normed_one * hat_one, axis=0)
    token_gradient = d_residual + norm_back(d_normed_one * gain_one, hat_one, inv_one)

    def make_wide(first_src, attn_src, second_src):

        def wide_terms(row_start, row_total):
            return jnp.concatenate(
                [
                    contract_rows(first_src, d_projected),
                    contract_rows(attn_src, d_branch),
                    contract_rows(second_src, d_gate_both),
                ],
                axis=1,
            )

        return wide_terms

    def make_down(hidden_src):

        def down_terms(row_start, row_total):
            return contract_rows(hidden_src, output_cotangent)

        return down_terms

    shard_rows = attn_input.shape[0]
    down_rows = down_weight.shape[0]
    wide_fn = make_wide(
        owner_order(normed_one, data_count, context_count),
        owner_order(attn_flat, data_count, context_count),
        owner_order(normed_two, data_count, context_count),
    )
    down_fn = make_down(owner_order(hidden, data_count, context_count))
    group_wide = lax.psum_scatter(
        wide_fn(jnp.int32(0), lax.axis_size("cp") * (shard_rows * data_count)).astype(jnp.bfloat16),
        "cp",
        scatter_dimension=0,
        tiled=True,
    )
    group_down = lax.psum_scatter(
        down_fn(jnp.int32(0), lax.axis_size("cp") * (down_rows * data_count)).astype(jnp.bfloat16),
        "cp",
        scatter_dimension=0,
        tiled=True,
    )
    wide_grads, down_grads = (
        lax.psum_scatter(group_wide, "dp", scatter_dimension=0, tiled=True).astype(jnp.float32),
        lax.psum_scatter(group_down, "dp", scatter_dimension=0, tiled=True).astype(jnp.float32),
    )
    gain_grads = lax.psum(
        jnp.concatenate([grad_gain_one, grad_gain_two, grad_gain_query, grad_gain_key]),
        ("dp", "cp"),
    )
    grad_input = wide_grads[:, :proj_width]
    grad_output = wide_grads[:, proj_width : proj_width + model_width]
    grad_gateup = wide_grads[:, proj_width + model_width :]
    input_next, input_moment_next, input_square_next = adam_update(
        attn_input, input_moment, input_square, grad_input, rate_input, weight_decay
    )
    output_next, output_moment_next, output_square_next = adam_update(
        attn_output, output_moment, output_square, grad_output, rate_output, weight_decay
    )
    gateup_next, gateup_moment_next, gateup_square_next = adam_update(
        gate_up, gateup_moment, gateup_square, grad_gateup, rate_gateup, weight_decay
    )
    down_next, down_moment_next, down_square_next = adam_update(
        down_weight, down_moment, down_square, down_grads, rate_down, weight_decay
    )
    gains_next, gains_moment_next, gains_square_next = adam_update(
        norm_gains, gains_moment, gains_square, gain_grads, rate_gains, 0.0
    )
    return (
        mixed,
        token_gradient,
        input_next,
        input_moment_next,
        input_square_next,
        output_next,
        output_moment_next,
        output_square_next,
        gateup_next,
        gateup_moment_next,
        gateup_square_next,
        down_next,
        down_moment_next,
        down_square_next,
        gains_next,
        gains_moment_next,
        gains_square_next,
    )


MESH = pl.DeviceIdType.MESH


def place():
    dp = lax.axis_index("dp")
    cp = lax.axis_index("cp")
    return dp, cp, cp // 2, cp % 2


def greet(targets):
    barrier = pltpu.get_barrier_semaphore()
    for target in targets:
        pl.semaphore_signal(barrier, inc=1, device_id=target, device_id_type=MESH)
    pl.semaphore_wait(barrier, len(targets))


def send(source, target, send_sem, recv_sem, device):
    return pltpu.make_async_remote_copy(
        src_ref=source,
        dst_ref=target,
        send_sem=send_sem,
        recv_sem=recv_sem,
        device_id=device,
        device_id_type=MESH,
    )


class LineGather:
    def __init__(self, own_ref, all_ref, sems, where, depth, both=True):
        self.own, self.where, self.depth, self.both = own_ref, where, depth, both
        self.slot = all_ref if callable(all_ref) else lambda slot: all_ref.at[slot]
        self.right, self.left, self.sib, self.recv, self.local = sems

    @staticmethod
    def scratch(depth):
        return [pltpu.SemaphoreType.DMA((2 * depth,))] * 4 + [pltpu.SemaphoreType.DMA]

    def copy(self, kind, slot, source):
        dp, cp, z, core = self.where
        device = {"right": (dp, cp + 2), "left": (dp, cp - 2), "sib": (dp, cp ^ 1)}[kind]
        sem = {"right": self.right, "left": self.left, "sib": self.sib}[kind]
        return send(source, self.slot(slot), sem.at[slot], self.recv.at[slot], device)

    def keep(self):
        return pltpu.make_async_copy(self.own, self.slot(self.where[1]), self.local)

    def start(self):
        dp, cp, z, core = self.where

        @pl.when(z < self.depth - 1)
        def _():
            self.copy("right", cp, self.own).start()

        @pl.when(z > 0)
        def _():
            self.copy("left", cp, self.own).start()

        if self.both:
            self.copy("sib", cp, self.own).start()
        self.keep().start()

    def step(self, far):
        dp, cp, z, core = self.where

        @pl.when(z >= far)
        def _():
            slot = cp - 2 * far
            self.copy("right", slot, self.own).wait_recv()

            @pl.when(z < self.depth - 1)
            def _():
                self.copy("right", slot, self.slot(slot)).start()

            if self.both:
                self.copy("sib", slot, self.slot(slot)).start()

        @pl.when(z + far < self.depth)
        def _():
            slot = cp + 2 * far
            self.copy("left", slot, self.own).wait_recv()

            @pl.when(z > 0)
            def _():
                self.copy("left", slot, self.slot(slot)).start()

            if self.both:
                self.copy("sib", slot, self.slot(slot)).start()

    def arrive(self, spot):
        self.copy("sib", 1 - self.where[3] + 2 * spot, self.own).wait_recv()

    def finish(self, arrived=False):
        dp, cp, z, core = self.where
        if self.both and not arrived:
            for spot in range(self.depth):
                self.arrive(spot)
        if not arrived:
            self.keep().wait()
        for spot in range(self.depth):
            slot = 2 * spot + core
            if self.both:
                self.copy("sib", slot, self.own).wait_send()

            @pl.when((spot <= z) & (z < self.depth - 1))
            def _():
                self.copy("right", slot, self.own).wait_send()

            @pl.when((spot >= z) & (z > 0))
            def _():
                self.copy("left", slot, self.own).wait_send()


class Swap:
    def __init__(self, source_ref, target_ref, sems, where, count):
        self.source, self.where, self.count = source_ref, where, count
        self.slot = target_ref if callable(target_ref) else lambda slot: target_ref.at[slot]
        self.origin = source_ref if callable(source_ref) else lambda slot: source_ref.at[slot]
        self.sent, self.recv, self.local = sems

    @staticmethod
    def scratch(count):
        return [pltpu.SemaphoreType.DMA((count,))] * 2 + [pltpu.SemaphoreType.DMA]

    def copy(self, peer):
        dp, cp, z, core = self.where
        return send(
            self.origin(peer),
            self.slot(cp),
            self.sent.at[peer],
            self.recv.at[cp],
            (dp, peer),
        )

    def keep(self):
        cp = self.where[1]
        return pltpu.make_async_copy(self.origin(cp), self.slot(cp), self.local)

    def start(self):
        cp = self.where[1]
        for turn in range(self.count - 1, 0, -1):
            self.copy(cp ^ turn).start()
        self.keep().start()

    def arrive(self, peer):
        dp, cp, z, core = self.where
        send(
            self.origin(peer),
            self.slot(peer),
            self.sent.at[peer],
            self.recv.at[peer],
            (dp, peer),
        ).wait_recv()

    def finish_recv(self):
        cp = self.where[1]
        for turn in range(1, self.count):
            self.arrive(cp ^ turn)
        self.keep().wait()

    def finish_send(self):
        cp = self.where[1]
        for turn in range(1, self.count):
            self.copy(cp ^ turn).wait_send()


class RingSpread:
    def __init__(self, block, half, sems, where):
        self.block, self.half, self.where = block, half, where
        self.sent, self.recv = sems

    @staticmethod
    def scratch():
        return [pltpu.SemaphoreType.DMA((4,))] * 2

    def copy(self, kind, mine):
        dp, cp, z, core = self.where
        turn = (1, 2, 2, 1)[kind]
        if kind < 2:
            part = self.block(dp if mine else dp ^ turn)
        else:
            part = self.half(dp ^ (3 - turn) if mine else dp ^ 3, kind - 2)
        return send(part, part, self.sent.at[kind], self.recv.at[kind], (dp ^ turn, cp))

    def start(self):
        self.copy(0, True).start()
        self.copy(1, True).start()

    def forward(self):
        self.copy(0, False).wait_recv()
        self.copy(2, True).start()
        self.copy(1, False).wait_recv()
        self.copy(3, True).start()

    def finish(self):
        self.copy(2, False).wait_recv()
        self.copy(3, False).wait_recv()
        for kind in range(4):
            self.copy(kind, True).wait_send()


def turn_heads(values, cosine, sine):
    half = values.shape[0] // 2
    first, second = values[:half], values[half:]
    return jnp.concatenate([first * cosine - second * sine, second * cosine + first * sine], axis=0)


def head_hat(values):
    inverse = lax.rsqrt(jnp.mean(values * values, axis=0, keepdims=True) + norm_eps)
    return values * inverse, inverse


def lay_places(order_ref, lengths_ref, rows, count):
    spots = [order_ref[0, index] * rows for index in range(count)]
    lanes = lax.broadcasted_iota(jnp.int32, (1, rows), 1)
    lines = lax.broadcasted_iota(jnp.int32, (rows, 1), 0)
    place_row = jnp.concatenate([spot + lanes for spot in spots], axis=1)
    place_column = jnp.concatenate([spot + lines for spot in spots], axis=0)
    starts = jnp.zeros_like(place_row)
    begin = jnp.int32(0)
    for index in range(lengths_ref.shape[1] - 1):
        begin = begin + lengths_ref[0, index]
        starts = jnp.where(place_row >= begin, begin, starts)
    return place_row, place_column, starts


def to_column(row):
    size = row.shape[1]
    down = lax.broadcasted_iota(jnp.int32, (size, size), 0)
    across = lax.broadcasted_iota(jnp.int32, (size, size), 1)
    return jnp.sum(jnp.where(down == across, row, 0.0), axis=1, keepdims=True)


def split_gains(gains_ref, width):
    gain_one = gains_ref[:, :width]
    gain_two = gains_ref[:, width : 2 * width]
    gain_query = to_column(gains_ref[:, 2 * width : 2 * width + HEAD_DIM])
    gain_key = to_column(gains_ref[:, 2 * width + HEAD_DIM :])
    return gain_one, gain_two, gain_query, gain_key


def score_block(keys, queries, key_place, query_place, query_start):
    scores = jnp.dot(keys, queries, preferred_element_type=jnp.float32) * HEAD_DIM ** (-0.5)
    allowed = (key_place <= query_place) & (key_place >= query_start)
    return jnp.where(allowed, scores, masked_score), allowed


def front_kernel(
    tile,
    tokens_ref,
    gains_ref,
    order_ref,
    lengths_ref,
    input_ref,
    output_ref,
    gateup_ref,
    cotangent_own,
    normed_one_out,
    own_two,
    cotangent_all,
    input_out,
    output_out,
    gateup_out,
    raw_out,
    flat_out,
    total_out,
    residual_out,
    cosine_ref,
    sine_ref,
    input_send,
    output_own,
    gate_send,
    up_send,
    key_place_ref,
    query_place_ref,
    query_start_ref,
    normed_one,
    own_one,
    inputs,
    outputs,
    raw,
    queries,
    keys_up,
    values,
    flat_send,
    flat_recv,
    out_sems,
    *sems,
):
    where = place()
    dp, cp, z, core = where
    context_count = normed_one.shape[0]
    depth = context_count // 2
    rows = tokens_ref.shape[0]
    width = tokens_ref.shape[1]
    q_each = HEADS // KV_HEADS * HEAD_DIM
    take = iter(range(len(sems)))

    def some(count):
        return [sems[next(take)] for _ in range(count)]

    kv_each = HEAD_DIM
    for head in range(context_count):
        for start, begin, size in (
            (head * q_each, 0, q_each),
            (HEADS * HEAD_DIM + head * kv_each, q_each, kv_each),
            ((HEADS + KV_HEADS) * HEAD_DIM + head * kv_each, q_each + kv_each, kv_each),
        ):
            input_send[head, :, begin : begin + size] = input_ref[:, start : start + size].astype(
                jnp.bfloat16
            )
    hidden = gate_send.shape[2]
    piece = hidden // inputs.shape[0]
    half_width = gateup_ref.shape[1] // 2

    def cut_columns(target, base):
        for head in range(context_count):
            target[head] = jnp.concatenate(
                [
                    gateup_ref[:, pl.ds(base + (group * context_count + head) * piece, piece)]
                    for group in range(inputs.shape[0])
                ],
                axis=1,
            ).astype(jnp.bfloat16)

    cut_columns(gate_send, 0)
    greet([(dp, cp ^ turn) for turn in range(1, context_count)] + [(dp ^ 1, cp), (dp ^ 2, cp)])
    token_line = LineGather(own_one, normed_one, some(5), where, depth)
    cotangent_line = LineGather(cotangent_own, cotangent_all, some(5), where, depth)
    output_line = LineGather(
        output_own, lambda slot: outputs.at[dp, slot // 2, core], some(5), where, depth, False
    )
    input_swap = Swap(input_send, inputs.at[dp], some(3), where, context_count)
    shard = input_send.shape[1]

    def gateup_slot(index):
        return lambda slot: gateup_out.at[index, dp, pl.ds(pl.multiple_of(slot * shard, 16), shard)]

    gate_swap = Swap(gate_send, gateup_slot(0), some(3), where, context_count)
    up_swap = Swap(up_send, gateup_slot(1), some(3), where, context_count)
    flat_swap = Swap(flat_send, flat_recv, some(3), where, context_count)
    input_ring = RingSpread(
        lambda d: inputs.at[d],
        lambda d, h: inputs.at[d, pl.ds(h * (context_count // 2), context_count // 2)],
        some(2),
        where,
    )
    output_ring = RingSpread(
        lambda d: outputs.at[d, :, core],
        lambda d, h: outputs.at[d, pl.ds(h * (depth // 2), depth // 2), core],
        some(2),
        where,
    )
    half_rows = gateup_out.shape[2] // 2

    def gateup_ring(index):
        return RingSpread(
            lambda d: gateup_out.at[index, d],
            lambda d, h: gateup_out.at[index, d, pl.ds(h * half_rows, half_rows)],
            some(2),
            where,
        )

    gate_ring, up_ring = gateup_ring(0), gateup_ring(1)
    share_sent, share_recv = some(2)

    def share(mine):
        part = outputs.at[:, :, core if mine else 1 - core]
        return send(part, part, share_sent, share_recv, (dp, cp ^ 1))

    input_swap.start()
    gate_swap.start()
    gain_one, gain_two, gain_query, gain_key = split_gains(gains_ref, width)
    x_float = tokens_ref[...].astype(jnp.float32)
    hat_one, _ = rms_parts(x_float)
    own_one[...] = (hat_one * gain_one).astype(jnp.bfloat16)
    output_own[...] = output_ref[...].astype(jnp.bfloat16)
    cut_columns(up_send, half_width)
    place_row, place_column, starts = lay_places(order_ref, lengths_ref, rows, context_count)
    query_place_ref[...] = place_row
    key_place_ref[...] = place_column
    query_start_ref[...] = starts
    pair_index = lax.broadcasted_iota(jnp.int32, (HEAD_DIM // 2, 1), 0).astype(jnp.float32)
    angles = (place_row - starts).astype(jnp.float32) * jnp.exp(
        pair_index * (-2.0 * math.log(rope_base) / HEAD_DIM)
    )
    cosine_ref[...] = jnp.cos(angles)
    sine_ref[...] = jnp.sin(angles)
    input_swap.finish_recv()
    input_ring.start()
    gate_swap.finish_recv()
    gate_ring.start()
    up_swap.start()
    input_ring.forward()
    token_line.start()
    token_line.step(1)
    up_swap.finish_recv()
    up_ring.start()
    token_line.step(2)
    gate_ring.forward()
    output_line.start()
    token_line.step(3)
    token_line.finish()
    input_ring.finish()
    one_copy = pltpu.make_async_copy(normed_one, normed_one_out, out_sems.at[0])
    one_copy.start()
    input_copy = pltpu.make_async_copy(inputs, input_out, out_sems.at[1])
    input_copy.start()

    weights = inputs[...].reshape(width, inputs.shape[-1])

    def project(turn, carry):
        lanes = pl.ds(pl.multiple_of(turn * tile, tile), tile)
        block = normed_one[pl.ds(turn * (tile // rows), tile // rows)].reshape(tile, width)
        part = jnp.dot(block, weights, preferred_element_type=jnp.float32).T
        raw[:, lanes] = part
        cosine, sine = cosine_ref[:, lanes], sine_ref[:, lanes]
        for head in range(HEADS // KV_HEADS):
            hat, _ = head_hat(part[head * HEAD_DIM : (head + 1) * HEAD_DIM])
            queries[head * HEAD_DIM : (head + 1) * HEAD_DIM, lanes] = turn_heads(
                hat * gain_query, cosine, sine
            ).astype(jnp.bfloat16)
        hat, _ = head_hat(part[q_each : q_each + HEAD_DIM])
        key = turn_heads(hat * gain_key, cosine, sine)
        keys_up[pl.ds(pl.multiple_of(turn * tile, tile), tile)] = key.T.astype(jnp.bfloat16)
        values[:, lanes] = part[q_each + HEAD_DIM :].astype(jnp.bfloat16)
        return carry

    lax.fori_loop(0, normed_one.shape[0] * rows // tile, project, 0)
    raw_copy = pltpu.make_async_copy(raw, raw_out, out_sems.at[2])
    raw_copy.start()

    def attend(turn, carry):
        lanes = pl.ds(pl.multiple_of(turn * tile, tile), tile)
        query_place, query_start = query_place_ref[:, lanes], query_start_ref[:, lanes]

        @pl.when(turn == 0)
        def _():
            output_line.step(1)

        @pl.when(turn == 1)
        def _():
            output_line.step(2)
            output_line.step(3)

        @pl.when(turn == 2)
        def _():
            output_line.finish()
            output_ring.start()

        @pl.when(turn == 3)
        def _():
            cotangent_line.start()

        for head in range(HEADS // KV_HEADS):
            spot = pl.ds(head * HEAD_DIM, HEAD_DIM)
            scores, allowed = score_block(
                keys_up[...], queries[spot, lanes], key_place_ref[...], query_place, query_start
            )
            top = jnp.max(scores, axis=0, keepdims=True)
            exps = jnp.exp(scores - top)
            total = jnp.sum(exps, axis=0, keepdims=True)
            total_out[pl.ds(head, 1), lanes] = top + jnp.log(total)
            probs = (exps * (1.0 / total)).astype(jnp.bfloat16)
            attended = jnp.dot(values[...], probs, preferred_element_type=jnp.float32)
            for part in range(tile // rows):
                flat_send[turn * (tile // rows) + part, spot] = attended[
                    :, part * rows : (part + 1) * rows
                ].astype(jnp.bfloat16)
        return carry

    lax.fori_loop(0, depth, attend, 0)
    flat_swap.start()
    output_ring.forward()
    cotangent_line.step(1)
    output_ring.finish()
    share(True).start()
    share(False).wait_recv()
    output_copy = pltpu.make_async_copy(outputs, output_out, out_sems.at[3])
    output_copy.start()
    flat_swap.finish_recv()
    flat_copy = pltpu.make_async_copy(flat_recv, flat_out, out_sems.at[4])
    flat_copy.start()
    flat = flat_recv[...].reshape(HEADS * HEAD_DIM, rows).astype(jnp.float32).T.astype(jnp.bfloat16)
    residual = x_float + jnp.dot(
        flat, outputs[...].reshape(HEADS * HEAD_DIM, width), preferred_element_type=jnp.float32
    )
    residual_out[...] = residual
    hat_two, _ = rms_parts(residual)
    own_two[...] = (hat_two * gain_two).astype(jnp.bfloat16)
    cotangent_line.step(2)
    up_ring.forward()
    cotangent_line.step(3)
    cotangent_line.finish()
    gate_ring.finish()
    up_ring.finish()
    share(True).wait_send()
    for swap in (input_swap, gate_swap, up_swap, flat_swap):
        swap.finish_send()
    for copy in (one_copy, input_copy, raw_copy, output_copy, flat_copy):
        copy.wait()


def front(
    tokens,
    gains,
    order,
    lengths,
    attn_input,
    attn_output,
    gate_up,
    cotangent,
    data_count,
    context_count,
):
    rows, width = tokens.shape
    depth = context_count // 2
    group_rows = rows * context_count
    shard = attn_input.shape[0]
    each = attn_input.shape[1] // context_count
    hidden = gate_up.shape[1] // 2 // context_count
    q_each = HEADS // KV_HEADS * HEAD_DIM
    flat_width = HEADS * HEAD_DIM
    bf = jnp.bfloat16
    any_space = pl.BlockSpec(memory_space=pl.ANY)
    in_vmem = pl.BlockSpec(memory_space=pltpu.VMEM)
    in_smem = pl.BlockSpec(memory_space=pltpu.SMEM)
    shapes = [
        ((context_count, rows, width), bf, any_space),
        ((rows, width), bf, in_vmem),
        ((context_count, rows, width), bf, any_space),
        ((data_count, context_count, shard, each), bf, any_space),
        ((data_count, depth, 2, shard, width), bf, any_space),
        ((2, data_count, context_count * shard, hidden), bf, any_space),
        ((each, group_rows), jnp.float32, any_space),
        ((context_count, q_each, rows), bf, any_space),
        ((HEADS // KV_HEADS, group_rows), jnp.float32, in_vmem),
        ((rows, width), jnp.float32, in_vmem),
        ((HEAD_DIM // 2, group_rows), jnp.float32, in_vmem),
        ((HEAD_DIM // 2, group_rows), jnp.float32, in_vmem),
    ]
    return pl.pallas_call(
        functools.partial(front_kernel, 2 * rows),
        out_shape=[jax.ShapeDtypeStruct(shape, kind) for shape, kind, _ in shapes],
        in_specs=[in_vmem] * 2 + [in_smem] * 2 + [in_vmem] * 3 + [any_space],
        out_specs=[space for _, _, space in shapes],
        scratch_shapes=[
            pltpu.VMEM((context_count, shard, each), bf),
            pltpu.VMEM((shard, width), bf),
            pltpu.VMEM((context_count, shard, hidden), bf),
            pltpu.VMEM((context_count, shard, hidden), bf),
            pltpu.VMEM((group_rows, 1), jnp.int32),
            pltpu.VMEM((1, group_rows), jnp.int32),
            pltpu.VMEM((1, group_rows), jnp.int32),
            pltpu.VMEM((context_count, rows, width), bf),
            pltpu.VMEM((rows, width), bf),
            pltpu.VMEM((data_count, context_count, shard, each), bf),
            pltpu.VMEM((data_count, depth, 2, shard, width), bf),
            pltpu.VMEM((each, group_rows), jnp.float32),
            pltpu.VMEM((q_each, group_rows), bf),
            pltpu.VMEM((group_rows, HEAD_DIM), bf),
            pltpu.VMEM((HEAD_DIM, group_rows), bf),
            pltpu.VMEM((context_count, q_each, rows), bf),
            pltpu.VMEM((context_count, q_each, rows), bf),
            pltpu.SemaphoreType.DMA((6,)),
        ]
        + LineGather.scratch(depth) * 3
        + Swap.scratch(context_count) * 4
        + RingSpread.scratch() * 4
        + [pltpu.SemaphoreType.DMA] * 2,
        compiler_params=pltpu.CompilerParams(
            collective_id=0, has_side_effects=True, vmem_limit_bytes=56 * 2**20
        ),
        name="front",
    )(tokens, gains, order, lengths, attn_input, attn_output, gate_up, cotangent)


class LineScatter:
    cuts = 2

    def __init__(self, part_ref, out_ref, scratch, where, depth):
        self.part, self.out, self.where, self.depth = part_ref, out_ref, where, depth
        self.sib, self.line = scratch[:2]
        (
            self.sib_sent,
            self.sib_recv,
            self.right_sent,
            self.right_recv,
            self.left_sent,
            self.left_recv,
        ) = scratch[2:]
        self.size = part_ref.shape[1] // self.cuts

    @classmethod
    def scratch(cls, depth, rows, width):
        return [
            pltpu.VMEM((depth, rows, width), jnp.bfloat16),
            pltpu.VMEM((depth + 1, rows, width), jnp.bfloat16),
        ] + [pltpu.SemaphoreType.DMA((depth,))] * 2 + [
            pltpu.SemaphoreType.DMA((depth * cls.cuts,))
        ] * 4

    def pair(self, spot):
        dp, cp, z, core = self.where
        return send(
            self.part.at[2 * spot + 1 - core],
            self.sib.at[spot],
            self.sib_sent.at[spot],
            self.sib_recv.at[spot],
            (dp, cp ^ 1),
        )

    def rows(self, cut):
        return pl.ds(cut * self.size, self.size)

    def hop_right(self, spot, cut):
        dp, cp, z, core = self.where
        index = spot * self.cuts + cut
        return send(
            self.part.at[2 * spot + core, self.rows(cut)],
            self.line.at[spot + 1, self.rows(cut)],
            self.right_sent.at[index],
            self.right_recv.at[index],
            (dp, cp + 2),
        )

    def hop_left(self, spot, cut):
        dp, cp, z, core = self.where
        index = spot * self.cuts + cut
        return send(
            self.part.at[2 * spot + core, self.rows(cut)],
            self.line.at[spot, self.rows(cut)],
            self.left_sent.at[index],
            self.left_recv.at[index],
            (dp, cp - 2),
        )

    def order(self):
        spots = []
        for turn in range(self.depth):
            spots += [self.depth - 1 - turn, turn]
        return list(dict.fromkeys(spots))

    def chip_sum(self, spot, cut):
        rows = self.rows(cut)
        mine = self.part[2 * spot + self.where[3], rows].astype(jnp.float32)
        return mine + self.sib[spot, rows].astype(jnp.float32)

    def pass_on(self, spot, cut, arrived, slot, hop):
        total = self.chip_sum(spot, cut)
        if arrived is not None:
            arrived.wait_recv()
            total = total + self.line[slot, self.rows(cut)].astype(jnp.float32)
        self.part[2 * spot + self.where[3], self.rows(cut)] = total.astype(jnp.bfloat16)
        hop.start()

    def forward(self, spot, cuts=None):
        z, core = self.where[2], self.where[3]
        cuts = range(self.cuts) if cuts is None else cuts
        if 0 in cuts:

            @pl.when(z != spot)
            def _():
                self.pair(spot).wait_recv()

        for cut in cuts:
            right, left = self.hop_right(spot, cut), self.hop_left(spot, cut)

            @pl.when((z < spot) & (z > 0))
            def _():
                self.pass_on(spot, cut, right, spot + 1, right)

            @pl.when((z < spot) & (z == 0))
            def _():
                self.pass_on(spot, cut, None, None, right)

            @pl.when((z > spot) & (z < self.depth - 1))
            def _():
                self.pass_on(spot, cut, left, spot, left)

            @pl.when((z > spot) & (z == self.depth - 1))
            def _():
                self.pass_on(spot, cut, None, None, left)

    def finish(self):
        z = self.where[2]
        self.pair(z).wait_recv()
        for cut in range(self.cuts):
            rows = self.rows(cut)
            self.out[rows] = self.chip_sum(z, cut)

            @pl.when(z > 0)
            def _():
                self.hop_right(z, cut).wait_recv()
                self.out[rows] += self.line[z + 1, rows].astype(jnp.float32)

            @pl.when(z < self.depth - 1)
            def _():
                self.hop_left(z, cut).wait_recv()
                self.out[rows] += self.line[z, rows].astype(jnp.float32)

        for spot in range(self.depth):
            self.pair(spot).wait_send()

            @pl.when(z < spot)
            def _():
                for cut in range(self.cuts):
                    self.hop_right(spot, cut).wait_send()

            @pl.when(z > spot)
            def _():
                for cut in range(self.cuts):
                    self.hop_left(spot, cut).wait_send()


class RingReduce:
    def __init__(self, part, work, scratch, where):
        self.part, self.work, self.where = part, work, where
        self.from_x, self.from_y, self.x_sent, self.x_recv, self.y_sent, self.y_recv = scratch

    @staticmethod
    def scratch(*half):
        return [pltpu.VMEM((3,) + half, jnp.bfloat16)] * 2 + [pltpu.SemaphoreType.DMA((3,))] * 4

    def to_x(self, kind):
        dp, cp, z, core = self.where
        source = (
            self.part(dp ^ 3, 0) if kind == 0 else self.part(dp ^ 1, 0) if kind == 1 else self.work(1)
        )
        return send(
            source, self.from_x.at[kind], self.x_sent.at[kind], self.x_recv.at[kind], (dp ^ 1, cp)
        )

    def to_y(self, kind):
        dp, cp, z, core = self.where
        source = (
            self.part(dp ^ 3, 1) if kind == 0 else self.part(dp ^ 2, 1) if kind == 1 else self.work(0)
        )
        return send(
            source, self.from_y.at[kind], self.y_sent.at[kind], self.y_recv.at[kind], (dp ^ 2, cp)
        )

    def start(self):
        for kind in range(2):
            self.to_x(kind).start()
            self.to_y(kind).start()

    def add(self, index, *arrived):
        target = self.work(index)
        total = target[...].astype(jnp.float32)
        for block in arrived:
            total = total + block[...].astype(jnp.float32)
        target[...] = total.astype(jnp.bfloat16)

    def middle(self):
        self.to_x(0).wait_recv()
        self.add(0, self.from_x.at[0])
        self.to_y(2).start()
        self.to_y(0).wait_recv()
        self.add(1, self.from_y.at[0])
        self.to_x(2).start()

    def finish(self):
        for kind in (1, 2):
            self.to_x(kind).wait_recv()
            self.to_y(kind).wait_recv()
        self.add(2, self.from_x.at[1], self.from_y.at[2])
        self.add(3, self.from_y.at[1], self.from_x.at[2])

    def finish_send(self):
        for kind in range(3):
            self.to_x(kind).wait_send()
            self.to_y(kind).wait_send()

    def places(self):
        dp = self.where[0]
        return [(dp ^ 2, 0), (dp ^ 1, 1), (dp, 0), (dp, 1)]


def far_first(turn, z, depth):
    order = []
    for spot in range(depth):
        rest = sorted((other for other in range(depth) if other != spot), key=lambda other: (-abs(other - spot), other))
        ends = [other for other in rest if other in (0, depth - 1)]
        order.append(ends + [other for other in rest if other not in ends] + [spot])
    picked = 0
    for step in range(depth):
        for spot in range(depth):
            picked = picked + order[spot][step] * ((turn == step) & (z == spot)).astype(jnp.int32)
    return picked


def near_first(turn, z, depth):
    picked = 0
    for step in range(depth):
        for spot in range(depth):
            order = sorted(range(depth), key=lambda other: (abs(other - spot), other))
            picked = picked + order[step] * ((turn == step) & (z == spot)).astype(jnp.int32)
    return picked


def middle_kernel(
    own_ref,
    cotangent_in,
    gateup_in,
    down_in,
    d_normed_out,
    forward_out,
    down_out,
    gateup_out,
    normed,
    cotangent,
    gate_weight,
    up_weight,
    down_weight,
    hidden_up,
    d_gates,
    d_ups,
    parts,
    forwards,
    down_grad,
    gateup_grad,
    load_sems,
    save_sems,
    *scratch,
):
    where = place()
    dp, cp, z, core = where
    count, rows, width = normed.shape
    depth = count // 2
    tile = 2 * rows
    group_rows = count * rows
    loads = [
        pltpu.make_async_copy(source, target, load_sems.at[index])
        for index, (source, target) in enumerate(
            [
                (gateup_in.at[0], gate_weight),
                (gateup_in.at[1], up_weight),
                (cotangent_in, cotangent),
                (down_in, down_weight),
            ]
        )
    ]
    greet(
        [(dp, cp ^ turn) for turn in range(1, count)]
        + [(dp ^ 1, cp), (dp ^ 2, cp)]
    )
    second_line = LineGather(own_ref, normed, scratch[:5], where, depth)
    line = LineScatter(parts, d_normed_out, scratch[5:13], where, depth)
    lane_half = width // 2

    def down_part(d, h):
        return down_grad.at[d, :, pl.ds(h * lane_half, lane_half)]

    def down_work(index):
        return down_part(*down_ring.places()[index])

    down_ring = RingReduce(down_part, down_work, scratch[13:], where)
    second_line.start()
    for load in loads:
        load.start()
    at_end = (z == 0) | (z == depth - 1)
    for load in loads:
        load.wait()

    def feed(turn, carry):
        spot = near_first(turn, z, depth)
        far = jnp.abs(spot - z)

        @pl.when((turn > 0) & (far != jnp.abs(near_first(turn - 1, z, depth) - z)))
        def _():
            second_line.step(far)

        @pl.when(turn == 0)
        def _():
            second_line.keep().wait()

        second_line.arrive(spot)
        pair = pl.ds(2 * spot, 2)
        lanes = pl.ds(pl.multiple_of(spot * tile, tile), tile)
        block = normed[pair].reshape(tile, width)
        gate = jnp.dot(block, gate_weight[...], preferred_element_type=jnp.float32)
        up = jnp.dot(block, up_weight[...], preferred_element_type=jnp.float32)
        sig = 1.0 / (1.0 + jnp.exp(-gate))
        act = gate * sig
        hidden_up[:, lanes] = (act * up).T.astype(jnp.bfloat16)
        d_hidden = contract_cols(cotangent[pair].reshape(tile, width), down_weight[...])
        d_gate = (d_hidden * up * (sig * (1.0 + gate * (1.0 - sig)))).astype(jnp.bfloat16)
        d_up = (d_hidden * act).astype(jnp.bfloat16)
        d_gates[lanes] = d_gate
        d_ups[lanes] = d_up
        part = contract_cols(d_gate, gate_weight[...]) + contract_cols(d_up, up_weight[...])
        parts[pair] = part.astype(jnp.bfloat16).reshape(2, rows, width)
        line.pair(spot).start()

        @pl.when(at_end & (turn > 0))
        def _():
            line.forward(spot)

        return carry

    lax.fori_loop(0, depth, feed, 0)
    chunk = 256
    inner = depth - 1 - z
    outer = [inner, (depth - 1) * (z // 2 == 0).astype(jnp.int32), (depth - 1) * (z // 2 == 1).astype(jnp.int32)]

    def relay(index):
        @pl.when(jnp.logical_not(at_end))
        def _():
            line.forward(outer[index])

    def down_step(step, carry):
        lanes = pl.ds(pl.multiple_of(step * chunk, chunk), chunk)
        right = cotangent[:, :, lanes].reshape(group_rows, chunk)
        down_grad[:, :, lanes] = (
            jnp.dot(hidden_up[...], right, preferred_element_type=jnp.float32)
            .reshape(down_grad.shape[:2] + (chunk,))
            .astype(jnp.bfloat16)
        )
        return carry

    lax.fori_loop(0, width // chunk, down_step, 0)
    down_ring.start()
    relay(0)

    def gateup_step(step, carry):
        lanes = pl.ds(pl.multiple_of(step * chunk, chunk), chunk)
        left = normed[:, :, lanes].reshape(group_rows, chunk)
        gateup_grad[0, lanes] = contract_rows(left, d_gates[...]).astype(jnp.bfloat16)
        gateup_grad[1, lanes] = contract_rows(left, d_ups[...]).astype(jnp.bfloat16)
        return carry

    steps = width // chunk
    lax.fori_loop(0, steps // 2, gateup_step, 0)
    relay(1)
    lax.fori_loop(steps // 2, steps, gateup_step, 0)
    relay(2)
    saves = [pltpu.make_async_copy(gateup_grad, gateup_out, save_sems.at[0])]
    saves[0].start()
    down_ring.middle()

    def forward_step(step, carry):
        lanes = pl.ds(pl.multiple_of(step * tile, tile), tile)
        forwards[pl.ds(2 * step, 2)] = (
            contract_rows(hidden_up[:, lanes], down_weight[...])
            .astype(jnp.bfloat16)
            .reshape(2, rows, width)
        )
        return carry

    lax.fori_loop(0, depth, forward_step, 0)
    saves.append(pltpu.make_async_copy(forwards, forward_out, save_sems.at[1]))
    saves[1].start()
    line.finish()
    second_line.finish(True)
    down_ring.finish()
    for half in range(2):
        down_out[:, pl.ds(half * lane_half, lane_half)] = down_grad[
            dp, :, pl.ds(half * lane_half, lane_half)
        ].astype(jnp.float32)
    down_ring.finish_send()
    for save in saves:
        save.wait()


def middle(own, cotangent, gateup, down, data_count, collective_id):
    count, rows, width = cotangent.shape
    depth = count // 2
    hidden = down.shape[0]
    group_rows = count * rows
    bf = jnp.bfloat16
    any_space = pl.BlockSpec(memory_space=pl.ANY)
    in_vmem = pl.BlockSpec(memory_space=pltpu.VMEM)
    return pl.pallas_call(
        middle_kernel,
        out_shape=[
            jax.ShapeDtypeStruct((rows, width), jnp.float32),
            jax.ShapeDtypeStruct((count, rows, width), bf),
            jax.ShapeDtypeStruct((hidden // data_count, width), jnp.float32),
            jax.ShapeDtypeStruct((2, width, hidden), bf),
        ],
        in_specs=[in_vmem] + [any_space] * 3,
        out_specs=[in_vmem, any_space, in_vmem, any_space],
        scratch_shapes=[
            pltpu.VMEM((count, rows, width), bf),
            pltpu.VMEM((count, rows, width), bf),
            pltpu.VMEM((width, hidden), bf),
            pltpu.VMEM((width, hidden), bf),
            pltpu.VMEM((hidden, width), bf),
            pltpu.VMEM((hidden, group_rows), bf),
            pltpu.VMEM((group_rows, hidden), bf),
            pltpu.VMEM((group_rows, hidden), bf),
            pltpu.VMEM((count, rows, width), bf),
            pltpu.VMEM((count, rows, width), bf),
            pltpu.VMEM((data_count, hidden // data_count, width), bf),
            pltpu.VMEM((2, width, hidden), bf),
            pltpu.SemaphoreType.DMA((4,)),
            pltpu.SemaphoreType.DMA((2,)),
        ]
        + LineGather.scratch(depth)
        + LineScatter.scratch(depth, rows, width)
        + RingReduce.scratch(hidden // data_count, width // 2),
        compiler_params=pltpu.CompilerParams(
            collective_id=collective_id, has_side_effects=True, vmem_limit_bytes=60 * 2**20
        ),
        name="middle",
    )(own, cotangent, gateup, down)


def back_kernel(
    tokens_ref,
    cotangent_ref,
    residual_ref,
    d_normed_ref,
    gains_ref,
    order_ref,
    lengths_ref,
    cosine_ref,
    sine_ref,
    total_ref,
    normed_in,
    input_in,
    output_in,
    raw_in,
    flat_in,
    forward_in,
    gateup_in,
    mixed_out,
    token_out,
    gains_out,
    output_grad_out,
    input_grad_out,
    gateup_grad_out,
    inputs,
    outputs,
    raw,
    flat,
    forwards,
    forward_sum,
    d_first,
    d_residual,
    branch,
    swap_send,
    swap_recv,
    queries,
    keys,
    keys_up,
    values_up,
    d_query,
    d_key,
    d_value,
    d_projected,
    parts,
    input_grad,
    output_sib,
    output_line,
    gateup_work,
    gain_sums,
    own_gains,
    line_gains,
    all_gains,
    key_place_ref,
    query_place_ref,
    query_start_ref,
    load_sems,
    work_sems,
    share_sems,
    output_sent,
    output_recv,
    line_sent,
    line_recv,
    all_sent,
    all_recv,
    *scratch,
):
    where = place()
    dp, cp, z, core = where
    count, rows, width = forwards.shape
    depth = count // 2
    data_count = all_gains.shape[0]
    shard = inputs.shape[2]
    tile = 2 * rows
    group_rows = count * rows
    heads = HEADS // KV_HEADS
    q_each = heads * HEAD_DIM
    flat_width = HEADS * HEAD_DIM
    score_scale = HEAD_DIM ** (-0.5)
    load_pairs = [
        (output_in, outputs),
        (raw_in, raw),
        (forward_in, forwards),
        (flat_in, flat),
        (normed_in, forwards),
        (input_in, inputs),
    ]
    loads = [
        pltpu.make_async_copy(source, target, load_sems.at[index])
        for index, (source, target) in enumerate(load_pairs)
    ]
    for index in (0, 1, 2, 3, 5):
        loads[index].start()
    greet(
        [(dp, cp ^ turn) for turn in range(1, count)]
        + [(dp ^ turn, cp) for turn in range(1, data_count)]
    )
    swap = Swap(swap_send, swap_recv, scratch[:3], where, count)
    take = iter(scratch[3:])

    def some(amount):
        return [next(take) for _ in range(amount)]

    forward_line = LineScatter(forwards, forward_sum, some(8), where, depth)
    first_line = LineScatter(parts, d_first, some(8), where, depth)
    gateup_rows = data_count * count * shard // data_count

    def in_place(part):
        spots = [(dp ^ 2, 0), (dp ^ 1, 1), (dp, 0), (dp, 1)]
        return lambda index: part(*spots[index])

    gateup_half = gateup_rows // 2

    def gateup_part(index):
        return lambda d, h: gateup_in.at[
            index, pl.ds(pl.multiple_of(d * gateup_rows + h * gateup_half, 16), gateup_half)
        ]

    def gateup_ring(index):
        return RingReduce(
            gateup_part(index), lambda spot: gateup_work.at[index, spot], some(6), where
        )

    def gateup_own(index):
        each = gateup_half // shard
        return lambda slot: gateup_work.at[
            index, 2 + slot // each, pl.ds(pl.multiple_of(slot % each * shard, 16), shard)
        ]

    def output_part(d, h):
        return outputs.at[d, pl.ds(h * (depth // 2), depth // 2), core]

    def input_part(d, h):
        half = gateup_rows // 2
        return input_grad.at[pl.ds(pl.multiple_of(d * gateup_rows + h * half, 16), half)]

    gate_ring, up_ring = gateup_ring(0), gateup_ring(1)
    output_ring = RingReduce(output_part, in_place(output_part), some(6), where)
    input_ring = RingReduce(input_part, in_place(input_part), some(6), where)

    def own_shard(source):
        return lambda slot: source.at[pl.ds(pl.multiple_of(slot * shard, 16), shard)]

    gate_swap = Swap(gateup_own(0), gateup_grad_out.at[0], some(3), where, count)
    up_swap = Swap(gateup_own(1), gateup_grad_out.at[1], some(3), where, count)
    own_rows = input_grad.at[pl.ds(pl.multiple_of(dp * gateup_rows, 16), gateup_rows)]
    input_swap = Swap(own_shard(own_rows), input_grad_out, some(3), where, count)
    works = [
        pltpu.make_async_copy(ring.part(*spot), ring.work(index), work_sems.at[4 * turn + index])
        for turn, ring in enumerate((gate_ring, up_ring))
        for index, spot in enumerate(ring.places())
    ]
    gate_ring.start()
    for work in works:
        work.start()

    def share(mine):
        return send(
            outputs.at[:, :, 1 - core], output_sib, share_sems.at[0], share_sems.at[1], (dp, cp ^ 1)
        )

    def output_hop(far, mine):
        return send(
            outputs.at[dp, z ^ far, core],
            output_line.at[z if mine else z ^ far],
            output_sent.at[far],
            output_recv.at[far],
            (dp, cp ^ (2 * far)),
        )

    at_end = (z == 0) | (z == depth - 1)
    chunk = 256

    gain_one, gain_two, gain_query, gain_key = split_gains(gains_ref, width)
    hat_two, inv_two = rms_parts(residual_ref[...])
    d_normed = d_normed_ref[...]
    own_gains[:, pl.ds(width, width)] = jnp.sum(d_normed * hat_two, axis=0, keepdims=True)
    d_res = cotangent_ref[...].astype(jnp.float32) + norm_back(
        d_normed * gain_two, hat_two, inv_two
    )
    d_residual[...] = d_res
    branch[...] = d_res.astype(jnp.bfloat16)
    loads[0].wait()
    swap_send[...] = (
        contract_cols(outputs[...].reshape(flat_width, width), branch[...])
        .astype(jnp.bfloat16)
        .reshape(count, q_each, rows)
    )
    swap.start()
    loads[2].wait()
    for spot in forward_line.order():
        forward_line.pair(spot).start()
    loads[1].wait()

    def prepare(turn, carry):
        lanes = pl.ds(pl.multiple_of(turn * tile, tile), tile)
        cosine, sine = cosine_ref[:, lanes], sine_ref[:, lanes]
        for head in range(heads):
            spot = pl.ds(head * HEAD_DIM, HEAD_DIM)
            hat, _ = head_hat(raw[spot, lanes])
            queries[spot, lanes] = turn_heads(hat * gain_query, cosine, sine).astype(
                jnp.bfloat16
            )
        hat, _ = head_hat(raw[pl.ds(q_each, HEAD_DIM), lanes])
        key = turn_heads(hat * gain_key, cosine, sine)
        keys[:, lanes] = key.astype(jnp.bfloat16)
        keys_up[lanes] = key.T.astype(jnp.bfloat16)
        values_up[lanes] = raw[pl.ds(q_each + HEAD_DIM, HEAD_DIM), lanes].T.astype(jnp.bfloat16)
        return carry

    lax.fori_loop(0, depth, prepare, 0)
    place_row, place_column, starts = lay_places(order_ref, lengths_ref, rows, count)
    query_place_ref[...] = place_row
    key_place_ref[...] = place_column
    query_start_ref[...] = starts
    d_key[...] = jnp.zeros_like(d_key)
    d_value[...] = jnp.zeros_like(d_value)
    gain_sums[...] = jnp.zeros_like(gain_sums)

    @pl.when(at_end)
    def _():
        for turn in range(depth - 1):
            forward_line.forward(far_first(turn, z, depth))

    loads[3].wait()

    def output_step(step, carry):
        lanes = pl.ds(pl.multiple_of(step * chunk, chunk), chunk)
        outputs[:, :, :, :, lanes] = (
            jnp.dot(
                flat[...].reshape(flat_width, rows),
                branch[:, lanes],
                preferred_element_type=jnp.float32,
            )
            .astype(jnp.bfloat16)
            .reshape(outputs.shape[:4] + (chunk,))
        )
        return carry

    lax.fori_loop(0, width // chunk, output_step, 0)
    share(True).start()
    for work in works:
        work.wait()
    gate_ring.middle()
    up_ring.start()
    swap.finish_recv()

    def attend(turn, carry):
        lanes = pl.ds(pl.multiple_of(turn * tile, tile), tile)
        query_place, query_start = query_place_ref[:, lanes], query_start_ref[:, lanes]

        @pl.when(jnp.logical_not(at_end) & (turn >= 1))
        def _():
            forward_line.forward(far_first(turn - 1, z, depth))

        @pl.when(turn == 1)
        def _():
            gate_ring.finish()
            gate_swap.start()

        @pl.when(turn == 3)
        def _():
            up_ring.middle()

        for head in range(heads):
            spot = pl.ds(head * HEAD_DIM, HEAD_DIM)
            scores, allowed = score_block(
                keys_up[...], queries[spot, lanes], key_place_ref[...], query_place, query_start
            )
            probs = jnp.where(allowed, jnp.exp(scores - total_ref[pl.ds(head, 1), lanes]), 0.0)
            d_out = jnp.concatenate(
                [swap_recv[2 * turn, spot], swap_recv[2 * turn + 1, spot]], axis=1
            )
            d_probs = jnp.dot(values_up[...], d_out, preferred_element_type=jnp.float32)
            delta = jnp.sum(probs * d_probs, axis=0, keepdims=True)
            d_scores = (probs * (d_probs - delta)).astype(jnp.bfloat16)
            d_query[spot, lanes] = (
                jnp.dot(keys[...], d_scores, preferred_element_type=jnp.float32) * score_scale
            )
            d_key[...] += contract_cols(queries[spot, lanes], d_scores) * score_scale
            d_value[...] += contract_cols(d_out, probs.astype(jnp.bfloat16))
        return carry

    lax.fori_loop(0, depth, attend, 0)
    loads[5].wait()
    share(False).wait_recv()

    def share_step(step, carry):
        total = outputs[step, :, core].astype(jnp.float32) + output_sib[step].astype(jnp.float32)
        outputs[step, :, core] = total.astype(jnp.bfloat16)
        return carry

    lax.fori_loop(0, data_count, share_step, 0)
    output_ring.start()

    def feed(turn, carry):
        spot = far_first(turn, z, depth)
        lanes = pl.ds(pl.multiple_of(spot * tile, tile), tile)
        cosine, sine = cosine_ref[:, lanes], sine_ref[:, lanes]
        pieces = []
        for head in range(heads + 1):
            place_in = pl.ds(head * HEAD_DIM, HEAD_DIM)
            hat, inverse = head_hat(raw[place_in, lanes])
            if head < heads:
                turned = turn_heads(d_query[place_in, lanes], cosine, -sine)
                gain, kind = gain_query, 0
            else:
                turned = turn_heads(d_key[:, lanes], cosine, -sine)
                gain, kind = gain_key, 1
            gain_sums[kind] += turned * hat
            scaled = turned * gain
            pieces.append(
                inverse * (scaled - hat * jnp.mean(scaled * hat, axis=0, keepdims=True))
            )
        pieces.append(d_value[:, lanes])
        block = jnp.concatenate(pieces, axis=0).T.astype(jnp.bfloat16)
        d_projected[lanes] = block
        part = contract_cols(block, inputs[...].reshape(width, block.shape[1]))
        parts[pl.ds(2 * spot, 2)] = part.astype(jnp.bfloat16).reshape(2, rows, width)
        first_line.pair(spot).start()

        @pl.when(at_end & (turn < depth - 1))
        def _():
            first_line.forward(spot)

        return carry

    lax.fori_loop(0, depth, feed, 0)
    up_ring.finish()
    up_swap.start()
    forward_line.finish()
    loads[4].start()
    mixed_out[...] = (residual_ref[...] + forward_sum[...]).astype(jnp.bfloat16)
    for kind in range(2):
        own_gains[:, pl.ds(2 * width + kind * HEAD_DIM, HEAD_DIM)] = jnp.sum(
            gain_sums[kind].T, axis=0, keepdims=True
        )
    @pl.when(jnp.logical_not(at_end))
    def _():
        first_line.forward(far_first(0, z, depth))

    loads[4].wait()

    def input_step(step, carry):
        lanes = pl.ds(pl.multiple_of(step * chunk, chunk), chunk)
        left = forwards[:, :, lanes].reshape(group_rows, chunk)
        input_grad[lanes] = contract_rows(left, d_projected[...]).astype(jnp.bfloat16)
        return carry

    lax.fori_loop(0, width // chunk, input_step, 0)
    input_ring.start()
    output_ring.middle()

    @pl.when(jnp.logical_not(at_end))
    def _():
        first_line.forward(far_first(1, z, depth))

    input_ring.middle()

    @pl.when(jnp.logical_not(at_end))
    def _():
        first_line.forward(far_first(2, z, depth))

    output_ring.finish()
    for far in range(depth - 1, 0, -1):
        output_hop(far, True).start()
    input_ring.finish()
    input_swap.start()
    first_line.finish()
    hat_one, inv_one = rms_parts(tokens_ref[...].astype(jnp.float32))
    d_one = d_first[...]
    own_gains[:, pl.ds(0, width)] = jnp.sum(d_one * hat_one, axis=0, keepdims=True)
    line_gains[cp] = own_gains[...]
    for turn in range(1, count):
        send(
            own_gains, line_gains.at[cp], line_sent.at[turn], line_recv.at[turn], (dp, cp ^ turn)
        ).start()
    token_out[...] = d_residual[...] + norm_back(d_one * gain_one, hat_one, inv_one)
    for turn in range(1, count):
        copy = send(
            own_gains,
            line_gains.at[cp ^ turn],
            line_sent.at[turn],
            line_recv.at[turn],
            (dp, cp ^ turn),
        )
        copy.wait_recv()
        copy.wait_send()
    all_gains[dp] = jnp.sum(line_gains[...], axis=0)
    for turn in range(1, data_count):
        send(
            all_gains.at[dp],
            all_gains.at[dp],
            all_sent.at[turn],
            all_recv.at[turn],
            (dp ^ turn, cp),
        ).start()
    for turn in range(1, data_count):
        copy = send(
            all_gains.at[dp],
            all_gains.at[dp ^ turn],
            all_sent.at[turn],
            all_recv.at[turn],
            (dp ^ turn, cp),
        )
        copy.wait_recv()
        copy.wait_send()
    gains_out[...] = jnp.sum(all_gains[...], axis=0)
    total = outputs[dp, z, core].astype(jnp.float32)
    for far in range(1, depth):
        output_hop(far, False).wait_recv()
        total = total + output_line[z ^ far].astype(jnp.float32)
    output_grad_out[...] = total
    for done in (input_swap, gate_swap, up_swap):
        done.finish_recv()
    for done in (swap, input_swap, gate_swap, up_swap, gate_ring, up_ring, output_ring, input_ring):
        done.finish_send()
    for far in range(1, depth):
        output_hop(far, True).wait_send()
    share(True).wait_send()


def back(
    tokens,
    cotangent,
    residual,
    d_normed,
    gains,
    order,
    lengths,
    cosine,
    sine,
    log_total,
    normed,
    inputs,
    outputs,
    raw,
    flat,
    forwards,
    gateup_grad,
    collective_id,
):
    count, rows, width = normed.shape
    depth = count // 2
    data_count = inputs.shape[0]
    shard, each = inputs.shape[2:]
    hidden = gateup_grad.shape[2]
    group_rows = count * rows
    heads = HEADS // KV_HEADS
    q_each = heads * HEAD_DIM
    flat_width = HEADS * HEAD_DIM
    gain_width = 2 * width + 2 * HEAD_DIM
    bf = jnp.bfloat16
    f32 = jnp.float32
    any_space = pl.BlockSpec(memory_space=pl.ANY)
    in_vmem = pl.BlockSpec(memory_space=pltpu.VMEM)
    in_smem = pl.BlockSpec(memory_space=pltpu.SMEM)
    return pl.pallas_call(
        back_kernel,
        out_shape=[
            jax.ShapeDtypeStruct((rows, width), bf),
            jax.ShapeDtypeStruct((rows, width), f32),
            jax.ShapeDtypeStruct((1, gain_width), f32),
            jax.ShapeDtypeStruct((shard, width), f32),
            jax.ShapeDtypeStruct((count, shard, each), bf),
            jax.ShapeDtypeStruct((2, count, shard, hidden), bf),
        ],
        in_specs=[in_vmem] * 5 + [in_smem] * 2 + [in_vmem] * 3 + [any_space] * 7,
        out_specs=[in_vmem] * 4 + [any_space] * 2,
        scratch_shapes=[
            pltpu.VMEM(inputs.shape, bf),
            pltpu.VMEM(outputs.shape, bf),
            pltpu.VMEM(raw.shape, f32),
            pltpu.VMEM(flat.shape, bf),
            pltpu.VMEM(forwards.shape, bf),
            pltpu.VMEM((rows, width), f32),
            pltpu.VMEM((rows, width), f32),
            pltpu.VMEM((rows, width), f32),
            pltpu.VMEM((rows, width), bf),
            pltpu.VMEM((count, q_each, rows), bf),
            pltpu.VMEM((count, q_each, rows), bf),
            pltpu.VMEM((q_each, group_rows), bf),
            pltpu.VMEM((HEAD_DIM, group_rows), bf),
            pltpu.VMEM((group_rows, HEAD_DIM), bf),
            pltpu.VMEM((group_rows, HEAD_DIM), bf),
            pltpu.VMEM((q_each, group_rows), f32),
            pltpu.VMEM((HEAD_DIM, group_rows), f32),
            pltpu.VMEM((HEAD_DIM, group_rows), f32),
            pltpu.VMEM((group_rows, each), bf),
            pltpu.VMEM(forwards.shape, bf),
            pltpu.VMEM((width, each), bf),
            pltpu.VMEM((data_count, depth, shard, width), bf),
            pltpu.VMEM((depth, shard, width), bf),
            pltpu.VMEM((2, 4, count * shard // 2, hidden), bf),
            pltpu.VMEM((2, HEAD_DIM, 2 * rows), f32),
            pltpu.VMEM((1, gain_width), f32),
            pltpu.VMEM((count, 1, gain_width), f32),
            pltpu.VMEM((data_count, 1, gain_width), f32),
            pltpu.VMEM((group_rows, 1), jnp.int32),
            pltpu.VMEM((1, group_rows), jnp.int32),
            pltpu.VMEM((1, group_rows), jnp.int32),
            pltpu.SemaphoreType.DMA((6,)),
            pltpu.SemaphoreType.DMA((8,)),
            pltpu.SemaphoreType.DMA((2,)),
            pltpu.SemaphoreType.DMA((depth,)),
            pltpu.SemaphoreType.DMA((depth,)),
            pltpu.SemaphoreType.DMA((count,)),
            pltpu.SemaphoreType.DMA((count,)),
            pltpu.SemaphoreType.DMA((data_count,)),
            pltpu.SemaphoreType.DMA((data_count,)),
        ]
        + Swap.scratch(count)
        + LineScatter.scratch(depth, rows, width) * 2
        + RingReduce.scratch(count * shard // 2, hidden) * 2
        + RingReduce.scratch(depth // 2, shard, width)
        + RingReduce.scratch(count * shard // 2, each)
        + Swap.scratch(count) * 3,
        compiler_params=pltpu.CompilerParams(
            collective_id=collective_id, has_side_effects=True, vmem_limit_bytes=63 * 2**20
        ),
        name="back",
    )(
        tokens,
        cotangent,
        residual,
        d_normed,
        gains,
        order,
        lengths,
        cosine,
        sine,
        log_total,
        normed,
        inputs,
        outputs,
        raw,
        flat,
        forwards,
        gateup_grad,
    )


def update_kernel(
    data_count,
    gateup_grad,
    input_grad,
    output_grad,
    down_grad,
    gains_grad,
    *refs,
):
    states, results = refs[:15], refs[15:30]
    scratch = refs[30]
    input_full = refs[31]
    context_count = gateup_grad.shape[1]
    piece = gateup_grad.shape[3] // data_count
    half = scratch.shape[1] // 2
    for side in range(2):
        for group in range(data_count):
            scratch[:, pl.ds(side * half + group * context_count * piece, context_count * piece)] = (
                jnp.concatenate(
                    [
                        gateup_grad[side, head, :, pl.ds(group * piece, piece)]
                        for head in range(context_count)
                    ],
                    axis=1,
                ).astype(jnp.float32)
            )
    q_each = HEADS // KV_HEADS * HEAD_DIM
    for start, size in ((0, q_each), (q_each, HEAD_DIM), (q_each + HEAD_DIM, HEAD_DIM)):
        input_full[:, pl.ds(start * context_count, size * context_count)] = jnp.concatenate(
            [input_grad[head, :, pl.ds(start, size)] for head in range(context_count)], axis=1
        ).astype(jnp.float32)
    jobs = (
        (input_full, rate_input, weight_decay),
        (output_grad, rate_output, weight_decay),
        (scratch, rate_gateup, weight_decay),
        (down_grad, rate_down, weight_decay),
        (gains_grad, rate_gains, 0.0),
    )
    for index, (gradient, rate, decay) in enumerate(jobs):
        weight, first, second = (state[...] for state in states[3 * index : 3 * index + 3])
        for result, value in zip(
            results[3 * index : 3 * index + 3],
            adam_update(weight, first, second, gradient[...], rate, decay),
        ):
            result[...] = value


def update(gateup_grad, input_grad, output_grad, down_grad, gains_grad, states, data_count):
    parts = 3

    def rows_of(array):
        axis = array.ndim - 2
        shape = list(array.shape)
        if shape[axis] > 1:
            shape[axis] //= parts
            return pl.BlockSpec(
                tuple(shape), lambda step: tuple(step if d == axis else 0 for d in range(len(shape)))
            )
        return pl.BlockSpec(tuple(shape), lambda step: (0,) * len(shape))

    arrays = [gateup_grad, input_grad, output_grad, down_grad, gains_grad] + list(states)
    shard = states[0].shape[0] // parts
    return pl.pallas_call(
        functools.partial(update_kernel, data_count),
        grid=(parts,),
        out_shape=[jax.ShapeDtypeStruct(state.shape, jnp.float32) for state in states],
        in_specs=[rows_of(array) for array in arrays],
        out_specs=[rows_of(state) for state in states],
        scratch_shapes=[
            pltpu.VMEM((shard, states[6].shape[1]), jnp.float32),
            pltpu.VMEM((shard, states[0].shape[1]), jnp.float32),
        ],
        compiler_params=pltpu.CompilerParams(vmem_limit_bytes=56 * 2**20),
        name="update",
    )(*arrays)


def on_device_split(
    tokens,
    output_cotangent,
    sequence_lengths,
    block_order,
    attn_input,
    input_moment,
    input_square,
    attn_output,
    output_moment,
    output_square,
    gate_up,
    gateup_moment,
    gateup_square,
    down_weight,
    down_moment,
    down_square,
    norm_gains,
    gains_moment,
    gains_square,
):
    context_count = lax.axis_size("cp")
    data_count = lax.axis_size("dp")
    model_width = tokens.shape[1]
    gains_row = norm_gains.reshape(1, -1)
    down_part = lax.all_gather(down_weight.astype(jnp.bfloat16), "dp", axis=0, tiled=True)
    (
        normed_one,
        own_two,
        cotangent_all,
        input_part,
        output_all,
        gateup_part,
        raw,
        flat_parts,
        log_total,
        residual,
        cosine,
        sine,
    ) = front(
        tokens,
        gains_row,
        block_order,
        sequence_lengths,
        attn_input,
        attn_output,
        gate_up,
        output_cotangent,
        data_count,
        context_count,
    )
    d_normed_two, forward_parts, grad_down, gateup_grad = middle(
        own_two,
        cotangent_all,
        gateup_part.reshape(2, model_width, -1),
        down_part,
        data_count,
        3,
    )
    mixed, token_gradient, grad_gains, grad_output, grad_input, grad_gateup = back(
        tokens,
        output_cotangent,
        residual,
        d_normed_two,
        gains_row,
        block_order,
        sequence_lengths,
        cosine,
        sine,
        log_total,
        normed_one,
        input_part,
        output_all,
        raw,
        flat_parts,
        forward_parts,
        gateup_grad,
        4,
    )
    states = (
        attn_input,
        input_moment,
        input_square,
        attn_output,
        output_moment,
        output_square,
        gate_up,
        gateup_moment,
        gateup_square,
        down_weight,
        down_moment,
        down_square,
        gains_row,
        gains_moment.reshape(1, -1),
        gains_square.reshape(1, -1),
    )
    results = update(
        grad_gateup, grad_input, grad_output, grad_down, grad_gains, states, data_count
    )
    return (
        mixed,
        token_gradient,
        *results[:12],
        *(result.reshape(-1) for result in results[12:]),
    )


def solution(mesh):
    in_specs = (
        P(("dp", "cp"), None),
        P(("dp", "cp"), None),
        P("dp", None),
        P("dp", None),
        P(("dp", "cp"), None),
        P(("dp", "cp"), None),
        P(("dp", "cp"), None),
        P(("dp", "cp"), None),
        P(("dp", "cp"), None),
        P(("dp", "cp"), None),
        P(("dp", "cp"), None),
        P(("dp", "cp"), None),
        P(("dp", "cp"), None),
        P(("dp", "cp"), None),
        P(("dp", "cp"), None),
        P(("dp", "cp"), None),
        P(),
        P(),
        P(),
    )
    out_specs = (
        P(("dp", "cp"), None),
        P(("dp", "cp"), None),
        P(("dp", "cp"), None),
        P(("dp", "cp"), None),
        P(("dp", "cp"), None),
        P(("dp", "cp"), None),
        P(("dp", "cp"), None),
        P(("dp", "cp"), None),
        P(("dp", "cp"), None),
        P(("dp", "cp"), None),
        P(("dp", "cp"), None),
        P(("dp", "cp"), None),
        P(("dp", "cp"), None),
        P(("dp", "cp"), None),
        P(),
        P(),
        P(),
    )
    sizes = (mesh.shape["dp"], mesh.shape["cp"])
    body = on_device_split if sizes == (4, KV_HEADS) else on_device
    return jax.shard_map(
        body, mesh=mesh, in_specs=in_specs, out_specs=out_specs, check_vma=False
    )
```

```python
import functools
import math

import jax
import jax.numpy as jnp
from jax import lax
from jax.experimental import pallas as pl
from jax.experimental.pallas import tpu as pltpu
from jax.sharding import PartitionSpec as P

HEADS = 24
KV_HEADS = 8
HEAD_DIM = 64
FF = 6912
STEP = 10


norm_eps = 1e-05
rope_base = 1000000.0
beta_one = 0.9
beta_two = 0.95
adam_eps = 1e-08
rate_input = 0.06
rate_output = 0.9
rate_gateup = 0.06
rate_down = 0.03
rate_gains = 0.5
weight_decay = 0.1
masked_score = -1e30


def rope_tables(offsets):
    half_dim = HEAD_DIM // 2
    freqs = jnp.exp(
        jnp.arange(half_dim, dtype=jnp.float32) * (-2.0 * math.log(rope_base) / HEAD_DIM)
    )
    angles = offsets.astype(jnp.float32)[:, None] * freqs[None, :]
    return (jnp.cos(angles), jnp.sin(angles))


def rotate(values, cosine, sine):
    half_dim = HEAD_DIM // 2
    first_half = values[..., :half_dim]
    second_half = values[..., half_dim:]
    cos_wide = cosine[:, None, :]
    sin_wide = sine[:, None, :]
    return jnp.concatenate(
        [
            first_half * cos_wide - second_half * sin_wide,
            second_half * cos_wide + first_half * sin_wide,
        ],
        axis=-1,
    )


def locate(positions, lengths):
    seq_ends = jnp.cumsum(lengths)
    starts = seq_ends - lengths
    doc_index = jnp.sum((positions[:, None] >= seq_ends[None, :]).astype(jnp.int32), axis=1)
    picked = (doc_index[:, None] == jnp.arange(lengths.shape[0], dtype=jnp.int32)[None, :]).astype(
        jnp.int32
    )
    return (doc_index, positions - jnp.sum(picked * starts[None, :], axis=1))


def rms_parts(values):
    inverse = lax.rsqrt(jnp.mean(values * values, axis=-1, keepdims=True) + norm_eps)
    return (values * inverse, inverse)


def norm_back(d_normed, normal_hat, inverse):
    return inverse * (
        d_normed - normal_hat * jnp.mean(d_normed * normal_hat, axis=-1, keepdims=True)
    )


def contract_rows(left, right):
    return lax.dot_general(
        left, right, (((0,), (0,)), ((), ())), preferred_element_type=jnp.float32
    )


def contract_cols(left, right):
    return lax.dot_general(
        left, right, (((1,), (1,)), ((), ())), preferred_element_type=jnp.float32
    )


def owner_order(values, data_count, context_count):
    lead = values.shape[0]
    each = values.shape[1] // (data_count * context_count)
    return (
        values.reshape(lead, data_count, context_count, each)
        .transpose(0, 2, 1, 3)
        .reshape(lead, values.shape[1])
    )


def adam_update(weight, first_moment, second_moment, gradient, rate, decay):
    first_moment = beta_one * first_moment + (1.0 - beta_one) * gradient
    second_moment = beta_two * second_moment + (1.0 - beta_two) * gradient * gradient
    first_fix = 1.0 - beta_one**STEP
    second_fix = 1.0 - beta_two**STEP
    direction = first_moment / first_fix / (jnp.sqrt(second_moment / second_fix) + adam_eps)
    return (weight - rate * (direction + decay * weight), first_moment, second_moment)


def on_device(
    tokens,
    output_cotangent,
    sequence_lengths,
    block_order,
    attn_input,
    input_moment,
    input_square,
    attn_output,
    output_moment,
    output_square,
    gate_up,
    gateup_moment,
    gateup_square,
    down_weight,
    down_moment,
    down_square,
    norm_gains,
    gains_moment,
    gains_square,
):
    row_count = tokens.shape[0]
    model_width = tokens.shape[1]
    q_width = HEADS * HEAD_DIM
    kv_width = KV_HEADS * HEAD_DIM
    proj_width = q_width + 2 * kv_width
    head_groups = HEADS // KV_HEADS
    score_scale = HEAD_DIM ** (-0.5)
    gain_one = norm_gains[:model_width]
    gain_two = norm_gains[model_width : 2 * model_width]
    gain_query = norm_gains[2 * model_width : 2 * model_width + HEAD_DIM]
    gain_key = norm_gains[2 * model_width + HEAD_DIM :]
    seq_lens = sequence_lengths[0]
    order_row = block_order[0]
    context_count = lax.axis_size("cp")
    data_count = lax.axis_size("dp")
    own_slot = lax.axis_index("cp")
    offsets = jnp.arange(row_count, dtype=jnp.int32)
    own_block = jnp.sum(
        jnp.where(jnp.arange(context_count, dtype=jnp.int32) == own_slot, order_row, 0)
    )
    positions = own_block * row_count + offsets
    key_positions = (order_row[:, None] * row_count + offsets[None, :]).reshape(
        context_count * row_count
    )
    doc_index, seq_offset = locate(positions, seq_lens)
    key_doc = locate(key_positions, seq_lens)[0]
    cosine, sine = rope_tables(seq_offset)
    input_bf = attn_input.astype(jnp.bfloat16)
    output_bf = attn_output.astype(jnp.bfloat16)
    gateup_bf = gate_up.astype(jnp.bfloat16)
    down_bf = down_weight.astype(jnp.bfloat16)
    input_all, output_all = (
        lax.all_gather(input_bf, ("dp", "cp"), axis=0, tiled=True),
        lax.all_gather(output_bf, ("dp", "cp"), axis=0, tiled=True),
    )
    x_float = tokens.astype(jnp.float32)
    hat_one, inv_one = rms_parts(x_float)
    normed_one = (hat_one * gain_one).astype(jnp.bfloat16)
    projected = jnp.dot(normed_one, input_all, preferred_element_type=jnp.float32)
    query_raw = projected[:, :q_width].reshape(row_count, HEADS, HEAD_DIM)
    key_raw = projected[:, q_width : q_width + kv_width].reshape(row_count, KV_HEADS, HEAD_DIM)
    value_raw = projected[:, q_width + kv_width :]
    hat_query, inv_query = rms_parts(query_raw)
    hat_key, inv_key = rms_parts(key_raw)
    queries = rotate(hat_query * gain_query, cosine, sine).astype(jnp.bfloat16)
    key_rot = rotate(hat_key * gain_key, cosine, sine)
    key_value = jnp.concatenate([key_rot.reshape(row_count, kv_width), value_raw], axis=1).astype(
        jnp.bfloat16
    )
    kv_all = lax.all_gather(key_value, "cp", axis=0, tiled=True)
    total_keys = kv_all.shape[0]
    key_span = min(512, total_keys)
    block_count = total_keys // key_span
    kv_blocks = kv_all.reshape(block_count, key_span, 2 * kv_width)
    pos_blocks = key_positions.reshape(block_count, key_span)
    doc_blocks = key_doc.reshape(block_count, key_span)
    query_group = queries.reshape(row_count, KV_HEADS, head_groups, HEAD_DIM)

    def block_scores(kv_block, key_pos, key_docs):
        key_block = kv_block[:, :kv_width].reshape(key_span, KV_HEADS, HEAD_DIM)
        value_block = kv_block[:, kv_width:].reshape(key_span, KV_HEADS, HEAD_DIM)
        scores = (
            jnp.einsum("qhgd,khd->hgqk", query_group, key_block, preferred_element_type=jnp.float32)
            * score_scale
        )
        allowed = (doc_index[:, None] == key_docs[None, :]) & (
            key_pos[None, :] <= positions[:, None]
        )
        return (key_block, value_block, jnp.where(allowed, scores, masked_score), allowed)

    def forward_block(carry, items):
        run_max, run_total, run_sum = carry
        key_block, value_block, scores, allowed = block_scores(*items)
        new_max = jnp.maximum(run_max, jnp.max(scores, axis=-1))
        weights = jnp.where(allowed, jnp.exp(scores - new_max[..., None]), 0.0)
        factor = jnp.exp(run_max - new_max)
        run_total = run_total * factor + jnp.sum(weights, axis=-1)
        run_sum = run_sum * factor[..., None] + jnp.einsum(
            "hgqk,khd->hgqd",
            weights.astype(jnp.bfloat16),
            value_block,
            preferred_element_type=jnp.float32,
        )
        return ((new_max, run_total, run_sum), None)

    start_state = (
        jnp.full((KV_HEADS, head_groups, row_count), masked_score, jnp.float32),
        jnp.zeros((KV_HEADS, head_groups, row_count), jnp.float32),
        jnp.zeros((KV_HEADS, head_groups, row_count, HEAD_DIM), jnp.float32),
    )
    (run_max, run_total, run_sum), unused = lax.scan(
        forward_block, start_state, (kv_blocks, pos_blocks, doc_blocks)
    )
    attended = run_sum / run_total[..., None]
    log_total = run_max + jnp.log(run_total)
    attn_flat = attended.transpose(2, 0, 1, 3).reshape(row_count, q_width).astype(jnp.bfloat16)
    residual = x_float + jnp.dot(attn_flat, output_all, preferred_element_type=jnp.float32)
    hat_two, inv_two = rms_parts(residual)
    normed_two = (hat_two * gain_two).astype(jnp.bfloat16)
    columns = normed_two
    gate_both = jnp.dot(
        columns,
        lax.all_gather(gateup_bf, ("dp", "cp"), axis=0, tiled=True),
        preferred_element_type=jnp.float32,
    )
    gate_part = gate_both[:, :FF]
    up_part = gate_both[:, FF:]
    gate_sig = jax.nn.sigmoid(gate_part)
    gate_act = gate_part * gate_sig
    hidden = (gate_act * up_part).astype(jnp.bfloat16)
    columns = hidden
    ff_result = jnp.dot(
        columns,
        lax.all_gather(down_bf, ("dp", "cp"), axis=0, tiled=True),
        preferred_element_type=jnp.float32,
    )
    mixed = (residual + ff_result).astype(jnp.bfloat16)
    d_hidden = contract_cols(
        output_cotangent, lax.all_gather(down_bf, ("dp", "cp"), axis=0, tiled=True)
    )
    d_gate = d_hidden * up_part * (gate_sig * (1.0 + gate_part * (1.0 - gate_sig)))
    d_up = d_hidden * gate_act
    d_gate_both = jnp.concatenate([d_gate, d_up], axis=1).astype(jnp.bfloat16)
    d_normed_two = contract_cols(
        d_gate_both, lax.all_gather(gateup_bf, ("dp", "cp"), axis=0, tiled=True)
    )
    grad_gain_two = jnp.sum(d_normed_two * hat_two, axis=0)
    d_residual = output_cotangent.astype(jnp.float32) + norm_back(
        d_normed_two * gain_two, hat_two, inv_two
    )
    d_branch = d_residual.astype(jnp.bfloat16)
    input_back, output_back = (input_all, output_all)
    d_flat = contract_cols(d_branch, output_back).astype(jnp.bfloat16)
    d_attended = d_flat.reshape(row_count, KV_HEADS, head_groups, HEAD_DIM).transpose(1, 2, 0, 3)
    delta = jnp.sum(d_attended.astype(jnp.float32) * attended, axis=-1)

    def backward_block(d_query_sum, items):
        key_block, value_block, scores, allowed = block_scores(*items)
        probs = jnp.where(allowed, jnp.exp(scores - log_total[..., None]), 0.0)
        d_probs = jnp.einsum(
            "hgqd,khd->hgqk", d_attended, value_block, preferred_element_type=jnp.float32
        )
        d_scores = (probs * (d_probs - delta[..., None])).astype(jnp.bfloat16)
        d_query_sum = (
            d_query_sum
            + jnp.einsum("hgqk,khd->hgqd", d_scores, key_block, preferred_element_type=jnp.float32)
            * score_scale
        )
        d_keys = (
            jnp.einsum("hgqk,qhgd->khd", d_scores, query_group, preferred_element_type=jnp.float32)
            * score_scale
        )
        d_values = jnp.einsum(
            "hgqk,hgqd->khd",
            probs.astype(jnp.bfloat16),
            d_attended,
            preferred_element_type=jnp.float32,
        )
        return (
            d_query_sum,
            jnp.concatenate(
                [d_keys.reshape(key_span, kv_width), d_values.reshape(key_span, kv_width)], axis=1
            ),
        )

    d_query_sum, d_kv_blocks = lax.scan(
        backward_block,
        jnp.zeros((KV_HEADS, head_groups, row_count, HEAD_DIM), jnp.float32),
        (kv_blocks, pos_blocks, doc_blocks),
    )
    d_kv = lax.psum_scatter(
        d_kv_blocks.reshape(total_keys, 2 * kv_width).astype(jnp.bfloat16),
        "cp",
        scatter_dimension=0,
        tiled=True,
    ).astype(jnp.float32)
    d_query_rot = rotate(
        d_query_sum.transpose(2, 0, 1, 3).reshape(row_count, HEADS, HEAD_DIM), cosine, -sine
    )
    grad_gain_query = jnp.sum(d_query_rot * hat_query, axis=(0, 1))
    d_query_raw = norm_back(d_query_rot * gain_query, hat_query, inv_query)
    d_key_rot = rotate(d_kv[:, :kv_width].reshape(row_count, KV_HEADS, HEAD_DIM), cosine, -sine)
    grad_gain_key = jnp.sum(d_key_rot * hat_key, axis=(0, 1))
    d_key_raw = norm_back(d_key_rot * gain_key, hat_key, inv_key)
    d_projected = jnp.concatenate(
        [
            d_query_raw.reshape(row_count, q_width),
            d_key_raw.reshape(row_count, kv_width),
            d_kv[:, kv_width:],
        ],
        axis=1,
    ).astype(jnp.bfloat16)
    d_normed_one = contract_cols(d_projected, input_back)
    grad_gain_one = jnp.sum(d_normed_one * hat_one, axis=0)
    token_gradient = d_residual + norm_back(d_normed_one * gain_one, hat_one, inv_one)

    def make_wide(first_src, attn_src, second_src):

        def wide_terms(row_start, row_total):
            return jnp.concatenate(
                [
                    contract_rows(first_src, d_projected),
                    contract_rows(attn_src, d_branch),
                    contract_rows(second_src, d_gate_both),
                ],
                axis=1,
            )

        return wide_terms

    def make_down(hidden_src):

        def down_terms(row_start, row_total):
            return contract_rows(hidden_src, output_cotangent)

        return down_terms

    shard_rows = attn_input.shape[0]
    down_rows = down_weight.shape[0]
    wide_fn = make_wide(
        owner_order(normed_one, data_count, context_count),
        owner_order(attn_flat, data_count, context_count),
        owner_order(normed_two, data_count, context_count),
    )
    down_fn = make_down(owner_order(hidden, data_count, context_count))
    group_wide = lax.psum_scatter(
        wide_fn(jnp.int32(0), lax.axis_size("cp") * (shard_rows * data_count)).astype(jnp.bfloat16),
        "cp",
        scatter_dimension=0,
        tiled=True,
    )
    group_down = lax.psum_scatter(
        down_fn(jnp.int32(0), lax.axis_size("cp") * (down_rows * data_count)).astype(jnp.bfloat16),
        "cp",
        scatter_dimension=0,
        tiled=True,
    )
    wide_grads, down_grads = (
        lax.psum_scatter(group_wide, "dp", scatter_dimension=0, tiled=True).astype(jnp.float32),
        lax.psum_scatter(group_down, "dp", scatter_dimension=0, tiled=True).astype(jnp.float32),
    )
    gain_grads = lax.psum(
        jnp.concatenate([grad_gain_one, grad_gain_two, grad_gain_query, grad_gain_key]),
        ("dp", "cp"),
    )
    grad_input = wide_grads[:, :proj_width]
    grad_output = wide_grads[:, proj_width : proj_width + model_width]
    grad_gateup = wide_grads[:, proj_width + model_width :]
    input_next, input_moment_next, input_square_next = adam_update(
        attn_input, input_moment, input_square, grad_input, rate_input, weight_decay
    )
    output_next, output_moment_next, output_square_next = adam_update(
        attn_output, output_moment, output_square, grad_output, rate_output, weight_decay
    )
    gateup_next, gateup_moment_next, gateup_square_next = adam_update(
        gate_up, gateup_moment, gateup_square, grad_gateup, rate_gateup, weight_decay
    )
    down_next, down_moment_next, down_square_next = adam_update(
        down_weight, down_moment, down_square, down_grads, rate_down, weight_decay
    )
    gains_next, gains_moment_next, gains_square_next = adam_update(
        norm_gains, gains_moment, gains_square, gain_grads, rate_gains, 0.0
    )
    return (
        mixed,
        token_gradient,
        input_next,
        input_moment_next,
        input_square_next,
        output_next,
        output_moment_next,
        output_square_next,
        gateup_next,
        gateup_moment_next,
        gateup_square_next,
        down_next,
        down_moment_next,
        down_square_next,
        gains_next,
        gains_moment_next,
        gains_square_next,
    )


MESH = pl.DeviceIdType.MESH


def place():
    dp = lax.axis_index("dp")
    cp = lax.axis_index("cp")
    return dp, cp, cp // 2, cp % 2


def greet(targets):
    barrier = pltpu.get_barrier_semaphore()
    for target in targets:
        pl.semaphore_signal(barrier, inc=1, device_id=target, device_id_type=MESH)
    pl.semaphore_wait(barrier, len(targets))


def send(source, target, send_sem, recv_sem, device):
    return pltpu.make_async_remote_copy(
        src_ref=source,
        dst_ref=target,
        send_sem=send_sem,
        recv_sem=recv_sem,
        device_id=device,
        device_id_type=MESH,
    )


class LineGather:
    def __init__(self, own_ref, all_ref, sems, where, depth, both=True):
        self.own, self.where, self.depth, self.both = own_ref, where, depth, both
        self.slot = all_ref if callable(all_ref) else lambda slot: all_ref.at[slot]
        self.right, self.left, self.sib, self.recv, self.local = sems

    @staticmethod
    def scratch(depth):
        return [pltpu.SemaphoreType.DMA((2 * depth,))] * 4 + [pltpu.SemaphoreType.DMA]

    def copy(self, kind, slot, source):
        dp, cp, z, core = self.where
        device = {"right": (dp, cp + 2), "left": (dp, cp - 2), "sib": (dp, cp ^ 1)}[kind]
        sem = {"right": self.right, "left": self.left, "sib": self.sib}[kind]
        return send(source, self.slot(slot), sem.at[slot], self.recv.at[slot], device)

    def keep(self):
        return pltpu.make_async_copy(self.own, self.slot(self.where[1]), self.local)

    def start(self):
        dp, cp, z, core = self.where

        @pl.when(z < self.depth - 1)
        def _():
            self.copy("right", cp, self.own).start()

        @pl.when(z > 0)
        def _():
            self.copy("left", cp, self.own).start()

        if self.both:
            self.copy("sib", cp, self.own).start()
        self.keep().start()

    def step(self, far):
        dp, cp, z, core = self.where

        @pl.when(z >= far)
        def _():
            slot = cp - 2 * far
            self.copy("right", slot, self.own).wait_recv()

            @pl.when(z < self.depth - 1)
            def _():
                self.copy("right", slot, self.slot(slot)).start()

            if self.both:
                self.copy("sib", slot, self.slot(slot)).start()

        @pl.when(z + far < self.depth)
        def _():
            slot = cp + 2 * far
            self.copy("left", slot, self.own).wait_recv()

            @pl.when(z > 0)
            def _():
                self.copy("left", slot, self.slot(slot)).start()

            if self.both:
                self.copy("sib", slot, self.slot(slot)).start()

    def arrive(self, spot):
        self.copy("sib", 1 - self.where[3] + 2 * spot, self.own).wait_recv()

    def finish(self, arrived=False):
        dp, cp, z, core = self.where
        if self.both and not arrived:
            for spot in range(self.depth):
                self.arrive(spot)
        if not arrived:
            self.keep().wait()
        for spot in range(self.depth):
            slot = 2 * spot + core
            if self.both:
                self.copy("sib", slot, self.own).wait_send()

            @pl.when((spot <= z) & (z < self.depth - 1))
            def _():
                self.copy("right", slot, self.own).wait_send()

            @pl.when((spot >= z) & (z > 0))
            def _():
                self.copy("left", slot, self.own).wait_send()


class Swap:
    def __init__(self, source_ref, target_ref, sems, where, count):
        self.source, self.where, self.count = source_ref, where, count
        self.slot = target_ref if callable(target_ref) else lambda slot: target_ref.at[slot]
        self.origin = source_ref if callable(source_ref) else lambda slot: source_ref.at[slot]
        self.sent, self.recv, self.local = sems

    @staticmethod
    def scratch(count):
        return [pltpu.SemaphoreType.DMA((count,))] * 2 + [pltpu.SemaphoreType.DMA]

    def copy(self, peer):
        dp, cp, z, core = self.where
        return send(
            self.origin(peer),
            self.slot(cp),
            self.sent.at[peer],
            self.recv.at[cp],
            (dp, peer),
        )

    def keep(self):
        cp = self.where[1]
        return pltpu.make_async_copy(self.origin(cp), self.slot(cp), self.local)

    def start(self):
        cp = self.where[1]
        for turn in range(self.count - 1, 0, -1):
            self.copy(cp ^ turn).start()
        self.keep().start()

    def arrive(self, peer):
        dp, cp, z, core = self.where
        send(
            self.origin(peer),
            self.slot(peer),
            self.sent.at[peer],
            self.recv.at[peer],
            (dp, peer),
        ).wait_recv()

    def finish_recv(self):
        cp = self.where[1]
        for turn in range(1, self.count):
            self.arrive(cp ^ turn)
        self.keep().wait()

    def finish_send(self):
        cp = self.where[1]
        for turn in range(1, self.count):
            self.copy(cp ^ turn).wait_send()


class RingSpread:
    def __init__(self, block, half, sems, where):
        self.block, self.half, self.where = block, half, where
        self.sent, self.recv = sems

    @staticmethod
    def scratch():
        return [pltpu.SemaphoreType.DMA((4,))] * 2

    def copy(self, kind, mine):
        dp, cp, z, core = self.where
        turn = (1, 2, 2, 1)[kind]
        if kind < 2:
            part = self.block(dp if mine else dp ^ turn)
        else:
            part = self.half(dp ^ (3 - turn) if mine else dp ^ 3, kind - 2)
        return send(part, part, self.sent.at[kind], self.recv.at[kind], (dp ^ turn, cp))

    def start(self):
        self.copy(0, True).start()
        self.copy(1, True).start()

    def forward(self):
        self.copy(0, False).wait_recv()
        self.copy(2, True).start()
        self.copy(1, False).wait_recv()
        self.copy(3, True).start()

    def finish(self):
        self.copy(2, False).wait_recv()
        self.copy(3, False).wait_recv()
        for kind in range(4):
            self.copy(kind, True).wait_send()


def turn_heads(values, cosine, sine):
    half = values.shape[0] // 2
    first, second = values[:half], values[half:]
    return jnp.concatenate([first * cosine - second * sine, second * cosine + first * sine], axis=0)


def head_hat(values):
    inverse = lax.rsqrt(jnp.mean(values * values, axis=0, keepdims=True) + norm_eps)
    return values * inverse, inverse


def lay_places(order_ref, lengths_ref, rows, count):
    spots = [order_ref[0, index] * rows for index in range(count)]
    lanes = lax.broadcasted_iota(jnp.int32, (1, rows), 1)
    lines = lax.broadcasted_iota(jnp.int32, (rows, 1), 0)
    place_row = jnp.concatenate([spot + lanes for spot in spots], axis=1)
    place_column = jnp.concatenate([spot + lines for spot in spots], axis=0)
    starts = jnp.zeros_like(place_row)
    begin = jnp.int32(0)
    for index in range(lengths_ref.shape[1] - 1):
        begin = begin + lengths_ref[0, index]
        starts = jnp.where(place_row >= begin, begin, starts)
    return place_row, place_column, starts


def to_column(row):
    size = row.shape[1]
    down = lax.broadcasted_iota(jnp.int32, (size, size), 0)
    across = lax.broadcasted_iota(jnp.int32, (size, size), 1)
    return jnp.sum(jnp.where(down == across, row, 0.0), axis=1, keepdims=True)


def split_gains(gains_ref, width):
    lines = width // gains_ref.shape[1]

    def row(begin, end):
        return jnp.concatenate([gains_ref[line : line + 1] for line in range(begin, end)], axis=1)

    gain_one, gain_two = row(0, lines), row(lines, 2 * lines)
    gain_heads = row(2 * lines, gains_ref.shape[0])
    gain_query = to_column(gain_heads[:, :HEAD_DIM])
    gain_key = to_column(gain_heads[:, HEAD_DIM:])
    return gain_one, gain_two, gain_query, gain_key


def score_block(keys, queries, key_place, query_place, query_start):
    scores = jnp.dot(keys, queries, preferred_element_type=jnp.float32) * HEAD_DIM ** (-0.5)
    allowed = (key_place <= query_place) & (key_place >= query_start)
    return jnp.where(allowed, scores, masked_score), allowed


class LineScatter:
    cuts = 2

    def __init__(self, part_ref, out_ref, scratch, where, depth):
        self.part, self.out, self.where, self.depth = part_ref, out_ref, where, depth
        self.sib, self.line = scratch[:2]
        (
            self.sib_sent,
            self.sib_recv,
            self.right_sent,
            self.right_recv,
            self.left_sent,
            self.left_recv,
        ) = scratch[2:]
        self.size = part_ref.shape[1] // self.cuts

    @classmethod
    def scratch(cls, depth, rows, width):
        return [
            pltpu.VMEM((depth, rows, width), jnp.bfloat16),
            pltpu.VMEM((depth + 1, rows, width), jnp.bfloat16),
        ] + [pltpu.SemaphoreType.DMA((depth,))] * 2 + [
            pltpu.SemaphoreType.DMA((depth * cls.cuts,))
        ] * 4

    def pair(self, spot):
        dp, cp, z, core = self.where
        return send(
            self.part.at[2 * spot + 1 - core],
            self.sib.at[spot],
            self.sib_sent.at[spot],
            self.sib_recv.at[spot],
            (dp, cp ^ 1),
        )

    def rows(self, cut):
        return pl.ds(cut * self.size, self.size)

    def hop_right(self, spot, cut):
        dp, cp, z, core = self.where
        index = spot * self.cuts + cut
        return send(
            self.part.at[2 * spot + core, self.rows(cut)],
            self.line.at[spot + 1, self.rows(cut)],
            self.right_sent.at[index],
            self.right_recv.at[index],
            (dp, cp + 2),
        )

    def hop_left(self, spot, cut):
        dp, cp, z, core = self.where
        index = spot * self.cuts + cut
        return send(
            self.part.at[2 * spot + core, self.rows(cut)],
            self.line.at[spot, self.rows(cut)],
            self.left_sent.at[index],
            self.left_recv.at[index],
            (dp, cp - 2),
        )

    def order(self):
        spots = []
        for turn in range(self.depth):
            spots += [self.depth - 1 - turn, turn]
        return list(dict.fromkeys(spots))

    def chip_sum(self, spot, cut):
        rows = self.rows(cut)
        mine = self.part[2 * spot + self.where[3], rows].astype(jnp.float32)
        return mine + self.sib[spot, rows].astype(jnp.float32)

    def pass_on(self, spot, cut, arrived, slot, hop):
        total = self.chip_sum(spot, cut)
        if arrived is not None:
            arrived.wait_recv()
            total = total + self.line[slot, self.rows(cut)].astype(jnp.float32)
        self.part[2 * spot + self.where[3], self.rows(cut)] = total.astype(jnp.bfloat16)
        hop.start()

    def forward(self, spot, cuts=None):
        z, core = self.where[2], self.where[3]
        cuts = range(self.cuts) if cuts is None else cuts
        if 0 in cuts:

            @pl.when(z != spot)
            def _():
                self.pair(spot).wait_recv()

        for cut in cuts:
            right, left = self.hop_right(spot, cut), self.hop_left(spot, cut)

            @pl.when((z < spot) & (z > 0))
            def _():
                self.pass_on(spot, cut, right, spot + 1, right)

            @pl.when((z < spot) & (z == 0))
            def _():
                self.pass_on(spot, cut, None, None, right)

            @pl.when((z > spot) & (z < self.depth - 1))
            def _():
                self.pass_on(spot, cut, left, spot, left)

            @pl.when((z > spot) & (z == self.depth - 1))
            def _():
                self.pass_on(spot, cut, None, None, left)

    def finish(self):
        z = self.where[2]
        self.pair(z).wait_recv()
        for cut in range(self.cuts):
            rows = self.rows(cut)
            self.out[rows] = self.chip_sum(z, cut)

            @pl.when(z > 0)
            def _():
                self.hop_right(z, cut).wait_recv()
                self.out[rows] += self.line[z + 1, rows].astype(jnp.float32)

            @pl.when(z < self.depth - 1)
            def _():
                self.hop_left(z, cut).wait_recv()
                self.out[rows] += self.line[z, rows].astype(jnp.float32)

        for spot in range(self.depth):
            self.pair(spot).wait_send()

            @pl.when(z < spot)
            def _():
                for cut in range(self.cuts):
                    self.hop_right(spot, cut).wait_send()

            @pl.when(z > spot)
            def _():
                for cut in range(self.cuts):
                    self.hop_left(spot, cut).wait_send()


class RingReduce:
    def __init__(self, part, work, scratch, where):
        self.part, self.work, self.where = part, work, where
        self.from_x, self.from_y, self.x_sent, self.x_recv, self.y_sent, self.y_recv = scratch

    @staticmethod
    def scratch(*half):
        return [pltpu.VMEM((3,) + half, jnp.bfloat16)] * 2 + [pltpu.SemaphoreType.DMA((3,))] * 4

    def to_x(self, kind):
        dp, cp, z, core = self.where
        source = (
            self.part(dp ^ 3, 0) if kind == 0 else self.part(dp ^ 1, 0) if kind == 1 else self.work(1)
        )
        return send(
            source, self.from_x.at[kind], self.x_sent.at[kind], self.x_recv.at[kind], (dp ^ 1, cp)
        )

    def to_y(self, kind):
        dp, cp, z, core = self.where
        source = (
            self.part(dp ^ 3, 1) if kind == 0 else self.part(dp ^ 2, 1) if kind == 1 else self.work(0)
        )
        return send(
            source, self.from_y.at[kind], self.y_sent.at[kind], self.y_recv.at[kind], (dp ^ 2, cp)
        )

    def start(self):
        for kind in range(2):
            self.to_x(kind).start()
            self.to_y(kind).start()

    def add(self, index, *arrived):
        target = self.work(index)
        total = target[...].astype(jnp.float32)
        for block in arrived:
            total = total + block[...].astype(jnp.float32)
        target[...] = total.astype(jnp.bfloat16)

    def middle(self):
        self.to_x(0).wait_recv()
        self.add(0, self.from_x.at[0])
        self.to_y(2).start()
        self.to_y(0).wait_recv()
        self.add(1, self.from_y.at[0])
        self.to_x(2).start()

    def finish(self):
        for kind in (1, 2):
            self.to_x(kind).wait_recv()
            self.to_y(kind).wait_recv()
        self.add(2, self.from_x.at[1], self.from_y.at[2])
        self.add(3, self.from_y.at[1], self.from_x.at[2])

    def finish_send(self):
        for kind in range(3):
            self.to_x(kind).wait_send()
            self.to_y(kind).wait_send()

    def places(self):
        dp = self.where[0]
        return [(dp ^ 2, 0), (dp ^ 1, 1), (dp, 0), (dp, 1)]


def far_first(turn, z, depth):
    order = []
    for spot in range(depth):
        rest = sorted((other for other in range(depth) if other != spot), key=lambda other: (-abs(other - spot), other))
        ends = [other for other in rest if other in (0, depth - 1)]
        order.append(ends + [other for other in rest if other not in ends] + [spot])
    picked = 0
    for step in range(depth):
        for spot in range(depth):
            picked = picked + order[spot][step] * ((turn == step) & (z == spot)).astype(jnp.int32)
    return picked


def near_first(turn, z, depth):
    picked = 0
    for step in range(depth):
        for spot in range(depth):
            order = sorted(range(depth), key=lambda other: (abs(other - spot), other))
            picked = picked + order[step] * ((turn == step) & (z == spot)).astype(jnp.int32)
    return picked


def fore_kernel(
    tile,
    tokens_ref,
    gains_ref,
    order_ref,
    lengths_ref,
    input_ref,
    output_ref,
    gateup_ref,
    down_ref,
    cotangent_own,
    normed_one_out,
    input_out,
    output_out,
    raw_out,
    flat_out,
    forward_out,
    gateup_out,
    total_out,
    residual_out,
    cosine_ref,
    sine_ref,
    d_normed_out,
    down_out,
    input_send,
    output_own,
    gate_send,
    up_send,
    key_place_ref,
    query_place_ref,
    query_start_ref,
    normed_one,
    own_one,
    inputs,
    outputs,
    raw,
    queries,
    keys_up,
    values,
    flat_send,
    flat_recv,
    own_two,
    normed,
    cotangent,
    gate_weight,
    up_weight,
    down_weight,
    hidden_up,
    d_gates,
    d_ups,
    down_grad,
    out_sems,
    *sems,
):
    where = place()
    dp, cp, z, core = where
    context_count = normed_one.shape[0]
    depth = context_count // 2
    rows = tokens_ref.shape[0]
    width = tokens_ref.shape[1]
    q_each = HEADS // KV_HEADS * HEAD_DIM
    take = iter(range(len(sems)))

    def some(count):
        return [sems[next(take)] for _ in range(count)]

    kv_each = HEAD_DIM
    for head in range(context_count):
        for start, begin, size in (
            (head * q_each, 0, q_each),
            (HEADS * HEAD_DIM + head * kv_each, q_each, kv_each),
            ((HEADS + KV_HEADS) * HEAD_DIM + head * kv_each, q_each + kv_each, kv_each),
        ):
            input_send[head, :, begin : begin + size] = input_ref[:, start : start + size].astype(
                jnp.bfloat16
            )
    hidden = gate_send.shape[2]
    piece = hidden // inputs.shape[0]
    half_width = gateup_ref.shape[1] // 2

    def cut_columns(target, base):
        for head in range(context_count):
            target[head] = jnp.concatenate(
                [
                    gateup_ref[:, pl.ds(base + (group * context_count + head) * piece, piece)]
                    for group in range(inputs.shape[0])
                ],
                axis=1,
            ).astype(jnp.bfloat16)

    cut_columns(gate_send, 0)
    greet([(dp, cp ^ turn) for turn in range(1, context_count)] + [(dp ^ 1, cp), (dp ^ 2, cp)])
    token_line = LineGather(own_one, normed_one, some(5), where, depth)
    second_line = LineGather(own_two, normed, some(5), where, depth)
    cotangent_line = LineGather(cotangent_own, cotangent, some(5), where, depth)
    output_line = LineGather(
        output_own, lambda slot: outputs.at[dp, slot // 2, core], some(5), where, depth, False
    )
    input_swap = Swap(input_send, inputs.at[dp], some(3), where, context_count)
    shard = input_send.shape[1]

    each_rows = context_count * shard

    def weight_slot(target):
        return lambda slot: target.at[
            pl.ds(pl.multiple_of(dp * each_rows + slot * shard, 16), shard)
        ]

    gate_swap = Swap(gate_send, weight_slot(gate_weight), some(3), where, context_count)
    up_swap = Swap(up_send, weight_slot(up_weight), some(3), where, context_count)
    flat_swap = Swap(flat_send, flat_recv, some(3), where, context_count)
    input_ring = RingSpread(
        lambda d: inputs.at[d],
        lambda d, h: inputs.at[d, pl.ds(h * (context_count // 2), context_count // 2)],
        some(2),
        where,
    )
    output_ring = RingSpread(
        lambda d: outputs.at[d, :, core],
        lambda d, h: outputs.at[d, pl.ds(h * (depth // 2), depth // 2), core],
        some(2),
        where,
    )
    half_rows = each_rows // 2

    def weight_ring(target):
        return RingSpread(
            lambda d: target.at[pl.ds(pl.multiple_of(d * each_rows, 16), each_rows)],
            lambda d, h: target.at[
                pl.ds(pl.multiple_of(d * each_rows + h * half_rows, 16), half_rows)
            ],
            some(2),
            where,
        )

    gate_ring, up_ring = weight_ring(gate_weight), weight_ring(up_weight)
    lane_half = width // 2

    def down_part(d, h):
        return down_grad.at[d, :, pl.ds(h * lane_half, lane_half)]

    down_spread = RingSpread(lambda d: down_grad.at[d], down_part, some(2), where)
    line = LineScatter(normed_one, d_normed_out, some(8), where, depth)

    def down_work(index):
        return down_part(*down_ring.places()[index])

    down_ring = RingReduce(down_part, down_work, some(6), where)
    at_end = (z == 0) | (z == depth - 1)
    share_sent, share_recv = some(2)

    def share(mine):
        part = outputs.at[:, :, core if mine else 1 - core]
        return send(part, part, share_sent, share_recv, (dp, cp ^ 1))

    input_swap.start()
    gate_swap.start()
    down_grad[dp] = down_ref[...].astype(jnp.bfloat16)
    down_spread.start()
    gain_one, gain_two, gain_query, gain_key = split_gains(gains_ref, width)
    hat_one, _ = rms_parts(tokens_ref[...].astype(jnp.float32))
    own_one[...] = (hat_one * gain_one).astype(jnp.bfloat16)
    output_own[...] = output_ref[...].astype(jnp.bfloat16)
    place_row, place_column, starts = lay_places(order_ref, lengths_ref, rows, context_count)
    query_place_ref[...] = place_row
    key_place_ref[...] = place_column
    query_start_ref[...] = starts
    pair_index = lax.broadcasted_iota(jnp.int32, (HEAD_DIM // 2, 1), 0).astype(jnp.float32)
    angles = (place_row - starts).astype(jnp.float32) * jnp.exp(
        pair_index * (-2.0 * math.log(rope_base) / HEAD_DIM)
    )
    cosine_ref[...] = jnp.cos(angles)
    sine_ref[...] = jnp.sin(angles)
    cut_columns(up_send, half_width)
    token_line.start()
    input_swap.finish_recv()
    input_ring.start()
    gate_swap.finish_recv()
    gate_ring.start()
    output_line.start()
    token_line.step(1)
    output_line.step(1)
    input_ring.forward()
    token_line.step(2)
    output_line.step(2)
    token_line.step(3)
    output_line.step(3)
    down_spread.forward()
    up_swap.start()
    output_line.finish()
    output_ring.start()
    token_line.finish()
    input_ring.finish()
    one_copy = pltpu.make_async_copy(normed_one, normed_one_out, out_sems.at[0])
    one_copy.start()
    input_copy = pltpu.make_async_copy(inputs, input_out, out_sems.at[1])
    input_copy.start()

    weights = inputs[...].reshape(width, inputs.shape[-1])

    def project(turn, carry):
        lanes = pl.ds(pl.multiple_of(turn * tile, tile), tile)
        block = normed_one[pl.ds(turn * (tile // rows), tile // rows)].reshape(tile, width)
        part = jnp.dot(block, weights, preferred_element_type=jnp.float32).T
        raw[:, lanes] = part
        cosine, sine = cosine_ref[:, lanes], sine_ref[:, lanes]
        for head in range(HEADS // KV_HEADS):
            hat, _ = head_hat(part[head * HEAD_DIM : (head + 1) * HEAD_DIM])
            queries[head * HEAD_DIM : (head + 1) * HEAD_DIM, lanes] = turn_heads(
                hat * gain_query, cosine, sine
            ).astype(jnp.bfloat16)
        hat, _ = head_hat(part[q_each : q_each + HEAD_DIM])
        key = turn_heads(hat * gain_key, cosine, sine)
        keys_up[pl.ds(pl.multiple_of(turn * tile, tile), tile)] = key.T.astype(jnp.bfloat16)
        values[:, lanes] = part[q_each + HEAD_DIM :].astype(jnp.bfloat16)
        return carry

    lax.fori_loop(0, normed_one.shape[0] * rows // tile, project, 0)
    raw_copy = pltpu.make_async_copy(raw, raw_out, out_sems.at[2])
    raw_copy.start()

    def attend(turn, carry):
        lanes = pl.ds(pl.multiple_of(turn * tile, tile), tile)
        query_place, query_start = query_place_ref[:, lanes], query_start_ref[:, lanes]

        @pl.when(turn == 1)
        def _():
            gate_ring.forward()
            cotangent_line.start()

        @pl.when(turn == 2)
        def _():
            output_ring.forward()

        @pl.when(turn == 3)
        def _():
            up_swap.finish_recv()
            up_ring.start()
            cotangent_line.step(1)

        for head in range(HEADS // KV_HEADS):
            spot = pl.ds(head * HEAD_DIM, HEAD_DIM)
            scores, allowed = score_block(
                keys_up[...], queries[spot, lanes], key_place_ref[...], query_place, query_start
            )
            top = jnp.max(scores, axis=0, keepdims=True)
            exps = jnp.exp(scores - top)
            total = jnp.sum(exps, axis=0, keepdims=True)
            total_out[pl.ds(head, 1), lanes] = top + jnp.log(total)
            probs = (exps * (1.0 / total)).astype(jnp.bfloat16)
            attended = jnp.dot(values[...], probs, preferred_element_type=jnp.float32)
            for part in range(tile // rows):
                flat_send[turn * (tile // rows) + part, spot] = attended[
                    :, part * rows : (part + 1) * rows
                ].astype(jnp.bfloat16)
        return carry

    lax.fori_loop(0, depth, attend, 0)
    flat_swap.start()
    output_ring.finish()
    share(True).start()
    cotangent_line.step(2)
    share(False).wait_recv()
    output_copy = pltpu.make_async_copy(outputs, output_out, out_sems.at[3])
    output_copy.start()
    flat_swap.finish_recv()
    flat_copy = pltpu.make_async_copy(flat_recv, flat_out, out_sems.at[4])
    flat_copy.start()
    flat = flat_recv[...].reshape(HEADS * HEAD_DIM, rows).astype(jnp.float32).T.astype(jnp.bfloat16)
    residual = tokens_ref[...].astype(jnp.float32) + jnp.dot(
        flat, outputs[...].reshape(HEADS * HEAD_DIM, width), preferred_element_type=jnp.float32
    )
    residual_out[...] = residual
    hat_two, _ = rms_parts(residual)
    own_two[...] = (hat_two * gain_two).astype(jnp.bfloat16)
    second_line.start()
    down_spread.finish()

    def lay_down(step, carry):
        lanes = pl.ds(pl.multiple_of(step * tile, tile), tile)
        down_weight[:, lanes] = (
            down_grad[:, :, lanes]
            .astype(jnp.float32)
            .reshape(down_weight.shape[0], tile)
            .astype(jnp.bfloat16)
        )
        return carry

    lax.fori_loop(0, width // tile, lay_down, 0)
    up_ring.forward()
    cotangent_line.step(3)
    gate_ring.finish()
    cotangent_line.finish()
    up_ring.finish()
    one_copy.wait()
    group_rows = context_count * rows
    parts = normed_one

    def feed(turn, carry):
        spot = near_first(turn, z, depth)
        far = jnp.abs(spot - z)

        @pl.when((turn > 0) & (far != jnp.abs(near_first(turn - 1, z, depth) - z)))
        def _():
            second_line.step(far)

        @pl.when(turn == 0)
        def _():
            second_line.keep().wait()

        second_line.arrive(spot)
        pair = pl.ds(2 * spot, 2)
        lanes = pl.ds(pl.multiple_of(spot * tile, tile), tile)
        block = normed[pair].reshape(tile, width)
        gate = jnp.dot(block, gate_weight[...], preferred_element_type=jnp.float32)
        up = jnp.dot(block, up_weight[...], preferred_element_type=jnp.float32)
        sig = 1.0 / (1.0 + jnp.exp(-gate))
        act = gate * sig
        hidden_up[:, lanes] = (act * up).T.astype(jnp.bfloat16)
        d_hidden = contract_cols(cotangent[pair].reshape(tile, width), down_weight[...])
        d_gate = (d_hidden * up * (sig * (1.0 + gate * (1.0 - sig)))).astype(jnp.bfloat16)
        d_up = (d_hidden * act).astype(jnp.bfloat16)
        d_gates[lanes] = d_gate
        d_ups[lanes] = d_up
        part = contract_cols(d_gate, gate_weight[...]) + contract_cols(d_up, up_weight[...])
        parts[pair] = part.astype(jnp.bfloat16).reshape(2, rows, width)
        line.pair(spot).start()

        @pl.when(at_end & (turn > 0))
        def _():
            line.forward(spot)

        return carry

    lax.fori_loop(0, depth, feed, 0)
    chunk = 256
    inner = depth - 1 - z
    outer = [inner, (depth - 1) * (z // 2 == 0).astype(jnp.int32), (depth - 1) * (z // 2 == 1).astype(jnp.int32)]

    def relay(index):
        @pl.when(jnp.logical_not(at_end))
        def _():
            line.forward(outer[index])

    def down_step(step, carry):
        lanes = pl.ds(pl.multiple_of(step * chunk, chunk), chunk)
        right = cotangent[:, :, lanes].reshape(group_rows, chunk)
        down_grad[:, :, lanes] = (
            jnp.dot(hidden_up[...], right, preferred_element_type=jnp.float32)
            .reshape(down_grad.shape[:2] + (chunk,))
            .astype(jnp.bfloat16)
        )
        return carry

    lax.fori_loop(0, width // chunk, down_step, 0)
    down_ring.start()
    relay(0)

    def gateup_step(step, carry):
        lanes = pl.ds(pl.multiple_of(step * chunk, chunk), chunk)
        left = normed[:, :, lanes].reshape(group_rows, chunk)
        gate_weight[lanes] = contract_rows(left, d_gates[...]).astype(jnp.bfloat16)
        up_weight[lanes] = contract_rows(left, d_ups[...]).astype(jnp.bfloat16)
        return carry

    steps = width // chunk
    lax.fori_loop(0, steps // 2, gateup_step, 0)
    relay(1)
    lax.fori_loop(steps // 2, steps, gateup_step, 0)
    relay(2)
    saves = [
        pltpu.make_async_copy(gate_weight, gateup_out.at[0], out_sems.at[0]),
        pltpu.make_async_copy(up_weight, gateup_out.at[1], out_sems.at[5]),
    ]
    for save in saves:
        save.start()
    down_ring.middle()

    second_line.finish(True)

    def forward_step(step, carry):
        lanes = pl.ds(pl.multiple_of(step * tile, tile), tile)
        normed[pl.ds(2 * step, 2)] = (
            contract_rows(hidden_up[:, lanes], down_weight[...])
            .astype(jnp.bfloat16)
            .reshape(2, rows, width)
        )
        return carry

    lax.fori_loop(0, depth, forward_step, 0)
    saves.append(pltpu.make_async_copy(normed, forward_out, out_sems.at[6]))
    saves[2].start()
    line.finish()
    down_ring.finish()
    for half in range(2):
        down_out[:, pl.ds(half * lane_half, lane_half)] = down_grad[
            dp, :, pl.ds(half * lane_half, lane_half)
        ].astype(jnp.float32)
    down_ring.finish_send()
    share(True).wait_send()
    for swap in (input_swap, gate_swap, up_swap, flat_swap):
        swap.finish_send()
    for copy in (input_copy, raw_copy, output_copy, flat_copy, *saves):
        copy.wait()


def fore(
    tokens,
    gains,
    order,
    lengths,
    attn_input,
    attn_output,
    gate_up,
    down,
    cotangent,
    data_count,
    context_count,
):
    rows, width = tokens.shape
    depth = context_count // 2
    group_rows = rows * context_count
    shard = attn_input.shape[0]
    each = attn_input.shape[1] // context_count
    hidden = gate_up.shape[1] // 2 // context_count
    q_each = HEADS // KV_HEADS * HEAD_DIM
    flat_width = HEADS * HEAD_DIM
    bf = jnp.bfloat16
    any_space = pl.BlockSpec(memory_space=pl.ANY)
    in_vmem = pl.BlockSpec(memory_space=pltpu.VMEM)
    in_smem = pl.BlockSpec(memory_space=pltpu.SMEM)
    down_rows = down.shape[0]
    shapes = [
        ((context_count, rows, width), bf, any_space),
        ((data_count, context_count, shard, each), bf, any_space),
        ((data_count, depth, 2, shard, width), bf, any_space),
        ((each, group_rows), jnp.float32, any_space),
        ((context_count, q_each, rows), bf, any_space),
        ((context_count, rows, width), bf, any_space),
        ((2, width, hidden), bf, any_space),
        ((HEADS // KV_HEADS, group_rows), jnp.float32, in_vmem),
        ((rows, width), jnp.float32, in_vmem),
        ((HEAD_DIM // 2, group_rows), jnp.float32, in_vmem),
        ((HEAD_DIM // 2, group_rows), jnp.float32, in_vmem),
        ((rows, width), jnp.float32, in_vmem),
        ((down_rows, width), jnp.float32, in_vmem),
    ]
    return pl.pallas_call(
        functools.partial(fore_kernel, 2 * rows),
        out_shape=[jax.ShapeDtypeStruct(shape, kind) for shape, kind, _ in shapes],
        in_specs=[in_vmem] * 2 + [in_smem] * 2 + [in_vmem] * 4 + [any_space],
        out_specs=[space for _, _, space in shapes],
        scratch_shapes=[
            pltpu.VMEM((context_count, shard, each), bf),
            pltpu.VMEM((shard, width), bf),
            pltpu.VMEM((context_count, shard, hidden), bf),
            pltpu.VMEM((context_count, shard, hidden), bf),
            pltpu.VMEM((group_rows, 1), jnp.int32),
            pltpu.VMEM((1, group_rows), jnp.int32),
            pltpu.VMEM((1, group_rows), jnp.int32),
            pltpu.VMEM((context_count, rows, width), bf),
            pltpu.VMEM((rows, width), bf),
            pltpu.VMEM((data_count, context_count, shard, each), bf),
            pltpu.VMEM((data_count, depth, 2, shard, width), bf),
            pltpu.VMEM((each, group_rows), jnp.float32),
            pltpu.VMEM((q_each, group_rows), bf),
            pltpu.VMEM((group_rows, HEAD_DIM), bf),
            pltpu.VMEM((HEAD_DIM, group_rows), bf),
            pltpu.VMEM((context_count, q_each, rows), bf),
            pltpu.VMEM((context_count, q_each, rows), bf),
            pltpu.VMEM((rows, width), bf),
            pltpu.VMEM((context_count, rows, width), bf),
            pltpu.VMEM((context_count, rows, width), bf),
            pltpu.VMEM((width, hidden), bf),
            pltpu.VMEM((width, hidden), bf),
            pltpu.VMEM((hidden, width), bf),
            pltpu.VMEM((hidden, group_rows), bf),
            pltpu.VMEM((group_rows, hidden), bf),
            pltpu.VMEM((group_rows, hidden), bf),
            pltpu.VMEM((data_count, down_rows, width), bf),
            pltpu.SemaphoreType.DMA((7,)),
        ]
        + LineGather.scratch(depth) * 4
        + Swap.scratch(context_count) * 4
        + RingSpread.scratch() * 5
        + LineScatter.scratch(depth, rows, width)
        + RingReduce.scratch(down_rows, width // 2)
        + [pltpu.SemaphoreType.DMA] * 2,
        compiler_params=pltpu.CompilerParams(
            collective_id=0, has_side_effects=True, vmem_limit_bytes=63 * 2**20
        ),
        name="fore",
    )(tokens, gains, order, lengths, attn_input, attn_output, gate_up, down, cotangent)


def back_kernel(
    tokens_ref,
    cotangent_ref,
    residual_ref,
    d_normed_ref,
    gains_ref,
    order_ref,
    lengths_ref,
    cosine_ref,
    sine_ref,
    total_ref,
    normed_in,
    input_in,
    output_in,
    raw_in,
    flat_in,
    forward_in,
    gateup_in,
    mixed_out,
    token_out,
    gains_out,
    output_grad_out,
    input_grad_out,
    gateup_grad_out,
    inputs,
    outputs,
    raw,
    flat,
    forwards,
    forward_sum,
    d_first,
    d_residual,
    branch,
    swap_send,
    swap_recv,
    queries,
    keys,
    keys_up,
    values_up,
    d_query,
    d_key,
    d_value,
    d_projected,
    parts,
    input_grad,
    output_sib,
    output_line,
    gateup_work,
    gain_sums,
    own_gains,
    line_gains,
    all_gains,
    key_place_ref,
    query_place_ref,
    query_start_ref,
    load_sems,
    work_sems,
    share_sems,
    output_sent,
    output_recv,
    line_sent,
    line_recv,
    all_sent,
    all_recv,
    *scratch,
):
    where = place()
    dp, cp, z, core = where
    count, rows, width = forwards.shape
    depth = count // 2
    data_count = all_gains.shape[0]
    shard = inputs.shape[2]
    tile = 2 * rows
    group_rows = count * rows
    heads = HEADS // KV_HEADS
    q_each = heads * HEAD_DIM
    flat_width = HEADS * HEAD_DIM
    score_scale = HEAD_DIM ** (-0.5)
    load_pairs = [
        (output_in, outputs),
        (raw_in, raw),
        (forward_in, forwards),
        (flat_in, flat),
        (normed_in, forwards),
        (input_in, inputs),
    ]
    loads = [
        pltpu.make_async_copy(source, target, load_sems.at[index])
        for index, (source, target) in enumerate(load_pairs)
    ]
    for index in (0, 1, 2, 3, 5):
        loads[index].start()
    greet(
        [(dp, cp ^ turn) for turn in range(1, count)]
        + [(dp ^ turn, cp) for turn in range(1, data_count)]
    )
    swap = Swap(swap_send, swap_recv, scratch[:3], where, count)
    take = iter(scratch[3:])

    def some(amount):
        return [next(take) for _ in range(amount)]

    forward_line = LineScatter(forwards, forward_sum, some(8), where, depth)
    first_line = LineScatter(parts, d_first, some(8), where, depth)
    gateup_rows = data_count * count * shard // data_count

    def in_place(part):
        spots = [(dp ^ 2, 0), (dp ^ 1, 1), (dp, 0), (dp, 1)]
        return lambda index: part(*spots[index])

    gateup_half = gateup_rows // 2

    def gateup_part(index):
        return lambda d, h: gateup_in.at[
            index, pl.ds(pl.multiple_of(d * gateup_rows + h * gateup_half, 16), gateup_half)
        ]

    def gateup_ring(index):
        return RingReduce(
            gateup_part(index), lambda spot: gateup_work.at[index, spot], some(6), where
        )

    def gateup_own(index):
        each = gateup_half // shard
        return lambda slot: gateup_work.at[
            index, 2 + slot // each, pl.ds(pl.multiple_of(slot % each * shard, 16), shard)
        ]

    def output_part(d, h):
        return outputs.at[d, pl.ds(h * (depth // 2), depth // 2), core]

    def input_part(d, h):
        half = gateup_rows // 2
        return input_grad.at[pl.ds(pl.multiple_of(d * gateup_rows + h * half, 16), half)]

    gate_ring, up_ring = gateup_ring(0), gateup_ring(1)
    output_ring = RingReduce(output_part, in_place(output_part), some(6), where)
    input_ring = RingReduce(input_part, in_place(input_part), some(6), where)

    def own_shard(source):
        return lambda slot: source.at[pl.ds(pl.multiple_of(slot * shard, 16), shard)]

    gate_swap = Swap(gateup_own(0), gateup_grad_out.at[0], some(3), where, count)
    up_swap = Swap(gateup_own(1), gateup_grad_out.at[1], some(3), where, count)
    own_rows = input_grad.at[pl.ds(pl.multiple_of(dp * gateup_rows, 16), gateup_rows)]
    input_swap = Swap(own_shard(own_rows), input_grad_out, some(3), where, count)
    works = [
        pltpu.make_async_copy(ring.part(*spot), ring.work(index), work_sems.at[4 * turn + index])
        for turn, ring in enumerate((gate_ring, up_ring))
        for index, spot in enumerate(ring.places())
    ]
    gate_ring.start()
    for work in works:
        work.start()

    def share(mine):
        return send(
            outputs.at[:, :, 1 - core], output_sib, share_sems.at[0], share_sems.at[1], (dp, cp ^ 1)
        )

    def output_hop(far, mine):
        return send(
            outputs.at[dp, z ^ far, core],
            output_line.at[z if mine else z ^ far],
            output_sent.at[far],
            output_recv.at[far],
            (dp, cp ^ (2 * far)),
        )

    at_end = (z == 0) | (z == depth - 1)
    chunk = 256

    gain_one, gain_two, gain_query, gain_key = split_gains(gains_ref, width)
    hat_two, inv_two = rms_parts(residual_ref[...])
    d_normed = d_normed_ref[...]
    own_gains[:, pl.ds(width, width)] = jnp.sum(d_normed * hat_two, axis=0, keepdims=True)
    d_res = cotangent_ref[...].astype(jnp.float32) + norm_back(
        d_normed * gain_two, hat_two, inv_two
    )
    d_residual[...] = d_res
    branch[...] = d_res.astype(jnp.bfloat16)
    loads[0].wait()
    swap_send[...] = (
        contract_cols(outputs[...].reshape(flat_width, width), branch[...])
        .astype(jnp.bfloat16)
        .reshape(count, q_each, rows)
    )
    swap.start()
    loads[2].wait()
    for spot in forward_line.order():
        forward_line.pair(spot).start()
    loads[1].wait()

    def prepare(turn, carry):
        lanes = pl.ds(pl.multiple_of(turn * tile, tile), tile)
        cosine, sine = cosine_ref[:, lanes], sine_ref[:, lanes]
        for head in range(heads):
            spot = pl.ds(head * HEAD_DIM, HEAD_DIM)
            hat, _ = head_hat(raw[spot, lanes])
            queries[spot, lanes] = turn_heads(hat * gain_query, cosine, sine).astype(
                jnp.bfloat16
            )
        hat, _ = head_hat(raw[pl.ds(q_each, HEAD_DIM), lanes])
        key = turn_heads(hat * gain_key, cosine, sine)
        keys[:, lanes] = key.astype(jnp.bfloat16)
        keys_up[lanes] = key.T.astype(jnp.bfloat16)
        values_up[lanes] = raw[pl.ds(q_each + HEAD_DIM, HEAD_DIM), lanes].T.astype(jnp.bfloat16)
        return carry

    lax.fori_loop(0, depth, prepare, 0)
    place_row, place_column, starts = lay_places(order_ref, lengths_ref, rows, count)
    query_place_ref[...] = place_row
    key_place_ref[...] = place_column
    query_start_ref[...] = starts
    d_key[...] = jnp.zeros_like(d_key)
    d_value[...] = jnp.zeros_like(d_value)
    gain_sums[...] = jnp.zeros_like(gain_sums)

    @pl.when(at_end)
    def _():
        for turn in range(depth - 1):
            forward_line.forward(far_first(turn, z, depth))

    loads[3].wait()

    def output_step(step, carry):
        lanes = pl.ds(pl.multiple_of(step * chunk, chunk), chunk)
        outputs[:, :, :, :, lanes] = (
            jnp.dot(
                flat[...].reshape(flat_width, rows),
                branch[:, lanes],
                preferred_element_type=jnp.float32,
            )
            .astype(jnp.bfloat16)
            .reshape(outputs.shape[:4] + (chunk,))
        )
        return carry

    lax.fori_loop(0, width // chunk, output_step, 0)
    share(True).start()
    for work in works:
        work.wait()
    gate_ring.middle()
    up_ring.start()
    swap.finish_recv()

    def attend(turn, carry):
        lanes = pl.ds(pl.multiple_of(turn * tile, tile), tile)
        query_place, query_start = query_place_ref[:, lanes], query_start_ref[:, lanes]

        @pl.when(jnp.logical_not(at_end) & (turn >= 1))
        def _():
            forward_line.forward(far_first(turn - 1, z, depth))

        @pl.when(turn == 1)
        def _():
            gate_ring.finish()
            gate_swap.start()

        @pl.when(turn == 3)
        def _():
            up_ring.middle()

        for head in range(heads):
            spot = pl.ds(head * HEAD_DIM, HEAD_DIM)
            scores, allowed = score_block(
                keys_up[...], queries[spot, lanes], key_place_ref[...], query_place, query_start
            )
            probs = jnp.where(allowed, jnp.exp(scores - total_ref[pl.ds(head, 1), lanes]), 0.0)
            d_out = jnp.concatenate(
                [swap_recv[2 * turn, spot], swap_recv[2 * turn + 1, spot]], axis=1
            )
            d_probs = jnp.dot(values_up[...], d_out, preferred_element_type=jnp.float32)
            delta = jnp.sum(probs * d_probs, axis=0, keepdims=True)
            d_scores = (probs * (d_probs - delta)).astype(jnp.bfloat16)
            d_query[spot, lanes] = (
                jnp.dot(keys[...], d_scores, preferred_element_type=jnp.float32) * score_scale
            )
            d_key[...] += contract_cols(queries[spot, lanes], d_scores) * score_scale
            d_value[...] += contract_cols(d_out, probs.astype(jnp.bfloat16))
        return carry

    lax.fori_loop(0, depth, attend, 0)
    loads[5].wait()
    share(False).wait_recv()

    def share_step(step, carry):
        total = outputs[step, :, core].astype(jnp.float32) + output_sib[step].astype(jnp.float32)
        outputs[step, :, core] = total.astype(jnp.bfloat16)
        return carry

    lax.fori_loop(0, data_count, share_step, 0)
    output_ring.start()

    def feed(turn, carry):
        spot = far_first(turn, z, depth)
        lanes = pl.ds(pl.multiple_of(spot * tile, tile), tile)
        cosine, sine = cosine_ref[:, lanes], sine_ref[:, lanes]
        pieces = []
        for head in range(heads + 1):
            place_in = pl.ds(head * HEAD_DIM, HEAD_DIM)
            hat, inverse = head_hat(raw[place_in, lanes])
            if head < heads:
                turned = turn_heads(d_query[place_in, lanes], cosine, -sine)
                gain, kind = gain_query, 0
            else:
                turned = turn_heads(d_key[:, lanes], cosine, -sine)
                gain, kind = gain_key, 1
            gain_sums[kind] += turned * hat
            scaled = turned * gain
            pieces.append(
                inverse * (scaled - hat * jnp.mean(scaled * hat, axis=0, keepdims=True))
            )
        pieces.append(d_value[:, lanes])
        block = jnp.concatenate(pieces, axis=0).T.astype(jnp.bfloat16)
        d_projected[lanes] = block
        part = contract_cols(block, inputs[...].reshape(width, block.shape[1]))
        parts[pl.ds(2 * spot, 2)] = part.astype(jnp.bfloat16).reshape(2, rows, width)
        first_line.pair(spot).start()

        @pl.when(at_end & (turn < depth - 1))
        def _():
            first_line.forward(spot)

        return carry

    lax.fori_loop(0, depth, feed, 0)
    up_ring.finish()
    up_swap.start()
    forward_line.finish()
    loads[4].start()
    mixed_out[...] = (residual_ref[...] + forward_sum[...]).astype(jnp.bfloat16)
    for kind in range(2):
        own_gains[:, pl.ds(2 * width + kind * HEAD_DIM, HEAD_DIM)] = jnp.sum(
            gain_sums[kind].T, axis=0, keepdims=True
        )
    @pl.when(jnp.logical_not(at_end))
    def _():
        first_line.forward(far_first(0, z, depth))

    loads[4].wait()

    def input_step(step, carry):
        lanes = pl.ds(pl.multiple_of(step * chunk, chunk), chunk)
        left = forwards[:, :, lanes].reshape(group_rows, chunk)
        input_grad[lanes] = contract_rows(left, d_projected[...]).astype(jnp.bfloat16)
        return carry

    lax.fori_loop(0, width // chunk, input_step, 0)
    input_ring.start()
    output_ring.middle()

    @pl.when(jnp.logical_not(at_end))
    def _():
        first_line.forward(far_first(1, z, depth))

    input_ring.middle()

    @pl.when(jnp.logical_not(at_end))
    def _():
        first_line.forward(far_first(2, z, depth))

    output_ring.finish()
    for far in range(depth - 1, 0, -1):
        output_hop(far, True).start()
    input_ring.finish()
    input_swap.start()
    first_line.finish()
    hat_one, inv_one = rms_parts(tokens_ref[...].astype(jnp.float32))
    d_one = d_first[...]
    own_gains[:, pl.ds(0, width)] = jnp.sum(d_one * hat_one, axis=0, keepdims=True)
    line_gains[cp] = own_gains[...]
    for turn in range(1, count):
        send(
            own_gains, line_gains.at[cp], line_sent.at[turn], line_recv.at[turn], (dp, cp ^ turn)
        ).start()
    token_out[...] = d_residual[...] + norm_back(d_one * gain_one, hat_one, inv_one)
    for turn in range(1, count):
        copy = send(
            own_gains,
            line_gains.at[cp ^ turn],
            line_sent.at[turn],
            line_recv.at[turn],
            (dp, cp ^ turn),
        )
        copy.wait_recv()
        copy.wait_send()
    all_gains[dp] = jnp.sum(line_gains[...], axis=0)
    for turn in range(1, data_count):
        send(
            all_gains.at[dp],
            all_gains.at[dp],
            all_sent.at[turn],
            all_recv.at[turn],
            (dp ^ turn, cp),
        ).start()
    for turn in range(1, data_count):
        copy = send(
            all_gains.at[dp],
            all_gains.at[dp ^ turn],
            all_sent.at[turn],
            all_recv.at[turn],
            (dp ^ turn, cp),
        )
        copy.wait_recv()
        copy.wait_send()
    gain_total = jnp.sum(all_gains[...], axis=0)
    lanes = gains_out.shape[1]
    for line in range(gains_out.shape[0]):
        gains_out[line : line + 1] = gain_total[:, line * lanes : (line + 1) * lanes]
    total = outputs[dp, z, core].astype(jnp.float32)
    for far in range(1, depth):
        output_hop(far, False).wait_recv()
        total = total + output_line[z ^ far].astype(jnp.float32)
    output_grad_out[...] = total
    for done in (input_swap, gate_swap, up_swap):
        done.finish_recv()
    for done in (swap, input_swap, gate_swap, up_swap, gate_ring, up_ring, output_ring, input_ring):
        done.finish_send()
    for far in range(1, depth):
        output_hop(far, True).wait_send()
    share(True).wait_send()


def back(
    tokens,
    cotangent,
    residual,
    d_normed,
    gains,
    order,
    lengths,
    cosine,
    sine,
    log_total,
    normed,
    inputs,
    outputs,
    raw,
    flat,
    forwards,
    gateup_grad,
    collective_id,
):
    count, rows, width = normed.shape
    depth = count // 2
    data_count = inputs.shape[0]
    shard, each = inputs.shape[2:]
    hidden = gateup_grad.shape[2]
    group_rows = count * rows
    heads = HEADS // KV_HEADS
    q_each = heads * HEAD_DIM
    flat_width = HEADS * HEAD_DIM
    gain_width = 2 * width + 2 * HEAD_DIM
    bf = jnp.bfloat16
    f32 = jnp.float32
    any_space = pl.BlockSpec(memory_space=pl.ANY)
    in_vmem = pl.BlockSpec(memory_space=pltpu.VMEM)
    in_smem = pl.BlockSpec(memory_space=pltpu.SMEM)
    return pl.pallas_call(
        back_kernel,
        out_shape=[
            jax.ShapeDtypeStruct((rows, width), bf),
            jax.ShapeDtypeStruct((rows, width), f32),
            jax.ShapeDtypeStruct(gains.shape, f32),
            jax.ShapeDtypeStruct((shard, width), f32),
            jax.ShapeDtypeStruct((count, shard, each), bf),
            jax.ShapeDtypeStruct((2, count, shard, hidden), bf),
        ],
        in_specs=[in_vmem] * 5 + [in_smem] * 2 + [in_vmem] * 3 + [any_space] * 7,
        out_specs=[in_vmem] * 4 + [any_space] * 2,
        scratch_shapes=[
            pltpu.VMEM(inputs.shape, bf),
            pltpu.VMEM(outputs.shape, bf),
            pltpu.VMEM(raw.shape, f32),
            pltpu.VMEM(flat.shape, bf),
            pltpu.VMEM(forwards.shape, bf),
            pltpu.VMEM((rows, width), f32),
            pltpu.VMEM((rows, width), f32),
            pltpu.VMEM((rows, width), f32),
            pltpu.VMEM((rows, width), bf),
            pltpu.VMEM((count, q_each, rows), bf),
            pltpu.VMEM((count, q_each, rows), bf),
            pltpu.VMEM((q_each, group_rows), bf),
            pltpu.VMEM((HEAD_DIM, group_rows), bf),
            pltpu.VMEM((group_rows, HEAD_DIM), bf),
            pltpu.VMEM((group_rows, HEAD_DIM), bf),
            pltpu.VMEM((q_each, group_rows), f32),
            pltpu.VMEM((HEAD_DIM, group_rows), f32),
            pltpu.VMEM((HEAD_DIM, group_rows), f32),
            pltpu.VMEM((group_rows, each), bf),
            pltpu.VMEM(forwards.shape, bf),
            pltpu.VMEM((width, each), bf),
            pltpu.VMEM((data_count, depth, shard, width), bf),
            pltpu.VMEM((depth, shard, width), bf),
            pltpu.VMEM((2, 4, count * shard // 2, hidden), bf),
            pltpu.VMEM((2, HEAD_DIM, 2 * rows), f32),
            pltpu.VMEM((1, gain_width), f32),
            pltpu.VMEM((count, 1, gain_width), f32),
            pltpu.VMEM((data_count, 1, gain_width), f32),
            pltpu.VMEM((group_rows, 1), jnp.int32),
            pltpu.VMEM((1, group_rows), jnp.int32),
            pltpu.VMEM((1, group_rows), jnp.int32),
            pltpu.SemaphoreType.DMA((6,)),
            pltpu.SemaphoreType.DMA((8,)),
            pltpu.SemaphoreType.DMA((2,)),
            pltpu.SemaphoreType.DMA((depth,)),
            pltpu.SemaphoreType.DMA((depth,)),
            pltpu.SemaphoreType.DMA((count,)),
            pltpu.SemaphoreType.DMA((count,)),
            pltpu.SemaphoreType.DMA((data_count,)),
            pltpu.SemaphoreType.DMA((data_count,)),
        ]
        + Swap.scratch(count)
        + LineScatter.scratch(depth, rows, width) * 2
        + RingReduce.scratch(count * shard // 2, hidden) * 2
        + RingReduce.scratch(depth // 2, shard, width)
        + RingReduce.scratch(count * shard // 2, each)
        + Swap.scratch(count) * 3,
        compiler_params=pltpu.CompilerParams(
            collective_id=collective_id, has_side_effects=True, vmem_limit_bytes=63 * 2**20
        ),
        name="back",
    )(
        tokens,
        cotangent,
        residual,
        d_normed,
        gains,
        order,
        lengths,
        cosine,
        sine,
        log_total,
        normed,
        inputs,
        outputs,
        raw,
        flat,
        forwards,
        gateup_grad,
    )


def update_kernel(
    data_count,
    gateup_grad,
    input_grad,
    output_grad,
    down_grad,
    gains_grad,
    *refs,
):
    states, results = refs[:15], refs[15:30]
    scratch = refs[30]
    input_full = refs[31]
    context_count = gateup_grad.shape[1]
    piece = gateup_grad.shape[3] // data_count
    half = scratch.shape[1] // 2
    for side in range(2):
        for group in range(data_count):
            scratch[:, pl.ds(side * half + group * context_count * piece, context_count * piece)] = (
                jnp.concatenate(
                    [
                        gateup_grad[side, head, :, pl.ds(group * piece, piece)]
                        for head in range(context_count)
                    ],
                    axis=1,
                ).astype(jnp.float32)
            )
    q_each = HEADS // KV_HEADS * HEAD_DIM
    for start, size in ((0, q_each), (q_each, HEAD_DIM), (q_each + HEAD_DIM, HEAD_DIM)):
        input_full[:, pl.ds(start * context_count, size * context_count)] = jnp.concatenate(
            [input_grad[head, :, pl.ds(start, size)] for head in range(context_count)], axis=1
        ).astype(jnp.float32)
    jobs = (
        (input_full, rate_input, weight_decay),
        (output_grad, rate_output, weight_decay),
        (scratch, rate_gateup, weight_decay),
        (down_grad, rate_down, weight_decay),
        (gains_grad, rate_gains, 0.0),
    )
    for index, (gradient, rate, decay) in enumerate(jobs):
        weight, first, second = (state[...] for state in states[3 * index : 3 * index + 3])
        for result, value in zip(
            results[3 * index : 3 * index + 3],
            adam_update(weight, first, second, gradient[...], rate, decay),
        ):
            result[...] = value


def update(gateup_grad, input_grad, output_grad, down_grad, gains_grad, states, data_count):
    parts = 3

    def rows_of(array):
        axis = array.ndim - 2
        shape = list(array.shape)
        if shape[axis] % (8 * parts) == 0:
            shape[axis] //= parts
            return pl.BlockSpec(
                tuple(shape), lambda step: tuple(step if d == axis else 0 for d in range(len(shape)))
            )
        return pl.BlockSpec(tuple(shape), lambda step: (0,) * len(shape))

    arrays = [gateup_grad, input_grad, output_grad, down_grad, gains_grad] + list(states)
    shard = states[0].shape[0] // parts
    return pl.pallas_call(
        functools.partial(update_kernel, data_count),
        grid=(parts,),
        out_shape=[jax.ShapeDtypeStruct(state.shape, jnp.float32) for state in states],
        in_specs=[rows_of(array) for array in arrays],
        out_specs=[rows_of(state) for state in states],
        scratch_shapes=[
            pltpu.VMEM((shard, states[6].shape[1]), jnp.float32),
            pltpu.VMEM((shard, states[0].shape[1]), jnp.float32),
        ],
        compiler_params=pltpu.CompilerParams(vmem_limit_bytes=56 * 2**20),
        name="update",
    )(*arrays)


def on_device_split(
    tokens,
    output_cotangent,
    sequence_lengths,
    block_order,
    attn_input,
    input_moment,
    input_square,
    attn_output,
    output_moment,
    output_square,
    gate_up,
    gateup_moment,
    gateup_square,
    down_weight,
    down_moment,
    down_square,
    norm_gains,
    gains_moment,
    gains_square,
):
    context_count = lax.axis_size("cp")
    data_count = lax.axis_size("dp")
    gain_lines = norm_gains.reshape(-1, 2 * HEAD_DIM)
    (
        normed_one,
        input_part,
        output_all,
        raw,
        flat_parts,
        forward_parts,
        gateup_grad,
        log_total,
        residual,
        cosine,
        sine,
        d_normed_two,
        grad_down,
    ) = fore(
        tokens,
        gain_lines,
        block_order,
        sequence_lengths,
        attn_input,
        attn_output,
        gate_up,
        down_weight,
        output_cotangent,
        data_count,
        context_count,
    )
    mixed, token_gradient, grad_gains, grad_output, grad_input, grad_gateup = back(
        tokens,
        output_cotangent,
        residual,
        d_normed_two,
        gain_lines,
        block_order,
        sequence_lengths,
        cosine,
        sine,
        log_total,
        normed_one,
        input_part,
        output_all,
        raw,
        flat_parts,
        forward_parts,
        gateup_grad,
        4,
    )
    states = (
        attn_input,
        input_moment,
        input_square,
        attn_output,
        output_moment,
        output_square,
        gate_up,
        gateup_moment,
        gateup_square,
        down_weight,
        down_moment,
        down_square,
        gain_lines,
        gains_moment.reshape(gain_lines.shape),
        gains_square.reshape(gain_lines.shape),
    )
    results = update(
        grad_gateup, grad_input, grad_output, grad_down, grad_gains, states, data_count
    )
    return (
        mixed,
        token_gradient,
        *results[:12],
        *(result.reshape(-1) for result in results[12:]),
    )


def solution(mesh):
    in_specs = (
        P(("dp", "cp"), None),
        P(("dp", "cp"), None),
        P("dp", None),
        P("dp", None),
        P(("dp", "cp"), None),
        P(("dp", "cp"), None),
        P(("dp", "cp"), None),
        P(("dp", "cp"), None),
        P(("dp", "cp"), None),
        P(("dp", "cp"), None),
        P(("dp", "cp"), None),
        P(("dp", "cp"), None),
        P(("dp", "cp"), None),
        P(("dp", "cp"), None),
        P(("dp", "cp"), None),
        P(("dp", "cp"), None),
        P(),
        P(),
        P(),
    )
    out_specs = (
        P(("dp", "cp"), None),
        P(("dp", "cp"), None),
        P(("dp", "cp"), None),
        P(("dp", "cp"), None),
        P(("dp", "cp"), None),
        P(("dp", "cp"), None),
        P(("dp", "cp"), None),
        P(("dp", "cp"), None),
        P(("dp", "cp"), None),
        P(("dp", "cp"), None),
        P(("dp", "cp"), None),
        P(("dp", "cp"), None),
        P(("dp", "cp"), None),
        P(("dp", "cp"), None),
        P(),
        P(),
        P(),
    )
    sizes = (mesh.shape["dp"], mesh.shape["cp"])
    body = on_device_split if sizes == (4, KV_HEADS) else on_device
    return jax.shard_map(
        body, mesh=mesh, in_specs=in_specs, out_specs=out_specs, check_vma=False
    )
```

```python
import functools
import math

import jax
import jax.numpy as jnp
from jax import lax
from jax.experimental import pallas as pl
from jax.experimental.pallas import tpu as pltpu
from jax.sharding import PartitionSpec as P

HEADS = 24
KV_HEADS = 8
HEAD_DIM = 64
FF = 6912
STEP = 10


norm_eps = 1e-05
rope_base = 1000000.0
beta_one = 0.9
beta_two = 0.95
adam_eps = 1e-08
rate_input = 0.06
rate_output = 0.9
rate_gateup = 0.06
rate_down = 0.03
rate_gains = 0.5
weight_decay = 0.1
masked_score = -1e30


def rope_tables(offsets):
    half_dim = HEAD_DIM // 2
    freqs = jnp.exp(
        jnp.arange(half_dim, dtype=jnp.float32) * (-2.0 * math.log(rope_base) / HEAD_DIM)
    )
    angles = offsets.astype(jnp.float32)[:, None] * freqs[None, :]
    return (jnp.cos(angles), jnp.sin(angles))


def rotate(values, cosine, sine):
    half_dim = HEAD_DIM // 2
    first_half = values[..., :half_dim]
    second_half = values[..., half_dim:]
    cos_wide = cosine[:, None, :]
    sin_wide = sine[:, None, :]
    return jnp.concatenate(
        [
            first_half * cos_wide - second_half * sin_wide,
            second_half * cos_wide + first_half * sin_wide,
        ],
        axis=-1,
    )


def locate(positions, lengths):
    seq_ends = jnp.cumsum(lengths)
    starts = seq_ends - lengths
    doc_index = jnp.sum((positions[:, None] >= seq_ends[None, :]).astype(jnp.int32), axis=1)
    picked = (doc_index[:, None] == jnp.arange(lengths.shape[0], dtype=jnp.int32)[None, :]).astype(
        jnp.int32
    )
    return (doc_index, positions - jnp.sum(picked * starts[None, :], axis=1))


def rms_parts(values):
    inverse = lax.rsqrt(jnp.mean(values * values, axis=-1, keepdims=True) + norm_eps)
    return (values * inverse, inverse)


def norm_back(d_normed, normal_hat, inverse):
    return inverse * (
        d_normed - normal_hat * jnp.mean(d_normed * normal_hat, axis=-1, keepdims=True)
    )


def contract_rows(left, right):
    return lax.dot_general(
        left, right, (((0,), (0,)), ((), ())), preferred_element_type=jnp.float32
    )


def contract_cols(left, right):
    return lax.dot_general(
        left, right, (((1,), (1,)), ((), ())), preferred_element_type=jnp.float32
    )


def owner_order(values, data_count, context_count):
    lead = values.shape[0]
    each = values.shape[1] // (data_count * context_count)
    return (
        values.reshape(lead, data_count, context_count, each)
        .transpose(0, 2, 1, 3)
        .reshape(lead, values.shape[1])
    )


def adam_update(weight, first_moment, second_moment, gradient, rate, decay):
    first_moment = beta_one * first_moment + (1.0 - beta_one) * gradient
    second_moment = beta_two * second_moment + (1.0 - beta_two) * gradient * gradient
    first_fix = 1.0 - beta_one**STEP
    second_fix = 1.0 - beta_two**STEP
    direction = first_moment / first_fix / (jnp.sqrt(second_moment / second_fix) + adam_eps)
    return (weight - rate * (direction + decay * weight), first_moment, second_moment)


def on_device(
    tokens,
    output_cotangent,
    sequence_lengths,
    block_order,
    attn_input,
    input_moment,
    input_square,
    attn_output,
    output_moment,
    output_square,
    gate_up,
    gateup_moment,
    gateup_square,
    down_weight,
    down_moment,
    down_square,
    norm_gains,
    gains_moment,
    gains_square,
):
    row_count = tokens.shape[0]
    model_width = tokens.shape[1]
    q_width = HEADS * HEAD_DIM
    kv_width = KV_HEADS * HEAD_DIM
    proj_width = q_width + 2 * kv_width
    head_groups = HEADS // KV_HEADS
    score_scale = HEAD_DIM ** (-0.5)
    gain_one = norm_gains[:model_width]
    gain_two = norm_gains[model_width : 2 * model_width]
    gain_query = norm_gains[2 * model_width : 2 * model_width + HEAD_DIM]
    gain_key = norm_gains[2 * model_width + HEAD_DIM :]
    seq_lens = sequence_lengths[0]
    order_row = block_order[0]
    context_count = lax.axis_size("cp")
    data_count = lax.axis_size("dp")
    own_slot = lax.axis_index("cp")
    offsets = jnp.arange(row_count, dtype=jnp.int32)
    own_block = jnp.sum(
        jnp.where(jnp.arange(context_count, dtype=jnp.int32) == own_slot, order_row, 0)
    )
    positions = own_block * row_count + offsets
    key_positions = (order_row[:, None] * row_count + offsets[None, :]).reshape(
        context_count * row_count
    )
    doc_index, seq_offset = locate(positions, seq_lens)
    key_doc = locate(key_positions, seq_lens)[0]
    cosine, sine = rope_tables(seq_offset)
    input_bf = attn_input.astype(jnp.bfloat16)
    output_bf = attn_output.astype(jnp.bfloat16)
    gateup_bf = gate_up.astype(jnp.bfloat16)
    down_bf = down_weight.astype(jnp.bfloat16)
    input_all, output_all = (
        lax.all_gather(input_bf, ("dp", "cp"), axis=0, tiled=True),
        lax.all_gather(output_bf, ("dp", "cp"), axis=0, tiled=True),
    )
    x_float = tokens.astype(jnp.float32)
    hat_one, inv_one = rms_parts(x_float)
    normed_one = (hat_one * gain_one).astype(jnp.bfloat16)
    projected = jnp.dot(normed_one, input_all, preferred_element_type=jnp.float32)
    query_raw = projected[:, :q_width].reshape(row_count, HEADS, HEAD_DIM)
    key_raw = projected[:, q_width : q_width + kv_width].reshape(row_count, KV_HEADS, HEAD_DIM)
    value_raw = projected[:, q_width + kv_width :]
    hat_query, inv_query = rms_parts(query_raw)
    hat_key, inv_key = rms_parts(key_raw)
    queries = rotate(hat_query * gain_query, cosine, sine).astype(jnp.bfloat16)
    key_rot = rotate(hat_key * gain_key, cosine, sine)
    key_value = jnp.concatenate([key_rot.reshape(row_count, kv_width), value_raw], axis=1).astype(
        jnp.bfloat16
    )
    kv_all = lax.all_gather(key_value, "cp", axis=0, tiled=True)
    total_keys = kv_all.shape[0]
    key_span = min(512, total_keys)
    block_count = total_keys // key_span
    kv_blocks = kv_all.reshape(block_count, key_span, 2 * kv_width)
    pos_blocks = key_positions.reshape(block_count, key_span)
    doc_blocks = key_doc.reshape(block_count, key_span)
    query_group = queries.reshape(row_count, KV_HEADS, head_groups, HEAD_DIM)

    def block_scores(kv_block, key_pos, key_docs):
        key_block = kv_block[:, :kv_width].reshape(key_span, KV_HEADS, HEAD_DIM)
        value_block = kv_block[:, kv_width:].reshape(key_span, KV_HEADS, HEAD_DIM)
        scores = (
            jnp.einsum("qhgd,khd->hgqk", query_group, key_block, preferred_element_type=jnp.float32)
            * score_scale
        )
        allowed = (doc_index[:, None] == key_docs[None, :]) & (
            key_pos[None, :] <= positions[:, None]
        )
        return (key_block, value_block, jnp.where(allowed, scores, masked_score), allowed)

    def forward_block(carry, items):
        run_max, run_total, run_sum = carry
        key_block, value_block, scores, allowed = block_scores(*items)
        new_max = jnp.maximum(run_max, jnp.max(scores, axis=-1))
        weights = jnp.where(allowed, jnp.exp(scores - new_max[..., None]), 0.0)
        factor = jnp.exp(run_max - new_max)
        run_total = run_total * factor + jnp.sum(weights, axis=-1)
        run_sum = run_sum * factor[..., None] + jnp.einsum(
            "hgqk,khd->hgqd",
            weights.astype(jnp.bfloat16),
            value_block,
            preferred_element_type=jnp.float32,
        )
        return ((new_max, run_total, run_sum), None)

    start_state = (
        jnp.full((KV_HEADS, head_groups, row_count), masked_score, jnp.float32),
        jnp.zeros((KV_HEADS, head_groups, row_count), jnp.float32),
        jnp.zeros((KV_HEADS, head_groups, row_count, HEAD_DIM), jnp.float32),
    )
    (run_max, run_total, run_sum), unused = lax.scan(
        forward_block, start_state, (kv_blocks, pos_blocks, doc_blocks)
    )
    attended = run_sum / run_total[..., None]
    log_total = run_max + jnp.log(run_total)
    attn_flat = attended.transpose(2, 0, 1, 3).reshape(row_count, q_width).astype(jnp.bfloat16)
    residual = x_float + jnp.dot(attn_flat, output_all, preferred_element_type=jnp.float32)
    hat_two, inv_two = rms_parts(residual)
    normed_two = (hat_two * gain_two).astype(jnp.bfloat16)
    columns = normed_two
    gate_both = jnp.dot(
        columns,
        lax.all_gather(gateup_bf, ("dp", "cp"), axis=0, tiled=True),
        preferred_element_type=jnp.float32,
    )
    gate_part = gate_both[:, :FF]
    up_part = gate_both[:, FF:]
    gate_sig = jax.nn.sigmoid(gate_part)
    gate_act = gate_part * gate_sig
    hidden = (gate_act * up_part).astype(jnp.bfloat16)
    columns = hidden
    ff_result = jnp.dot(
        columns,
        lax.all_gather(down_bf, ("dp", "cp"), axis=0, tiled=True),
        preferred_element_type=jnp.float32,
    )
    mixed = (residual + ff_result).astype(jnp.bfloat16)
    d_hidden = contract_cols(
        output_cotangent, lax.all_gather(down_bf, ("dp", "cp"), axis=0, tiled=True)
    )
    d_gate = d_hidden * up_part * (gate_sig * (1.0 + gate_part * (1.0 - gate_sig)))
    d_up = d_hidden * gate_act
    d_gate_both = jnp.concatenate([d_gate, d_up], axis=1).astype(jnp.bfloat16)
    d_normed_two = contract_cols(
        d_gate_both, lax.all_gather(gateup_bf, ("dp", "cp"), axis=0, tiled=True)
    )
    grad_gain_two = jnp.sum(d_normed_two * hat_two, axis=0)
    d_residual = output_cotangent.astype(jnp.float32) + norm_back(
        d_normed_two * gain_two, hat_two, inv_two
    )
    d_branch = d_residual.astype(jnp.bfloat16)
    input_back, output_back = (input_all, output_all)
    d_flat = contract_cols(d_branch, output_back).astype(jnp.bfloat16)
    d_attended = d_flat.reshape(row_count, KV_HEADS, head_groups, HEAD_DIM).transpose(1, 2, 0, 3)
    delta = jnp.sum(d_attended.astype(jnp.float32) * attended, axis=-1)

    def backward_block(d_query_sum, items):
        key_block, value_block, scores, allowed = block_scores(*items)
        probs = jnp.where(allowed, jnp.exp(scores - log_total[..., None]), 0.0)
        d_probs = jnp.einsum(
            "hgqd,khd->hgqk", d_attended, value_block, preferred_element_type=jnp.float32
        )
        d_scores = (probs * (d_probs - delta[..., None])).astype(jnp.bfloat16)
        d_query_sum = (
            d_query_sum
            + jnp.einsum("hgqk,khd->hgqd", d_scores, key_block, preferred_element_type=jnp.float32)
            * score_scale
        )
        d_keys = (
            jnp.einsum("hgqk,qhgd->khd", d_scores, query_group, preferred_element_type=jnp.float32)
            * score_scale
        )
        d_values = jnp.einsum(
            "hgqk,hgqd->khd",
            probs.astype(jnp.bfloat16),
            d_attended,
            preferred_element_type=jnp.float32,
        )
        return (
            d_query_sum,
            jnp.concatenate(
                [d_keys.reshape(key_span, kv_width), d_values.reshape(key_span, kv_width)], axis=1
            ),
        )

    d_query_sum, d_kv_blocks = lax.scan(
        backward_block,
        jnp.zeros((KV_HEADS, head_groups, row_count, HEAD_DIM), jnp.float32),
        (kv_blocks, pos_blocks, doc_blocks),
    )
    d_kv = lax.psum_scatter(
        d_kv_blocks.reshape(total_keys, 2 * kv_width).astype(jnp.bfloat16),
        "cp",
        scatter_dimension=0,
        tiled=True,
    ).astype(jnp.float32)
    d_query_rot = rotate(
        d_query_sum.transpose(2, 0, 1, 3).reshape(row_count, HEADS, HEAD_DIM), cosine, -sine
    )
    grad_gain_query = jnp.sum(d_query_rot * hat_query, axis=(0, 1))
    d_query_raw = norm_back(d_query_rot * gain_query, hat_query, inv_query)
    d_key_rot = rotate(d_kv[:, :kv_width].reshape(row_count, KV_HEADS, HEAD_DIM), cosine, -sine)
    grad_gain_key = jnp.sum(d_key_rot * hat_key, axis=(0, 1))
    d_key_raw = norm_back(d_key_rot * gain_key, hat_key, inv_key)
    d_projected = jnp.concatenate(
        [
            d_query_raw.reshape(row_count, q_width),
            d_key_raw.reshape(row_count, kv_width),
            d_kv[:, kv_width:],
        ],
        axis=1,
    ).astype(jnp.bfloat16)
    d_normed_one = contract_cols(d_projected, input_back)
    grad_gain_one = jnp.sum(d_normed_one * hat_one, axis=0)
    token_gradient = d_residual + norm_back(d_normed_one * gain_one, hat_one, inv_one)

    def make_wide(first_src, attn_src, second_src):

        def wide_terms(row_start, row_total):
            return jnp.concatenate(
                [
                    contract_rows(first_src, d_projected),
                    contract_rows(attn_src, d_branch),
                    contract_rows(second_src, d_gate_both),
                ],
                axis=1,
            )

        return wide_terms

    def make_down(hidden_src):

        def down_terms(row_start, row_total):
            return contract_rows(hidden_src, output_cotangent)

        return down_terms

    shard_rows = attn_input.shape[0]
    down_rows = down_weight.shape[0]
    wide_fn = make_wide(
        owner_order(normed_one, data_count, context_count),
        owner_order(attn_flat, data_count, context_count),
        owner_order(normed_two, data_count, context_count),
    )
    down_fn = make_down(owner_order(hidden, data_count, context_count))
    group_wide = lax.psum_scatter(
        wide_fn(jnp.int32(0), lax.axis_size("cp") * (shard_rows * data_count)).astype(jnp.bfloat16),
        "cp",
        scatter_dimension=0,
        tiled=True,
    )
    group_down = lax.psum_scatter(
        down_fn(jnp.int32(0), lax.axis_size("cp") * (down_rows * data_count)).astype(jnp.bfloat16),
        "cp",
        scatter_dimension=0,
        tiled=True,
    )
    wide_grads, down_grads = (
        lax.psum_scatter(group_wide, "dp", scatter_dimension=0, tiled=True).astype(jnp.float32),
        lax.psum_scatter(group_down, "dp", scatter_dimension=0, tiled=True).astype(jnp.float32),
    )
    gain_grads = lax.psum(
        jnp.concatenate([grad_gain_one, grad_gain_two, grad_gain_query, grad_gain_key]),
        ("dp", "cp"),
    )
    grad_input = wide_grads[:, :proj_width]
    grad_output = wide_grads[:, proj_width : proj_width + model_width]
    grad_gateup = wide_grads[:, proj_width + model_width :]
    input_next, input_moment_next, input_square_next = adam_update(
        attn_input, input_moment, input_square, grad_input, rate_input, weight_decay
    )
    output_next, output_moment_next, output_square_next = adam_update(
        attn_output, output_moment, output_square, grad_output, rate_output, weight_decay
    )
    gateup_next, gateup_moment_next, gateup_square_next = adam_update(
        gate_up, gateup_moment, gateup_square, grad_gateup, rate_gateup, weight_decay
    )
    down_next, down_moment_next, down_square_next = adam_update(
        down_weight, down_moment, down_square, down_grads, rate_down, weight_decay
    )
    gains_next, gains_moment_next, gains_square_next = adam_update(
        norm_gains, gains_moment, gains_square, gain_grads, rate_gains, 0.0
    )
    return (
        mixed,
        token_gradient,
        input_next,
        input_moment_next,
        input_square_next,
        output_next,
        output_moment_next,
        output_square_next,
        gateup_next,
        gateup_moment_next,
        gateup_square_next,
        down_next,
        down_moment_next,
        down_square_next,
        gains_next,
        gains_moment_next,
        gains_square_next,
    )


MESH = pl.DeviceIdType.MESH


def place():
    dp = lax.axis_index("dp")
    cp = lax.axis_index("cp")
    return dp, cp, cp // 2, cp % 2


def greet(targets):
    barrier = pltpu.get_barrier_semaphore()
    for target in targets:
        pl.semaphore_signal(barrier, inc=1, device_id=target, device_id_type=MESH)
    pl.semaphore_wait(barrier, len(targets))


def send(source, target, send_sem, recv_sem, device):
    return pltpu.make_async_remote_copy(
        src_ref=source,
        dst_ref=target,
        send_sem=send_sem,
        recv_sem=recv_sem,
        device_id=device,
        device_id_type=MESH,
    )


class LineGather:
    def __init__(self, own_ref, all_ref, sems, where, depth, both=True):
        self.own, self.where, self.depth, self.both = own_ref, where, depth, both
        self.slot = all_ref if callable(all_ref) else lambda slot: all_ref.at[slot]
        self.right, self.left, self.sib, self.recv, self.local = sems

    @staticmethod
    def scratch(depth):
        return [pltpu.SemaphoreType.DMA((2 * depth,))] * 4 + [pltpu.SemaphoreType.DMA]

    def copy(self, kind, slot, source):
        dp, cp, z, core = self.where
        device = {"right": (dp, cp + 2), "left": (dp, cp - 2), "sib": (dp, cp ^ 1)}[kind]
        sem = {"right": self.right, "left": self.left, "sib": self.sib}[kind]
        return send(source, self.slot(slot), sem.at[slot], self.recv.at[slot], device)

    def keep(self):
        return pltpu.make_async_copy(self.own, self.slot(self.where[1]), self.local)

    def start(self):
        dp, cp, z, core = self.where

        @pl.when(z < self.depth - 1)
        def _():
            self.copy("right", cp, self.own).start()

        @pl.when(z > 0)
        def _():
            self.copy("left", cp, self.own).start()

        if self.both:
            self.copy("sib", cp, self.own).start()
        self.keep().start()

    def step(self, far):
        dp, cp, z, core = self.where

        @pl.when(z >= far)
        def _():
            slot = cp - 2 * far
            self.copy("right", slot, self.own).wait_recv()

            @pl.when(z < self.depth - 1)
            def _():
                self.copy("right", slot, self.slot(slot)).start()

            if self.both:
                self.copy("sib", slot, self.slot(slot)).start()

        @pl.when(z + far < self.depth)
        def _():
            slot = cp + 2 * far
            self.copy("left", slot, self.own).wait_recv()

            @pl.when(z > 0)
            def _():
                self.copy("left", slot, self.slot(slot)).start()

            if self.both:
                self.copy("sib", slot, self.slot(slot)).start()

    def arrive(self, spot):
        self.copy("sib", 1 - self.where[3] + 2 * spot, self.own).wait_recv()

    def finish(self, arrived=False):
        dp, cp, z, core = self.where
        if self.both and not arrived:
            for spot in range(self.depth):
                self.arrive(spot)
        if not arrived:
            self.keep().wait()
        for spot in range(self.depth):
            slot = 2 * spot + core
            if self.both:
                self.copy("sib", slot, self.own).wait_send()

            @pl.when((spot <= z) & (z < self.depth - 1))
            def _():
                self.copy("right", slot, self.own).wait_send()

            @pl.when((spot >= z) & (z > 0))
            def _():
                self.copy("left", slot, self.own).wait_send()


class HalvedGather:
    def __init__(self, own_ref, all_ref, sems, where, depth):
        half = own_ref.shape[0] // 2
        count = len(sems) // 2

        def line(index):
            rows = pl.ds(index * half, half)
            return LineGather(
                own_ref.at[rows],
                lambda slot: all_ref.at[slot, rows],
                sems[index * count : (index + 1) * count],
                where,
                depth,
            )

        self.lines = [line(0), line(1)]

    def start(self):
        for line in self.lines:
            line.start()

    def step(self, far):
        for line in self.lines:
            line.step(far)

    def arrive(self, spot):
        for line in self.lines:
            line.arrive(spot)

    def keep_wait(self):
        for line in self.lines:
            line.keep().wait()

    def finish(self, arrived=False):
        for line in self.lines:
            line.finish(arrived)


class Swap:
    def __init__(self, source_ref, target_ref, sems, where, count):
        self.source, self.where, self.count = source_ref, where, count
        self.slot = target_ref if callable(target_ref) else lambda slot: target_ref.at[slot]
        self.origin = source_ref if callable(source_ref) else lambda slot: source_ref.at[slot]
        self.sent, self.recv, self.local = sems

    @staticmethod
    def scratch(count):
        return [pltpu.SemaphoreType.DMA((count,))] * 2 + [pltpu.SemaphoreType.DMA]

    def copy(self, peer):
        dp, cp, z, core = self.where
        return send(
            self.origin(peer),
            self.slot(cp),
            self.sent.at[peer],
            self.recv.at[cp],
            (dp, peer),
        )

    def keep(self):
        cp = self.where[1]
        return pltpu.make_async_copy(self.origin(cp), self.slot(cp), self.local)

    def start(self):
        cp = self.where[1]
        for turn in range(self.count - 1, 0, -1):
            self.copy(cp ^ turn).start()
        self.keep().start()

    def arrive(self, peer):
        dp, cp, z, core = self.where
        send(
            self.origin(peer),
            self.slot(peer),
            self.sent.at[peer],
            self.recv.at[peer],
            (dp, peer),
        ).wait_recv()

    def finish_recv(self):
        cp = self.where[1]
        for turn in range(1, self.count):
            self.arrive(cp ^ turn)
        self.keep().wait()

    def finish_send(self):
        cp = self.where[1]
        for turn in range(1, self.count):
            self.copy(cp ^ turn).wait_send()


class RingSpread:
    def __init__(self, block, half, sems, where):
        self.block, self.half, self.where = block, half, where
        self.sent, self.recv = sems

    @staticmethod
    def scratch():
        return [pltpu.SemaphoreType.DMA((4,))] * 2

    def copy(self, kind, mine):
        dp, cp, z, core = self.where
        turn = (1, 2, 2, 1)[kind]
        if kind < 2:
            part = self.block(dp if mine else dp ^ turn)
        else:
            part = self.half(dp ^ (3 - turn) if mine else dp ^ 3, kind - 2)
        return send(part, part, self.sent.at[kind], self.recv.at[kind], (dp ^ turn, cp))

    def start(self):
        self.copy(0, True).start()
        self.copy(1, True).start()

    def forward(self):
        self.copy(0, False).wait_recv()
        self.copy(2, True).start()
        self.copy(1, False).wait_recv()
        self.copy(3, True).start()

    def finish(self):
        self.copy(2, False).wait_recv()
        self.copy(3, False).wait_recv()
        for kind in range(4):
            self.copy(kind, True).wait_send()


def turn_heads(values, cosine, sine):
    half = values.shape[0] // 2
    first, second = values[:half], values[half:]
    return jnp.concatenate([first * cosine - second * sine, second * cosine + first * sine], axis=0)


def head_hat(values):
    inverse = lax.rsqrt(jnp.mean(values * values, axis=0, keepdims=True) + norm_eps)
    return values * inverse, inverse


def lay_places(order_ref, lengths_ref, rows, count):
    spots = [order_ref[0, index] * rows for index in range(count)]
    lanes = lax.broadcasted_iota(jnp.int32, (1, rows), 1)
    lines = lax.broadcasted_iota(jnp.int32, (rows, 1), 0)
    place_row = jnp.concatenate([spot + lanes for spot in spots], axis=1)
    place_column = jnp.concatenate([spot + lines for spot in spots], axis=0)
    starts = jnp.zeros_like(place_row)
    begin = jnp.int32(0)
    for index in range(lengths_ref.shape[1] - 1):
        begin = begin + lengths_ref[0, index]
        starts = jnp.where(place_row >= begin, begin, starts)
    return place_row, place_column, starts


def to_column(row):
    size = row.shape[1]
    down = lax.broadcasted_iota(jnp.int32, (size, size), 0)
    across = lax.broadcasted_iota(jnp.int32, (size, size), 1)
    return jnp.sum(jnp.where(down == across, row, 0.0), axis=1, keepdims=True)


def split_gains(gains_ref, width):
    lines = width // gains_ref.shape[1]

    def row(begin, end):
        return jnp.concatenate([gains_ref[line : line + 1] for line in range(begin, end)], axis=1)

    gain_one, gain_two = row(0, lines), row(lines, 2 * lines)
    gain_heads = row(2 * lines, gains_ref.shape[0])
    gain_query = to_column(gain_heads[:, :HEAD_DIM])
    gain_key = to_column(gain_heads[:, HEAD_DIM:])
    return gain_one, gain_two, gain_query, gain_key


def score_block(keys, queries, key_place, query_place, query_start):
    scores = jnp.dot(keys, queries, preferred_element_type=jnp.float32) * HEAD_DIM ** (-0.5)
    allowed = (key_place <= query_place) & (key_place >= query_start)
    return jnp.where(allowed, scores, masked_score), allowed


class LineScatter:
    cuts = 2

    def __init__(self, part_ref, out_ref, scratch, where, depth):
        self.part, self.out, self.where, self.depth = part_ref, out_ref, where, depth
        self.sib, self.line = scratch[:2]
        (
            self.sib_sent,
            self.sib_recv,
            self.right_sent,
            self.right_recv,
            self.left_sent,
            self.left_recv,
        ) = scratch[2:]
        self.size = part_ref.shape[1] // self.cuts

    @classmethod
    def scratch(cls, depth, rows, width):
        return [
            pltpu.VMEM((depth, rows, width), jnp.bfloat16),
            pltpu.VMEM((depth + 1, rows, width), jnp.bfloat16),
        ] + [pltpu.SemaphoreType.DMA((depth,))] * 2 + [
            pltpu.SemaphoreType.DMA((depth * cls.cuts,))
        ] * 4

    def pair(self, spot):
        dp, cp, z, core = self.where
        return send(
            self.part.at[2 * spot + 1 - core],
            self.sib.at[spot],
            self.sib_sent.at[spot],
            self.sib_recv.at[spot],
            (dp, cp ^ 1),
        )

    def rows(self, cut):
        return pl.ds(cut * self.size, self.size)

    def hop_right(self, spot, cut):
        dp, cp, z, core = self.where
        index = spot * self.cuts + cut
        return send(
            self.part.at[2 * spot + core, self.rows(cut)],
            self.line.at[spot + 1, self.rows(cut)],
            self.right_sent.at[index],
            self.right_recv.at[index],
            (dp, cp + 2),
        )

    def hop_left(self, spot, cut):
        dp, cp, z, core = self.where
        index = spot * self.cuts + cut
        return send(
            self.part.at[2 * spot + core, self.rows(cut)],
            self.line.at[spot, self.rows(cut)],
            self.left_sent.at[index],
            self.left_recv.at[index],
            (dp, cp - 2),
        )

    def order(self):
        spots = []
        for turn in range(self.depth):
            spots += [self.depth - 1 - turn, turn]
        return list(dict.fromkeys(spots))

    def chip_sum(self, spot, cut):
        rows = self.rows(cut)
        mine = self.part[2 * spot + self.where[3], rows].astype(jnp.float32)
        return mine + self.sib[spot, rows].astype(jnp.float32)

    def pass_on(self, spot, cut, arrived, slot, hop):
        total = self.chip_sum(spot, cut)
        if arrived is not None:
            arrived.wait_recv()
            total = total + self.line[slot, self.rows(cut)].astype(jnp.float32)
        self.part[2 * spot + self.where[3], self.rows(cut)] = total.astype(jnp.bfloat16)
        hop.start()

    def forward(self, spot, cuts=None):
        z, core = self.where[2], self.where[3]
        cuts = range(self.cuts) if cuts is None else cuts
        if 0 in cuts:

            @pl.when(z != spot)
            def _():
                self.pair(spot).wait_recv()

        for cut in cuts:
            right, left = self.hop_right(spot, cut), self.hop_left(spot, cut)

            @pl.when((z < spot) & (z > 0))
            def _():
                self.pass_on(spot, cut, right, spot + 1, right)

            @pl.when((z < spot) & (z == 0))
            def _():
                self.pass_on(spot, cut, None, None, right)

            @pl.when((z > spot) & (z < self.depth - 1))
            def _():
                self.pass_on(spot, cut, left, spot, left)

            @pl.when((z > spot) & (z == self.depth - 1))
            def _():
                self.pass_on(spot, cut, None, None, left)

    def finish(self):
        z = self.where[2]
        self.pair(z).wait_recv()
        for cut in range(self.cuts):
            rows = self.rows(cut)
            self.out[rows] = self.chip_sum(z, cut)

            @pl.when(z > 0)
            def _():
                self.hop_right(z, cut).wait_recv()
                self.out[rows] += self.line[z + 1, rows].astype(jnp.float32)

            @pl.when(z < self.depth - 1)
            def _():
                self.hop_left(z, cut).wait_recv()
                self.out[rows] += self.line[z, rows].astype(jnp.float32)

        for spot in range(self.depth):
            self.pair(spot).wait_send()

            @pl.when(z < spot)
            def _():
                for cut in range(self.cuts):
                    self.hop_right(spot, cut).wait_send()

            @pl.when(z > spot)
            def _():
                for cut in range(self.cuts):
                    self.hop_left(spot, cut).wait_send()


class RingReduce:
    def __init__(self, part, work, scratch, where):
        self.part, self.work, self.where = part, work, where
        self.from_x, self.from_y, self.x_sent, self.x_recv, self.y_sent, self.y_recv = scratch

    @staticmethod
    def scratch(*half):
        return [pltpu.VMEM((3,) + half, jnp.bfloat16)] * 2 + [pltpu.SemaphoreType.DMA((3,))] * 4

    def to_x(self, kind):
        dp, cp, z, core = self.where
        source = (
            self.part(dp ^ 3, 0) if kind == 0 else self.part(dp ^ 1, 0) if kind == 1 else self.work(1)
        )
        return send(
            source, self.from_x.at[kind], self.x_sent.at[kind], self.x_recv.at[kind], (dp ^ 1, cp)
        )

    def to_y(self, kind):
        dp, cp, z, core = self.where
        source = (
            self.part(dp ^ 3, 1) if kind == 0 else self.part(dp ^ 2, 1) if kind == 1 else self.work(0)
        )
        return send(
            source, self.from_y.at[kind], self.y_sent.at[kind], self.y_recv.at[kind], (dp ^ 2, cp)
        )

    def start(self):
        for kind in range(2):
            self.to_x(kind).start()
            self.to_y(kind).start()

    def add(self, index, *arrived):
        target = self.work(index)
        total = target[...].astype(jnp.float32)
        for block in arrived:
            total = total + block[...].astype(jnp.float32)
        target[...] = total.astype(jnp.bfloat16)

    def middle(self):
        self.to_x(0).wait_recv()
        self.add(0, self.from_x.at[0])
        self.to_y(2).start()
        self.to_y(0).wait_recv()
        self.add(1, self.from_y.at[0])
        self.to_x(2).start()

    def finish(self):
        for kind in (1, 2):
            self.to_x(kind).wait_recv()
            self.to_y(kind).wait_recv()
        self.add(2, self.from_x.at[1], self.from_y.at[2])
        self.add(3, self.from_y.at[1], self.from_x.at[2])

    def finish_send(self):
        for kind in range(3):
            self.to_x(kind).wait_send()
            self.to_y(kind).wait_send()

    def places(self):
        dp = self.where[0]
        return [(dp ^ 2, 0), (dp ^ 1, 1), (dp, 0), (dp, 1)]


def far_first(turn, z, depth):
    order = []
    for spot in range(depth):
        rest = sorted((other for other in range(depth) if other != spot), key=lambda other: (-abs(other - spot), other))
        ends = [other for other in rest if other in (0, depth - 1)]
        order.append(ends + [other for other in rest if other not in ends] + [spot])
    picked = 0
    for step in range(depth):
        for spot in range(depth):
            picked = picked + order[spot][step] * ((turn == step) & (z == spot)).astype(jnp.int32)
    return picked


def near_first(turn, z, depth):
    picked = 0
    for step in range(depth):
        for spot in range(depth):
            order = sorted(range(depth), key=lambda other: (abs(other - spot), other))
            picked = picked + order[step] * ((turn == step) & (z == spot)).astype(jnp.int32)
    return picked


def fore_kernel(
    tile,
    tokens_ref,
    gains_ref,
    order_ref,
    lengths_ref,
    input_ref,
    output_ref,
    gateup_ref,
    down_ref,
    cotangent_own,
    normed_one_out,
    input_out,
    output_out,
    raw_out,
    flat_out,
    forward_out,
    gateup_out,
    total_out,
    residual_out,
    cosine_ref,
    sine_ref,
    d_normed_out,
    down_out,
    input_send,
    output_own,
    gate_send,
    up_send,
    key_place_ref,
    query_place_ref,
    query_start_ref,
    normed_one,
    own_one,
    inputs,
    outputs,
    raw,
    queries,
    keys_up,
    values,
    flat_send,
    flat_recv,
    own_two,
    normed,
    cotangent,
    gate_weight,
    up_weight,
    down_weight,
    hidden_up,
    d_gates,
    d_ups,
    down_grad,
    out_sems,
    *sems,
):
    where = place()
    dp, cp, z, core = where
    context_count = normed_one.shape[0]
    depth = context_count // 2
    rows = tokens_ref.shape[0]
    width = tokens_ref.shape[1]
    q_each = HEADS // KV_HEADS * HEAD_DIM
    take = iter(range(len(sems)))

    def some(count):
        return [sems[next(take)] for _ in range(count)]

    kv_each = HEAD_DIM
    for head in range(context_count):
        for start, begin, size in (
            (head * q_each, 0, q_each),
            (HEADS * HEAD_DIM + head * kv_each, q_each, kv_each),
            ((HEADS + KV_HEADS) * HEAD_DIM + head * kv_each, q_each + kv_each, kv_each),
        ):
            input_send[head, :, begin : begin + size] = input_ref[:, start : start + size].astype(
                jnp.bfloat16
            )
    hidden = gate_send.shape[2]
    piece = hidden // inputs.shape[0]
    half_width = gateup_ref.shape[1] // 2

    def cut_columns(target, base):
        for head in range(context_count):
            target[head] = jnp.concatenate(
                [
                    gateup_ref[:, pl.ds(base + (group * context_count + head) * piece, piece)]
                    for group in range(inputs.shape[0])
                ],
                axis=1,
            ).astype(jnp.bfloat16)

    cut_columns(gate_send, 0)
    greet([(dp, cp ^ turn) for turn in range(1, context_count)] + [(dp ^ 1, cp), (dp ^ 2, cp)])
    token_line = HalvedGather(own_one, normed_one, some(10), where, depth)
    second_line = HalvedGather(own_two, normed, some(10), where, depth)
    cotangent_line = LineGather(cotangent_own, cotangent, some(5), where, depth)
    output_line = LineGather(
        output_own, lambda slot: outputs.at[dp, slot // 2, core], some(5), where, depth, False
    )
    input_swap = Swap(input_send, inputs.at[dp], some(3), where, context_count)
    shard = input_send.shape[1]

    each_rows = context_count * shard

    def weight_slot(target):
        return lambda slot: target.at[
            pl.ds(pl.multiple_of(dp * each_rows + slot * shard, 16), shard)
        ]

    gate_swap = Swap(gate_send, weight_slot(gate_weight), some(3), where, context_count)
    up_swap = Swap(up_send, weight_slot(up_weight), some(3), where, context_count)
    flat_swap = Swap(flat_send, flat_recv, some(3), where, context_count)
    input_ring = RingSpread(
        lambda d: inputs.at[d],
        lambda d, h: inputs.at[d, pl.ds(h * (context_count // 2), context_count // 2)],
        some(2),
        where,
    )
    output_ring = RingSpread(
        lambda d: outputs.at[d, :, core],
        lambda d, h: outputs.at[d, pl.ds(h * (depth // 2), depth // 2), core],
        some(2),
        where,
    )
    half_rows = each_rows // 2

    def weight_ring(target):
        return RingSpread(
            lambda d: target.at[pl.ds(pl.multiple_of(d * each_rows, 16), each_rows)],
            lambda d, h: target.at[
                pl.ds(pl.multiple_of(d * each_rows + h * half_rows, 16), half_rows)
            ],
            some(2),
            where,
        )

    gate_ring, up_ring = weight_ring(gate_weight), weight_ring(up_weight)
    lane_half = width // 2

    def down_part(d, h):
        return down_grad.at[d, :, pl.ds(h * lane_half, lane_half)]

    down_spread = RingSpread(lambda d: down_grad.at[d], down_part, some(2), where)
    line = LineScatter(normed_one, d_normed_out, some(8), where, depth)

    def down_work(index):
        return down_part(*down_ring.places()[index])

    down_ring = RingReduce(down_part, down_work, some(6), where)
    at_end = (z == 0) | (z == depth - 1)
    share_sent, share_recv = some(2)

    def share(mine):
        part = outputs.at[:, :, core if mine else 1 - core]
        return send(part, part, share_sent, share_recv, (dp, cp ^ 1))

    input_swap.start()
    gate_swap.start()
    down_grad[dp] = down_ref[...].astype(jnp.bfloat16)
    down_spread.start()
    gain_one, gain_two, gain_query, gain_key = split_gains(gains_ref, width)
    hat_one, _ = rms_parts(tokens_ref[...].astype(jnp.float32))
    own_one[...] = (hat_one * gain_one).astype(jnp.bfloat16)
    output_own[...] = output_ref[...].astype(jnp.bfloat16)
    place_row, place_column, starts = lay_places(order_ref, lengths_ref, rows, context_count)
    query_place_ref[...] = place_row
    key_place_ref[...] = place_column
    query_start_ref[...] = starts
    pair_index = lax.broadcasted_iota(jnp.int32, (HEAD_DIM // 2, 1), 0).astype(jnp.float32)
    angles = (place_row - starts).astype(jnp.float32) * jnp.exp(
        pair_index * (-2.0 * math.log(rope_base) / HEAD_DIM)
    )
    cosine_ref[...] = jnp.cos(angles)
    sine_ref[...] = jnp.sin(angles)
    cut_columns(up_send, half_width)
    token_line.start()
    input_swap.finish_recv()
    input_ring.start()
    gate_swap.finish_recv()
    gate_ring.start()
    output_line.start()
    token_line.step(1)
    output_line.step(1)
    input_ring.forward()
    token_line.step(2)
    output_line.step(2)
    token_line.step(3)
    output_line.step(3)
    down_spread.forward()
    up_swap.start()
    output_line.finish()
    output_ring.start()
    token_line.finish()
    input_ring.finish()
    one_copy = pltpu.make_async_copy(normed_one, normed_one_out, out_sems.at[0])
    one_copy.start()
    input_copy = pltpu.make_async_copy(inputs, input_out, out_sems.at[1])
    input_copy.start()

    weights = inputs[...].reshape(width, inputs.shape[-1])

    def project(turn, carry):
        lanes = pl.ds(pl.multiple_of(turn * tile, tile), tile)
        block = normed_one[pl.ds(turn * (tile // rows), tile // rows)].reshape(tile, width)
        part = jnp.dot(block, weights, preferred_element_type=jnp.float32).T
        raw[:, lanes] = part
        cosine, sine = cosine_ref[:, lanes], sine_ref[:, lanes]
        for head in range(HEADS // KV_HEADS):
            hat, _ = head_hat(part[head * HEAD_DIM : (head + 1) * HEAD_DIM])
            queries[head * HEAD_DIM : (head + 1) * HEAD_DIM, lanes] = turn_heads(
                hat * gain_query, cosine, sine
            ).astype(jnp.bfloat16)
        hat, _ = head_hat(part[q_each : q_each + HEAD_DIM])
        key = turn_heads(hat * gain_key, cosine, sine)
        keys_up[pl.ds(pl.multiple_of(turn * tile, tile), tile)] = key.T.astype(jnp.bfloat16)
        values[:, lanes] = part[q_each + HEAD_DIM :].astype(jnp.bfloat16)
        return carry

    lax.fori_loop(0, normed_one.shape[0] * rows // tile, project, 0)
    raw_copy = pltpu.make_async_copy(raw, raw_out, out_sems.at[2])
    raw_copy.start()

    def attend(turn, carry):
        lanes = pl.ds(pl.multiple_of(turn * tile, tile), tile)
        query_place, query_start = query_place_ref[:, lanes], query_start_ref[:, lanes]

        @pl.when(turn == 1)
        def _():
            gate_ring.forward()
            cotangent_line.start()

        @pl.when(turn == 2)
        def _():
            output_ring.forward()

        @pl.when(turn == 3)
        def _():
            up_swap.finish_recv()
            up_ring.start()
            cotangent_line.step(1)

        for head in range(HEADS // KV_HEADS):
            spot = pl.ds(head * HEAD_DIM, HEAD_DIM)
            scores, allowed = score_block(
                keys_up[...], queries[spot, lanes], key_place_ref[...], query_place, query_start
            )
            top = jnp.max(scores, axis=0, keepdims=True)
            exps = jnp.exp(scores - top)
            total = jnp.sum(exps, axis=0, keepdims=True)
            total_out[pl.ds(head, 1), lanes] = top + jnp.log(total)
            probs = (exps * (1.0 / total)).astype(jnp.bfloat16)
            attended = jnp.dot(values[...], probs, preferred_element_type=jnp.float32)
            for part in range(tile // rows):
                flat_send[turn * (tile // rows) + part, spot] = attended[
                    :, part * rows : (part + 1) * rows
                ].astype(jnp.bfloat16)
        return carry

    lax.fori_loop(0, depth, attend, 0)
    flat_swap.start()
    output_ring.finish()
    share(True).start()
    cotangent_line.step(2)
    share(False).wait_recv()
    output_copy = pltpu.make_async_copy(outputs, output_out, out_sems.at[3])
    output_copy.start()
    flat_swap.finish_recv()
    flat_copy = pltpu.make_async_copy(flat_recv, flat_out, out_sems.at[4])
    flat_copy.start()
    flat = flat_recv[...].reshape(HEADS * HEAD_DIM, rows).astype(jnp.float32).T.astype(jnp.bfloat16)
    residual = tokens_ref[...].astype(jnp.float32) + jnp.dot(
        flat, outputs[...].reshape(HEADS * HEAD_DIM, width), preferred_element_type=jnp.float32
    )
    residual_out[...] = residual
    hat_two, _ = rms_parts(residual)
    own_two[...] = (hat_two * gain_two).astype(jnp.bfloat16)
    second_line.start()
    down_spread.finish()

    def lay_down(step, carry):
        lanes = pl.ds(pl.multiple_of(step * tile, tile), tile)
        down_weight[:, lanes] = (
            down_grad[:, :, lanes]
            .astype(jnp.float32)
            .reshape(down_weight.shape[0], tile)
            .astype(jnp.bfloat16)
        )
        return carry

    lax.fori_loop(0, width // tile, lay_down, 0)
    up_ring.forward()
    cotangent_line.step(3)
    gate_ring.finish()
    cotangent_line.finish()
    up_ring.finish()
    one_copy.wait()
    group_rows = context_count * rows
    parts = normed_one

    def feed(turn, carry):
        spot = near_first(turn, z, depth)
        far = jnp.abs(spot - z)

        @pl.when((turn > 0) & (far != jnp.abs(near_first(turn - 1, z, depth) - z)))
        def _():
            second_line.step(far)

        @pl.when(turn == 0)
        def _():
            second_line.keep_wait()

        second_line.arrive(spot)
        pair = pl.ds(2 * spot, 2)
        lanes = pl.ds(pl.multiple_of(spot * tile, tile), tile)
        block = normed[pair].reshape(tile, width)
        gate = jnp.dot(block, gate_weight[...], preferred_element_type=jnp.float32)
        up = jnp.dot(block, up_weight[...], preferred_element_type=jnp.float32)
        sig = 1.0 / (1.0 + jnp.exp(-gate))
        act = gate * sig
        hidden_up[:, lanes] = (act * up).T.astype(jnp.bfloat16)
        d_hidden = contract_cols(cotangent[pair].reshape(tile, width), down_weight[...])
        d_gate = (d_hidden * up * (sig * (1.0 + gate * (1.0 - sig)))).astype(jnp.bfloat16)
        d_up = (d_hidden * act).astype(jnp.bfloat16)
        d_gates[lanes] = d_gate
        d_ups[lanes] = d_up
        part = contract_cols(d_gate, gate_weight[...]) + contract_cols(d_up, up_weight[...])
        parts[pair] = part.astype(jnp.bfloat16).reshape(2, rows, width)
        line.pair(spot).start()

        @pl.when(at_end & (turn > 0))
        def _():
            line.forward(spot)

        return carry

    lax.fori_loop(0, depth, feed, 0)
    chunk = 256
    inner = depth - 1 - z
    outer = [inner, (depth - 1) * (z // 2 == 0).astype(jnp.int32), (depth - 1) * (z // 2 == 1).astype(jnp.int32)]

    def relay(index):
        @pl.when(jnp.logical_not(at_end))
        def _():
            line.forward(outer[index])

    def down_step(step, carry):
        lanes = pl.ds(pl.multiple_of(step * chunk, chunk), chunk)
        right = cotangent[:, :, lanes].reshape(group_rows, chunk)
        down_grad[:, :, lanes] = (
            jnp.dot(hidden_up[...], right, preferred_element_type=jnp.float32)
            .reshape(down_grad.shape[:2] + (chunk,))
            .astype(jnp.bfloat16)
        )
        return carry

    lax.fori_loop(0, width // chunk, down_step, 0)
    down_ring.start()
    relay(0)

    def gateup_step(step, carry):
        lanes = pl.ds(pl.multiple_of(step * chunk, chunk), chunk)
        left = normed[:, :, lanes].reshape(group_rows, chunk)
        gate_weight[lanes] = contract_rows(left, d_gates[...]).astype(jnp.bfloat16)
        up_weight[lanes] = contract_rows(left, d_ups[...]).astype(jnp.bfloat16)
        return carry

    steps = width // chunk
    lax.fori_loop(0, steps // 2, gateup_step, 0)
    relay(1)
    lax.fori_loop(steps // 2, steps, gateup_step, 0)
    relay(2)
    saves = [
        pltpu.make_async_copy(gate_weight, gateup_out.at[0], out_sems.at[0]),
        pltpu.make_async_copy(up_weight, gateup_out.at[1], out_sems.at[5]),
    ]
    for save in saves:
        save.start()
    down_ring.middle()

    second_line.finish(True)

    def forward_step(step, carry):
        lanes = pl.ds(pl.multiple_of(step * tile, tile), tile)
        normed[pl.ds(2 * step, 2)] = (
            contract_rows(hidden_up[:, lanes], down_weight[...])
            .astype(jnp.bfloat16)
            .reshape(2, rows, width)
        )
        return carry

    lax.fori_loop(0, depth, forward_step, 0)
    saves.append(pltpu.make_async_copy(normed, forward_out, out_sems.at[6]))
    saves[2].start()
    line.finish()
    down_ring.finish()
    for half in range(2):
        down_out[:, pl.ds(half * lane_half, lane_half)] = down_grad[
            dp, :, pl.ds(half * lane_half, lane_half)
        ].astype(jnp.float32)
    down_ring.finish_send()
    share(True).wait_send()
    for swap in (input_swap, gate_swap, up_swap, flat_swap):
        swap.finish_send()
    for copy in (input_copy, raw_copy, output_copy, flat_copy, *saves):
        copy.wait()


def fore(
    tokens,
    gains,
    order,
    lengths,
    attn_input,
    attn_output,
    gate_up,
    down,
    cotangent,
    data_count,
    context_count,
):
    rows, width = tokens.shape
    depth = context_count // 2
    group_rows = rows * context_count
    shard = attn_input.shape[0]
    each = attn_input.shape[1] // context_count
    hidden = gate_up.shape[1] // 2 // context_count
    q_each = HEADS // KV_HEADS * HEAD_DIM
    flat_width = HEADS * HEAD_DIM
    bf = jnp.bfloat16
    any_space = pl.BlockSpec(memory_space=pl.ANY)
    in_vmem = pl.BlockSpec(memory_space=pltpu.VMEM)
    in_smem = pl.BlockSpec(memory_space=pltpu.SMEM)
    down_rows = down.shape[0]
    shapes = [
        ((context_count, rows, width), bf, any_space),
        ((data_count, context_count, shard, each), bf, any_space),
        ((data_count, depth, 2, shard, width), bf, any_space),
        ((each, group_rows), jnp.float32, any_space),
        ((context_count, q_each, rows), bf, any_space),
        ((context_count, rows, width), bf, any_space),
        ((2, width, hidden), bf, any_space),
        ((HEADS // KV_HEADS, group_rows), jnp.float32, in_vmem),
        ((rows, width), jnp.float32, in_vmem),
        ((HEAD_DIM // 2, group_rows), jnp.float32, in_vmem),
        ((HEAD_DIM // 2, group_rows), jnp.float32, in_vmem),
        ((rows, width), jnp.float32, in_vmem),
        ((down_rows, width), jnp.float32, in_vmem),
    ]
    return pl.pallas_call(
        functools.partial(fore_kernel, 2 * rows),
        out_shape=[jax.ShapeDtypeStruct(shape, kind) for shape, kind, _ in shapes],
        in_specs=[in_vmem] * 2 + [in_smem] * 2 + [in_vmem] * 4 + [any_space],
        out_specs=[space for _, _, space in shapes],
        scratch_shapes=[
            pltpu.VMEM((context_count, shard, each), bf),
            pltpu.VMEM((shard, width), bf),
            pltpu.VMEM((context_count, shard, hidden), bf),
            pltpu.VMEM((context_count, shard, hidden), bf),
            pltpu.VMEM((group_rows, 1), jnp.int32),
            pltpu.VMEM((1, group_rows), jnp.int32),
            pltpu.VMEM((1, group_rows), jnp.int32),
            pltpu.VMEM((context_count, rows, width), bf),
            pltpu.VMEM((rows, width), bf),
            pltpu.VMEM((data_count, context_count, shard, each), bf),
            pltpu.VMEM((data_count, depth, 2, shard, width), bf),
            pltpu.VMEM((each, group_rows), jnp.float32),
            pltpu.VMEM((q_each, group_rows), bf),
            pltpu.VMEM((group_rows, HEAD_DIM), bf),
            pltpu.VMEM((HEAD_DIM, group_rows), bf),
            pltpu.VMEM((context_count, q_each, rows), bf),
            pltpu.VMEM((context_count, q_each, rows), bf),
            pltpu.VMEM((rows, width), bf),
            pltpu.VMEM((context_count, rows, width), bf),
            pltpu.VMEM((context_count, rows, width), bf),
            pltpu.VMEM((width, hidden), bf),
            pltpu.VMEM((width, hidden), bf),
            pltpu.VMEM((hidden, width), bf),
            pltpu.VMEM((hidden, group_rows), bf),
            pltpu.VMEM((group_rows, hidden), bf),
            pltpu.VMEM((group_rows, hidden), bf),
            pltpu.VMEM((data_count, down_rows, width), bf),
            pltpu.SemaphoreType.DMA((7,)),
        ]
        + LineGather.scratch(depth) * 6
        + Swap.scratch(context_count) * 4
        + RingSpread.scratch() * 5
        + LineScatter.scratch(depth, rows, width)
        + RingReduce.scratch(down_rows, width // 2)
        + [pltpu.SemaphoreType.DMA] * 2,
        compiler_params=pltpu.CompilerParams(
            collective_id=0, has_side_effects=True, vmem_limit_bytes=63 * 2**20
        ),
        name="fore",
    )(tokens, gains, order, lengths, attn_input, attn_output, gate_up, down, cotangent)


def back_kernel(
    tokens_ref,
    cotangent_ref,
    residual_ref,
    d_normed_ref,
    gains_ref,
    order_ref,
    lengths_ref,
    cosine_ref,
    sine_ref,
    total_ref,
    normed_in,
    input_in,
    output_in,
    raw_in,
    flat_in,
    forward_in,
    gateup_in,
    mixed_out,
    token_out,
    gains_out,
    output_grad_out,
    input_grad_out,
    gateup_grad_out,
    inputs,
    outputs,
    raw,
    flat,
    forwards,
    forward_sum,
    d_first,
    d_residual,
    branch,
    swap_send,
    swap_recv,
    queries,
    keys,
    keys_up,
    values_up,
    d_query,
    d_key,
    d_value,
    d_projected,
    parts,
    input_grad,
    output_sib,
    output_line,
    gateup_work,
    gain_sums,
    own_gains,
    line_gains,
    all_gains,
    key_place_ref,
    query_place_ref,
    query_start_ref,
    load_sems,
    work_sems,
    share_sems,
    output_sent,
    output_recv,
    line_sent,
    line_recv,
    all_sent,
    all_recv,
    *scratch,
):
    where = place()
    dp, cp, z, core = where
    count, rows, width = forwards.shape
    depth = count // 2
    data_count = all_gains.shape[0]
    shard = inputs.shape[2]
    tile = 2 * rows
    group_rows = count * rows
    heads = HEADS // KV_HEADS
    q_each = heads * HEAD_DIM
    flat_width = HEADS * HEAD_DIM
    score_scale = HEAD_DIM ** (-0.5)
    load_pairs = [
        (output_in, outputs),
        (raw_in, raw),
        (forward_in, forwards),
        (flat_in, flat),
        (normed_in, forwards),
        (input_in, inputs),
    ]
    loads = [
        pltpu.make_async_copy(source, target, load_sems.at[index])
        for index, (source, target) in enumerate(load_pairs)
    ]
    for index in (0, 1, 2, 3, 5):
        loads[index].start()
    greet(
        [(dp, cp ^ turn) for turn in range(1, count)]
        + [(dp ^ turn, cp) for turn in range(1, data_count)]
    )
    swap = Swap(swap_send, swap_recv, scratch[:3], where, count)
    take = iter(scratch[3:])

    def some(amount):
        return [next(take) for _ in range(amount)]

    forward_line = LineScatter(forwards, forward_sum, some(8), where, depth)
    first_line = LineScatter(parts, d_first, some(8), where, depth)
    gateup_rows = data_count * count * shard // data_count

    def in_place(part):
        spots = [(dp ^ 2, 0), (dp ^ 1, 1), (dp, 0), (dp, 1)]
        return lambda index: part(*spots[index])

    gateup_half = gateup_rows // 2

    def gateup_part(index):
        return lambda d, h: gateup_in.at[
            index, pl.ds(pl.multiple_of(d * gateup_rows + h * gateup_half, 16), gateup_half)
        ]

    def gateup_ring(index):
        return RingReduce(
            gateup_part(index), lambda spot: gateup_work.at[index, spot], some(6), where
        )

    def gateup_own(index):
        each = gateup_half // shard
        return lambda slot: gateup_work.at[
            index, 2 + slot // each, pl.ds(pl.multiple_of(slot % each * shard, 16), shard)
        ]

    def output_part(d, h):
        return outputs.at[d, pl.ds(h * (depth // 2), depth // 2), core]

    def input_part(d, h):
        half = gateup_rows // 2
        return input_grad.at[pl.ds(pl.multiple_of(d * gateup_rows + h * half, 16), half)]

    gate_ring, up_ring = gateup_ring(0), gateup_ring(1)
    output_ring = RingReduce(output_part, in_place(output_part), some(6), where)
    input_ring = RingReduce(input_part, in_place(input_part), some(6), where)

    def own_shard(source):
        return lambda slot: source.at[pl.ds(pl.multiple_of(slot * shard, 16), shard)]

    gate_swap = Swap(gateup_own(0), gateup_grad_out.at[0], some(3), where, count)
    up_swap = Swap(gateup_own(1), gateup_grad_out.at[1], some(3), where, count)
    own_rows = input_grad.at[pl.ds(pl.multiple_of(dp * gateup_rows, 16), gateup_rows)]
    input_swap = Swap(own_shard(own_rows), input_grad_out, some(3), where, count)
    works = [
        pltpu.make_async_copy(ring.part(*spot), ring.work(index), work_sems.at[4 * turn + index])
        for turn, ring in enumerate((gate_ring, up_ring))
        for index, spot in enumerate(ring.places())
    ]
    gate_ring.start()
    for work in works:
        work.start()

    def share(mine):
        return send(
            outputs.at[:, :, 1 - core], output_sib, share_sems.at[0], share_sems.at[1], (dp, cp ^ 1)
        )

    def output_hop(far, mine):
        return send(
            outputs.at[dp, z ^ far, core],
            output_line.at[z if mine else z ^ far],
            output_sent.at[far],
            output_recv.at[far],
            (dp, cp ^ (2 * far)),
        )

    at_end = (z == 0) | (z == depth - 1)
    chunk = 256

    gain_one, gain_two, gain_query, gain_key = split_gains(gains_ref, width)
    hat_two, inv_two = rms_parts(residual_ref[...])
    d_normed = d_normed_ref[...]
    own_gains[:, pl.ds(width, width)] = jnp.sum(d_normed * hat_two, axis=0, keepdims=True)
    d_res = cotangent_ref[...].astype(jnp.float32) + norm_back(
        d_normed * gain_two, hat_two, inv_two
    )
    d_residual[...] = d_res
    branch[...] = d_res.astype(jnp.bfloat16)
    loads[0].wait()
    swap_send[...] = (
        contract_cols(outputs[...].reshape(flat_width, width), branch[...])
        .astype(jnp.bfloat16)
        .reshape(count, q_each, rows)
    )
    swap.start()
    loads[2].wait()
    for spot in forward_line.order():
        forward_line.pair(spot).start()
    loads[1].wait()

    def prepare(turn, carry):
        lanes = pl.ds(pl.multiple_of(turn * tile, tile), tile)
        cosine, sine = cosine_ref[:, lanes], sine_ref[:, lanes]
        for head in range(heads):
            spot = pl.ds(head * HEAD_DIM, HEAD_DIM)
            hat, _ = head_hat(raw[spot, lanes])
            queries[spot, lanes] = turn_heads(hat * gain_query, cosine, sine).astype(
                jnp.bfloat16
            )
        hat, _ = head_hat(raw[pl.ds(q_each, HEAD_DIM), lanes])
        key = turn_heads(hat * gain_key, cosine, sine)
        keys[:, lanes] = key.astype(jnp.bfloat16)
        keys_up[lanes] = key.T.astype(jnp.bfloat16)
        values_up[lanes] = raw[pl.ds(q_each + HEAD_DIM, HEAD_DIM), lanes].T.astype(jnp.bfloat16)
        return carry

    lax.fori_loop(0, depth, prepare, 0)
    place_row, place_column, starts = lay_places(order_ref, lengths_ref, rows, count)
    query_place_ref[...] = place_row
    key_place_ref[...] = place_column
    query_start_ref[...] = starts
    d_key[...] = jnp.zeros_like(d_key)
    d_value[...] = jnp.zeros_like(d_value)
    gain_sums[...] = jnp.zeros_like(gain_sums)

    @pl.when(at_end)
    def _():
        for turn in range(depth - 1):
            forward_line.forward(far_first(turn, z, depth))

    loads[3].wait()

    def output_step(step, carry):
        lanes = pl.ds(pl.multiple_of(step * chunk, chunk), chunk)
        outputs[:, :, :, :, lanes] = (
            jnp.dot(
                flat[...].reshape(flat_width, rows),
                branch[:, lanes],
                preferred_element_type=jnp.float32,
            )
            .astype(jnp.bfloat16)
            .reshape(outputs.shape[:4] + (chunk,))
        )
        return carry

    lax.fori_loop(0, width // chunk, output_step, 0)
    share(True).start()
    for work in works:
        work.wait()
    gate_ring.middle()
    up_ring.start()
    swap.finish_recv()

    def attend(turn, carry):
        lanes = pl.ds(pl.multiple_of(turn * tile, tile), tile)
        query_place, query_start = query_place_ref[:, lanes], query_start_ref[:, lanes]

        @pl.when(jnp.logical_not(at_end) & (turn >= 1))
        def _():
            forward_line.forward(far_first(turn - 1, z, depth))

        @pl.when(turn == 1)
        def _():
            gate_ring.finish()
            gate_swap.start()

        @pl.when(turn == 3)
        def _():
            up_ring.middle()

        for head in range(heads):
            spot = pl.ds(head * HEAD_DIM, HEAD_DIM)
            scores, allowed = score_block(
                keys_up[...], queries[spot, lanes], key_place_ref[...], query_place, query_start
            )
            probs = jnp.where(allowed, jnp.exp(scores - total_ref[pl.ds(head, 1), lanes]), 0.0)
            d_out = jnp.concatenate(
                [swap_recv[2 * turn, spot], swap_recv[2 * turn + 1, spot]], axis=1
            )
            d_probs = jnp.dot(values_up[...], d_out, preferred_element_type=jnp.float32)
            delta = jnp.sum(probs * d_probs, axis=0, keepdims=True)
            d_scores = (probs * (d_probs - delta)).astype(jnp.bfloat16)
            d_query[spot, lanes] = (
                jnp.dot(keys[...], d_scores, preferred_element_type=jnp.float32) * score_scale
            )
            d_key[...] += contract_cols(queries[spot, lanes], d_scores) * score_scale
            d_value[...] += contract_cols(d_out, probs.astype(jnp.bfloat16))
        return carry

    lax.fori_loop(0, depth, attend, 0)
    loads[5].wait()
    share(False).wait_recv()

    def share_step(step, carry):
        total = outputs[step, :, core].astype(jnp.float32) + output_sib[step].astype(jnp.float32)
        outputs[step, :, core] = total.astype(jnp.bfloat16)
        return carry

    lax.fori_loop(0, data_count, share_step, 0)
    output_ring.start()

    def feed(turn, carry):
        spot = far_first(turn, z, depth)
        lanes = pl.ds(pl.multiple_of(spot * tile, tile), tile)
        cosine, sine = cosine_ref[:, lanes], sine_ref[:, lanes]
        pieces = []
        for head in range(heads + 1):
            place_in = pl.ds(head * HEAD_DIM, HEAD_DIM)
            hat, inverse = head_hat(raw[place_in, lanes])
            if head < heads:
                turned = turn_heads(d_query[place_in, lanes], cosine, -sine)
                gain, kind = gain_query, 0
            else:
                turned = turn_heads(d_key[:, lanes], cosine, -sine)
                gain, kind = gain_key, 1
            gain_sums[kind] += turned * hat
            scaled = turned * gain
            pieces.append(
                inverse * (scaled - hat * jnp.mean(scaled * hat, axis=0, keepdims=True))
            )
        pieces.append(d_value[:, lanes])
        block = jnp.concatenate(pieces, axis=0).T.astype(jnp.bfloat16)
        d_projected[lanes] = block
        part = contract_cols(block, inputs[...].reshape(width, block.shape[1]))
        parts[pl.ds(2 * spot, 2)] = part.astype(jnp.bfloat16).reshape(2, rows, width)
        first_line.pair(spot).start()

        @pl.when(at_end & (turn < depth - 1))
        def _():
            first_line.forward(spot)

        return carry

    lax.fori_loop(0, depth, feed, 0)
    up_ring.finish()
    up_swap.start()
    forward_line.finish()
    loads[4].start()
    mixed_out[...] = (residual_ref[...] + forward_sum[...]).astype(jnp.bfloat16)
    for kind in range(2):
        own_gains[:, pl.ds(2 * width + kind * HEAD_DIM, HEAD_DIM)] = jnp.sum(
            gain_sums[kind].T, axis=0, keepdims=True
        )
    @pl.when(jnp.logical_not(at_end))
    def _():
        first_line.forward(far_first(0, z, depth))

    loads[4].wait()

    def input_step(step, carry):
        lanes = pl.ds(pl.multiple_of(step * chunk, chunk), chunk)
        left = forwards[:, :, lanes].reshape(group_rows, chunk)
        input_grad[lanes] = contract_rows(left, d_projected[...]).astype(jnp.bfloat16)
        return carry

    lax.fori_loop(0, width // chunk, input_step, 0)
    input_ring.start()
    output_ring.middle()

    @pl.when(jnp.logical_not(at_end))
    def _():
        first_line.forward(far_first(1, z, depth))

    input_ring.middle()

    @pl.when(jnp.logical_not(at_end))
    def _():
        first_line.forward(far_first(2, z, depth))

    input_ring.finish()
    input_swap.start()
    first_line.finish()
    hat_one, inv_one = rms_parts(tokens_ref[...].astype(jnp.float32))
    d_one = d_first[...]
    own_gains[:, pl.ds(0, width)] = jnp.sum(d_one * hat_one, axis=0, keepdims=True)
    line_gains[cp] = own_gains[...]
    for turn in range(1, count):
        send(
            own_gains, line_gains.at[cp], line_sent.at[turn], line_recv.at[turn], (dp, cp ^ turn)
        ).start()
    output_ring.finish()
    for far in range(depth - 1, 0, -1):
        output_hop(far, True).start()
    token_out[...] = d_residual[...] + norm_back(d_one * gain_one, hat_one, inv_one)
    for turn in range(1, count):
        copy = send(
            own_gains,
            line_gains.at[cp ^ turn],
            line_sent.at[turn],
            line_recv.at[turn],
            (dp, cp ^ turn),
        )
        copy.wait_recv()
        copy.wait_send()
    all_gains[dp] = jnp.sum(line_gains[...], axis=0)
    for turn in range(1, data_count):
        send(
            all_gains.at[dp],
            all_gains.at[dp],
            all_sent.at[turn],
            all_recv.at[turn],
            (dp ^ turn, cp),
        ).start()
    for turn in range(1, data_count):
        copy = send(
            all_gains.at[dp],
            all_gains.at[dp ^ turn],
            all_sent.at[turn],
            all_recv.at[turn],
            (dp ^ turn, cp),
        )
        copy.wait_recv()
        copy.wait_send()
    gain_total = jnp.sum(all_gains[...], axis=0)
    lanes = gains_out.shape[1]
    for line in range(gains_out.shape[0]):
        gains_out[line : line + 1] = gain_total[:, line * lanes : (line + 1) * lanes]
    total = outputs[dp, z, core].astype(jnp.float32)
    for far in range(1, depth):
        output_hop(far, False).wait_recv()
        total = total + output_line[z ^ far].astype(jnp.float32)
    output_grad_out[...] = total
    for done in (input_swap, gate_swap, up_swap):
        done.finish_recv()
    for done in (swap, input_swap, gate_swap, up_swap, gate_ring, up_ring, output_ring, input_ring):
        done.finish_send()
    for far in range(1, depth):
        output_hop(far, True).wait_send()
    share(True).wait_send()


def back(
    tokens,
    cotangent,
    residual,
    d_normed,
    gains,
    order,
    lengths,
    cosine,
    sine,
    log_total,
    normed,
    inputs,
    outputs,
    raw,
    flat,
    forwards,
    gateup_grad,
    collective_id,
):
    count, rows, width = normed.shape
    depth = count // 2
    data_count = inputs.shape[0]
    shard, each = inputs.shape[2:]
    hidden = gateup_grad.shape[2]
    group_rows = count * rows
    heads = HEADS // KV_HEADS
    q_each = heads * HEAD_DIM
    flat_width = HEADS * HEAD_DIM
    gain_width = 2 * width + 2 * HEAD_DIM
    bf = jnp.bfloat16
    f32 = jnp.float32
    any_space = pl.BlockSpec(memory_space=pl.ANY)
    in_vmem = pl.BlockSpec(memory_space=pltpu.VMEM)
    in_smem = pl.BlockSpec(memory_space=pltpu.SMEM)
    return pl.pallas_call(
        back_kernel,
        out_shape=[
            jax.ShapeDtypeStruct((rows, width), bf),
            jax.ShapeDtypeStruct((rows, width), f32),
            jax.ShapeDtypeStruct(gains.shape, f32),
            jax.ShapeDtypeStruct((shard, width), f32),
            jax.ShapeDtypeStruct((count, shard, each), bf),
            jax.ShapeDtypeStruct((2, count, shard, hidden), bf),
        ],
        in_specs=[in_vmem] * 5 + [in_smem] * 2 + [in_vmem] * 3 + [any_space] * 7,
        out_specs=[in_vmem] * 4 + [any_space] * 2,
        scratch_shapes=[
            pltpu.VMEM(inputs.shape, bf),
            pltpu.VMEM(outputs.shape, bf),
            pltpu.VMEM(raw.shape, f32),
            pltpu.VMEM(flat.shape, bf),
            pltpu.VMEM(forwards.shape, bf),
            pltpu.VMEM((rows, width), f32),
            pltpu.VMEM((rows, width), f32),
            pltpu.VMEM((rows, width), f32),
            pltpu.VMEM((rows, width), bf),
            pltpu.VMEM((count, q_each, rows), bf),
            pltpu.VMEM((count, q_each, rows), bf),
            pltpu.VMEM((q_each, group_rows), bf),
            pltpu.VMEM((HEAD_DIM, group_rows), bf),
            pltpu.VMEM((group_rows, HEAD_DIM), bf),
            pltpu.VMEM((group_rows, HEAD_DIM), bf),
            pltpu.VMEM((q_each, group_rows), f32),
            pltpu.VMEM((HEAD_DIM, group_rows), f32),
            pltpu.VMEM((HEAD_DIM, group_rows), f32),
            pltpu.VMEM((group_rows, each), bf),
            pltpu.VMEM(forwards.shape, bf),
            pltpu.VMEM((width, each), bf),
            pltpu.VMEM((data_count, depth, shard, width), bf),
            pltpu.VMEM((depth, shard, width), bf),
            pltpu.VMEM((2, 4, count * shard // 2, hidden), bf),
            pltpu.VMEM((2, HEAD_DIM, 2 * rows), f32),
            pltpu.VMEM((1, gain_width), f32),
            pltpu.VMEM((count, 1, gain_width), f32),
            pltpu.VMEM((data_count, 1, gain_width), f32),
            pltpu.VMEM((group_rows, 1), jnp.int32),
            pltpu.VMEM((1, group_rows), jnp.int32),
            pltpu.VMEM((1, group_rows), jnp.int32),
            pltpu.SemaphoreType.DMA((6,)),
            pltpu.SemaphoreType.DMA((8,)),
            pltpu.SemaphoreType.DMA((2,)),
            pltpu.SemaphoreType.DMA((depth,)),
            pltpu.SemaphoreType.DMA((depth,)),
            pltpu.SemaphoreType.DMA((count,)),
            pltpu.SemaphoreType.DMA((count,)),
            pltpu.SemaphoreType.DMA((data_count,)),
            pltpu.SemaphoreType.DMA((data_count,)),
        ]
        + Swap.scratch(count)
        + LineScatter.scratch(depth, rows, width) * 2
        + RingReduce.scratch(count * shard // 2, hidden) * 2
        + RingReduce.scratch(depth // 2, shard, width)
        + RingReduce.scratch(count * shard // 2, each)
        + Swap.scratch(count) * 3,
        compiler_params=pltpu.CompilerParams(
            collective_id=collective_id, has_side_effects=True, vmem_limit_bytes=63 * 2**20
        ),
        name="back",
    )(
        tokens,
        cotangent,
        residual,
        d_normed,
        gains,
        order,
        lengths,
        cosine,
        sine,
        log_total,
        normed,
        inputs,
        outputs,
        raw,
        flat,
        forwards,
        gateup_grad,
    )


def update_kernel(
    data_count,
    gateup_grad,
    input_grad,
    output_grad,
    down_grad,
    gains_grad,
    *refs,
):
    states, results = refs[:15], refs[15:30]
    scratch = refs[30]
    input_full = refs[31]
    context_count = gateup_grad.shape[1]
    piece = gateup_grad.shape[3] // data_count
    half = scratch.shape[1] // 2
    for side in range(2):
        for group in range(data_count):
            scratch[:, pl.ds(side * half + group * context_count * piece, context_count * piece)] = (
                jnp.concatenate(
                    [
                        gateup_grad[side, head, :, pl.ds(group * piece, piece)]
                        for head in range(context_count)
                    ],
                    axis=1,
                ).astype(jnp.float32)
            )
    q_each = HEADS // KV_HEADS * HEAD_DIM
    for start, size in ((0, q_each), (q_each, HEAD_DIM), (q_each + HEAD_DIM, HEAD_DIM)):
        input_full[:, pl.ds(start * context_count, size * context_count)] = jnp.concatenate(
            [input_grad[head, :, pl.ds(start, size)] for head in range(context_count)], axis=1
        ).astype(jnp.float32)
    jobs = (
        (input_full, rate_input, weight_decay),
        (output_grad, rate_output, weight_decay),
        (scratch, rate_gateup, weight_decay),
        (down_grad, rate_down, weight_decay),
        (gains_grad, rate_gains, 0.0),
    )
    for index, (gradient, rate, decay) in enumerate(jobs):
        weight, first, second = (state[...] for state in states[3 * index : 3 * index + 3])
        for result, value in zip(
            results[3 * index : 3 * index + 3],
            adam_update(weight, first, second, gradient[...], rate, decay),
        ):
            result[...] = value


def update(gateup_grad, input_grad, output_grad, down_grad, gains_grad, states, data_count):
    parts = 3

    def rows_of(array):
        axis = array.ndim - 2
        shape = list(array.shape)
        if shape[axis] % (8 * parts) == 0:
            shape[axis] //= parts
            return pl.BlockSpec(
                tuple(shape), lambda step: tuple(step if d == axis else 0 for d in range(len(shape)))
            )
        return pl.BlockSpec(tuple(shape), lambda step: (0,) * len(shape))

    arrays = [gateup_grad, input_grad, output_grad, down_grad, gains_grad] + list(states)
    shard = states[0].shape[0] // parts
    return pl.pallas_call(
        functools.partial(update_kernel, data_count),
        grid=(parts,),
        out_shape=[jax.ShapeDtypeStruct(state.shape, jnp.float32) for state in states],
        in_specs=[rows_of(array) for array in arrays],
        out_specs=[rows_of(state) for state in states],
        scratch_shapes=[
            pltpu.VMEM((shard, states[6].shape[1]), jnp.float32),
            pltpu.VMEM((shard, states[0].shape[1]), jnp.float32),
        ],
        compiler_params=pltpu.CompilerParams(vmem_limit_bytes=56 * 2**20),
        name="update",
    )(*arrays)


def on_device_split(
    tokens,
    output_cotangent,
    sequence_lengths,
    block_order,
    attn_input,
    input_moment,
    input_square,
    attn_output,
    output_moment,
    output_square,
    gate_up,
    gateup_moment,
    gateup_square,
    down_weight,
    down_moment,
    down_square,
    norm_gains,
    gains_moment,
    gains_square,
):
    context_count = lax.axis_size("cp")
    data_count = lax.axis_size("dp")
    gain_lines = norm_gains.reshape(-1, 2 * HEAD_DIM)
    (
        normed_one,
        input_part,
        output_all,
        raw,
        flat_parts,
        forward_parts,
        gateup_grad,
        log_total,
        residual,
        cosine,
        sine,
        d_normed_two,
        grad_down,
    ) = fore(
        tokens,
        gain_lines,
        block_order,
        sequence_lengths,
        attn_input,
        attn_output,
        gate_up,
        down_weight,
        output_cotangent,
        data_count,
        context_count,
    )
    mixed, token_gradient, grad_gains, grad_output, grad_input, grad_gateup = back(
        tokens,
        output_cotangent,
        residual,
        d_normed_two,
        gain_lines,
        block_order,
        sequence_lengths,
        cosine,
        sine,
        log_total,
        normed_one,
        input_part,
        output_all,
        raw,
        flat_parts,
        forward_parts,
        gateup_grad,
        4,
    )
    states = (
        attn_input,
        input_moment,
        input_square,
        attn_output,
        output_moment,
        output_square,
        gate_up,
        gateup_moment,
        gateup_square,
        down_weight,
        down_moment,
        down_square,
        gain_lines,
        gains_moment.reshape(gain_lines.shape),
        gains_square.reshape(gain_lines.shape),
    )
    results = update(
        grad_gateup, grad_input, grad_output, grad_down, grad_gains, states, data_count
    )
    return (
        mixed,
        token_gradient,
        *results[:12],
        *(result.reshape(-1) for result in results[12:]),
    )


def solution(mesh):
    in_specs = (
        P(("dp", "cp"), None),
        P(("dp", "cp"), None),
        P("dp", None),
        P("dp", None),
        P(("dp", "cp"), None),
        P(("dp", "cp"), None),
        P(("dp", "cp"), None),
        P(("dp", "cp"), None),
        P(("dp", "cp"), None),
        P(("dp", "cp"), None),
        P(("dp", "cp"), None),
        P(("dp", "cp"), None),
        P(("dp", "cp"), None),
        P(("dp", "cp"), None),
        P(("dp", "cp"), None),
        P(("dp", "cp"), None),
        P(),
        P(),
        P(),
    )
    out_specs = (
        P(("dp", "cp"), None),
        P(("dp", "cp"), None),
        P(("dp", "cp"), None),
        P(("dp", "cp"), None),
        P(("dp", "cp"), None),
        P(("dp", "cp"), None),
        P(("dp", "cp"), None),
        P(("dp", "cp"), None),
        P(("dp", "cp"), None),
        P(("dp", "cp"), None),
        P(("dp", "cp"), None),
        P(("dp", "cp"), None),
        P(("dp", "cp"), None),
        P(("dp", "cp"), None),
        P(),
        P(),
        P(),
    )
    sizes = (mesh.shape["dp"], mesh.shape["cp"])
    body = on_device_split if sizes == (4, KV_HEADS) else on_device
    return jax.shard_map(
        body, mesh=mesh, in_specs=in_specs, out_specs=out_specs, check_vma=False
    )
```

```python
import functools
import math

import jax
import jax.numpy as jnp
from jax import lax
from jax.experimental import pallas as pl
from jax.experimental.pallas import tpu as pltpu
from jax.sharding import PartitionSpec as P

HEADS = 24
KV_HEADS = 8
HEAD_DIM = 64
FF = 6912
STEP = 10


norm_eps = 1e-05
rope_base = 1000000.0
beta_one = 0.9
beta_two = 0.95
adam_eps = 1e-08
rate_input = 0.06
rate_output = 0.9
rate_gateup = 0.06
rate_down = 0.03
rate_gains = 0.5
weight_decay = 0.1
masked_score = -1e30


def rope_tables(offsets):
    half_dim = HEAD_DIM // 2
    freqs = jnp.exp(
        jnp.arange(half_dim, dtype=jnp.float32) * (-2.0 * math.log(rope_base) / HEAD_DIM)
    )
    angles = offsets.astype(jnp.float32)[:, None] * freqs[None, :]
    return (jnp.cos(angles), jnp.sin(angles))


def rotate(values, cosine, sine):
    half_dim = HEAD_DIM // 2
    first_half = values[..., :half_dim]
    second_half = values[..., half_dim:]
    cos_wide = cosine[:, None, :]
    sin_wide = sine[:, None, :]
    return jnp.concatenate(
        [
            first_half * cos_wide - second_half * sin_wide,
            second_half * cos_wide + first_half * sin_wide,
        ],
        axis=-1,
    )


def locate(positions, lengths):
    seq_ends = jnp.cumsum(lengths)
    starts = seq_ends - lengths
    doc_index = jnp.sum((positions[:, None] >= seq_ends[None, :]).astype(jnp.int32), axis=1)
    picked = (doc_index[:, None] == jnp.arange(lengths.shape[0], dtype=jnp.int32)[None, :]).astype(
        jnp.int32
    )
    return (doc_index, positions - jnp.sum(picked * starts[None, :], axis=1))


def rms_parts(values):
    inverse = lax.rsqrt(jnp.mean(values * values, axis=-1, keepdims=True) + norm_eps)
    return (values * inverse, inverse)


def norm_back(d_normed, normal_hat, inverse):
    return inverse * (
        d_normed - normal_hat * jnp.mean(d_normed * normal_hat, axis=-1, keepdims=True)
    )


def contract_rows(left, right):
    return lax.dot_general(
        left, right, (((0,), (0,)), ((), ())), preferred_element_type=jnp.float32
    )


def contract_cols(left, right):
    return lax.dot_general(
        left, right, (((1,), (1,)), ((), ())), preferred_element_type=jnp.float32
    )


def owner_order(values, data_count, context_count):
    lead = values.shape[0]
    each = values.shape[1] // (data_count * context_count)
    return (
        values.reshape(lead, data_count, context_count, each)
        .transpose(0, 2, 1, 3)
        .reshape(lead, values.shape[1])
    )


def adam_update(weight, first_moment, second_moment, gradient, rate, decay):
    first_moment = beta_one * first_moment + (1.0 - beta_one) * gradient
    second_moment = beta_two * second_moment + (1.0 - beta_two) * gradient * gradient
    first_fix = 1.0 - beta_one**STEP
    second_fix = 1.0 - beta_two**STEP
    direction = first_moment / first_fix / (jnp.sqrt(second_moment / second_fix) + adam_eps)
    return (weight - rate * (direction + decay * weight), first_moment, second_moment)


def on_device(
    tokens,
    output_cotangent,
    sequence_lengths,
    block_order,
    attn_input,
    input_moment,
    input_square,
    attn_output,
    output_moment,
    output_square,
    gate_up,
    gateup_moment,
    gateup_square,
    down_weight,
    down_moment,
    down_square,
    norm_gains,
    gains_moment,
    gains_square,
):
    row_count = tokens.shape[0]
    model_width = tokens.shape[1]
    q_width = HEADS * HEAD_DIM
    kv_width = KV_HEADS * HEAD_DIM
    proj_width = q_width + 2 * kv_width
    head_groups = HEADS // KV_HEADS
    score_scale = HEAD_DIM ** (-0.5)
    gain_one = norm_gains[:model_width]
    gain_two = norm_gains[model_width : 2 * model_width]
    gain_query = norm_gains[2 * model_width : 2 * model_width + HEAD_DIM]
    gain_key = norm_gains[2 * model_width + HEAD_DIM :]
    seq_lens = sequence_lengths[0]
    order_row = block_order[0]
    context_count = lax.axis_size("cp")
    data_count = lax.axis_size("dp")
    own_slot = lax.axis_index("cp")
    offsets = jnp.arange(row_count, dtype=jnp.int32)
    own_block = jnp.sum(
        jnp.where(jnp.arange(context_count, dtype=jnp.int32) == own_slot, order_row, 0)
    )
    positions = own_block * row_count + offsets
    key_positions = (order_row[:, None] * row_count + offsets[None, :]).reshape(
        context_count * row_count
    )
    doc_index, seq_offset = locate(positions, seq_lens)
    key_doc = locate(key_positions, seq_lens)[0]
    cosine, sine = rope_tables(seq_offset)
    input_bf = attn_input.astype(jnp.bfloat16)
    output_bf = attn_output.astype(jnp.bfloat16)
    gateup_bf = gate_up.astype(jnp.bfloat16)
    down_bf = down_weight.astype(jnp.bfloat16)
    input_all, output_all = (
        lax.all_gather(input_bf, ("dp", "cp"), axis=0, tiled=True),
        lax.all_gather(output_bf, ("dp", "cp"), axis=0, tiled=True),
    )
    x_float = tokens.astype(jnp.float32)
    hat_one, inv_one = rms_parts(x_float)
    normed_one = (hat_one * gain_one).astype(jnp.bfloat16)
    projected = jnp.dot(normed_one, input_all, preferred_element_type=jnp.float32)
    query_raw = projected[:, :q_width].reshape(row_count, HEADS, HEAD_DIM)
    key_raw = projected[:, q_width : q_width + kv_width].reshape(row_count, KV_HEADS, HEAD_DIM)
    value_raw = projected[:, q_width + kv_width :]
    hat_query, inv_query = rms_parts(query_raw)
    hat_key, inv_key = rms_parts(key_raw)
    queries = rotate(hat_query * gain_query, cosine, sine).astype(jnp.bfloat16)
    key_rot = rotate(hat_key * gain_key, cosine, sine)
    key_value = jnp.concatenate([key_rot.reshape(row_count, kv_width), value_raw], axis=1).astype(
        jnp.bfloat16
    )
    kv_all = lax.all_gather(key_value, "cp", axis=0, tiled=True)
    total_keys = kv_all.shape[0]
    key_span = min(512, total_keys)
    block_count = total_keys // key_span
    kv_blocks = kv_all.reshape(block_count, key_span, 2 * kv_width)
    pos_blocks = key_positions.reshape(block_count, key_span)
    doc_blocks = key_doc.reshape(block_count, key_span)
    query_group = queries.reshape(row_count, KV_HEADS, head_groups, HEAD_DIM)

    def block_scores(kv_block, key_pos, key_docs):
        key_block = kv_block[:, :kv_width].reshape(key_span, KV_HEADS, HEAD_DIM)
        value_block = kv_block[:, kv_width:].reshape(key_span, KV_HEADS, HEAD_DIM)
        scores = (
            jnp.einsum("qhgd,khd->hgqk", query_group, key_block, preferred_element_type=jnp.float32)
            * score_scale
        )
        allowed = (doc_index[:, None] == key_docs[None, :]) & (
            key_pos[None, :] <= positions[:, None]
        )
        return (key_block, value_block, jnp.where(allowed, scores, masked_score), allowed)

    def forward_block(carry, items):
        run_max, run_total, run_sum = carry
        key_block, value_block, scores, allowed = block_scores(*items)
        new_max = jnp.maximum(run_max, jnp.max(scores, axis=-1))
        weights = jnp.where(allowed, jnp.exp(scores - new_max[..., None]), 0.0)
        factor = jnp.exp(run_max - new_max)
        run_total = run_total * factor + jnp.sum(weights, axis=-1)
        run_sum = run_sum * factor[..., None] + jnp.einsum(
            "hgqk,khd->hgqd",
            weights.astype(jnp.bfloat16),
            value_block,
            preferred_element_type=jnp.float32,
        )
        return ((new_max, run_total, run_sum), None)

    start_state = (
        jnp.full((KV_HEADS, head_groups, row_count), masked_score, jnp.float32),
        jnp.zeros((KV_HEADS, head_groups, row_count), jnp.float32),
        jnp.zeros((KV_HEADS, head_groups, row_count, HEAD_DIM), jnp.float32),
    )
    (run_max, run_total, run_sum), unused = lax.scan(
        forward_block, start_state, (kv_blocks, pos_blocks, doc_blocks)
    )
    attended = run_sum / run_total[..., None]
    log_total = run_max + jnp.log(run_total)
    attn_flat = attended.transpose(2, 0, 1, 3).reshape(row_count, q_width).astype(jnp.bfloat16)
    residual = x_float + jnp.dot(attn_flat, output_all, preferred_element_type=jnp.float32)
    hat_two, inv_two = rms_parts(residual)
    normed_two = (hat_two * gain_two).astype(jnp.bfloat16)
    columns = normed_two
    gate_both = jnp.dot(
        columns,
        lax.all_gather(gateup_bf, ("dp", "cp"), axis=0, tiled=True),
        preferred_element_type=jnp.float32,
    )
    gate_part = gate_both[:, :FF]
    up_part = gate_both[:, FF:]
    gate_sig = jax.nn.sigmoid(gate_part)
    gate_act = gate_part * gate_sig
    hidden = (gate_act * up_part).astype(jnp.bfloat16)
    columns = hidden
    ff_result = jnp.dot(
        columns,
        lax.all_gather(down_bf, ("dp", "cp"), axis=0, tiled=True),
        preferred_element_type=jnp.float32,
    )
    mixed = (residual + ff_result).astype(jnp.bfloat16)
    d_hidden = contract_cols(
        output_cotangent, lax.all_gather(down_bf, ("dp", "cp"), axis=0, tiled=True)
    )
    d_gate = d_hidden * up_part * (gate_sig * (1.0 + gate_part * (1.0 - gate_sig)))
    d_up = d_hidden * gate_act
    d_gate_both = jnp.concatenate([d_gate, d_up], axis=1).astype(jnp.bfloat16)
    d_normed_two = contract_cols(
        d_gate_both, lax.all_gather(gateup_bf, ("dp", "cp"), axis=0, tiled=True)
    )
    grad_gain_two = jnp.sum(d_normed_two * hat_two, axis=0)
    d_residual = output_cotangent.astype(jnp.float32) + norm_back(
        d_normed_two * gain_two, hat_two, inv_two
    )
    d_branch = d_residual.astype(jnp.bfloat16)
    input_back, output_back = (input_all, output_all)
    d_flat = contract_cols(d_branch, output_back).astype(jnp.bfloat16)
    d_attended = d_flat.reshape(row_count, KV_HEADS, head_groups, HEAD_DIM).transpose(1, 2, 0, 3)
    delta = jnp.sum(d_attended.astype(jnp.float32) * attended, axis=-1)

    def backward_block(d_query_sum, items):
        key_block, value_block, scores, allowed = block_scores(*items)
        probs = jnp.where(allowed, jnp.exp(scores - log_total[..., None]), 0.0)
        d_probs = jnp.einsum(
            "hgqd,khd->hgqk", d_attended, value_block, preferred_element_type=jnp.float32
        )
        d_scores = (probs * (d_probs - delta[..., None])).astype(jnp.bfloat16)
        d_query_sum = (
            d_query_sum
            + jnp.einsum("hgqk,khd->hgqd", d_scores, key_block, preferred_element_type=jnp.float32)
            * score_scale
        )
        d_keys = (
            jnp.einsum("hgqk,qhgd->khd", d_scores, query_group, preferred_element_type=jnp.float32)
            * score_scale
        )
        d_values = jnp.einsum(
            "hgqk,hgqd->khd",
            probs.astype(jnp.bfloat16),
            d_attended,
            preferred_element_type=jnp.float32,
        )
        return (
            d_query_sum,
            jnp.concatenate(
                [d_keys.reshape(key_span, kv_width), d_values.reshape(key_span, kv_width)], axis=1
            ),
        )

    d_query_sum, d_kv_blocks = lax.scan(
        backward_block,
        jnp.zeros((KV_HEADS, head_groups, row_count, HEAD_DIM), jnp.float32),
        (kv_blocks, pos_blocks, doc_blocks),
    )
    d_kv = lax.psum_scatter(
        d_kv_blocks.reshape(total_keys, 2 * kv_width).astype(jnp.bfloat16),
        "cp",
        scatter_dimension=0,
        tiled=True,
    ).astype(jnp.float32)
    d_query_rot = rotate(
        d_query_sum.transpose(2, 0, 1, 3).reshape(row_count, HEADS, HEAD_DIM), cosine, -sine
    )
    grad_gain_query = jnp.sum(d_query_rot * hat_query, axis=(0, 1))
    d_query_raw = norm_back(d_query_rot * gain_query, hat_query, inv_query)
    d_key_rot = rotate(d_kv[:, :kv_width].reshape(row_count, KV_HEADS, HEAD_DIM), cosine, -sine)
    grad_gain_key = jnp.sum(d_key_rot * hat_key, axis=(0, 1))
    d_key_raw = norm_back(d_key_rot * gain_key, hat_key, inv_key)
    d_projected = jnp.concatenate(
        [
            d_query_raw.reshape(row_count, q_width),
            d_key_raw.reshape(row_count, kv_width),
            d_kv[:, kv_width:],
        ],
        axis=1,
    ).astype(jnp.bfloat16)
    d_normed_one = contract_cols(d_projected, input_back)
    grad_gain_one = jnp.sum(d_normed_one * hat_one, axis=0)
    token_gradient = d_residual + norm_back(d_normed_one * gain_one, hat_one, inv_one)

    def make_wide(first_src, attn_src, second_src):

        def wide_terms(row_start, row_total):
            return jnp.concatenate(
                [
                    contract_rows(first_src, d_projected),
                    contract_rows(attn_src, d_branch),
                    contract_rows(second_src, d_gate_both),
                ],
                axis=1,
            )

        return wide_terms

    def make_down(hidden_src):

        def down_terms(row_start, row_total):
            return contract_rows(hidden_src, output_cotangent)

        return down_terms

    shard_rows = attn_input.shape[0]
    down_rows = down_weight.shape[0]
    wide_fn = make_wide(
        owner_order(normed_one, data_count, context_count),
        owner_order(attn_flat, data_count, context_count),
        owner_order(normed_two, data_count, context_count),
    )
    down_fn = make_down(owner_order(hidden, data_count, context_count))
    group_wide = lax.psum_scatter(
        wide_fn(jnp.int32(0), lax.axis_size("cp") * (shard_rows * data_count)).astype(jnp.bfloat16),
        "cp",
        scatter_dimension=0,
        tiled=True,
    )
    group_down = lax.psum_scatter(
        down_fn(jnp.int32(0), lax.axis_size("cp") * (down_rows * data_count)).astype(jnp.bfloat16),
        "cp",
        scatter_dimension=0,
        tiled=True,
    )
    wide_grads, down_grads = (
        lax.psum_scatter(group_wide, "dp", scatter_dimension=0, tiled=True).astype(jnp.float32),
        lax.psum_scatter(group_down, "dp", scatter_dimension=0, tiled=True).astype(jnp.float32),
    )
    gain_grads = lax.psum(
        jnp.concatenate([grad_gain_one, grad_gain_two, grad_gain_query, grad_gain_key]),
        ("dp", "cp"),
    )
    grad_input = wide_grads[:, :proj_width]
    grad_output = wide_grads[:, proj_width : proj_width + model_width]
    grad_gateup = wide_grads[:, proj_width + model_width :]
    input_next, input_moment_next, input_square_next = adam_update(
        attn_input, input_moment, input_square, grad_input, rate_input, weight_decay
    )
    output_next, output_moment_next, output_square_next = adam_update(
        attn_output, output_moment, output_square, grad_output, rate_output, weight_decay
    )
    gateup_next, gateup_moment_next, gateup_square_next = adam_update(
        gate_up, gateup_moment, gateup_square, grad_gateup, rate_gateup, weight_decay
    )
    down_next, down_moment_next, down_square_next = adam_update(
        down_weight, down_moment, down_square, down_grads, rate_down, weight_decay
    )
    gains_next, gains_moment_next, gains_square_next = adam_update(
        norm_gains, gains_moment, gains_square, gain_grads, rate_gains, 0.0
    )
    return (
        mixed,
        token_gradient,
        input_next,
        input_moment_next,
        input_square_next,
        output_next,
        output_moment_next,
        output_square_next,
        gateup_next,
        gateup_moment_next,
        gateup_square_next,
        down_next,
        down_moment_next,
        down_square_next,
        gains_next,
        gains_moment_next,
        gains_square_next,
    )


MESH = pl.DeviceIdType.MESH


def place():
    dp = lax.axis_index("dp")
    cp = lax.axis_index("cp")
    return dp, cp, cp // 2, cp % 2


def greet(targets):
    barrier = pltpu.get_barrier_semaphore()
    for target in targets:
        pl.semaphore_signal(barrier, inc=1, device_id=target, device_id_type=MESH)
    pl.semaphore_wait(barrier, len(targets))


def send(source, target, send_sem, recv_sem, device):
    return pltpu.make_async_remote_copy(
        src_ref=source,
        dst_ref=target,
        send_sem=send_sem,
        recv_sem=recv_sem,
        device_id=device,
        device_id_type=MESH,
    )


class LineGather:
    def __init__(self, own_ref, all_ref, sems, where, depth, both=True):
        self.own, self.where, self.depth, self.both = own_ref, where, depth, both
        self.slot = all_ref if callable(all_ref) else lambda slot: all_ref.at[slot]
        self.right, self.left, self.sib, self.recv, self.local = sems

    @staticmethod
    def scratch(depth):
        return [pltpu.SemaphoreType.DMA((2 * depth,))] * 4 + [pltpu.SemaphoreType.DMA]

    def copy(self, kind, slot, source):
        dp, cp, z, core = self.where
        device = {"right": (dp, cp + 2), "left": (dp, cp - 2), "sib": (dp, cp ^ 1)}[kind]
        sem = {"right": self.right, "left": self.left, "sib": self.sib}[kind]
        return send(source, self.slot(slot), sem.at[slot], self.recv.at[slot], device)

    def keep(self):
        return pltpu.make_async_copy(self.own, self.slot(self.where[1]), self.local)

    def start(self):
        dp, cp, z, core = self.where

        @pl.when(z < self.depth - 1)
        def _():
            self.copy("right", cp, self.own).start()

        @pl.when(z > 0)
        def _():
            self.copy("left", cp, self.own).start()

        if self.both:
            self.copy("sib", cp, self.own).start()
        self.keep().start()

    def step(self, far):
        dp, cp, z, core = self.where

        @pl.when(z >= far)
        def _():
            slot = cp - 2 * far
            self.copy("right", slot, self.own).wait_recv()

            @pl.when(z < self.depth - 1)
            def _():
                self.copy("right", slot, self.slot(slot)).start()

            if self.both:
                self.copy("sib", slot, self.slot(slot)).start()

        @pl.when(z + far < self.depth)
        def _():
            slot = cp + 2 * far
            self.copy("left", slot, self.own).wait_recv()

            @pl.when(z > 0)
            def _():
                self.copy("left", slot, self.slot(slot)).start()

            if self.both:
                self.copy("sib", slot, self.slot(slot)).start()

    def arrive(self, spot):
        self.copy("sib", 1 - self.where[3] + 2 * spot, self.own).wait_recv()

    def finish(self, arrived=False):
        dp, cp, z, core = self.where
        if self.both and not arrived:
            for spot in range(self.depth):
                self.arrive(spot)
        if not arrived:
            self.keep().wait()
        for spot in range(self.depth):
            slot = 2 * spot + core
            if self.both:
                self.copy("sib", slot, self.own).wait_send()

            @pl.when((spot <= z) & (z < self.depth - 1))
            def _():
                self.copy("right", slot, self.own).wait_send()

            @pl.when((spot >= z) & (z > 0))
            def _():
                self.copy("left", slot, self.own).wait_send()


class HalvedGather:
    def __init__(self, own_ref, all_ref, sems, where, depth):
        half = own_ref.shape[0] // 2
        count = len(sems) // 2

        def line(index):
            rows = pl.ds(index * half, half)
            return LineGather(
                own_ref.at[rows],
                lambda slot: all_ref.at[slot, rows],
                sems[index * count : (index + 1) * count],
                where,
                depth,
            )

        self.lines = [line(0), line(1)]

    def start(self):
        for line in self.lines:
            line.start()

    def step(self, far):
        for line in self.lines:
            line.step(far)

    def arrive(self, spot):
        for line in self.lines:
            line.arrive(spot)

    def keep_wait(self):
        for line in self.lines:
            line.keep().wait()

    def finish(self, arrived=False):
        for line in self.lines:
            line.finish(arrived)


class Swap:
    def __init__(self, source_ref, target_ref, sems, where, count):
        self.source, self.where, self.count = source_ref, where, count
        self.slot = target_ref if callable(target_ref) else lambda slot: target_ref.at[slot]
        self.origin = source_ref if callable(source_ref) else lambda slot: source_ref.at[slot]
        self.sent, self.recv, self.local = sems

    @staticmethod
    def scratch(count):
        return [pltpu.SemaphoreType.DMA((count,))] * 2 + [pltpu.SemaphoreType.DMA]

    def copy(self, peer):
        dp, cp, z, core = self.where
        return send(
            self.origin(peer),
            self.slot(cp),
            self.sent.at[peer],
            self.recv.at[cp],
            (dp, peer),
        )

    def keep(self):
        cp = self.where[1]
        return pltpu.make_async_copy(self.origin(cp), self.slot(cp), self.local)

    def start(self):
        cp = self.where[1]
        for turn in range(self.count - 1, 0, -1):
            self.copy(cp ^ turn).start()
        self.keep().start()

    def arrive(self, peer):
        dp, cp, z, core = self.where
        send(
            self.origin(peer),
            self.slot(peer),
            self.sent.at[peer],
            self.recv.at[peer],
            (dp, peer),
        ).wait_recv()

    def finish_recv(self):
        cp = self.where[1]
        for turn in range(1, self.count):
            self.arrive(cp ^ turn)
        self.keep().wait()

    def finish_send(self):
        cp = self.where[1]
        for turn in range(1, self.count):
            self.copy(cp ^ turn).wait_send()


class RingSpread:
    def __init__(self, block, half, sems, where):
        self.block, self.half, self.where = block, half, where
        self.sent, self.recv = sems

    @staticmethod
    def scratch():
        return [pltpu.SemaphoreType.DMA((4,))] * 2

    def copy(self, kind, mine):
        dp, cp, z, core = self.where
        turn = (1, 2, 2, 1)[kind]
        if kind < 2:
            part = self.block(dp if mine else dp ^ turn)
        else:
            part = self.half(dp ^ (3 - turn) if mine else dp ^ 3, kind - 2)
        return send(part, part, self.sent.at[kind], self.recv.at[kind], (dp ^ turn, cp))

    def start(self):
        self.copy(0, True).start()
        self.copy(1, True).start()

    def forward(self):
        self.copy(0, False).wait_recv()
        self.copy(2, True).start()
        self.copy(1, False).wait_recv()
        self.copy(3, True).start()

    def finish(self):
        self.copy(2, False).wait_recv()
        self.copy(3, False).wait_recv()
        for kind in range(4):
            self.copy(kind, True).wait_send()


def turn_heads(values, cosine, sine):
    half = values.shape[0] // 2
    first, second = values[:half], values[half:]
    return jnp.concatenate([first * cosine - second * sine, second * cosine + first * sine], axis=0)


def head_hat(values):
    inverse = lax.rsqrt(jnp.mean(values * values, axis=0, keepdims=True) + norm_eps)
    return values * inverse, inverse


def lay_places(order_ref, lengths_ref, rows, count):
    spots = [order_ref[0, index] * rows for index in range(count)]
    lanes = lax.broadcasted_iota(jnp.int32, (1, rows), 1)
    lines = lax.broadcasted_iota(jnp.int32, (rows, 1), 0)
    place_row = jnp.concatenate([spot + lanes for spot in spots], axis=1)
    place_column = jnp.concatenate([spot + lines for spot in spots], axis=0)
    starts = jnp.zeros_like(place_row)
    begin = jnp.int32(0)
    for index in range(lengths_ref.shape[1] - 1):
        begin = begin + lengths_ref[0, index]
        starts = jnp.where(place_row >= begin, begin, starts)
    return place_row, place_column, starts


def to_column(row):
    size = row.shape[1]
    down = lax.broadcasted_iota(jnp.int32, (size, size), 0)
    across = lax.broadcasted_iota(jnp.int32, (size, size), 1)
    return jnp.sum(jnp.where(down == across, row, 0.0), axis=1, keepdims=True)


def split_gains(gains_ref, width):
    lines = width // gains_ref.shape[1]

    def row(begin, end):
        return jnp.concatenate([gains_ref[line : line + 1] for line in range(begin, end)], axis=1)

    gain_one, gain_two = row(0, lines), row(lines, 2 * lines)
    gain_heads = row(2 * lines, gains_ref.shape[0])
    gain_query = to_column(gain_heads[:, :HEAD_DIM])
    gain_key = to_column(gain_heads[:, HEAD_DIM:])
    return gain_one, gain_two, gain_query, gain_key


def score_block(keys, queries, key_place, query_place, query_start):
    scores = jnp.dot(keys, queries, preferred_element_type=jnp.float32) * HEAD_DIM ** (-0.5)
    allowed = (key_place <= query_place) & (key_place >= query_start)
    return jnp.where(allowed, scores, masked_score), allowed


class LineScatter:
    cuts = 2

    def __init__(self, part_ref, out_ref, scratch, where, depth):
        self.part, self.out, self.where, self.depth = part_ref, out_ref, where, depth
        self.sib, self.line = scratch[:2]
        (
            self.sib_sent,
            self.sib_recv,
            self.right_sent,
            self.right_recv,
            self.left_sent,
            self.left_recv,
        ) = scratch[2:]
        self.size = part_ref.shape[1] // self.cuts

    @classmethod
    def scratch(cls, depth, rows, width):
        return [
            pltpu.VMEM((depth, rows, width), jnp.bfloat16),
            pltpu.VMEM((depth + 1, rows, width), jnp.bfloat16),
        ] + [pltpu.SemaphoreType.DMA((depth,))] * 2 + [
            pltpu.SemaphoreType.DMA((depth * cls.cuts,))
        ] * 4

    def pair(self, spot):
        dp, cp, z, core = self.where
        return send(
            self.part.at[2 * spot + 1 - core],
            self.sib.at[spot],
            self.sib_sent.at[spot],
            self.sib_recv.at[spot],
            (dp, cp ^ 1),
        )

    def rows(self, cut):
        return pl.ds(cut * self.size, self.size)

    def hop_right(self, spot, cut):
        dp, cp, z, core = self.where
        index = spot * self.cuts + cut
        return send(
            self.part.at[2 * spot + core, self.rows(cut)],
            self.line.at[spot + 1, self.rows(cut)],
            self.right_sent.at[index],
            self.right_recv.at[index],
            (dp, cp + 2),
        )

    def hop_left(self, spot, cut):
        dp, cp, z, core = self.where
        index = spot * self.cuts + cut
        return send(
            self.part.at[2 * spot + core, self.rows(cut)],
            self.line.at[spot, self.rows(cut)],
            self.left_sent.at[index],
            self.left_recv.at[index],
            (dp, cp - 2),
        )

    def order(self):
        spots = []
        for turn in range(self.depth):
            spots += [self.depth - 1 - turn, turn]
        return list(dict.fromkeys(spots))

    def chip_sum(self, spot, cut):
        rows = self.rows(cut)
        mine = self.part[2 * spot + self.where[3], rows].astype(jnp.float32)
        return mine + self.sib[spot, rows].astype(jnp.float32)

    def pass_on(self, spot, cut, arrived, slot, hop):
        total = self.chip_sum(spot, cut)
        if arrived is not None:
            arrived.wait_recv()
            total = total + self.line[slot, self.rows(cut)].astype(jnp.float32)
        self.part[2 * spot + self.where[3], self.rows(cut)] = total.astype(jnp.bfloat16)
        hop.start()

    def forward(self, spot, cuts=None):
        z, core = self.where[2], self.where[3]
        cuts = range(self.cuts) if cuts is None else cuts
        if 0 in cuts:

            @pl.when(z != spot)
            def _():
                self.pair(spot).wait_recv()

        for cut in cuts:
            right, left = self.hop_right(spot, cut), self.hop_left(spot, cut)

            @pl.when((z < spot) & (z > 0))
            def _():
                self.pass_on(spot, cut, right, spot + 1, right)

            @pl.when((z < spot) & (z == 0))
            def _():
                self.pass_on(spot, cut, None, None, right)

            @pl.when((z > spot) & (z < self.depth - 1))
            def _():
                self.pass_on(spot, cut, left, spot, left)

            @pl.when((z > spot) & (z == self.depth - 1))
            def _():
                self.pass_on(spot, cut, None, None, left)

    def finish(self):
        z = self.where[2]
        self.pair(z).wait_recv()
        for cut in range(self.cuts):
            rows = self.rows(cut)
            self.out[rows] = self.chip_sum(z, cut)

            @pl.when(z > 0)
            def _():
                self.hop_right(z, cut).wait_recv()
                self.out[rows] += self.line[z + 1, rows].astype(jnp.float32)

            @pl.when(z < self.depth - 1)
            def _():
                self.hop_left(z, cut).wait_recv()
                self.out[rows] += self.line[z, rows].astype(jnp.float32)

        for spot in range(self.depth):
            self.pair(spot).wait_send()

            @pl.when(z < spot)
            def _():
                for cut in range(self.cuts):
                    self.hop_right(spot, cut).wait_send()

            @pl.when(z > spot)
            def _():
                for cut in range(self.cuts):
                    self.hop_left(spot, cut).wait_send()


class RingReduce:
    def __init__(self, part, work, scratch, where):
        self.part, self.work, self.where = part, work, where
        self.from_x, self.from_y, self.x_sent, self.x_recv, self.y_sent, self.y_recv = scratch

    @staticmethod
    def scratch(*half):
        return [pltpu.VMEM((3,) + half, jnp.bfloat16)] * 2 + [pltpu.SemaphoreType.DMA((3,))] * 4

    def to_x(self, kind):
        dp, cp, z, core = self.where
        source = (
            self.part(dp ^ 3, 0) if kind == 0 else self.part(dp ^ 1, 0) if kind == 1 else self.work(1)
        )
        return send(
            source, self.from_x.at[kind], self.x_sent.at[kind], self.x_recv.at[kind], (dp ^ 1, cp)
        )

    def to_y(self, kind):
        dp, cp, z, core = self.where
        source = (
            self.part(dp ^ 3, 1) if kind == 0 else self.part(dp ^ 2, 1) if kind == 1 else self.work(0)
        )
        return send(
            source, self.from_y.at[kind], self.y_sent.at[kind], self.y_recv.at[kind], (dp ^ 2, cp)
        )

    def start(self):
        for kind in range(2):
            self.to_x(kind).start()
            self.to_y(kind).start()

    def add(self, index, *arrived):
        target = self.work(index)
        total = target[...].astype(jnp.float32)
        for block in arrived:
            total = total + block[...].astype(jnp.float32)
        target[...] = total.astype(jnp.bfloat16)

    def middle(self):
        self.to_x(0).wait_recv()
        self.add(0, self.from_x.at[0])
        self.to_y(2).start()
        self.to_y(0).wait_recv()
        self.add(1, self.from_y.at[0])
        self.to_x(2).start()

    def finish(self):
        for kind in (1, 2):
            self.to_x(kind).wait_recv()
            self.to_y(kind).wait_recv()
        self.add(2, self.from_x.at[1], self.from_y.at[2])
        self.add(3, self.from_y.at[1], self.from_x.at[2])

    def finish_send(self):
        for kind in range(3):
            self.to_x(kind).wait_send()
            self.to_y(kind).wait_send()

    def places(self):
        dp = self.where[0]
        return [(dp ^ 2, 0), (dp ^ 1, 1), (dp, 0), (dp, 1)]


def far_first(turn, z, depth):
    order = []
    for spot in range(depth):
        rest = sorted((other for other in range(depth) if other != spot), key=lambda other: (-abs(other - spot), other))
        ends = [other for other in rest if other in (0, depth - 1)]
        order.append(ends + [other for other in rest if other not in ends] + [spot])
    picked = 0
    for step in range(depth):
        for spot in range(depth):
            picked = picked + order[spot][step] * ((turn == step) & (z == spot)).astype(jnp.int32)
    return picked


def near_first(turn, z, depth):
    picked = 0
    for step in range(depth):
        for spot in range(depth):
            order = sorted(range(depth), key=lambda other: (abs(other - spot), other))
            picked = picked + order[step] * ((turn == step) & (z == spot)).astype(jnp.int32)
    return picked


def fore_kernel(
    tile,
    tokens_ref,
    gains_ref,
    order_ref,
    lengths_ref,
    input_ref,
    output_ref,
    gateup_ref,
    down_ref,
    cotangent_own,
    normed_one_out,
    input_out,
    output_out,
    raw_out,
    flat_out,
    forward_out,
    gateup_out,
    total_out,
    residual_out,
    cosine_ref,
    sine_ref,
    d_normed_out,
    down_out,
    input_send,
    output_own,
    gate_send,
    up_send,
    key_place_ref,
    query_place_ref,
    query_start_ref,
    normed_one,
    own_one,
    inputs,
    outputs,
    raw,
    queries,
    keys_up,
    values,
    flat_send,
    flat_recv,
    own_two,
    normed,
    cotangent,
    gate_weight,
    up_weight,
    down_weight,
    hidden_up,
    d_gates,
    d_ups,
    down_grad,
    out_sems,
    *sems,
):
    where = place()
    dp, cp, z, core = where
    context_count = normed_one.shape[0]
    depth = context_count // 2
    rows = tokens_ref.shape[0]
    width = tokens_ref.shape[1]
    q_each = HEADS // KV_HEADS * HEAD_DIM
    take = iter(range(len(sems)))

    def some(count):
        return [sems[next(take)] for _ in range(count)]

    kv_each = HEAD_DIM
    for head in range(context_count):
        for start, begin, size in (
            (head * q_each, 0, q_each),
            (HEADS * HEAD_DIM + head * kv_each, q_each, kv_each),
            ((HEADS + KV_HEADS) * HEAD_DIM + head * kv_each, q_each + kv_each, kv_each),
        ):
            input_send[head, :, begin : begin + size] = input_ref[:, start : start + size].astype(
                jnp.bfloat16
            )
    hidden = gate_send.shape[2]
    piece = hidden // inputs.shape[0]
    half_width = gateup_ref.shape[1] // 2

    def cut_columns(target, base):
        for head in range(context_count):
            target[head] = jnp.concatenate(
                [
                    gateup_ref[:, pl.ds(base + (group * context_count + head) * piece, piece)]
                    for group in range(inputs.shape[0])
                ],
                axis=1,
            ).astype(jnp.bfloat16)

    cut_columns(gate_send, 0)
    greet([(dp, cp ^ turn) for turn in range(1, context_count)] + [(dp ^ 1, cp), (dp ^ 2, cp)])
    token_line = HalvedGather(own_one, normed_one, some(10), where, depth)
    second_line = HalvedGather(own_two, normed, some(10), where, depth)
    cotangent_line = LineGather(cotangent_own, cotangent, some(5), where, depth)
    output_line = LineGather(
        output_own, lambda slot: outputs.at[dp, slot // 2, core], some(5), where, depth, False
    )
    input_swap = Swap(input_send, inputs.at[dp], some(3), where, context_count)
    shard = input_send.shape[1]

    each_rows = context_count * shard

    def weight_slot(target):
        return lambda slot: target.at[
            pl.ds(pl.multiple_of(dp * each_rows + slot * shard, 16), shard)
        ]

    gate_swap = Swap(gate_send, weight_slot(gate_weight), some(3), where, context_count)
    up_swap = Swap(up_send, weight_slot(up_weight), some(3), where, context_count)
    flat_swap = Swap(flat_send, flat_recv, some(3), where, context_count)
    input_ring = RingSpread(
        lambda d: inputs.at[d],
        lambda d, h: inputs.at[d, pl.ds(h * (context_count // 2), context_count // 2)],
        some(2),
        where,
    )
    output_ring = RingSpread(
        lambda d: outputs.at[d, :, core],
        lambda d, h: outputs.at[d, pl.ds(h * (depth // 2), depth // 2), core],
        some(2),
        where,
    )
    half_rows = each_rows // 2

    def weight_ring(target):
        return RingSpread(
            lambda d: target.at[pl.ds(pl.multiple_of(d * each_rows, 16), each_rows)],
            lambda d, h: target.at[
                pl.ds(pl.multiple_of(d * each_rows + h * half_rows, 16), half_rows)
            ],
            some(2),
            where,
        )

    gate_ring, up_ring = weight_ring(gate_weight), weight_ring(up_weight)
    lane_half = width // 2

    def down_part(d, h):
        return down_grad.at[d, :, pl.ds(h * lane_half, lane_half)]

    down_spread = RingSpread(lambda d: down_grad.at[d], down_part, some(2), where)
    line = LineScatter(normed_one, d_normed_out, some(8), where, depth)

    def down_work(index):
        return down_part(*down_ring.places()[index])

    down_ring = RingReduce(down_part, down_work, some(6), where)
    at_end = (z == 0) | (z == depth - 1)
    share_sent, share_recv = some(2)

    def share(mine):
        part = outputs.at[:, :, core if mine else 1 - core]
        return send(part, part, share_sent, share_recv, (dp, cp ^ 1))

    input_swap.start()
    gate_swap.start()
    down_grad[dp] = down_ref[...].astype(jnp.bfloat16)
    down_spread.start()
    gain_one, gain_two, gain_query, gain_key = split_gains(gains_ref, width)
    hat_one, _ = rms_parts(tokens_ref[...].astype(jnp.float32))
    own_one[...] = (hat_one * gain_one).astype(jnp.bfloat16)
    output_own[...] = output_ref[...].astype(jnp.bfloat16)
    place_row, place_column, starts = lay_places(order_ref, lengths_ref, rows, context_count)
    query_place_ref[...] = place_row
    key_place_ref[...] = place_column
    query_start_ref[...] = starts
    pair_index = lax.broadcasted_iota(jnp.int32, (HEAD_DIM // 2, 1), 0).astype(jnp.float32)
    angles = (place_row - starts).astype(jnp.float32) * jnp.exp(
        pair_index * (-2.0 * math.log(rope_base) / HEAD_DIM)
    )
    cosine_ref[...] = jnp.cos(angles)
    sine_ref[...] = jnp.sin(angles)
    cut_columns(up_send, half_width)
    token_line.start()
    input_swap.finish_recv()
    input_ring.start()
    gate_swap.finish_recv()
    gate_ring.start()
    output_line.start()
    token_line.step(1)
    output_line.step(1)
    input_ring.forward()
    token_line.step(2)
    output_line.step(2)
    token_line.step(3)
    output_line.step(3)
    down_spread.forward()
    up_swap.start()
    output_line.finish()
    output_ring.start()
    token_line.finish()
    input_ring.finish()
    one_copy = pltpu.make_async_copy(normed_one, normed_one_out, out_sems.at[0])
    one_copy.start()
    input_copy = pltpu.make_async_copy(inputs, input_out, out_sems.at[1])
    input_copy.start()

    weights = inputs[...].reshape(width, inputs.shape[-1])

    def project(turn, carry):
        lanes = pl.ds(pl.multiple_of(turn * tile, tile), tile)
        block = normed_one[pl.ds(turn * (tile // rows), tile // rows)].reshape(tile, width)
        part = jnp.dot(block, weights, preferred_element_type=jnp.float32).T
        raw[:, lanes] = part
        cosine, sine = cosine_ref[:, lanes], sine_ref[:, lanes]
        for head in range(HEADS // KV_HEADS):
            hat, _ = head_hat(part[head * HEAD_DIM : (head + 1) * HEAD_DIM])
            queries[head * HEAD_DIM : (head + 1) * HEAD_DIM, lanes] = turn_heads(
                hat * gain_query, cosine, sine
            ).astype(jnp.bfloat16)
        hat, _ = head_hat(part[q_each : q_each + HEAD_DIM])
        key = turn_heads(hat * gain_key, cosine, sine)
        keys_up[pl.ds(pl.multiple_of(turn * tile, tile), tile)] = key.T.astype(jnp.bfloat16)
        values[:, lanes] = part[q_each + HEAD_DIM :].astype(jnp.bfloat16)
        return carry

    lax.fori_loop(0, normed_one.shape[0] * rows // tile, project, 0)
    raw_copy = pltpu.make_async_copy(raw, raw_out, out_sems.at[2])
    raw_copy.start()

    def attend(turn, carry):
        lanes = pl.ds(pl.multiple_of(turn * tile, tile), tile)
        query_place, query_start = query_place_ref[:, lanes], query_start_ref[:, lanes]

        @pl.when(turn == 1)
        def _():
            gate_ring.forward()
            cotangent_line.start()

        @pl.when(turn == 2)
        def _():
            output_ring.forward()

        @pl.when(turn == 3)
        def _():
            up_swap.finish_recv()
            up_ring.start()
            cotangent_line.step(1)

        for head in range(HEADS // KV_HEADS):
            spot = pl.ds(head * HEAD_DIM, HEAD_DIM)
            scores, allowed = score_block(
                keys_up[...], queries[spot, lanes], key_place_ref[...], query_place, query_start
            )
            top = jnp.max(scores, axis=0, keepdims=True)
            exps = jnp.exp(scores - top)
            total = jnp.sum(exps, axis=0, keepdims=True)
            total_out[pl.ds(head, 1), lanes] = top + jnp.log(total)
            probs = (exps * (1.0 / total)).astype(jnp.bfloat16)
            attended = jnp.dot(values[...], probs, preferred_element_type=jnp.float32)
            for part in range(tile // rows):
                flat_send[turn * (tile // rows) + part, spot] = attended[
                    :, part * rows : (part + 1) * rows
                ].astype(jnp.bfloat16)
        return carry

    lax.fori_loop(0, depth, attend, 0)
    flat_swap.start()
    output_ring.finish()
    share(True).start()
    cotangent_line.step(2)
    share(False).wait_recv()
    output_copy = pltpu.make_async_copy(outputs, output_out, out_sems.at[3])
    output_copy.start()
    flat_swap.finish_recv()
    flat_copy = pltpu.make_async_copy(flat_recv, flat_out, out_sems.at[4])
    flat_copy.start()
    flat = flat_recv[...].reshape(HEADS * HEAD_DIM, rows).astype(jnp.float32).T.astype(jnp.bfloat16)
    residual = tokens_ref[...].astype(jnp.float32) + jnp.dot(
        flat, outputs[...].reshape(HEADS * HEAD_DIM, width), preferred_element_type=jnp.float32
    )
    residual_out[...] = residual
    hat_two, _ = rms_parts(residual)
    own_two[...] = (hat_two * gain_two).astype(jnp.bfloat16)
    second_line.start()
    down_spread.finish()

    def lay_down(step, carry):
        lanes = pl.ds(pl.multiple_of(step * tile, tile), tile)
        down_weight[:, lanes] = (
            down_grad[:, :, lanes]
            .astype(jnp.float32)
            .reshape(down_weight.shape[0], tile)
            .astype(jnp.bfloat16)
        )
        return carry

    lax.fori_loop(0, width // tile, lay_down, 0)
    cotangent_line.step(3)
    up_ring.forward()
    gate_ring.finish()
    cotangent_line.finish()
    up_ring.finish()
    one_copy.wait()
    group_rows = context_count * rows
    parts = normed_one

    def feed(turn, carry):
        spot = near_first(turn, z, depth)
        far = jnp.abs(spot - z)

        @pl.when((turn > 0) & (far != jnp.abs(near_first(turn - 1, z, depth) - z)))
        def _():
            second_line.step(far)

        @pl.when(turn == 0)
        def _():
            second_line.keep_wait()

        second_line.arrive(spot)
        pair = pl.ds(2 * spot, 2)
        lanes = pl.ds(pl.multiple_of(spot * tile, tile), tile)
        block = normed[pair].reshape(tile, width)
        gate = jnp.dot(block, gate_weight[...], preferred_element_type=jnp.float32)
        up = jnp.dot(block, up_weight[...], preferred_element_type=jnp.float32)
        sig = 1.0 / (1.0 + jnp.exp(-gate))
        act = gate * sig
        hidden_up[:, lanes] = (act * up).T.astype(jnp.bfloat16)
        d_hidden = contract_cols(cotangent[pair].reshape(tile, width), down_weight[...])
        d_gate = (d_hidden * up * (sig * (1.0 + gate * (1.0 - sig)))).astype(jnp.bfloat16)
        d_up = (d_hidden * act).astype(jnp.bfloat16)
        d_gates[lanes] = d_gate
        d_ups[lanes] = d_up
        part = contract_cols(d_gate, gate_weight[...]) + contract_cols(d_up, up_weight[...])
        parts[pair] = part.astype(jnp.bfloat16).reshape(2, rows, width)
        line.pair(spot).start()

        @pl.when(at_end & (turn > 0))
        def _():
            line.forward(spot)

        return carry

    lax.fori_loop(0, depth, feed, 0)
    chunk = 256
    inner = depth - 1 - z
    outer = [inner, (depth - 1) * (z // 2 == 0).astype(jnp.int32), (depth - 1) * (z // 2 == 1).astype(jnp.int32)]

    def relay(index):
        @pl.when(jnp.logical_not(at_end))
        def _():
            line.forward(outer[index])

    def down_step(step, carry):
        lanes = pl.ds(pl.multiple_of(step * chunk, chunk), chunk)
        right = cotangent[:, :, lanes].reshape(group_rows, chunk)
        down_grad[:, :, lanes] = (
            jnp.dot(hidden_up[...], right, preferred_element_type=jnp.float32)
            .reshape(down_grad.shape[:2] + (chunk,))
            .astype(jnp.bfloat16)
        )
        return carry

    lax.fori_loop(0, width // chunk, down_step, 0)
    down_ring.start()
    relay(0)

    def gateup_step(step, carry):
        lanes = pl.ds(pl.multiple_of(step * chunk, chunk), chunk)
        left = normed[:, :, lanes].reshape(group_rows, chunk)
        gate_weight[lanes] = contract_rows(left, d_gates[...]).astype(jnp.bfloat16)
        up_weight[lanes] = contract_rows(left, d_ups[...]).astype(jnp.bfloat16)
        return carry

    steps = width // chunk
    lax.fori_loop(0, steps // 2, gateup_step, 0)
    relay(1)
    lax.fori_loop(steps // 2, steps, gateup_step, 0)
    relay(2)
    saves = [
        pltpu.make_async_copy(gate_weight, gateup_out.at[0], out_sems.at[0]),
        pltpu.make_async_copy(up_weight, gateup_out.at[1], out_sems.at[5]),
    ]
    for save in saves:
        save.start()
    down_ring.middle()

    second_line.finish(True)

    def forward_step(step, carry):
        lanes = pl.ds(pl.multiple_of(step * tile, tile), tile)
        normed[pl.ds(2 * step, 2)] = (
            contract_rows(hidden_up[:, lanes], down_weight[...])
            .astype(jnp.bfloat16)
            .reshape(2, rows, width)
        )
        return carry

    lax.fori_loop(0, depth, forward_step, 0)
    saves.append(pltpu.make_async_copy(normed, forward_out, out_sems.at[6]))
    saves[2].start()
    line.finish()
    down_ring.finish()
    for half in range(2):
        down_out[:, pl.ds(half * lane_half, lane_half)] = down_grad[
            dp, :, pl.ds(half * lane_half, lane_half)
        ].astype(jnp.float32)
    down_ring.finish_send()
    share(True).wait_send()
    for swap in (input_swap, gate_swap, up_swap, flat_swap):
        swap.finish_send()
    for copy in (input_copy, raw_copy, output_copy, flat_copy, *saves):
        copy.wait()


def fore(
    tokens,
    gains,
    order,
    lengths,
    attn_input,
    attn_output,
    gate_up,
    down,
    cotangent,
    data_count,
    context_count,
):
    rows, width = tokens.shape
    depth = context_count // 2
    group_rows = rows * context_count
    shard = attn_input.shape[0]
    each = attn_input.shape[1] // context_count
    hidden = gate_up.shape[1] // 2 // context_count
    q_each = HEADS // KV_HEADS * HEAD_DIM
    flat_width = HEADS * HEAD_DIM
    bf = jnp.bfloat16
    any_space = pl.BlockSpec(memory_space=pl.ANY)
    in_vmem = pl.BlockSpec(memory_space=pltpu.VMEM)
    in_smem = pl.BlockSpec(memory_space=pltpu.SMEM)
    down_rows = down.shape[0]
    shapes = [
        ((context_count, rows, width), bf, any_space),
        ((data_count, context_count, shard, each), bf, any_space),
        ((data_count, depth, 2, shard, width), bf, any_space),
        ((each, group_rows), jnp.float32, any_space),
        ((context_count, q_each, rows), bf, any_space),
        ((context_count, rows, width), bf, any_space),
        ((2, width, hidden), bf, any_space),
        ((HEADS // KV_HEADS, group_rows), jnp.float32, in_vmem),
        ((rows, width), jnp.float32, in_vmem),
        ((HEAD_DIM // 2, group_rows), jnp.float32, in_vmem),
        ((HEAD_DIM // 2, group_rows), jnp.float32, in_vmem),
        ((rows, width), jnp.float32, in_vmem),
        ((down_rows, width), jnp.float32, in_vmem),
    ]
    return pl.pallas_call(
        functools.partial(fore_kernel, 2 * rows),
        out_shape=[jax.ShapeDtypeStruct(shape, kind) for shape, kind, _ in shapes],
        in_specs=[in_vmem] * 2 + [in_smem] * 2 + [in_vmem] * 4 + [any_space],
        out_specs=[space for _, _, space in shapes],
        scratch_shapes=[
            pltpu.VMEM((context_count, shard, each), bf),
            pltpu.VMEM((shard, width), bf),
            pltpu.VMEM((context_count, shard, hidden), bf),
            pltpu.VMEM((context_count, shard, hidden), bf),
            pltpu.VMEM((group_rows, 1), jnp.int32),
            pltpu.VMEM((1, group_rows), jnp.int32),
            pltpu.VMEM((1, group_rows), jnp.int32),
            pltpu.VMEM((context_count, rows, width), bf),
            pltpu.VMEM((rows, width), bf),
            pltpu.VMEM((data_count, context_count, shard, each), bf),
            pltpu.VMEM((data_count, depth, 2, shard, width), bf),
            pltpu.VMEM((each, group_rows), jnp.float32),
            pltpu.VMEM((q_each, group_rows), bf),
            pltpu.VMEM((group_rows, HEAD_DIM), bf),
            pltpu.VMEM((HEAD_DIM, group_rows), bf),
            pltpu.VMEM((context_count, q_each, rows), bf),
            pltpu.VMEM((context_count, q_each, rows), bf),
            pltpu.VMEM((rows, width), bf),
            pltpu.VMEM((context_count, rows, width), bf),
            pltpu.VMEM((context_count, rows, width), bf),
            pltpu.VMEM((width, hidden), bf),
            pltpu.VMEM((width, hidden), bf),
            pltpu.VMEM((hidden, width), bf),
            pltpu.VMEM((hidden, group_rows), bf),
            pltpu.VMEM((group_rows, hidden), bf),
            pltpu.VMEM((group_rows, hidden), bf),
            pltpu.VMEM((data_count, down_rows, width), bf),
            pltpu.SemaphoreType.DMA((7,)),
        ]
        + LineGather.scratch(depth) * 6
        + Swap.scratch(context_count) * 4
        + RingSpread.scratch() * 5
        + LineScatter.scratch(depth, rows, width)
        + RingReduce.scratch(down_rows, width // 2)
        + [pltpu.SemaphoreType.DMA] * 2,
        compiler_params=pltpu.CompilerParams(
            collective_id=0, has_side_effects=True, vmem_limit_bytes=63 * 2**20
        ),
        name="fore",
    )(tokens, gains, order, lengths, attn_input, attn_output, gate_up, down, cotangent)


def back_kernel(
    tokens_ref,
    cotangent_ref,
    residual_ref,
    d_normed_ref,
    gains_ref,
    order_ref,
    lengths_ref,
    cosine_ref,
    sine_ref,
    total_ref,
    normed_in,
    input_in,
    output_in,
    raw_in,
    flat_in,
    forward_in,
    gateup_in,
    mixed_out,
    token_out,
    gains_out,
    output_grad_out,
    input_grad_out,
    gateup_grad_out,
    inputs,
    outputs,
    raw,
    flat,
    forwards,
    forward_sum,
    d_first,
    d_residual,
    branch,
    swap_send,
    swap_recv,
    queries,
    keys,
    keys_up,
    values_up,
    d_query,
    d_key,
    d_value,
    d_projected,
    parts,
    input_grad,
    output_sib,
    output_line,
    gateup_work,
    gain_sums,
    own_gains,
    line_gains,
    all_gains,
    key_place_ref,
    query_place_ref,
    query_start_ref,
    load_sems,
    work_sems,
    share_sems,
    output_sent,
    output_recv,
    line_sent,
    line_recv,
    all_sent,
    all_recv,
    *scratch,
):
    where = place()
    dp, cp, z, core = where
    count, rows, width = forwards.shape
    depth = count // 2
    data_count = all_gains.shape[0]
    shard = inputs.shape[2]
    tile = 2 * rows
    group_rows = count * rows
    heads = HEADS // KV_HEADS
    q_each = heads * HEAD_DIM
    flat_width = HEADS * HEAD_DIM
    score_scale = HEAD_DIM ** (-0.5)
    load_pairs = [
        (output_in, outputs),
        (raw_in, raw),
        (forward_in, forwards),
        (flat_in, flat),
        (normed_in, forwards),
        (input_in, inputs),
    ]
    loads = [
        pltpu.make_async_copy(source, target, load_sems.at[index])
        for index, (source, target) in enumerate(load_pairs)
    ]
    for index in (0, 1, 2, 3, 5):
        loads[index].start()
    greet(
        [(dp, cp ^ turn) for turn in range(1, count)]
        + [(dp ^ turn, cp) for turn in range(1, data_count)]
    )
    swap = Swap(swap_send, swap_recv, scratch[:3], where, count)
    take = iter(scratch[3:])

    def some(amount):
        return [next(take) for _ in range(amount)]

    forward_line = LineScatter(forwards, forward_sum, some(8), where, depth)
    first_line = LineScatter(parts, d_first, some(8), where, depth)
    gateup_rows = data_count * count * shard // data_count

    def in_place(part):
        spots = [(dp ^ 2, 0), (dp ^ 1, 1), (dp, 0), (dp, 1)]
        return lambda index: part(*spots[index])

    gateup_half = gateup_rows // 2

    def gateup_part(index):
        return lambda d, h: gateup_in.at[
            index, pl.ds(pl.multiple_of(d * gateup_rows + h * gateup_half, 16), gateup_half)
        ]

    def gateup_ring(index):
        return RingReduce(
            gateup_part(index), lambda spot: gateup_work.at[index, spot], some(6), where
        )

    def gateup_own(index):
        each = gateup_half // shard
        return lambda slot: gateup_work.at[
            index, 2 + slot // each, pl.ds(pl.multiple_of(slot % each * shard, 16), shard)
        ]

    def output_part(d, h):
        return outputs.at[d, pl.ds(h * (depth // 2), depth // 2), core]

    def input_part(d, h):
        half = gateup_rows // 2
        return input_grad.at[pl.ds(pl.multiple_of(d * gateup_rows + h * half, 16), half)]

    gate_ring, up_ring = gateup_ring(0), gateup_ring(1)
    output_ring = RingReduce(output_part, in_place(output_part), some(6), where)
    input_ring = RingReduce(input_part, in_place(input_part), some(6), where)

    def own_shard(source):
        return lambda slot: source.at[pl.ds(pl.multiple_of(slot * shard, 16), shard)]

    gate_swap = Swap(gateup_own(0), gateup_grad_out.at[0], some(3), where, count)
    up_swap = Swap(gateup_own(1), gateup_grad_out.at[1], some(3), where, count)
    own_rows = input_grad.at[pl.ds(pl.multiple_of(dp * gateup_rows, 16), gateup_rows)]
    input_swap = Swap(own_shard(own_rows), input_grad_out, some(3), where, count)
    works = [
        pltpu.make_async_copy(ring.part(*spot), ring.work(index), work_sems.at[4 * turn + index])
        for turn, ring in enumerate((gate_ring, up_ring))
        for index, spot in enumerate(ring.places())
    ]
    gate_ring.start()
    for work in works:
        work.start()

    def share(mine):
        return send(
            outputs.at[:, :, 1 - core], output_sib, share_sems.at[0], share_sems.at[1], (dp, cp ^ 1)
        )

    def output_hop(far, mine):
        return send(
            outputs.at[dp, z ^ far, core],
            output_line.at[z if mine else z ^ far],
            output_sent.at[far],
            output_recv.at[far],
            (dp, cp ^ (2 * far)),
        )

    at_end = (z == 0) | (z == depth - 1)
    chunk = 256

    gain_one, gain_two, gain_query, gain_key = split_gains(gains_ref, width)
    hat_two, inv_two = rms_parts(residual_ref[...])
    d_normed = d_normed_ref[...]
    own_gains[:, pl.ds(width, width)] = jnp.sum(d_normed * hat_two, axis=0, keepdims=True)
    d_res = cotangent_ref[...].astype(jnp.float32) + norm_back(
        d_normed * gain_two, hat_two, inv_two
    )
    d_residual[...] = d_res
    branch[...] = d_res.astype(jnp.bfloat16)
    loads[0].wait()
    swap_send[...] = (
        contract_cols(outputs[...].reshape(flat_width, width), branch[...])
        .astype(jnp.bfloat16)
        .reshape(count, q_each, rows)
    )
    swap.start()
    loads[2].wait()
    for spot in forward_line.order():
        forward_line.pair(spot).start()
    loads[1].wait()

    def prepare(turn, carry):
        lanes = pl.ds(pl.multiple_of(turn * tile, tile), tile)
        cosine, sine = cosine_ref[:, lanes], sine_ref[:, lanes]
        for head in range(heads):
            spot = pl.ds(head * HEAD_DIM, HEAD_DIM)
            hat, _ = head_hat(raw[spot, lanes])
            queries[spot, lanes] = turn_heads(hat * gain_query, cosine, sine).astype(
                jnp.bfloat16
            )
        hat, _ = head_hat(raw[pl.ds(q_each, HEAD_DIM), lanes])
        key = turn_heads(hat * gain_key, cosine, sine)
        keys[:, lanes] = key.astype(jnp.bfloat16)
        keys_up[lanes] = key.T.astype(jnp.bfloat16)
        values_up[lanes] = raw[pl.ds(q_each + HEAD_DIM, HEAD_DIM), lanes].T.astype(jnp.bfloat16)
        return carry

    lax.fori_loop(0, depth, prepare, 0)
    place_row, place_column, starts = lay_places(order_ref, lengths_ref, rows, count)
    query_place_ref[...] = place_row
    key_place_ref[...] = place_column
    query_start_ref[...] = starts
    d_key[...] = jnp.zeros_like(d_key)
    d_value[...] = jnp.zeros_like(d_value)
    gain_sums[...] = jnp.zeros_like(gain_sums)

    @pl.when(at_end)
    def _():
        for turn in range(depth - 1):
            forward_line.forward(far_first(turn, z, depth))

    loads[3].wait()

    def output_step(step, carry):
        lanes = pl.ds(pl.multiple_of(step * chunk, chunk), chunk)
        outputs[:, :, :, :, lanes] = (
            jnp.dot(
                flat[...].reshape(flat_width, rows),
                branch[:, lanes],
                preferred_element_type=jnp.float32,
            )
            .astype(jnp.bfloat16)
            .reshape(outputs.shape[:4] + (chunk,))
        )
        return carry

    lax.fori_loop(0, width // chunk, output_step, 0)
    share(True).start()
    for work in works:
        work.wait()
    gate_ring.middle()
    up_ring.start()
    swap.finish_recv()

    def attend(turn, carry):
        lanes = pl.ds(pl.multiple_of(turn * tile, tile), tile)
        query_place, query_start = query_place_ref[:, lanes], query_start_ref[:, lanes]

        @pl.when(jnp.logical_not(at_end) & (turn >= 1))
        def _():
            forward_line.forward(far_first(turn - 1, z, depth))

        @pl.when(turn == 1)
        def _():
            gate_ring.finish()
            gate_swap.start()

        @pl.when(turn == 3)
        def _():
            up_ring.middle()

        for head in range(heads):
            spot = pl.ds(head * HEAD_DIM, HEAD_DIM)
            scores, allowed = score_block(
                keys_up[...], queries[spot, lanes], key_place_ref[...], query_place, query_start
            )
            probs = jnp.where(allowed, jnp.exp(scores - total_ref[pl.ds(head, 1), lanes]), 0.0)
            d_out = jnp.concatenate(
                [swap_recv[2 * turn, spot], swap_recv[2 * turn + 1, spot]], axis=1
            )
            d_probs = jnp.dot(values_up[...], d_out, preferred_element_type=jnp.float32)
            delta = jnp.sum(probs * d_probs, axis=0, keepdims=True)
            d_scores = (probs * (d_probs - delta)).astype(jnp.bfloat16)
            d_query[spot, lanes] = (
                jnp.dot(keys[...], d_scores, preferred_element_type=jnp.float32) * score_scale
            )
            d_key[...] += contract_cols(queries[spot, lanes], d_scores) * score_scale
            d_value[...] += contract_cols(d_out, probs.astype(jnp.bfloat16))
        return carry

    lax.fori_loop(0, depth, attend, 0)
    loads[5].wait()
    share(False).wait_recv()

    def share_step(step, carry):
        total = outputs[step, :, core].astype(jnp.float32) + output_sib[step].astype(jnp.float32)
        outputs[step, :, core] = total.astype(jnp.bfloat16)
        return carry

    lax.fori_loop(0, data_count, share_step, 0)
    output_ring.start()

    def feed(turn, carry):
        spot = far_first(turn, z, depth)
        lanes = pl.ds(pl.multiple_of(spot * tile, tile), tile)
        cosine, sine = cosine_ref[:, lanes], sine_ref[:, lanes]
        pieces = []
        for head in range(heads + 1):
            place_in = pl.ds(head * HEAD_DIM, HEAD_DIM)
            hat, inverse = head_hat(raw[place_in, lanes])
            if head < heads:
                turned = turn_heads(d_query[place_in, lanes], cosine, -sine)
                gain, kind = gain_query, 0
            else:
                turned = turn_heads(d_key[:, lanes], cosine, -sine)
                gain, kind = gain_key, 1
            gain_sums[kind] += turned * hat
            scaled = turned * gain
            pieces.append(
                inverse * (scaled - hat * jnp.mean(scaled * hat, axis=0, keepdims=True))
            )
        pieces.append(d_value[:, lanes])
        block = jnp.concatenate(pieces, axis=0).T.astype(jnp.bfloat16)
        d_projected[lanes] = block
        part = contract_cols(block, inputs[...].reshape(width, block.shape[1]))
        parts[pl.ds(2 * spot, 2)] = part.astype(jnp.bfloat16).reshape(2, rows, width)
        first_line.pair(spot).start()

        @pl.when(at_end & (turn < depth - 1))
        def _():
            first_line.forward(spot)

        return carry

    lax.fori_loop(0, depth, feed, 0)
    up_ring.finish()
    up_swap.start()
    forward_line.finish()
    loads[4].start()
    mixed_out[...] = (residual_ref[...] + forward_sum[...]).astype(jnp.bfloat16)
    for kind in range(2):
        own_gains[:, pl.ds(2 * width + kind * HEAD_DIM, HEAD_DIM)] = jnp.sum(
            gain_sums[kind].T, axis=0, keepdims=True
        )
    @pl.when(jnp.logical_not(at_end))
    def _():
        first_line.forward(far_first(0, z, depth))

    loads[4].wait()

    def input_step(step, carry):
        lanes = pl.ds(pl.multiple_of(step * chunk, chunk), chunk)
        left = forwards[:, :, lanes].reshape(group_rows, chunk)
        input_grad[lanes] = contract_rows(left, d_projected[...]).astype(jnp.bfloat16)
        return carry

    lax.fori_loop(0, width // chunk, input_step, 0)
    input_ring.start()
    output_ring.middle()

    @pl.when(jnp.logical_not(at_end))
    def _():
        first_line.forward(far_first(1, z, depth))

    input_ring.middle()

    @pl.when(jnp.logical_not(at_end))
    def _():
        first_line.forward(far_first(2, z, depth))

    input_ring.finish()
    input_swap.start()
    first_line.finish()
    hat_one, inv_one = rms_parts(tokens_ref[...].astype(jnp.float32))
    d_one = d_first[...]
    own_gains[:, pl.ds(0, width)] = jnp.sum(d_one * hat_one, axis=0, keepdims=True)
    line_gains[cp] = own_gains[...]
    for turn in range(1, count):
        send(
            own_gains, line_gains.at[cp], line_sent.at[turn], line_recv.at[turn], (dp, cp ^ turn)
        ).start()
    output_ring.finish()
    for far in range(1, depth):
        output_hop(far, True).start()
    token_out[...] = d_residual[...] + norm_back(d_one * gain_one, hat_one, inv_one)
    for turn in range(1, count):
        copy = send(
            own_gains,
            line_gains.at[cp ^ turn],
            line_sent.at[turn],
            line_recv.at[turn],
            (dp, cp ^ turn),
        )
        copy.wait_recv()
        copy.wait_send()
    all_gains[dp] = jnp.sum(line_gains[...], axis=0)
    for turn in range(1, data_count):
        send(
            all_gains.at[dp],
            all_gains.at[dp],
            all_sent.at[turn],
            all_recv.at[turn],
            (dp ^ turn, cp),
        ).start()
    for turn in range(1, data_count):
        copy = send(
            all_gains.at[dp],
            all_gains.at[dp ^ turn],
            all_sent.at[turn],
            all_recv.at[turn],
            (dp ^ turn, cp),
        )
        copy.wait_recv()
        copy.wait_send()
    gain_total = jnp.sum(all_gains[...], axis=0)
    lanes = gains_out.shape[1]
    for line in range(gains_out.shape[0]):
        gains_out[line : line + 1] = gain_total[:, line * lanes : (line + 1) * lanes]
    total = outputs[dp, z, core].astype(jnp.float32)
    for far in range(1, depth):
        output_hop(far, False).wait_recv()
        total = total + output_line[z ^ far].astype(jnp.float32)
    output_grad_out[...] = total
    for done in (input_swap, gate_swap, up_swap):
        done.finish_recv()
    for done in (swap, input_swap, gate_swap, up_swap, gate_ring, up_ring, output_ring, input_ring):
        done.finish_send()
    for far in range(1, depth):
        output_hop(far, True).wait_send()
    share(True).wait_send()


def back(
    tokens,
    cotangent,
    residual,
    d_normed,
    gains,
    order,
    lengths,
    cosine,
    sine,
    log_total,
    normed,
    inputs,
    outputs,
    raw,
    flat,
    forwards,
    gateup_grad,
    collective_id,
):
    count, rows, width = normed.shape
    depth = count // 2
    data_count = inputs.shape[0]
    shard, each = inputs.shape[2:]
    hidden = gateup_grad.shape[2]
    group_rows = count * rows
    heads = HEADS // KV_HEADS
    q_each = heads * HEAD_DIM
    flat_width = HEADS * HEAD_DIM
    gain_width = 2 * width + 2 * HEAD_DIM
    bf = jnp.bfloat16
    f32 = jnp.float32
    any_space = pl.BlockSpec(memory_space=pl.ANY)
    in_vmem = pl.BlockSpec(memory_space=pltpu.VMEM)
    in_smem = pl.BlockSpec(memory_space=pltpu.SMEM)
    return pl.pallas_call(
        back_kernel,
        out_shape=[
            jax.ShapeDtypeStruct((rows, width), bf),
            jax.ShapeDtypeStruct((rows, width), f32),
            jax.ShapeDtypeStruct(gains.shape, f32),
            jax.ShapeDtypeStruct((shard, width), f32),
            jax.ShapeDtypeStruct((count, shard, each), bf),
            jax.ShapeDtypeStruct((2, count, shard, hidden), bf),
        ],
        in_specs=[in_vmem] * 5 + [in_smem] * 2 + [in_vmem] * 3 + [any_space] * 7,
        out_specs=[in_vmem] * 4 + [any_space] * 2,
        scratch_shapes=[
            pltpu.VMEM(inputs.shape, bf),
            pltpu.VMEM(outputs.shape, bf),
            pltpu.VMEM(raw.shape, f32),
            pltpu.VMEM(flat.shape, bf),
            pltpu.VMEM(forwards.shape, bf),
            pltpu.VMEM((rows, width), f32),
            pltpu.VMEM((rows, width), f32),
            pltpu.VMEM((rows, width), f32),
            pltpu.VMEM((rows, width), bf),
            pltpu.VMEM((count, q_each, rows), bf),
            pltpu.VMEM((count, q_each, rows), bf),
            pltpu.VMEM((q_each, group_rows), bf),
            pltpu.VMEM((HEAD_DIM, group_rows), bf),
            pltpu.VMEM((group_rows, HEAD_DIM), bf),
            pltpu.VMEM((group_rows, HEAD_DIM), bf),
            pltpu.VMEM((q_each, group_rows), f32),
            pltpu.VMEM((HEAD_DIM, group_rows), f32),
            pltpu.VMEM((HEAD_DIM, group_rows), f32),
            pltpu.VMEM((group_rows, each), bf),
            pltpu.VMEM(forwards.shape, bf),
            pltpu.VMEM((width, each), bf),
            pltpu.VMEM((data_count, depth, shard, width), bf),
            pltpu.VMEM((depth, shard, width), bf),
            pltpu.VMEM((2, 4, count * shard // 2, hidden), bf),
            pltpu.VMEM((2, HEAD_DIM, 2 * rows), f32),
            pltpu.VMEM((1, gain_width), f32),
            pltpu.VMEM((count, 1, gain_width), f32),
            pltpu.VMEM((data_count, 1, gain_width), f32),
            pltpu.VMEM((group_rows, 1), jnp.int32),
            pltpu.VMEM((1, group_rows), jnp.int32),
            pltpu.VMEM((1, group_rows), jnp.int32),
            pltpu.SemaphoreType.DMA((6,)),
            pltpu.SemaphoreType.DMA((8,)),
            pltpu.SemaphoreType.DMA((2,)),
            pltpu.SemaphoreType.DMA((depth,)),
            pltpu.SemaphoreType.DMA((depth,)),
            pltpu.SemaphoreType.DMA((count,)),
            pltpu.SemaphoreType.DMA((count,)),
            pltpu.SemaphoreType.DMA((data_count,)),
            pltpu.SemaphoreType.DMA((data_count,)),
        ]
        + Swap.scratch(count)
        + LineScatter.scratch(depth, rows, width) * 2
        + RingReduce.scratch(count * shard // 2, hidden) * 2
        + RingReduce.scratch(depth // 2, shard, width)
        + RingReduce.scratch(count * shard // 2, each)
        + Swap.scratch(count) * 3,
        compiler_params=pltpu.CompilerParams(
            collective_id=collective_id, has_side_effects=True, vmem_limit_bytes=63 * 2**20
        ),
        name="back",
    )(
        tokens,
        cotangent,
        residual,
        d_normed,
        gains,
        order,
        lengths,
        cosine,
        sine,
        log_total,
        normed,
        inputs,
        outputs,
        raw,
        flat,
        forwards,
        gateup_grad,
    )


def update_kernel(
    data_count,
    gateup_grad,
    input_grad,
    output_grad,
    down_grad,
    gains_grad,
    *refs,
):
    states, results = refs[:15], refs[15:30]
    scratch = refs[30]
    input_full = refs[31]
    context_count = gateup_grad.shape[1]
    piece = gateup_grad.shape[3] // data_count
    half = scratch.shape[1] // 2
    for side in range(2):
        for group in range(data_count):
            scratch[:, pl.ds(side * half + group * context_count * piece, context_count * piece)] = (
                jnp.concatenate(
                    [
                        gateup_grad[side, head, :, pl.ds(group * piece, piece)]
                        for head in range(context_count)
                    ],
                    axis=1,
                ).astype(jnp.float32)
            )
    q_each = HEADS // KV_HEADS * HEAD_DIM
    for start, size in ((0, q_each), (q_each, HEAD_DIM), (q_each + HEAD_DIM, HEAD_DIM)):
        input_full[:, pl.ds(start * context_count, size * context_count)] = jnp.concatenate(
            [input_grad[head, :, pl.ds(start, size)] for head in range(context_count)], axis=1
        ).astype(jnp.float32)
    jobs = (
        (input_full, rate_input, weight_decay),
        (output_grad, rate_output, weight_decay),
        (scratch, rate_gateup, weight_decay),
        (down_grad, rate_down, weight_decay),
        (gains_grad, rate_gains, 0.0),
    )
    for index, (gradient, rate, decay) in enumerate(jobs):
        weight, first, second = (state[...] for state in states[3 * index : 3 * index + 3])
        for result, value in zip(
            results[3 * index : 3 * index + 3],
            adam_update(weight, first, second, gradient[...], rate, decay),
        ):
            result[...] = value


def update(gateup_grad, input_grad, output_grad, down_grad, gains_grad, states, data_count):
    parts = 3

    def rows_of(array):
        axis = array.ndim - 2
        shape = list(array.shape)
        if shape[axis] % (8 * parts) == 0:
            shape[axis] //= parts
            return pl.BlockSpec(
                tuple(shape), lambda step: tuple(step if d == axis else 0 for d in range(len(shape)))
            )
        return pl.BlockSpec(tuple(shape), lambda step: (0,) * len(shape))

    arrays = [gateup_grad, input_grad, output_grad, down_grad, gains_grad] + list(states)
    shard = states[0].shape[0] // parts
    return pl.pallas_call(
        functools.partial(update_kernel, data_count),
        grid=(parts,),
        out_shape=[jax.ShapeDtypeStruct(state.shape, jnp.float32) for state in states],
        in_specs=[rows_of(array) for array in arrays],
        out_specs=[rows_of(state) for state in states],
        scratch_shapes=[
            pltpu.VMEM((shard, states[6].shape[1]), jnp.float32),
            pltpu.VMEM((shard, states[0].shape[1]), jnp.float32),
        ],
        compiler_params=pltpu.CompilerParams(vmem_limit_bytes=56 * 2**20),
        name="update",
    )(*arrays)


def on_device_split(
    tokens,
    output_cotangent,
    sequence_lengths,
    block_order,
    attn_input,
    input_moment,
    input_square,
    attn_output,
    output_moment,
    output_square,
    gate_up,
    gateup_moment,
    gateup_square,
    down_weight,
    down_moment,
    down_square,
    norm_gains,
    gains_moment,
    gains_square,
):
    context_count = lax.axis_size("cp")
    data_count = lax.axis_size("dp")
    gain_lines = norm_gains.reshape(-1, 2 * HEAD_DIM)
    (
        normed_one,
        input_part,
        output_all,
        raw,
        flat_parts,
        forward_parts,
        gateup_grad,
        log_total,
        residual,
        cosine,
        sine,
        d_normed_two,
        grad_down,
    ) = fore(
        tokens,
        gain_lines,
        block_order,
        sequence_lengths,
        attn_input,
        attn_output,
        gate_up,
        down_weight,
        output_cotangent,
        data_count,
        context_count,
    )
    mixed, token_gradient, grad_gains, grad_output, grad_input, grad_gateup = back(
        tokens,
        output_cotangent,
        residual,
        d_normed_two,
        gain_lines,
        block_order,
        sequence_lengths,
        cosine,
        sine,
        log_total,
        normed_one,
        input_part,
        output_all,
        raw,
        flat_parts,
        forward_parts,
        gateup_grad,
        4,
    )
    states = (
        attn_input,
        input_moment,
        input_square,
        attn_output,
        output_moment,
        output_square,
        gate_up,
        gateup_moment,
        gateup_square,
        down_weight,
        down_moment,
        down_square,
        gain_lines,
        gains_moment.reshape(gain_lines.shape),
        gains_square.reshape(gain_lines.shape),
    )
    results = update(
        grad_gateup, grad_input, grad_output, grad_down, grad_gains, states, data_count
    )
    return (
        mixed,
        token_gradient,
        *results[:12],
        *(result.reshape(-1) for result in results[12:]),
    )


def solution(mesh):
    in_specs = (
        P(("dp", "cp"), None),
        P(("dp", "cp"), None),
        P("dp", None),
        P("dp", None),
        P(("dp", "cp"), None),
        P(("dp", "cp"), None),
        P(("dp", "cp"), None),
        P(("dp", "cp"), None),
        P(("dp", "cp"), None),
        P(("dp", "cp"), None),
        P(("dp", "cp"), None),
        P(("dp", "cp"), None),
        P(("dp", "cp"), None),
        P(("dp", "cp"), None),
        P(("dp", "cp"), None),
        P(("dp", "cp"), None),
        P(),
        P(),
        P(),
    )
    out_specs = (
        P(("dp", "cp"), None),
        P(("dp", "cp"), None),
        P(("dp", "cp"), None),
        P(("dp", "cp"), None),
        P(("dp", "cp"), None),
        P(("dp", "cp"), None),
        P(("dp", "cp"), None),
        P(("dp", "cp"), None),
        P(("dp", "cp"), None),
        P(("dp", "cp"), None),
        P(("dp", "cp"), None),
        P(("dp", "cp"), None),
        P(("dp", "cp"), None),
        P(("dp", "cp"), None),
        P(),
        P(),
        P(),
    )
    sizes = (mesh.shape["dp"], mesh.shape["cp"])
    body = on_device_split if sizes == (4, KV_HEADS) else on_device
    return jax.shard_map(
        body, mesh=mesh, in_specs=in_specs, out_specs=out_specs, check_vma=False
    )
```
